32 devices in a mesh: gz: 8 (over y, x, core), gy: 4 (over z).
Axes of the slice: x: 2, y: 2, z: 4, core: 2. Of those that a mesh axis runs over, the one named last changes fastest.
Arguments:
- coarse_six: float32 [64, 1024, 512], P('gz', 'gy'), may hold values from 0.1 to 10
Outputs:
- detail_seven: float32 [64, 1024, 512], P('gz', 'gy')
- coarse_seven: float32 [64, 1024, 512], P('gz', 'gy')
The draws below stay inside these ranges and needn't reach their ends.
All inputs are finite; a program needn't handle non-finite values.
Results may differ from the reference program's by a relative error of at most 0.00002.
Values sent between devices are 32-bit elements; how exact they have to be, the bound alone decides.
No kernel may reach another device: no remote copies, remote signals or barrier semaphores. Data moves between devices by JAX's collectives and lax.ppermute only.
A program may use at most 128 MiB of HBM per device.

```python
import math
import jax
import jax.numpy as jnp

NX = 512
TAP_DILATION = 32
NZ = 64
NY = 1024


def steps_of(own_key, extent, cuts, smallest, top_value):
    def one(position, parts):
        heights = jax.random.uniform(jax.random.fold_in(jax.random.fold_in(own_key, 6), position), (parts,), jnp.float32, smallest / len(cuts), top_value / len(cuts))
        return jnp.repeat(jnp.exp(heights), extent[position] // parts).reshape((-1,) + (1,) * (len(extent) - position - 1))

    loudness = one(*cuts[0])
    for cut in cuts[1:]:
        loudness = loudness * one(*cut)
    return loudness


def setup_inputs(seed: int = 0) -> dict:
    key_of = jax.random.split(jax.random.key(seed), 2)
    coarse_six = jnp.clip(jnp.exp(math.log(10.0) - 4.6051702 * jax.random.uniform(key_of[0], (NZ, NY, NX), jnp.float32) ** steps_of(key_of[0], (NZ, NY, NX), ((0, 8), (1, 4)), -0.2, 0.2)), 0.1, 10.0)
    return {"coarse_six": coarse_six}


kernel_weights = (0.0625, 0.25, 0.375, 0.25, 0.0625)


def smooth_axis(density_field, axis_ordinal):
    weighted_total = jnp.zeros_like(density_field)
    for cell_position in range(5):
        weighted_total = weighted_total + kernel_weights[cell_position] * jnp.roll(density_field, -(cell_position - 2) * TAP_DILATION, axis=axis_ordinal)
    return weighted_total


def reference(coarse_six):
    along_z = smooth_axis(coarse_six, 0)
    along_y = smooth_axis(along_z, 1)
    coarse_seven = smooth_axis(along_y, 2)
    return coarse_six - coarse_seven, coarse_seven
```

```python
import functools

import jax
import jax.numpy as jnp
from jax import lax
from jax.experimental import pallas as pl
from jax.experimental.pallas import tpu as pltpu
from jax.sharding import PartitionSpec as P

TAP_DILATION = 32
REACH = 2 * TAP_DILATION
LANES = 128
STRIP = 8
FIRST_PLANES = 3
LATER_CHUNKS = (2, 2, 1)

kernel_weights = (0.0625, 0.25, 0.375, 0.25, 0.0625)


def passed_along(x, axis, by):
    peers = lax.axis_size(axis)
    return lax.ppermute(x, axis, [(i, (i + by) % peers) for i in range(peers)])


def z_taps(plane_stack, count):
    weights = {}
    for cell_position in range(5):
        filter_reach = (cell_position - 2) * TAP_DILATION // plane_stack
        moved = -filter_reach % count
        weights[moved] = weights.get(moved, 0.0) + kernel_weights[cell_position]
    own = weights.pop(0, 0.0)
    return own, weights


def lane_of(shape):
    return lax.broadcasted_iota(jnp.int32, shape, 1)


def x_sums(strip):
    width = strip.shape[1]
    for shift in (TAP_DILATION, TAP_DILATION, width - TAP_DILATION, width - TAP_DILATION):
        strip = strip + pltpu.roll(strip, shift, 1)
    return strip


def y_sums(groups):
    for _ in range(4):
        groups = [a + b for a, b in zip(groups[:-1], groups[1:])]
    return groups


def packed_rows(rows, width):
    return rows - rows * TAP_DILATION // width


def store_packed(out_ref, strip, source, number):
    width = strip.shape[1]
    piece = number // 2
    tile = piece * TAP_DILATION // LANES
    shift = (LANES - TAP_DILATION - piece * TAP_DILATION) % LANES
    moved = source[:, tile * LANES : (tile + 1) * LANES]
    if shift:
        moved = pltpu.roll(moved, shift, 1)
    last = strip[:, width - LANES :]
    kept = lane_of(last.shape) < LANES - TAP_DILATION
    rows = pl.ds(number * STRIP, STRIP)
    out_ref[0, rows, : width - LANES] = strip[:, : width - LANES]
    out_ref[0, rows, width - LANES :] = jnp.where(kept, last, moved)


def completed(strip):
    width = strip.shape[1]
    last = strip[:, width - LANES :]
    lane = lane_of(last.shape)
    kept = lane < LANES - TAP_DILATION
    total = jnp.where(kept, last, 0.0)
    for start in range(0, width - LANES, LANES):
        total = total + strip[:, start : start + LANES]
    odd = (lane // TAP_DILATION) % 2 == 1
    total = jnp.where(odd, -total, total)
    total = total + pltpu.roll(total, 2 * TAP_DILATION, 1)
    total = total + pltpu.roll(total, TAP_DILATION, 1)
    return jnp.concatenate([strip[:, : width - LANES], jnp.where(kept, last, total)], axis=1)


def unpacked(load, rows, width, use):
    pieces = width // TAP_DILATION - 1
    for half in range(2):
        tiles = [None] * (width // LANES)
        for piece in range(pieces):
            number = 2 * piece + half
            strip = load(number)
            tile = piece * TAP_DILATION // LANES
            shift = (piece * TAP_DILATION - (LANES - TAP_DILATION)) % LANES
            moved = strip[:, width - LANES :]
            if shift:
                moved = pltpu.roll(moved, shift, 1)
            if tiles[tile] is None:
                tiles[tile] = moved
            else:
                here = lane_of(moved.shape) // TAP_DILATION == piece % (LANES // TAP_DILATION)
                tiles[tile] = jnp.where(here, moved, tiles[tile])
            use(number, completed(strip))
        use(2 * pieces + half, completed(jnp.concatenate(tiles, axis=1)))


def x_kernel(c_ref, out_ref):
    rows, width = c_ref.shape[1:]
    scale = 1.0 / 16.0
    for half in range(2):
        source = x_sums(c_ref[0, pl.ds(rows - 16 + half * STRIP, STRIP), :] * scale)
        for number in range(half, out_ref.shape[1] // STRIP, 2):
            strip = x_sums(c_ref[0, pl.ds(number * STRIP, STRIP), :] * scale)
            store_packed(out_ref, strip, source, number)


def extended_groups(before_ref, c_ref, after_ref, offset):
    groups = []
    for ref in (before_ref, c_ref, after_ref):
        for start in range(0, ref.shape[1], TAP_DILATION):
            groups.append(ref[0, pl.ds(start + offset, STRIP), :])
    return groups


def yx_kernel(before_ref, c_ref, after_ref, out_ref):
    rows, width = c_ref.shape[1:]
    per_group = TAP_DILATION // STRIP
    scale = 1.0 / 256.0
    for half in range(2):
        source = None
        for within in (per_group - 2 + half, half):
            groups = y_sums(extended_groups(before_ref, c_ref, after_ref, within * STRIP))
            strips = [x_sums(group * scale) for group in groups]
            if source is None:
                source = strips.pop()
            for group, strip in enumerate(strips):
                store_packed(out_ref, strip, source, group * per_group + within)


def weighted(weights, refs, number):
    rows = pl.ds(number * STRIP, STRIP)
    total = None
    for weight, ref in zip(weights, refs):
        term = weight * ref[0, rows, :]
        total = term if total is None else total + term
    return total


def z_kernel(weights, *refs):
    packed, (whole_ref, top_ref, bottom_ref) = refs[: len(weights)], refs[len(weights) :]
    rows, width = whole_ref.shape[1:]

    def use(number, strip):
        start = number * STRIP
        whole_ref[0, pl.ds(start, STRIP), :] = strip
        if start < REACH:
            top_ref[0, pl.ds(start, STRIP), :] = strip
        if start >= rows - REACH:
            bottom_ref[0, pl.ds(start - (rows - REACH), STRIP), :] = strip

    unpacked(lambda number: weighted(weights, packed, number), rows, width, use)


def y_kernel(before_ref, whole_ref, after_ref, c_ref, detail_ref, coarse_ref):
    scale = 1.0 / 16.0
    for within in range(TAP_DILATION // STRIP):
        groups = y_sums(extended_groups(before_ref, whole_ref, after_ref, within * STRIP))
        for group, strip in enumerate(groups):
            rows = pl.ds(group * TAP_DILATION + within * STRIP, STRIP)
            coarse = strip * scale
            coarse_ref[0, rows, :] = coarse
            detail_ref[0, rows, :] = c_ref[0, rows, :] - coarse


def last_kernel(weights, *refs):
    packed = refs[: len(weights)]
    c_ref, _, _, detail_ref, coarse_ref = refs[len(weights) :]
    rows, width = c_ref.shape[1:]

    def use(number, strip):
        where = pl.ds(number * STRIP, STRIP)
        coarse_ref[0, where, :] = strip
        detail_ref[0, where, :] = c_ref[0, where, :] - strip

    unpacked(lambda number: weighted(weights, packed, number), rows, width, use)


def plane_block(rows, width, first=0):
    return pl.BlockSpec((1, rows, width), lambda plane: (first + plane, 0, 0))


def call(kernel, name, planes, in_specs, out_specs, out_shape, args, aliases=None):
    moved = sum(planes * s.block_shape[1] * s.block_shape[2] * 4 for s in (*in_specs, *out_specs) if s.block_shape)
    return pl.pallas_call(
        kernel,
        grid=(planes,),
        in_specs=in_specs,
        out_specs=out_specs,
        out_shape=out_shape,
        input_output_aliases=aliases or {},
        compiler_params=pltpu.CompilerParams(vmem_limit_bytes=24 * 1024 * 1024),
        cost_estimate=pl.CostEstimate(flops=moved * 2, bytes_accessed=moved, transcendentals=0),
        name=name,
    )(*args)


def f32(*shape):
    return jax.ShapeDtypeStruct(shape, jnp.float32)


def shards(coarse_six):
    planes, rows, width = coarse_six.shape
    short = packed_rows(rows, width)
    own, shifts = z_taps(planes, lax.axis_size("gz"))
    weights = (own, *shifts.values())
    whole, packed, edge = (functools.partial(plane_block, n, width) for n in (rows, short, REACH))

    def along_gz(x):
        return [passed_along(x, "gz", moved) for moved in shifts]

    def halo(top, bottom):
        return passed_along(bottom, "gy", 1), passed_along(top, "gy", -1)

    first = FIRST_PLANES
    x_smooth = call(x_kernel, "smooth_x", first, [whole()], [packed()], [f32(first, short, width)], [coarse_six])[0]
    first_moved = along_gz(x_smooth)

    starts = [first]
    for size in LATER_CHUNKS:
        starts.append(starts[-1] + size)
    later_halo = halo(coarse_six[first:, :REACH], coarse_six[first:, rows - REACH :])
    sent, moved = [], []
    for start, size in zip(starts, LATER_CHUNKS):
        block = call(
            yx_kernel,
            "smooth_yx",
            size,
            [edge(start - first), whole(start), edge(start - first)],
            [packed()],
            [f32(size, short, width)],
            [later_halo[0], coarse_six, later_halo[1]],
        )[0]
        sent.append(block)
        moved.append(along_gz(block))

    along_z, top, bottom = call(
        functools.partial(z_kernel, weights),
        "smooth_z",
        first,
        [packed()] * len(weights),
        [whole(), edge(), edge()],
        [f32(first, rows, width), f32(first, REACH, width), f32(first, REACH, width)],
        [x_smooth, *first_moved],
    )
    before, after = halo(top, bottom)
    outs = call(
        y_kernel,
        "smooth_y",
        first,
        [edge(), whole(), edge(), whole()],
        [whole(), whole()],
        [f32(planes, rows, width)] * 2,
        [before, along_z, after, coarse_six],
    )
    for start, size, block, others in zip(starts, LATER_CHUNKS, sent, moved):
        outs = call(
            functools.partial(last_kernel, weights),
            "finish",
            size,
            [packed()] * len(weights) + [whole(start)] + [pl.BlockSpec(memory_space=pl.ANY)] * 2,
            [whole(start)] * 2,
            [f32(planes, rows, width)] * 2,
            [block, *others, coarse_six, *outs],
            {len(weights) + 1: 0, len(weights) + 2: 1},
        )
    return tuple(outs)


def solution(mesh):
    return jax.shard_map(
        shards,
        mesh=mesh,
        in_specs=(P("gz", "gy", None),),
        out_specs=(P("gz", "gy", None), P("gz", "gy", None)),
        check_vma=False,
    )
```

```python
import functools

import jax
import jax.numpy as jnp
from jax import lax
from jax.experimental import pallas as pl
from jax.experimental.pallas import tpu as pltpu
from jax.sharding import PartitionSpec as P

TAP_DILATION = 32
REACH = 2 * TAP_DILATION
LANES = 128
STRIP = 8
FIRST_PLANES = 3
LATER_CHUNKS = (2, 2, 1)

kernel_weights = (0.0625, 0.25, 0.375, 0.25, 0.0625)


def passed_along(x, axis, by):
    peers = lax.axis_size(axis)
    return lax.ppermute(x, axis, [(i, (i + by) % peers) for i in range(peers)])


def z_taps(plane_stack, count):
    weights = {}
    for cell_position in range(5):
        filter_reach = (cell_position - 2) * TAP_DILATION // plane_stack
        moved = -filter_reach % count
        weights[moved] = weights.get(moved, 0.0) + kernel_weights[cell_position]
    own = weights.pop(0, 0.0)
    return own, weights


def lane_of(shape):
    return lax.broadcasted_iota(jnp.int32, shape, 1)


def fill_matrix(matrix_ref):
    @pl.when(pl.program_id(0) == 0)
    def _():
        depth, width = matrix_ref.shape
        for start in range(0, depth, LANES):
            shape = (LANES, width)
            row = start + lax.broadcasted_iota(jnp.int32, shape, 0)
            offset = row - lax.broadcasted_iota(jnp.int32, shape, 1)
            offset = jnp.where(offset < 0, offset + width, offset)
            values = jnp.zeros(shape, jnp.float32)
            for cell_position in range(5):
                here = offset == (cell_position - 2) * TAP_DILATION % width
                values = jnp.where(here, kernel_weights[cell_position], values)
            matrix_ref[pl.ds(start, LANES), :] = values.astype(jnp.bfloat16)


def x_smoothed(rows, matrix):
    total = None
    for _ in range(3):
        part = rows.astype(jnp.bfloat16)
        rows = rows - part.astype(jnp.float32)
        term = jnp.dot(part, matrix, preferred_element_type=jnp.float32)
        total = term if total is None else total + term
    return total


def y_sums(groups):
    for _ in range(4):
        groups = [a + b for a, b in zip(groups[:-1], groups[1:])]
    return groups


def packed_rows(rows, width):
    return rows - rows * TAP_DILATION // width


def store_packed(out_ref, smooth):
    rows, width = smooth.shape
    kept_rows = out_ref.shape[1]
    depth = rows - kept_rows
    out_ref[0, :, : width - LANES] = smooth[:kept_rows, : width - LANES]
    kept = lane_of((depth, LANES)) < LANES - TAP_DILATION
    for piece in range(kept_rows // depth):
        tile = piece * TAP_DILATION // LANES
        shift = (LANES - TAP_DILATION - piece * TAP_DILATION) % LANES
        moved = smooth[kept_rows:, tile * LANES : (tile + 1) * LANES]
        if shift:
            moved = pltpu.roll(moved, shift, 1)
        last = smooth[piece * depth : (piece + 1) * depth, width - LANES :]
        out_ref[0, pl.ds(piece * depth, depth), width - LANES :] = jnp.where(kept, last, moved)


def completed(strip):
    width = strip.shape[1]
    last = strip[:, width - LANES :]
    lane = lane_of(last.shape)
    kept = lane < LANES - TAP_DILATION
    total = jnp.where(kept, last, 0.0)
    for start in range(0, width - LANES, LANES):
        total = total + strip[:, start : start + LANES]
    odd = (lane // TAP_DILATION) % 2 == 1
    total = jnp.where(odd, -total, total)
    total = total + pltpu.roll(total, 2 * TAP_DILATION, 1)
    total = total + pltpu.roll(total, TAP_DILATION, 1)
    return jnp.concatenate([strip[:, : width - LANES], jnp.where(kept, last, total)], axis=1)


def unpacked(load, rows, width, use):
    pieces = width // TAP_DILATION - 1
    for half in range(2):
        tiles = [None] * (width // LANES)
        for piece in range(pieces):
            number = 2 * piece + half
            strip = load(number)
            tile = piece * TAP_DILATION // LANES
            shift = (piece * TAP_DILATION - (LANES - TAP_DILATION)) % LANES
            moved = strip[:, width - LANES :]
            if shift:
                moved = pltpu.roll(moved, shift, 1)
            if tiles[tile] is None:
                tiles[tile] = moved
            else:
                here = lane_of(moved.shape) // TAP_DILATION == piece % (LANES // TAP_DILATION)
                tiles[tile] = jnp.where(here, moved, tiles[tile])
            use(number, completed(strip))
        use(2 * pieces + half, completed(jnp.concatenate(tiles, axis=1)))


def x_kernel(c_ref, out_ref, matrix_ref):
    fill_matrix(matrix_ref)
    store_packed(out_ref, x_smoothed(c_ref[0], matrix_ref[...]))


def extended_groups(before_ref, c_ref, after_ref, offset):
    groups = []
    for ref in (before_ref, c_ref, after_ref):
        for start in range(0, ref.shape[1], TAP_DILATION):
            groups.append(ref[0, pl.ds(start + offset, STRIP), :])
    return groups


def yx_kernel(before_ref, c_ref, after_ref, out_ref, matrix_ref, smooth_ref):
    fill_matrix(matrix_ref)
    for within in range(TAP_DILATION // STRIP):
        groups = y_sums(extended_groups(before_ref, c_ref, after_ref, within * STRIP))
        for group, strip in enumerate(groups):
            smooth_ref[pl.ds(group * TAP_DILATION + within * STRIP, STRIP), :] = strip * (1.0 / 16.0)
    store_packed(out_ref, x_smoothed(smooth_ref[...], matrix_ref[...]))


def weighted(weights, refs, number):
    rows = pl.ds(number * STRIP, STRIP)
    total = None
    for weight, ref in zip(weights, refs):
        term = weight * ref[0, rows, :]
        total = term if total is None else total + term
    return total


def z_kernel(weights, *refs):
    packed, (whole_ref, top_ref, bottom_ref) = refs[: len(weights)], refs[len(weights) :]
    rows, width = whole_ref.shape[1:]

    def use(number, strip):
        start = number * STRIP
        whole_ref[0, pl.ds(start, STRIP), :] = strip
        if start < REACH:
            top_ref[0, pl.ds(start, STRIP), :] = strip
        if start >= rows - REACH:
            bottom_ref[0, pl.ds(start - (rows - REACH), STRIP), :] = strip

    unpacked(lambda number: weighted(weights, packed, number), rows, width, use)


def y_kernel(before_ref, whole_ref, after_ref, c_ref, detail_ref, coarse_ref):
    scale = 1.0 / 16.0
    for within in range(TAP_DILATION // STRIP):
        groups = y_sums(extended_groups(before_ref, whole_ref, after_ref, within * STRIP))
        for group, strip in enumerate(groups):
            rows = pl.ds(group * TAP_DILATION + within * STRIP, STRIP)
            coarse = strip * scale
            coarse_ref[0, rows, :] = coarse
            detail_ref[0, rows, :] = c_ref[0, rows, :] - coarse


def last_kernel(weights, *refs):
    packed = refs[: len(weights)]
    c_ref, _, _, detail_ref, coarse_ref = refs[len(weights) :]
    rows, width = c_ref.shape[1:]

    def use(number, strip):
        where = pl.ds(number * STRIP, STRIP)
        coarse_ref[0, where, :] = strip
        detail_ref[0, where, :] = c_ref[0, where, :] - strip

    unpacked(lambda number: weighted(weights, packed, number), rows, width, use)


def plane_block(rows, width, first=0):
    return pl.BlockSpec((1, rows, width), lambda plane: (first + plane, 0, 0))


def call(kernel, name, planes, in_specs, out_specs, out_shape, args, aliases=None, scratch=(), grant=24):
    moved = sum(planes * s.block_shape[-2] * s.block_shape[-1] * 4 for s in (*in_specs, *out_specs) if s.block_shape)
    return pl.pallas_call(
        kernel,
        grid=(planes,),
        in_specs=in_specs,
        out_specs=out_specs,
        out_shape=out_shape,
        scratch_shapes=scratch,
        input_output_aliases=aliases or {},
        compiler_params=pltpu.CompilerParams(vmem_limit_bytes=grant * 1024 * 1024),
        cost_estimate=pl.CostEstimate(flops=moved * 2, bytes_accessed=moved, transcendentals=0),
        name=name,
    )(*args)


def f32(*shape):
    return jax.ShapeDtypeStruct(shape, jnp.float32)


def shards(coarse_six):
    planes, rows, width = coarse_six.shape
    short = packed_rows(rows, width)
    own, shifts = z_taps(planes, lax.axis_size("gz"))
    weights = (own, *shifts.values())
    whole, packed, edge = (functools.partial(plane_block, n, width) for n in (rows, short, REACH))

    def along_gz(x):
        return [passed_along(x, "gz", moved) for moved in shifts]

    def halo(top, bottom):
        return passed_along(bottom, "gy", 1), passed_along(top, "gy", -1)

    first = FIRST_PLANES
    matrix = pltpu.VMEM((width, width), jnp.bfloat16)
    x_smooth = call(
        x_kernel,
        "smooth_x",
        first,
        [whole()],
        [packed()],
        [f32(first, short, width)],
        [coarse_six],
        scratch=[matrix],
        grant=60,
    )[0]
    first_moved = along_gz(x_smooth)

    starts = [first]
    for size in LATER_CHUNKS:
        starts.append(starts[-1] + size)
    later_halo = halo(coarse_six[first:, :REACH], coarse_six[first:, rows - REACH :])
    sent, moved = [], []
    for start, size in zip(starts, LATER_CHUNKS):
        block = call(
            yx_kernel,
            "smooth_yx",
            size,
            [edge(start - first), whole(start), edge(start - first)],
            [packed()],
            [f32(size, short, width)],
            [later_halo[0], coarse_six, later_halo[1]],
            scratch=[matrix, pltpu.VMEM((rows, width), jnp.float32)],
        )[0]
        sent.append(block)
        moved.append(along_gz(block))

    along_z, top, bottom = call(
        functools.partial(z_kernel, weights),
        "smooth_z",
        first,
        [packed()] * len(weights),
        [whole(), edge(), edge()],
        [f32(first, rows, width), f32(first, REACH, width), f32(first, REACH, width)],
        [x_smooth, *first_moved],
    )
    before, after = halo(top, bottom)
    outs = call(
        y_kernel,
        "smooth_y",
        first,
        [edge(), whole(), edge(), whole()],
        [whole(), whole()],
        [f32(planes, rows, width)] * 2,
        [before, along_z, after, coarse_six],
    )
    for start, size, block, others in zip(starts, LATER_CHUNKS, sent, moved):
        outs = call(
            functools.partial(last_kernel, weights),
            "finish",
            size,
            [packed()] * len(weights) + [whole(start)] + [pl.BlockSpec(memory_space=pl.ANY)] * 2,
            [whole(start)] * 2,
            [f32(planes, rows, width)] * 2,
            [block, *others, coarse_six, *outs],
            {len(weights) + 1: 0, len(weights) + 2: 1},
        )
    return tuple(outs)


def solution(mesh):
    return jax.shard_map(
        shards,
        mesh=mesh,
        in_specs=(P("gz", "gy", None),),
        out_specs=(P("gz", "gy", None), P("gz", "gy", None)),
        check_vma=False,
    )
```

```python
import functools

import jax
import jax.numpy as jnp
from jax import lax
from jax.experimental import pallas as pl
from jax.experimental.pallas import tpu as pltpu
from jax.sharding import PartitionSpec as P

TAP_DILATION = 32
REACH = 2 * TAP_DILATION
LANES = 128
STRIP = 8
FIRST_PLANES = 3
LATER_GROUPS = ((2,), (2, 1))

kernel_weights = (0.0625, 0.25, 0.375, 0.25, 0.0625)


def passed_along(x, axis, by):
    peers = lax.axis_size(axis)
    return lax.ppermute(x, axis, [(i, (i + by) % peers) for i in range(peers)])


def z_taps(plane_stack, count):
    weights = {}
    for cell_position in range(5):
        filter_reach = (cell_position - 2) * TAP_DILATION // plane_stack
        moved = -filter_reach % count
        weights[moved] = weights.get(moved, 0.0) + kernel_weights[cell_position]
    own = weights.pop(0, 0.0)
    return own, weights


def lane_of(shape):
    return lax.broadcasted_iota(jnp.int32, shape, 1)


def fill_matrix(matrix_ref):
    @pl.when(pl.program_id(0) == 0)
    def _():
        depth, width = matrix_ref.shape
        for start in range(0, depth, LANES):
            shape = (LANES, width)
            row = start + lax.broadcasted_iota(jnp.int32, shape, 0)
            offset = row - lax.broadcasted_iota(jnp.int32, shape, 1)
            offset = jnp.where(offset < 0, offset + width, offset)
            values = jnp.zeros(shape, jnp.float32)
            for cell_position in range(5):
                here = offset == (cell_position - 2) * TAP_DILATION % width
                values = jnp.where(here, kernel_weights[cell_position], values)
            matrix_ref[pl.ds(start, LANES), :] = values.astype(jnp.bfloat16)


def x_smoothed(rows, matrix):
    total = None
    for _ in range(3):
        part = rows.astype(jnp.bfloat16)
        rows = rows - part.astype(jnp.float32)
        term = jnp.dot(part, matrix, preferred_element_type=jnp.float32)
        total = term if total is None else total + term
    return total


def y_sums(groups):
    for _ in range(4):
        groups = [a + b for a, b in zip(groups[:-1], groups[1:])]
    return groups


def packed_rows(rows, width):
    return rows - rows * TAP_DILATION // width


def store_packed(out_ref, smooth):
    rows, width = smooth.shape
    kept_rows = out_ref.shape[1]
    depth = rows - kept_rows
    out_ref[0, :, : width - LANES] = smooth[:kept_rows, : width - LANES]
    kept = lane_of((depth, LANES)) < LANES - TAP_DILATION
    for piece in range(kept_rows // depth):
        tile = piece * TAP_DILATION // LANES
        shift = (LANES - TAP_DILATION - piece * TAP_DILATION) % LANES
        moved = smooth[kept_rows:, tile * LANES : (tile + 1) * LANES]
        if shift:
            moved = pltpu.roll(moved, shift, 1)
        last = smooth[piece * depth : (piece + 1) * depth, width - LANES :]
        out_ref[0, pl.ds(piece * depth, depth), width - LANES :] = jnp.where(kept, last, moved)


def completed(strip):
    width = strip.shape[1]
    last = strip[:, width - LANES :]
    lane = lane_of(last.shape)
    kept = lane < LANES - TAP_DILATION
    total = jnp.where(kept, last, 0.0)
    for start in range(0, width - LANES, LANES):
        total = total + strip[:, start : start + LANES]
    odd = (lane // TAP_DILATION) % 2 == 1
    total = jnp.where(odd, -total, total)
    total = total + pltpu.roll(total, 2 * TAP_DILATION, 1)
    total = total + pltpu.roll(total, TAP_DILATION, 1)
    return jnp.concatenate([strip[:, : width - LANES], jnp.where(kept, last, total)], axis=1)


def unpacked(load, rows, width, use):
    pieces = width // TAP_DILATION - 1
    for half in range(2):
        tiles = [None] * (width // LANES)
        for piece in range(pieces):
            number = 2 * piece + half
            strip = load(number)
            tile = piece * TAP_DILATION // LANES
            shift = (piece * TAP_DILATION - (LANES - TAP_DILATION)) % LANES
            moved = strip[:, width - LANES :]
            if shift:
                moved = pltpu.roll(moved, shift, 1)
            if tiles[tile] is None:
                tiles[tile] = moved
            else:
                here = lane_of(moved.shape) // TAP_DILATION == piece % (LANES // TAP_DILATION)
                tiles[tile] = jnp.where(here, moved, tiles[tile])
            use(number, completed(strip))
        use(2 * pieces + half, completed(jnp.concatenate(tiles, axis=1)))


def x_kernel(c_ref, out_ref, matrix_ref):
    fill_matrix(matrix_ref)
    store_packed(out_ref, x_smoothed(c_ref[0], matrix_ref[...]))


def extended_groups(before_ref, c_ref, after_ref, offset):
    groups = []
    for ref in (before_ref, c_ref, after_ref):
        for start in range(0, ref.shape[1], TAP_DILATION):
            groups.append(ref[0, pl.ds(start + offset, STRIP), :])
    return groups


def yx_kernel(before_ref, c_ref, after_ref, out_ref, matrix_ref, smooth_ref):
    fill_matrix(matrix_ref)
    for within in range(TAP_DILATION // STRIP):
        groups = y_sums(extended_groups(before_ref, c_ref, after_ref, within * STRIP))
        for group, strip in enumerate(groups):
            smooth_ref[pl.ds(group * TAP_DILATION + within * STRIP, STRIP), :] = strip * (1.0 / 16.0)
    store_packed(out_ref, x_smoothed(smooth_ref[...], matrix_ref[...]))


def weighted(weights, refs, number):
    rows = pl.ds(number * STRIP, STRIP)
    total = None
    for weight, ref in zip(weights, refs):
        term = weight * ref[0, rows, :]
        total = term if total is None else total + term
    return total


def z_kernel(weights, *refs):
    packed, (whole_ref, top_ref, bottom_ref) = refs[: len(weights)], refs[-3:]
    rows, width = whole_ref.shape[1:]

    def use(number, strip):
        start = number * STRIP
        whole_ref[0, pl.ds(start, STRIP), :] = strip
        if start < REACH:
            top_ref[0, pl.ds(start, STRIP), :] = strip
        if start >= rows - REACH:
            bottom_ref[0, pl.ds(start - (rows - REACH), STRIP), :] = strip

    unpacked(lambda number: weighted(weights, packed, number), rows, width, use)


def y_kernel(before_ref, whole_ref, after_ref, c_ref, detail_ref, coarse_ref):
    scale = 1.0 / 16.0
    for within in range(TAP_DILATION // STRIP):
        groups = y_sums(extended_groups(before_ref, whole_ref, after_ref, within * STRIP))
        for group, strip in enumerate(groups):
            rows = pl.ds(group * TAP_DILATION + within * STRIP, STRIP)
            coarse = strip * scale
            coarse_ref[0, rows, :] = coarse
            detail_ref[0, rows, :] = c_ref[0, rows, :] - coarse


def last_kernel(weights, *refs):
    packed = refs[: len(weights)]
    c_ref, _, _, detail_ref, coarse_ref = refs[len(weights) :]
    rows, width = c_ref.shape[1:]

    def use(number, strip):
        where = pl.ds(number * STRIP, STRIP)
        coarse_ref[0, where, :] = strip
        detail_ref[0, where, :] = c_ref[0, where, :] - strip

    unpacked(lambda number: weighted(weights, packed, number), rows, width, use)


def plane_block(rows, width, first=0):
    return pl.BlockSpec((1, rows, width), lambda plane: (first + plane, 0, 0))


def anywhere():
    return pl.BlockSpec(memory_space=pl.ANY)


def call(kernel, name, planes, in_specs, out_specs, out_shape, args, aliases=None, scratch=(), grant=24):
    moved = sum(planes * s.block_shape[-2] * s.block_shape[-1] * 4 for s in (*in_specs, *out_specs) if s.block_shape)
    return pl.pallas_call(
        kernel,
        grid=(planes,),
        in_specs=in_specs,
        out_specs=out_specs,
        out_shape=out_shape,
        scratch_shapes=scratch,
        input_output_aliases=aliases or {},
        compiler_params=pltpu.CompilerParams(vmem_limit_bytes=grant * 1024 * 1024),
        cost_estimate=pl.CostEstimate(flops=moved * 2, bytes_accessed=moved, transcendentals=0),
        name=name,
    )(*args)


def f32(*shape):
    return jax.ShapeDtypeStruct(shape, jnp.float32)


def shards(coarse_six):
    planes, rows, width = coarse_six.shape
    short = packed_rows(rows, width)
    own, shifts = z_taps(planes, lax.axis_size("gz"))
    weights = (own, *shifts.values())
    whole, packed, edge = (functools.partial(plane_block, n, width) for n in (rows, short, REACH))

    def along_gz(x):
        return [passed_along(x, "gz", moved) for moved in shifts]

    def halo(top, bottom):
        return passed_along(bottom, "gy", 1), passed_along(top, "gy", -1)

    first = FIRST_PLANES
    matrix = pltpu.VMEM((width, width), jnp.bfloat16)
    first_block = call(
        x_kernel,
        "smooth_x",
        first,
        [whole()],
        [packed()],
        [f32(first, short, width)],
        [coarse_six],
        scratch=[matrix],
        grant=60,
    )[0]
    first_block, ready = lax.optimization_barrier((first_block, coarse_six))
    first_moved = along_gz(first_block)

    def edges(source, start, stop):
        return halo(source[start:stop, :REACH], source[start:stop, rows - REACH :])

    def smooth_yx(near, start, offset, size):
        block = call(
            yx_kernel,
            "smooth_yx",
            size,
            [edge(offset), whole(start + offset), edge(offset)],
            [packed()],
            [f32(size, short, width)],
            [near[0], coarse_six, near[1]],
            scratch=[matrix, pltpu.VMEM((rows, width), jnp.float32)],
        )[0]
        return block

    later_chunks, later_sent = [], []
    start = first
    near = edges(ready, start, start + sum(LATER_GROUPS[0]))
    for number, sizes in enumerate(LATER_GROUPS):
        stop = start + sum(sizes)
        offset = 0
        for size in sizes:
            block = smooth_yx(near, start, offset, size)
            later_chunks.append((start + offset, size))
            later_sent.append((block, *along_gz(block)))
            offset += size
        if number == 0:
            *near, ready = lax.optimization_barrier((*near, ready))
            block, *first_moved = lax.optimization_barrier((block, *first_moved))
            along_z, top, bottom = call(
                functools.partial(z_kernel, weights),
                "smooth_z",
                first,
                [packed()] * len(weights),
                [whole(), edge(), edge()],
                [f32(first, rows, width), f32(first, REACH, width), f32(first, REACH, width)],
                [first_block, *first_moved],
            )
            sides = halo(top, bottom)
        if number + 1 < len(LATER_GROUPS):
            near = edges(ready, stop, stop + sum(LATER_GROUPS[number + 1]))
            *near, along_z, ready = lax.optimization_barrier((*near, along_z, ready))
        start = stop

    block, *sides = lax.optimization_barrier((block, *sides))
    outs = call(
        y_kernel,
        "smooth_y",
        first,
        [edge(), whole(), edge(), whole()],
        [whole(), whole()],
        [f32(planes, rows, width)] * 2,
        [sides[0], along_z, sides[1], coarse_six],
    )
    for (start, size), blocks in zip(later_chunks, later_sent):
        outs, blocks = lax.optimization_barrier((outs, blocks))
        outs = call(
            functools.partial(last_kernel, weights),
            "finish",
            size,
            [packed()] * len(weights) + [whole(start)] + [anywhere()] * 2,
            [whole(start)] * 2,
            [f32(planes, rows, width)] * 2,
            [*blocks, coarse_six, *outs],
            {len(weights) + 1: 0, len(weights) + 2: 1},
        )
    return tuple(outs)


def solution(mesh):
    return jax.shard_map(
        shards,
        mesh=mesh,
        in_specs=(P("gz", "gy", None),),
        out_specs=(P("gz", "gy", None), P("gz", "gy", None)),
        check_vma=False,
    )
```

```python
import functools

import jax
import jax.numpy as jnp
from jax import lax
from jax.experimental import pallas as pl
from jax.experimental.pallas import tpu as pltpu
from jax.sharding import PartitionSpec as P

TAP_DILATION = 32
REACH = 2 * TAP_DILATION
LANES = 128
STRIP = 8
FIRST_CHUNKS = (1, 2)
LATER_GROUPS = ((2,), (2, 1))

kernel_weights = (0.0625, 0.25, 0.375, 0.25, 0.0625)


def passed_along(x, axis, by):
    peers = lax.axis_size(axis)
    return lax.ppermute(x, axis, [(i, (i + by) % peers) for i in range(peers)])


def z_taps(plane_stack, count):
    weights = {}
    for cell_position in range(5):
        filter_reach = (cell_position - 2) * TAP_DILATION // plane_stack
        moved = -filter_reach % count
        weights[moved] = weights.get(moved, 0.0) + kernel_weights[cell_position]
    own = weights.pop(0, 0.0)
    return own, weights


def lane_of(shape):
    return lax.broadcasted_iota(jnp.int32, shape, 1)


def fill_matrix(matrix_ref):
    @pl.when(pl.program_id(0) == 0)
    def _():
        depth, width = matrix_ref.shape
        for start in range(0, depth, LANES):
            shape = (LANES, width)
            row = start + lax.broadcasted_iota(jnp.int32, shape, 0)
            offset = row - lax.broadcasted_iota(jnp.int32, shape, 1)
            offset = jnp.where(offset < 0, offset + width, offset)
            values = jnp.zeros(shape, jnp.float32)
            for cell_position in range(5):
                here = offset == (cell_position - 2) * TAP_DILATION % width
                values = jnp.where(here, kernel_weights[cell_position], values)
            matrix_ref[pl.ds(start, LANES), :] = values.astype(jnp.bfloat16)


def x_smoothed(rows, matrix):
    total = None
    for _ in range(3):
        part = rows.astype(jnp.bfloat16)
        rows = rows - part.astype(jnp.float32)
        term = jnp.dot(part, matrix, preferred_element_type=jnp.float32)
        total = term if total is None else total + term
    return total


def y_sums(groups):
    for _ in range(4):
        groups = [a + b for a, b in zip(groups[:-1], groups[1:])]
    return groups


def packed_rows(rows, width):
    return rows - rows * TAP_DILATION // width


def store_packed(out_ref, smooth):
    rows, width = smooth.shape
    kept_rows = out_ref.shape[1]
    depth = rows - kept_rows
    out_ref[0, :, : width - LANES] = smooth[:kept_rows, : width - LANES]
    kept = lane_of((depth, LANES)) < LANES - TAP_DILATION
    for piece in range(kept_rows // depth):
        tile = piece * TAP_DILATION // LANES
        shift = (LANES - TAP_DILATION - piece * TAP_DILATION) % LANES
        moved = smooth[kept_rows:, tile * LANES : (tile + 1) * LANES]
        if shift:
            moved = pltpu.roll(moved, shift, 1)
        last = smooth[piece * depth : (piece + 1) * depth, width - LANES :]
        out_ref[0, pl.ds(piece * depth, depth), width - LANES :] = jnp.where(kept, last, moved)


def completed(strip):
    width = strip.shape[1]
    last = strip[:, width - LANES :]
    lane = lane_of(last.shape)
    kept = lane < LANES - TAP_DILATION
    total = jnp.where(kept, last, 0.0)
    for start in range(0, width - LANES, LANES):
        total = total + strip[:, start : start + LANES]
    odd = (lane // TAP_DILATION) % 2 == 1
    total = jnp.where(odd, -total, total)
    total = total + pltpu.roll(total, 2 * TAP_DILATION, 1)
    total = total + pltpu.roll(total, TAP_DILATION, 1)
    return jnp.concatenate([strip[:, : width - LANES], jnp.where(kept, last, total)], axis=1)


def unpacked(load, rows, width, use):
    pieces = width // TAP_DILATION - 1
    for half in range(2):
        tiles = [None] * (width // LANES)
        for piece in range(pieces):
            number = 2 * piece + half
            strip = load(number)
            tile = piece * TAP_DILATION // LANES
            shift = (piece * TAP_DILATION - (LANES - TAP_DILATION)) % LANES
            moved = strip[:, width - LANES :]
            if shift:
                moved = pltpu.roll(moved, shift, 1)
            if tiles[tile] is None:
                tiles[tile] = moved
            else:
                here = lane_of(moved.shape) // TAP_DILATION == piece % (LANES // TAP_DILATION)
                tiles[tile] = jnp.where(here, moved, tiles[tile])
            use(number, completed(strip))
        use(2 * pieces + half, completed(jnp.concatenate(tiles, axis=1)))


def x_kernel(c_ref, out_ref, matrix_ref):
    fill_matrix(matrix_ref)
    store_packed(out_ref, x_smoothed(c_ref[0], matrix_ref[...]))


def extended_groups(before_ref, c_ref, after_ref, offset):
    groups = []
    for ref in (before_ref, c_ref, after_ref):
        for start in range(0, ref.shape[1], TAP_DILATION):
            groups.append(ref[0, pl.ds(start + offset, STRIP), :])
    return groups


def yx_kernel(before_ref, c_ref, after_ref, out_ref, matrix_ref, smooth_ref):
    fill_matrix(matrix_ref)
    for within in range(TAP_DILATION // STRIP):
        groups = y_sums(extended_groups(before_ref, c_ref, after_ref, within * STRIP))
        for group, strip in enumerate(groups):
            smooth_ref[pl.ds(group * TAP_DILATION + within * STRIP, STRIP), :] = strip * (1.0 / 16.0)
    store_packed(out_ref, x_smoothed(smooth_ref[...], matrix_ref[...]))


def weighted(weights, refs, number):
    rows = pl.ds(number * STRIP, STRIP)
    total = None
    for weight, ref in zip(weights, refs):
        term = weight * ref[0, rows, :]
        total = term if total is None else total + term
    return total


def z_kernel(weights, *refs):
    packed, (whole_ref, top_ref, bottom_ref) = refs[: len(weights)], refs[-3:]
    rows, width = whole_ref.shape[1:]

    def use(number, strip):
        start = number * STRIP
        whole_ref[0, pl.ds(start, STRIP), :] = strip
        if start < REACH:
            top_ref[0, pl.ds(start, STRIP), :] = strip
        if start >= rows - REACH:
            bottom_ref[0, pl.ds(start - (rows - REACH), STRIP), :] = strip

    unpacked(lambda number: weighted(weights, packed, number), rows, width, use)


def y_kernel(before_ref, whole_ref, after_ref, c_ref, detail_ref, coarse_ref):
    scale = 1.0 / 16.0
    for within in range(TAP_DILATION // STRIP):
        groups = y_sums(extended_groups(before_ref, whole_ref, after_ref, within * STRIP))
        for group, strip in enumerate(groups):
            rows = pl.ds(group * TAP_DILATION + within * STRIP, STRIP)
            coarse = strip * scale
            coarse_ref[0, rows, :] = coarse
            detail_ref[0, rows, :] = c_ref[0, rows, :] - coarse


def last_kernel(weights, *refs):
    packed = refs[: len(weights)]
    c_ref, _, _, detail_ref, coarse_ref = refs[len(weights) :]
    rows, width = c_ref.shape[1:]

    def use(number, strip):
        where = pl.ds(number * STRIP, STRIP)
        coarse_ref[0, where, :] = strip
        detail_ref[0, where, :] = c_ref[0, where, :] - strip

    unpacked(lambda number: weighted(weights, packed, number), rows, width, use)


def plane_block(rows, width, first=0):
    return pl.BlockSpec((1, rows, width), lambda plane: (first + plane, 0, 0))


def anywhere():
    return pl.BlockSpec(memory_space=pl.ANY)


def call(kernel, name, planes, in_specs, out_specs, out_shape, args, aliases=None, scratch=(), grant=24):
    moved = sum(planes * s.block_shape[-2] * s.block_shape[-1] * 4 for s in (*in_specs, *out_specs) if s.block_shape)
    return pl.pallas_call(
        kernel,
        grid=(planes,),
        in_specs=in_specs,
        out_specs=out_specs,
        out_shape=out_shape,
        scratch_shapes=scratch,
        input_output_aliases=aliases or {},
        compiler_params=pltpu.CompilerParams(vmem_limit_bytes=grant * 1024 * 1024),
        cost_estimate=pl.CostEstimate(flops=moved * 2, bytes_accessed=moved, transcendentals=0),
        name=name,
    )(*args)


def f32(*shape):
    return jax.ShapeDtypeStruct(shape, jnp.float32)


def shards(coarse_six):
    planes, rows, width = coarse_six.shape
    short = packed_rows(rows, width)
    own, shifts = z_taps(planes, lax.axis_size("gz"))
    weights = (own, *shifts.values())
    whole, packed, edge = (functools.partial(plane_block, n, width) for n in (rows, short, REACH))

    def along_gz(x):
        return [passed_along(x, "gz", moved) for moved in shifts]

    def halo(top, bottom):
        return passed_along(bottom, "gy", 1), passed_along(top, "gy", -1)

    first = sum(FIRST_CHUNKS)
    matrix = pltpu.VMEM((width, width), jnp.bfloat16)
    first_sent, start, ready = [], 0, coarse_six
    for size in FIRST_CHUNKS:
        block = call(
            x_kernel,
            "smooth_x",
            size,
            [whole(start)],
            [packed()],
            [f32(size, short, width)],
            [ready],
            scratch=[matrix],
            grant=60,
        )[0]
        block, ready = lax.optimization_barrier((block, ready))
        first_sent.append((start, size, block, along_gz(block)))
        start += size

    def edges(source, start, stop):
        return halo(source[start:stop, :REACH], source[start:stop, rows - REACH :])

    def smooth_yx(near, start, offset, size):
        block = call(
            yx_kernel,
            "smooth_yx",
            size,
            [edge(offset), whole(start + offset), edge(offset)],
            [packed()],
            [f32(size, short, width)],
            [near[0], coarse_six, near[1]],
            scratch=[matrix, pltpu.VMEM((rows, width), jnp.float32)],
        )[0]
        return block

    def smooth_z(sums, start, size, block, moved):
        count = len(weights)
        return call(
            functools.partial(z_kernel, weights),
            "smooth_z",
            size,
            [packed()] * count + [anywhere()] * len(sums),
            [whole(start), edge(start), edge(start)],
            [f32(first, rows, width), f32(first, REACH, width), f32(first, REACH, width)],
            [block, *moved, *sums],
            {count + at: at for at in range(len(sums))},
        )

    later_chunks, later_sent = [], []
    near = edges(ready, start, start + sum(LATER_GROUPS[0]))
    sums = smooth_z((), *first_sent[0])
    near, sums = lax.optimization_barrier((near, sums))
    for number, sizes in enumerate(LATER_GROUPS):
        stop = start + sum(sizes)
        offset = 0
        for size in sizes:
            block = smooth_yx(near, start, offset, size)
            later_chunks.append((start + offset, size))
            later_sent.append((block, *along_gz(block)))
            offset += size
        if number == 0:
            block, ready = lax.optimization_barrier((block, ready))
            for place, size, sent, moved in first_sent[1:]:
                block, *moved = lax.optimization_barrier((block, *moved))
                sums = smooth_z(sums, place, size, sent, moved)
            along_z, top, bottom = sums
            sides = halo(top, bottom)
        if number + 1 < len(LATER_GROUPS):
            near = edges(ready, stop, stop + sum(LATER_GROUPS[number + 1]))
            *near, along_z = lax.optimization_barrier((*near, along_z))
        start = stop

    block, *sides = lax.optimization_barrier((block, *sides))
    outs = call(
        y_kernel,
        "smooth_y",
        first,
        [edge(), whole(), edge(), whole()],
        [whole(), whole()],
        [f32(planes, rows, width)] * 2,
        [sides[0], along_z, sides[1], coarse_six],
    )
    for (start, size), blocks in zip(later_chunks, later_sent):
        outs, blocks = lax.optimization_barrier((outs, blocks))
        outs = call(
            functools.partial(last_kernel, weights),
            "finish",
            size,
            [packed()] * len(weights) + [whole(start)] + [anywhere()] * 2,
            [whole(start)] * 2,
            [f32(planes, rows, width)] * 2,
            [*blocks, coarse_six, *outs],
            {len(weights) + 1: 0, len(weights) + 2: 1},
        )
    return tuple(outs)


def solution(mesh):
    return jax.shard_map(
        shards,
        mesh=mesh,
        in_specs=(P("gz", "gy", None),),
        out_specs=(P("gz", "gy", None), P("gz", "gy", None)),
        check_vma=False,
    )
```

```python
import functools
import math

import jax
import jax.numpy as jnp
from jax import lax
from jax.experimental import pallas as pl
from jax.experimental.pallas import tpu as pltpu
from jax.sharding import PartitionSpec as P

TAP_DILATION = 32
REACH = 2 * TAP_DILATION
LANES = 128
STRIP = 8
UNIT_ROWS = 128
FIRST_PLANES = 3
RAW_UNITS = 2
LATER_GROUPS = (((2, 1),), ((2, 1), (1, 2)))

kernel_weights = (0.0625, 0.25, 0.375, 0.25, 0.0625)


def passed_along(x, axis, by):
    peers = lax.axis_size(axis)
    return lax.ppermute(x, axis, [(i, (i + by) % peers) for i in range(peers)])


def z_taps(plane_stack, count):
    weights = {}
    for cell_position in range(5):
        filter_reach = (cell_position - 2) * TAP_DILATION // plane_stack
        moved = -filter_reach % count
        weights[moved] = weights.get(moved, 0.0) + kernel_weights[cell_position]
    own = weights.pop(0, 0.0)
    return own, weights


def lane_of(shape):
    return lax.broadcasted_iota(jnp.int32, shape, 1)


def fill_matrix(matrix_ref):
    @pl.when(pl.program_id(0) == 0)
    def _():
        depth, width = matrix_ref.shape
        for start in range(0, depth, LANES):
            shape = (LANES, width)
            row = start + lax.broadcasted_iota(jnp.int32, shape, 0)
            offset = row - lax.broadcasted_iota(jnp.int32, shape, 1)
            offset = jnp.where(offset < 0, offset + width, offset)
            values = jnp.zeros(shape, jnp.float32)
            for cell_position in range(5):
                here = offset == (cell_position - 2) * TAP_DILATION % width
                values = jnp.where(here, kernel_weights[cell_position], values)
            matrix_ref[pl.ds(start, LANES), :] = values.astype(jnp.bfloat16)


def x_smoothed(rows, matrix):
    total = None
    for _ in range(3):
        part = rows.astype(jnp.bfloat16)
        rows = rows - part.astype(jnp.float32)
        term = jnp.dot(part, matrix, preferred_element_type=jnp.float32)
        total = term if total is None else total + term
    return total


def y_sums(groups):
    for _ in range(4):
        groups = [a + b for a, b in zip(groups[:-1], groups[1:])]
    return groups


def packed_rows(width):
    return UNIT_ROWS - UNIT_ROWS * TAP_DILATION // width


def store_packed(out_ref, place, smooth):
    rows, width = smooth.shape
    kept_rows = out_ref.shape[1]
    depth = rows - kept_rows
    out_ref[place, :, : width - LANES] = smooth[:kept_rows, : width - LANES]
    kept = lane_of((depth, LANES)) < LANES - TAP_DILATION
    for piece in range(kept_rows // depth):
        tile = piece * TAP_DILATION // LANES
        shift = (LANES - TAP_DILATION - piece * TAP_DILATION) % LANES
        moved = smooth[kept_rows:, tile * LANES : (tile + 1) * LANES]
        if shift:
            moved = pltpu.roll(moved, shift, 1)
        last = smooth[piece * depth : (piece + 1) * depth, width - LANES :]
        out_ref[place, pl.ds(piece * depth, depth), width - LANES :] = jnp.where(kept, last, moved)


def completed(strip):
    width = strip.shape[1]
    last = strip[:, width - LANES :]
    lane = lane_of(last.shape)
    kept = lane < LANES - TAP_DILATION
    total = jnp.where(kept, last, 0.0)
    for start in range(0, width - LANES, LANES):
        total = total + strip[:, start : start + LANES]
    odd = (lane // TAP_DILATION) % 2 == 1
    total = jnp.where(odd, -total, total)
    total = total + pltpu.roll(total, 2 * TAP_DILATION, 1)
    total = total + pltpu.roll(total, TAP_DILATION, 1)
    return jnp.concatenate([strip[:, : width - LANES], jnp.where(kept, last, total)], axis=1)


def unpacked(weights, refs, use):
    kept_rows, width = refs[0].shape[1:]
    depth = UNIT_ROWS - kept_rows
    tiles = [None] * (width // LANES)
    for piece in range(kept_rows // depth):
        rows = pl.ds(piece * depth, depth)
        strip = weighted(weights, [ref[0, rows, :] for ref in refs])
        tile = piece * TAP_DILATION // LANES
        shift = (piece * TAP_DILATION - (LANES - TAP_DILATION)) % LANES
        moved = strip[:, width - LANES :]
        if shift:
            moved = pltpu.roll(moved, shift, 1)
        if tiles[tile] is None:
            tiles[tile] = moved
        else:
            here = lane_of(moved.shape) // TAP_DILATION == piece % (LANES // TAP_DILATION)
            tiles[tile] = jnp.where(here, moved, tiles[tile])
        use(rows, completed(strip))
    use(pl.ds(kept_rows, depth), completed(jnp.concatenate(tiles, axis=1)))


def weighted(weights, values):
    total = None
    for weight, value in zip(weights, values):
        term = weight * value
        total = term if total is None else total + term
    return total


def x_kernel(c_ref, out_ref, matrix_ref):
    fill_matrix(matrix_ref)
    store_packed(out_ref, 0, x_smoothed(c_ref[0], matrix_ref[...]))


def extended_groups(before_ref, c_ref, after_ref, offset):
    groups = []
    for ref in (before_ref, c_ref, after_ref):
        for start in range(0, ref.shape[1], TAP_DILATION):
            groups.append(ref[0, pl.ds(start + offset, STRIP), :])
    return groups


def yx_kernel(before_ref, c_ref, after_ref, *refs):
    *out_refs, matrix_ref, smooth_ref = refs
    fill_matrix(matrix_ref)
    for within in range(TAP_DILATION // STRIP):
        groups = y_sums(extended_groups(before_ref, c_ref, after_ref, within * STRIP))
        for group, strip in enumerate(groups):
            smooth_ref[pl.ds(group * TAP_DILATION + within * STRIP, STRIP), :] = strip * (1.0 / 16.0)
    places = [(ref, place) for ref in out_refs for place in range(ref.shape[0])]
    for unit, (ref, place) in enumerate(places):
        smooth = x_smoothed(smooth_ref[pl.ds(unit * UNIT_ROWS, UNIT_ROWS), :], matrix_ref[...])
        store_packed(ref, place, smooth)


def raw_z_kernel(weights, *refs):
    raw, (whole_ref, matrix_ref) = refs[: len(weights)], refs[-2:]
    fill_matrix(matrix_ref)
    whole_ref[0] = x_smoothed(weighted(weights, [ref[0] for ref in raw]), matrix_ref[...])


def z_kernel(weights, *refs):
    whole_ref = refs[-1]

    def use(rows, strip):
        whole_ref[0, rows, :] = strip

    unpacked(weights, refs[: len(weights)], use)


def y_kernel(before_ref, whole_ref, after_ref, c_ref, detail_ref, coarse_ref):
    scale = 1.0 / 16.0
    for within in range(TAP_DILATION // STRIP):
        groups = y_sums(extended_groups(before_ref, whole_ref, after_ref, within * STRIP))
        for group, strip in enumerate(groups):
            rows = pl.ds(group * TAP_DILATION + within * STRIP, STRIP)
            coarse = strip * scale
            coarse_ref[0, rows, :] = coarse
            detail_ref[0, rows, :] = c_ref[0, rows, :] - coarse


def last_kernel(weights, *refs):
    c_ref, _, _, detail_ref, coarse_ref = refs[len(weights) :]

    def use(rows, strip):
        coarse_ref[0, rows, :] = strip
        detail_ref[0, rows, :] = c_ref[0, rows, :] - strip

    unpacked(weights, refs[: len(weights)], use)


def block_of(rows, width, first=0, depth=1):
    return pl.BlockSpec((depth, rows, width), lambda step: (first + step, 0, 0))


def anywhere():
    return pl.BlockSpec(memory_space=pl.ANY)


def call(kernel, name, steps, in_specs, out_specs, out_shape, args, aliases=None, scratch=(), grant=24):
    blocks = [spec.block_shape for spec in (*in_specs, *out_specs) if spec.block_shape]
    moved = 4 * steps * sum(math.prod(block) for block in blocks)
    return pl.pallas_call(
        kernel,
        grid=(steps,),
        in_specs=in_specs,
        out_specs=out_specs,
        out_shape=out_shape,
        scratch_shapes=scratch,
        input_output_aliases=aliases or {},
        compiler_params=pltpu.CompilerParams(vmem_limit_bytes=grant * 1024 * 1024),
        cost_estimate=pl.CostEstimate(flops=moved * 2, bytes_accessed=moved, transcendentals=0),
        name=name,
    )(*args)


def f32(*shape):
    return jax.ShapeDtypeStruct(shape, jnp.float32)


def shards(coarse_six):
    planes, rows, width = coarse_six.shape
    short = packed_rows(width)
    own, shifts = z_taps(planes, lax.axis_size("gz"))
    weights = (own, *shifts.values())
    count = len(weights)
    whole, unit, packed, edge = (functools.partial(block_of, n, width) for n in (rows, UNIT_ROWS, short, REACH))
    parts = rows // UNIT_ROWS
    units = coarse_six.reshape(planes * parts, UNIT_ROWS, width)
    matrix = pltpu.VMEM((width, width), jnp.bfloat16)
    sums_shape = f32(FIRST_PLANES * parts, UNIT_ROWS, width)

    def along_gz(x):
        return [passed_along(x, "gz", moved) for moved in shifts]

    def halo(source, start, stop):
        top, bottom = source[start:stop, :REACH], source[start:stop, rows - REACH :]
        return passed_along(bottom, "gy", 1), passed_along(top, "gy", -1)

    raw, ready = lax.optimization_barrier((units[:RAW_UNITS], units))
    raw_moved = along_gz(raw)
    first = FIRST_PLANES * parts - RAW_UNITS
    first_block = call(
        x_kernel, "smooth_x", first, [unit(RAW_UNITS)], [packed()], [f32(first, short, width)], [ready], scratch=[matrix], grant=60
    )[0]
    first_block, ready = lax.optimization_barrier((first_block, coarse_six))
    first_moved = along_gz(first_block)

    later = []
    start = FIRST_PLANES
    near = halo(ready, start, start + sum(size for size, _ in LATER_GROUPS[0]))
    sums = call(
        functools.partial(raw_z_kernel, weights),
        "smooth_zx",
        RAW_UNITS,
        [unit()] * count,
        [unit()],
        [sums_shape],
        [raw, *raw_moved],
        scratch=[matrix],
    )[0]
    near, sums = lax.optimization_barrier((near, sums))
    for number, sizes in enumerate(LATER_GROUPS):
        offset = 0
        for size, messages in sizes:
            depth = parts // messages
            blocks = call(
                yx_kernel,
                "smooth_yx",
                size,
                [edge(offset), whole(start + offset), edge(offset)],
                [packed(depth=depth)] * messages,
                [f32(size * depth, short, width)] * messages,
                [near[0], coarse_six, near[1]],
                scratch=[matrix, pltpu.VMEM((rows, width), jnp.float32)],
            )
            for message, block in enumerate(blocks):
                place = (start + offset) * parts + message * depth
                later.append((place, size * depth, (block, *along_gz(block))))
            offset += size
        start += offset
        if number == 0:
            block, ready = lax.optimization_barrier((block, ready))
            block, *first_moved = lax.optimization_barrier((block, *first_moved))
            sums = call(
                functools.partial(z_kernel, weights),
                "smooth_z",
                first,
                [packed()] * count + [anywhere()],
                [unit(RAW_UNITS)],
                [sums_shape],
                [first_block, *first_moved, sums],
                {count: 0},
            )[0]
            along_z = sums.reshape(FIRST_PLANES, rows, width)
            sides = halo(along_z, 0, FIRST_PLANES)
        if number + 1 < len(LATER_GROUPS):
            near = halo(ready, start, start + sum(size for size, _ in LATER_GROUPS[number + 1]))
            near, along_z = lax.optimization_barrier((near, along_z))

    block, sides = lax.optimization_barrier((block, sides))
    outs = call(
        y_kernel,
        "smooth_y",
        FIRST_PLANES,
        [edge(), whole(), edge(), whole()],
        [whole(), whole()],
        [f32(planes, rows, width)] * 2,
        [sides[0], along_z, sides[1], coarse_six],
    )
    outs = [out.reshape(units.shape) for out in outs]
    for place, size, blocks in later:
        outs, blocks = lax.optimization_barrier((outs, blocks))
        outs = call(
            functools.partial(last_kernel, weights),
            "finish",
            size,
            [packed()] * count + [unit(place)] + [anywhere()] * 2,
            [unit(place)] * 2,
            [f32(*units.shape)] * 2,
            [*blocks, units, *outs],
            {count + 1: 0, count + 2: 1},
        )
    return tuple(out.reshape(coarse_six.shape) for out in outs)


def solution(mesh):
    return jax.shard_map(
        shards,
        mesh=mesh,
        in_specs=(P("gz", "gy", None),),
        out_specs=(P("gz", "gy", None), P("gz", "gy", None)),
        check_vma=False,
    )
```

```python
import functools
import math

import jax
import jax.numpy as jnp
from jax import lax
from jax.experimental import pallas as pl
from jax.experimental.pallas import tpu as pltpu
from jax.sharding import PartitionSpec as P

TAP_DILATION = 32
REACH = 2 * TAP_DILATION
LANES = 128
STRIP = 8
UNIT_ROWS = 128
FIRST_PLANES = 3
RAW_UNITS = 1
LATER_GROUPS = (((2, 1),), ((2, 1), (1, 2)))

kernel_weights = (0.0625, 0.25, 0.375, 0.25, 0.0625)


def passed_along(x, axis, by):
    peers = lax.axis_size(axis)
    return lax.ppermute(x, axis, [(i, (i + by) % peers) for i in range(peers)])


def z_taps(plane_stack, count):
    weights = {}
    for cell_position in range(5):
        filter_reach = (cell_position - 2) * TAP_DILATION // plane_stack
        moved = -filter_reach % count
        weights[moved] = weights.get(moved, 0.0) + kernel_weights[cell_position]
    own = weights.pop(0, 0.0)
    return own, weights


def lane_of(shape):
    return lax.broadcasted_iota(jnp.int32, shape, 1)


def fill_matrix(matrix_ref):
    @pl.when(pl.program_id(0) == 0)
    def _():
        depth, width = matrix_ref.shape
        for start in range(0, depth, LANES):
            shape = (LANES, width)
            row = start + lax.broadcasted_iota(jnp.int32, shape, 0)
            offset = row - lax.broadcasted_iota(jnp.int32, shape, 1)
            offset = jnp.where(offset < 0, offset + width, offset)
            values = jnp.zeros(shape, jnp.float32)
            for cell_position in range(5):
                here = offset == (cell_position - 2) * TAP_DILATION % width
                values = jnp.where(here, kernel_weights[cell_position], values)
            matrix_ref[pl.ds(start, LANES), :] = values.astype(jnp.bfloat16)


def x_smoothed(rows, matrix):
    total = None
    for _ in range(3):
        part = rows.astype(jnp.bfloat16)
        rows = rows - part.astype(jnp.float32)
        term = jnp.dot(part, matrix, preferred_element_type=jnp.float32)
        total = term if total is None else total + term
    return total


def y_sums(groups):
    for _ in range(4):
        groups = [a + b for a, b in zip(groups[:-1], groups[1:])]
    return groups


def packed_rows(width):
    return UNIT_ROWS - UNIT_ROWS * TAP_DILATION // width


def store_packed(out_ref, place, smooth):
    rows, width = smooth.shape
    kept_rows = out_ref.shape[1]
    depth = rows - kept_rows
    out_ref[place, :, : width - LANES] = smooth[:kept_rows, : width - LANES]
    kept = lane_of((depth, LANES)) < LANES - TAP_DILATION
    for piece in range(kept_rows // depth):
        tile = piece * TAP_DILATION // LANES
        shift = (LANES - TAP_DILATION - piece * TAP_DILATION) % LANES
        moved = smooth[kept_rows:, tile * LANES : (tile + 1) * LANES]
        if shift:
            moved = pltpu.roll(moved, shift, 1)
        last = smooth[piece * depth : (piece + 1) * depth, width - LANES :]
        out_ref[place, pl.ds(piece * depth, depth), width - LANES :] = jnp.where(kept, last, moved)


def completed(strip):
    width = strip.shape[1]
    last = strip[:, width - LANES :]
    lane = lane_of(last.shape)
    kept = lane < LANES - TAP_DILATION
    total = jnp.where(kept, last, 0.0)
    for start in range(0, width - LANES, LANES):
        total = total + strip[:, start : start + LANES]
    odd = (lane // TAP_DILATION) % 2 == 1
    total = jnp.where(odd, -total, total)
    total = total + pltpu.roll(total, 2 * TAP_DILATION, 1)
    total = total + pltpu.roll(total, TAP_DILATION, 1)
    return jnp.concatenate([strip[:, : width - LANES], jnp.where(kept, last, total)], axis=1)


def unpacked(weights, refs, use):
    kept_rows, width = refs[0].shape[1:]
    depth = UNIT_ROWS - kept_rows
    tiles = [None] * (width // LANES)
    for piece in range(kept_rows // depth):
        rows = pl.ds(piece * depth, depth)
        strip = weighted(weights, [ref[0, rows, :] for ref in refs])
        tile = piece * TAP_DILATION // LANES
        shift = (piece * TAP_DILATION - (LANES - TAP_DILATION)) % LANES
        moved = strip[:, width - LANES :]
        if shift:
            moved = pltpu.roll(moved, shift, 1)
        if tiles[tile] is None:
            tiles[tile] = moved
        else:
            here = lane_of(moved.shape) // TAP_DILATION == piece % (LANES // TAP_DILATION)
            tiles[tile] = jnp.where(here, moved, tiles[tile])
        use(rows, completed(strip))
    use(pl.ds(kept_rows, depth), completed(jnp.concatenate(tiles, axis=1)))


def weighted(weights, values):
    total = None
    for weight, value in zip(weights, values):
        term = weight * value
        total = term if total is None else total + term
    return total


def x_kernel(first, units_ref, out_ref, read_ref, packed_ref, matrix_ref, read_sems, write_sems):
    count = out_ref.shape[0]

    def read(unit):
        return pltpu.make_async_copy(units_ref.at[first + unit], read_ref.at[unit], read_sems.at[unit])

    def write(unit):
        return pltpu.make_async_copy(packed_ref.at[unit], out_ref.at[unit], write_sems.at[unit])

    for unit in range(count):
        read(unit).start()
    fill_matrix(matrix_ref)

    @pl.loop(0, count)
    def _(unit):
        read(unit).wait()
        store_packed(packed_ref, unit, x_smoothed(read_ref[unit], matrix_ref[...]))
        write(unit).start()

    for unit in range(count):
        write(unit).wait()


def extended_groups(before_ref, c_ref, after_ref, offset):
    groups = []
    for ref in (before_ref, c_ref, after_ref):
        for start in range(0, ref.shape[1], TAP_DILATION):
            groups.append(ref[0, pl.ds(start + offset, STRIP), :])
    return groups


def yx_kernel(before_ref, c_ref, after_ref, *refs):
    *out_refs, matrix_ref, smooth_ref = refs
    fill_matrix(matrix_ref)
    for within in range(TAP_DILATION // STRIP):
        groups = y_sums(extended_groups(before_ref, c_ref, after_ref, within * STRIP))
        for group, strip in enumerate(groups):
            smooth_ref[pl.ds(group * TAP_DILATION + within * STRIP, STRIP), :] = strip * (1.0 / 16.0)
    places = [(ref, place) for ref in out_refs for place in range(ref.shape[0])]
    for unit, (ref, place) in enumerate(places):
        smooth = x_smoothed(smooth_ref[pl.ds(unit * UNIT_ROWS, UNIT_ROWS), :], matrix_ref[...])
        store_packed(ref, place, smooth)


def raw_z_kernel(weights, *refs):
    raw, (whole_ref, matrix_ref) = refs[: len(weights)], refs[-2:]
    fill_matrix(matrix_ref)
    whole_ref[0] = x_smoothed(weighted(weights, [ref[0] for ref in raw]), matrix_ref[...])


def z_kernel(weights, *refs):
    whole_ref = refs[-1]

    def use(rows, strip):
        whole_ref[0, rows, :] = strip

    unpacked(weights, refs[: len(weights)], use)


def y_kernel(before_ref, whole_ref, after_ref, c_ref, detail_ref, coarse_ref):
    scale = 1.0 / 16.0
    for within in range(TAP_DILATION // STRIP):
        groups = y_sums(extended_groups(before_ref, whole_ref, after_ref, within * STRIP))
        for group, strip in enumerate(groups):
            rows = pl.ds(group * TAP_DILATION + within * STRIP, STRIP)
            coarse = strip * scale
            coarse_ref[0, rows, :] = coarse
            detail_ref[0, rows, :] = c_ref[0, rows, :] - coarse


def last_kernel(weights, *refs):
    c_ref, _, _, detail_ref, coarse_ref = refs[len(weights) :]

    def use(rows, strip):
        coarse_ref[0, rows, :] = strip
        detail_ref[0, rows, :] = c_ref[0, rows, :] - strip

    unpacked(weights, refs[: len(weights)], use)


def block_of(rows, width, first=0, depth=1):
    return pl.BlockSpec((depth, rows, width), lambda step: (first + step, 0, 0))


def anywhere():
    return pl.BlockSpec(memory_space=pl.ANY)


def call(kernel, name, steps, in_specs, out_specs, out_shape, args, aliases=None, scratch=(), grant=24):
    blocks = [spec.block_shape for spec in (*in_specs, *out_specs) if spec.block_shape]
    moved = 4 * steps * sum(math.prod(block) for block in blocks)
    return pl.pallas_call(
        kernel,
        grid=(steps,),
        in_specs=in_specs,
        out_specs=out_specs,
        out_shape=out_shape,
        scratch_shapes=scratch,
        input_output_aliases=aliases or {},
        compiler_params=pltpu.CompilerParams(vmem_limit_bytes=grant * 1024 * 1024),
        cost_estimate=pl.CostEstimate(flops=moved * 2, bytes_accessed=moved, transcendentals=0),
        name=name,
    )(*args)


def f32(*shape):
    return jax.ShapeDtypeStruct(shape, jnp.float32)


def shards(coarse_six):
    planes, rows, width = coarse_six.shape
    short = packed_rows(width)
    own, shifts = z_taps(planes, lax.axis_size("gz"))
    weights = (own, *shifts.values())
    count = len(weights)
    whole, unit, packed, edge = (functools.partial(block_of, n, width) for n in (rows, UNIT_ROWS, short, REACH))
    parts = rows // UNIT_ROWS
    units = coarse_six.reshape(planes * parts, UNIT_ROWS, width)
    matrix = pltpu.VMEM((width, width), jnp.bfloat16)
    sums_shape = f32(FIRST_PLANES * parts, UNIT_ROWS, width)

    def along_gz(x):
        return [passed_along(x, "gz", moved) for moved in shifts]

    def halo(source, start, stop):
        top, bottom = source[start:stop, :REACH], source[start:stop, rows - REACH :]
        return passed_along(bottom, "gy", 1), passed_along(top, "gy", -1)

    raw, ready = lax.optimization_barrier((units[:RAW_UNITS], units))
    raw_moved = along_gz(raw)
    first = FIRST_PLANES * parts - RAW_UNITS
    first_block = call(
        functools.partial(x_kernel, RAW_UNITS),
        "smooth_x",
        1,
        [anywhere()],
        [anywhere()],
        [f32(first, short, width)],
        [ready],
        scratch=[
            pltpu.VMEM((first, UNIT_ROWS, width), jnp.float32),
            pltpu.VMEM((first, short, width), jnp.float32),
            matrix,
            pltpu.SemaphoreType.DMA((first,)),
            pltpu.SemaphoreType.DMA((first,)),
        ],
        grant=60,
    )[0]
    first_block, ready = lax.optimization_barrier((first_block, coarse_six))
    first_moved = along_gz(first_block)

    later = []
    start = FIRST_PLANES
    sums = call(
        functools.partial(raw_z_kernel, weights),
        "smooth_zx",
        RAW_UNITS,
        [unit()] * count,
        [unit()],
        [sums_shape],
        [raw, *raw_moved],
        scratch=[matrix],
    )[0]
    sums, ready = lax.optimization_barrier((sums, ready))
    near = halo(ready, start, start + sum(size for size, _ in LATER_GROUPS[0]))
    for number, sizes in enumerate(LATER_GROUPS):
        offset = 0
        for size, messages in sizes:
            depth = parts // messages
            blocks = call(
                yx_kernel,
                "smooth_yx",
                size,
                [edge(offset), whole(start + offset), edge(offset)],
                [packed(depth=depth)] * messages,
                [f32(size * depth, short, width)] * messages,
                [near[0], coarse_six, near[1]],
                scratch=[matrix, pltpu.VMEM((rows, width), jnp.float32)],
            )
            for message, block in enumerate(blocks):
                place = (start + offset) * parts + message * depth
                later.append((place, size * depth, (block, *along_gz(block))))
            offset += size
        start += offset
        if number == 0:
            block, ready = lax.optimization_barrier((block, ready))
            block, *first_moved = lax.optimization_barrier((block, *first_moved))
            sums = call(
                functools.partial(z_kernel, weights),
                "smooth_z",
                first,
                [packed()] * count + [anywhere()],
                [unit(RAW_UNITS)],
                [sums_shape],
                [first_block, *first_moved, sums],
                {count: 0},
            )[0]
            along_z = sums.reshape(FIRST_PLANES, rows, width)
            sides = halo(along_z, 0, FIRST_PLANES)
        if number + 1 < len(LATER_GROUPS):
            near = halo(ready, start, start + sum(size for size, _ in LATER_GROUPS[number + 1]))
            near, along_z = lax.optimization_barrier((near, along_z))

    block, sides = lax.optimization_barrier((block, sides))
    outs = call(
        y_kernel,
        "smooth_y",
        FIRST_PLANES,
        [edge(), whole(), edge(), whole()],
        [whole(), whole()],
        [f32(planes, rows, width)] * 2,
        [sides[0], along_z, sides[1], coarse_six],
    )
    outs = [out.reshape(units.shape) for out in outs]
    for place, size, blocks in later:
        outs, blocks = lax.optimization_barrier((outs, blocks))
        outs = call(
            functools.partial(last_kernel, weights),
            "finish",
            size,
            [packed()] * count + [unit(place)] + [anywhere()] * 2,
            [unit(place)] * 2,
            [f32(*units.shape)] * 2,
            [*blocks, units, *outs],
            {count + 1: 0, count + 2: 1},
        )
    return tuple(out.reshape(coarse_six.shape) for out in outs)


def solution(mesh):
    return jax.shard_map(
        shards,
        mesh=mesh,
        in_specs=(P("gz", "gy", None),),
        out_specs=(P("gz", "gy", None), P("gz", "gy", None)),
        check_vma=False,
    )
```

```python
import functools
import math

import jax
import jax.numpy as jnp
from jax import lax
from jax.experimental import pallas as pl
from jax.experimental.pallas import tpu as pltpu
from jax.sharding import PartitionSpec as P

TAP_DILATION = 32
REACH = 2 * TAP_DILATION
LANES = 128
STRIP = 8
UNIT_ROWS = 128
FIRST_PLANES = 3
LATER_GROUPS = (((2, 1),), ((2, 1), (1, 2)))

kernel_weights = (0.0625, 0.25, 0.375, 0.25, 0.0625)


def passed_along(x, axis, by):
    peers = lax.axis_size(axis)
    return lax.ppermute(x, axis, [(i, (i + by) % peers) for i in range(peers)])


def z_taps(plane_stack, count):
    weights = {}
    for cell_position in range(5):
        filter_reach = (cell_position - 2) * TAP_DILATION // plane_stack
        moved = -filter_reach % count
        weights[moved] = weights.get(moved, 0.0) + kernel_weights[cell_position]
    own = weights.pop(0, 0.0)
    return own, weights


def lane_of(shape):
    return lax.broadcasted_iota(jnp.int32, shape, 1)


def fill_matrix(matrix_ref):
    depth, width = matrix_ref.shape
    for start in range(0, depth, LANES):
        shape = (LANES, width)
        row = start + lax.broadcasted_iota(jnp.int32, shape, 0)
        offset = row - lax.broadcasted_iota(jnp.int32, shape, 1)
        offset = jnp.where(offset < 0, offset + width, offset)
        values = jnp.zeros(shape, jnp.float32)
        for cell_position in range(5):
            here = offset == (cell_position - 2) * TAP_DILATION % width
            values = jnp.where(here, kernel_weights[cell_position], values)
        matrix_ref[pl.ds(start, LANES), :] = values.astype(jnp.bfloat16)


def x_smoothed(rows, matrix):
    parts = []
    for _ in range(3):
        parts.append(rows.astype(jnp.bfloat16))
        rows = rows - parts[-1].astype(jnp.float32)
    terms = jnp.dot(jnp.concatenate(parts), matrix, preferred_element_type=jnp.float32)
    high, middle, low = jnp.split(terms, 3)
    return high + middle + low


def y_sums(groups):
    for _ in range(4):
        groups = [a + b for a, b in zip(groups[:-1], groups[1:])]
    return groups


def packed_rows(width):
    return UNIT_ROWS - UNIT_ROWS * TAP_DILATION // width


def store_packed(out_ref, place, smooth):
    rows, width = smooth.shape
    kept_rows = out_ref.shape[1]
    depth = rows - kept_rows
    out_ref[place, :, : width - LANES] = smooth[:kept_rows, : width - LANES]
    kept = lane_of((depth, LANES)) < LANES - TAP_DILATION
    for piece in range(kept_rows // depth):
        tile = piece * TAP_DILATION // LANES
        shift = (LANES - TAP_DILATION - piece * TAP_DILATION) % LANES
        moved = smooth[kept_rows:, tile * LANES : (tile + 1) * LANES]
        if shift:
            moved = pltpu.roll(moved, shift, 1)
        last = smooth[piece * depth : (piece + 1) * depth, width - LANES :]
        out_ref[place, pl.ds(piece * depth, depth), width - LANES :] = jnp.where(kept, last, moved)


def completed(strip):
    width = strip.shape[1]
    last = strip[:, width - LANES :]
    lane = lane_of(last.shape)
    kept = lane < LANES - TAP_DILATION
    total = jnp.where(kept, last, 0.0)
    for start in range(0, width - LANES, LANES):
        total = total + strip[:, start : start + LANES]
    odd = (lane // TAP_DILATION) % 2 == 1
    total = jnp.where(odd, -total, total)
    total = total + pltpu.roll(total, 2 * TAP_DILATION, 1)
    total = total + pltpu.roll(total, TAP_DILATION, 1)
    return jnp.concatenate([strip[:, : width - LANES], jnp.where(kept, last, total)], axis=1)


def unpacked(weights, refs, use):
    kept_rows, width = refs[0].shape[1:]
    depth = UNIT_ROWS - kept_rows
    tiles = [None] * (width // LANES)
    for piece in range(kept_rows // depth):
        rows = pl.ds(piece * depth, depth)
        strip = weighted(weights, [ref[0, rows, :] for ref in refs])
        tile = piece * TAP_DILATION // LANES
        shift = (piece * TAP_DILATION - (LANES - TAP_DILATION)) % LANES
        moved = strip[:, width - LANES :]
        if shift:
            moved = pltpu.roll(moved, shift, 1)
        if tiles[tile] is None:
            tiles[tile] = moved
        else:
            here = lane_of(moved.shape) // TAP_DILATION == piece % (LANES // TAP_DILATION)
            tiles[tile] = jnp.where(here, moved, tiles[tile])
        use(rows, completed(strip))
    use(pl.ds(kept_rows, depth), completed(jnp.concatenate(tiles, axis=1)))


def weighted(weights, values):
    total = None
    for weight, value in zip(weights, values):
        term = weight * value
        total = term if total is None else total + term
    return total


def x_kernel(first, units_ref, out_ref, read_ref, matrix_ref, read_sems):
    count = out_ref.shape[0]

    def read(unit):
        return pltpu.make_async_copy(units_ref.at[first + unit], read_ref.at[unit], read_sems.at[unit])

    for unit in range(count):
        read(unit).start()
    fill_matrix(matrix_ref)

    @pl.loop(0, count)
    def _(unit):
        read(unit).wait()
        store_packed(out_ref, unit, x_smoothed(read_ref[unit], matrix_ref[...]))


def extended_groups(before_ref, c_ref, after_ref, offset):
    groups = []
    for ref in (before_ref, c_ref, after_ref):
        for start in range(0, ref.shape[1], TAP_DILATION):
            groups.append(ref[0, pl.ds(start + offset, STRIP), :])
    return groups


def yx_kernel(before_ref, c_ref, after_ref, *refs):
    *out_refs, matrix_ref, smooth_ref = refs
    pl.when(pl.program_id(0) == 0)(lambda: fill_matrix(matrix_ref))
    for within in range(TAP_DILATION // STRIP):
        groups = y_sums(extended_groups(before_ref, c_ref, after_ref, within * STRIP))
        for group, strip in enumerate(groups):
            smooth_ref[pl.ds(group * TAP_DILATION + within * STRIP, STRIP), :] = strip * (1.0 / 16.0)
    places = [(ref, place) for ref in out_refs for place in range(ref.shape[0])]
    for unit, (ref, place) in enumerate(places):
        smooth = x_smoothed(smooth_ref[pl.ds(unit * UNIT_ROWS, UNIT_ROWS), :], matrix_ref[...])
        store_packed(ref, place, smooth)


def z_kernel(weights, *refs):
    whole_ref = refs[-1]

    def use(rows, strip):
        whole_ref[0, rows, :] = strip

    unpacked(weights, refs[: len(weights)], use)


def y_kernel(before_ref, whole_ref, after_ref, c_ref, detail_ref, coarse_ref):
    scale = 1.0 / 16.0
    for within in range(TAP_DILATION // STRIP):
        groups = y_sums(extended_groups(before_ref, whole_ref, after_ref, within * STRIP))
        for group, strip in enumerate(groups):
            rows = pl.ds(group * TAP_DILATION + within * STRIP, STRIP)
            coarse = strip * scale
            coarse_ref[0, rows, :] = coarse
            detail_ref[0, rows, :] = c_ref[0, rows, :] - coarse


def finish_kernel(weights, *refs):
    c_ref, _, _, detail_ref, coarse_ref = refs[len(weights) :]

    def use(rows, strip):
        coarse_ref[0, rows, :] = strip
        detail_ref[0, rows, :] = c_ref[0, rows, :] - strip

    unpacked(weights, refs[: len(weights)], use)


def last_kernel(weights, place, *refs):
    units_ref, _, _, detail_ref, coarse_ref, c_ref, results_ref, read_sem, write_sems = refs[len(weights) :]
    half = UNIT_ROWS // 2

    def write(piece, output, ref):
        rows = pl.ds(piece * half, half)
        source = results_ref.at[output, rows]
        return pltpu.make_async_copy(source, ref.at[place, rows], write_sems.at[piece, output])

    writes = [[write(piece, 0, detail_ref), write(piece, 1, coarse_ref)] for piece in range(2)]
    read = pltpu.make_async_copy(units_ref.at[place], c_ref, read_sem)
    read.start()
    read.wait()

    def use(rows, strip):
        results_ref[1, rows, :] = strip
        results_ref[0, rows, :] = c_ref[rows, :] - strip
        piece, left = divmod(rows.start + rows.size, half)
        if left == 0:
            for copy in writes[piece - 1]:
                copy.start()

    unpacked(weights, refs[: len(weights)], use)
    for copies in writes:
        for copy in copies:
            copy.wait()


def block_of(rows, width, first=0, depth=1):
    return pl.BlockSpec((depth, rows, width), lambda step: (first + step, 0, 0))


def anywhere():
    return pl.BlockSpec(memory_space=pl.ANY)


def in_vmem():
    return pl.BlockSpec(memory_space=pltpu.VMEM)


def call(kernel, name, steps, in_specs, out_specs, out_shape, args, aliases=None, scratch=(), grant=24):
    blocks = [spec.block_shape for spec in (*in_specs, *out_specs) if spec.block_shape]
    moved = 4 * max(steps, 1) * sum(math.prod(block) for block in blocks)
    return pl.pallas_call(
        kernel,
        grid=(steps,) if steps else (),
        in_specs=in_specs,
        out_specs=out_specs,
        out_shape=out_shape,
        scratch_shapes=scratch,
        input_output_aliases=aliases or {},
        compiler_params=pltpu.CompilerParams(vmem_limit_bytes=grant * 1024 * 1024),
        cost_estimate=pl.CostEstimate(flops=moved * 2, bytes_accessed=moved, transcendentals=0),
        name=name,
    )(*args)


def in_hbm(x):
    return pltpu.with_memory_space_constraint(x, pltpu.HBM)


def f32(*shape):
    return jax.ShapeDtypeStruct(shape, jnp.float32)


def shards(coarse_six):
    planes, rows, width = coarse_six.shape
    short = packed_rows(width)
    own, shifts = z_taps(planes, lax.axis_size("gz"))
    weights = (own, *shifts.values())
    count = len(weights)
    whole, unit, packed, edge = (functools.partial(block_of, n, width) for n in (rows, UNIT_ROWS, short, REACH))
    parts = rows // UNIT_ROWS
    units = coarse_six.reshape(planes * parts, UNIT_ROWS, width)
    matrix = pltpu.VMEM((width, width), jnp.bfloat16)
    sums_shape = f32(FIRST_PLANES * parts, UNIT_ROWS, width)

    def along_gz(x):
        return [passed_along(x, "gz", moved) for moved in shifts]

    def halo(source, start, stop):
        top, bottom = source[start:stop, :REACH], source[start:stop, rows - REACH :]
        return passed_along(bottom, "gy", 1), passed_along(top, "gy", -1)

    first_sent, ready, place = [], units, 0
    for size in (1, FIRST_PLANES * parts - 1):
        block = call(
            functools.partial(x_kernel, place),
            "smooth_x",
            0,
            [anywhere()],
            [in_vmem()],
            [pltpu.VMEM((size, short, width), jnp.float32)],
            [in_hbm(ready)],
            scratch=[
                pltpu.VMEM((size, UNIT_ROWS, width), jnp.float32),
                matrix,
                pltpu.SemaphoreType.DMA((size,)),
            ],
        )[0]
        block, ready = lax.optimization_barrier((block, ready))
        first_sent.append((place, size, block, along_gz(block)))
        place += size

    def smooth_z(sums, place, size, block, moved):
        return call(
            functools.partial(z_kernel, weights),
            "smooth_z",
            size,
            [packed()] * count + [anywhere()] * len(sums),
            [unit(place)],
            [sums_shape],
            [block, *moved, *sums],
            {count + at: at for at in range(len(sums))},
        )

    later = []
    start = FIRST_PLANES
    sums = smooth_z((), *first_sent[0])
    sums, ready = lax.optimization_barrier((sums, coarse_six))
    near = halo(ready, start, start + sum(size for size, _ in LATER_GROUPS[0]))
    for number, sizes in enumerate(LATER_GROUPS):
        offset = 0
        for size, messages in sizes:
            depth = parts // messages
            blocks = call(
                yx_kernel,
                "smooth_yx",
                size,
                [edge(offset), whole(start + offset), edge(offset)],
                [packed(depth=depth)] * messages,
                [f32(size * depth, short, width)] * messages,
                [near[0], in_hbm(coarse_six), near[1]],
                scratch=[matrix, pltpu.VMEM((rows, width), jnp.float32)],
            )
            for message, block in enumerate(blocks):
                place = (start + offset) * parts + message * depth
                later.append((place, size * depth, (block, *along_gz(block))))
            offset += size
        start += offset
        if number == 0:
            block, ready = lax.optimization_barrier((block, ready))
            place, size, sent, moved = first_sent[1]
            block, *moved = lax.optimization_barrier((block, *moved))
            sums = smooth_z(sums, place, size, sent, moved)[0]
            along_z = sums.reshape(FIRST_PLANES, rows, width)
            sides = halo(along_z, 0, FIRST_PLANES)
        if number + 1 < len(LATER_GROUPS):
            near = halo(ready, start, start + sum(size for size, _ in LATER_GROUPS[number + 1]))
            near, along_z = lax.optimization_barrier((near, along_z))

    block, sides = lax.optimization_barrier((block, sides))
    outs = call(
        y_kernel,
        "smooth_y",
        FIRST_PLANES,
        [edge(), whole(), edge(), whole()],
        [whole(), whole()],
        [f32(planes, rows, width)] * 2,
        [sides[0], along_z, sides[1], coarse_six],
    )
    outs = [out.reshape(units.shape) for out in outs]
    for place, size, blocks in later[:-1]:
        outs, blocks = lax.optimization_barrier((outs, blocks))
        outs = call(
            functools.partial(finish_kernel, weights),
            "finish",
            size,
            [packed()] * count + [unit(place)] + [anywhere()] * 2,
            [unit(place)] * 2,
            [f32(*units.shape)] * 2,
            [*blocks, units, *outs],
            {count + 1: 0, count + 2: 1},
        )
    place, _, blocks = later[-1]
    outs, blocks = lax.optimization_barrier((outs, blocks))
    outs = call(
        functools.partial(last_kernel, weights, place),
        "finish_last",
        0,
        [in_vmem()] * count + [anywhere()] * 3,
        [anywhere()] * 2,
        [f32(*units.shape)] * 2,
        [*blocks, units, *outs],
        {count + 1: 0, count + 2: 1},
        scratch=[
            pltpu.VMEM((UNIT_ROWS, width), jnp.float32),
            pltpu.VMEM((2, UNIT_ROWS, width), jnp.float32),
            pltpu.SemaphoreType.DMA(()),
            pltpu.SemaphoreType.DMA((2, 2)),
        ],
    )
    return tuple(out.reshape(coarse_six.shape) for out in outs)


def solution(mesh):
    return jax.shard_map(
        shards,
        mesh=mesh,
        in_specs=(P("gz", "gy", None),),
        out_specs=(P("gz", "gy", None), P("gz", "gy", None)),
        check_vma=False,
    )
```

```python
import functools
import math

import jax
import jax.numpy as jnp
from jax import lax
from jax.experimental import pallas as pl
from jax.experimental.pallas import tpu as pltpu
from jax.sharding import PartitionSpec as P

TAP_DILATION = 32
REACH = 2 * TAP_DILATION
LANES = 128
STRIP = 8
UNIT_ROWS = 128
FIRST_PLANES = 3
LATER_GROUPS = (((2, 1),), ((2, 1), (1, 2)))

kernel_weights = (0.0625, 0.25, 0.375, 0.25, 0.0625)


def passed_along(x, axis, by):
    peers = lax.axis_size(axis)
    return lax.ppermute(x, axis, [(i, (i + by) % peers) for i in range(peers)])


def z_taps(plane_stack, count):
    weights = {}
    for cell_position in range(5):
        filter_reach = (cell_position - 2) * TAP_DILATION // plane_stack
        moved = -filter_reach % count
        weights[moved] = weights.get(moved, 0.0) + kernel_weights[cell_position]
    own = weights.pop(0, 0.0)
    return own, weights


def lane_of(shape):
    return lax.broadcasted_iota(jnp.int32, shape, 1)


def x_taps():
    return {(cell_position - 2) * TAP_DILATION: kernel_weights[cell_position] for cell_position in range(5)}


def rest_taps():
    return {(cell_position - 2) * TAP_DILATION: weight for cell_position, weight in enumerate((0.125, 0.375, 0.375, 0.125))}


def pair_sums(rows):
    return (rows + pltpu.roll(rows, rows.shape[1] - TAP_DILATION, 1)) * 0.5


def fill_matrix(matrix_ref, taps):
    depth, width = matrix_ref.shape
    for start in range(0, depth, LANES):
        shape = (LANES, width)
        row = start + lax.broadcasted_iota(jnp.int32, shape, 0)
        offset = row - lax.broadcasted_iota(jnp.int32, shape, 1)
        offset = jnp.where(offset < 0, offset + width, offset)
        values = jnp.zeros(shape, jnp.float32)
        for tap, weight in taps.items():
            values = jnp.where(offset == tap % width, weight, values)
        matrix_ref[pl.ds(start, LANES), :] = values.astype(jnp.bfloat16)


def x_smoothed(rows, matrix):
    parts = []
    for _ in range(3):
        parts.append(rows.astype(jnp.bfloat16))
        rows = rows - parts[-1].astype(jnp.float32)
    terms = jnp.dot(jnp.concatenate(parts), matrix, preferred_element_type=jnp.float32)
    high, middle, low = jnp.split(terms, 3)
    return high + middle + low


def y_sums(groups):
    for _ in range(4):
        groups = [a + b for a, b in zip(groups[:-1], groups[1:])]
    return groups


def packed_rows(width):
    return UNIT_ROWS - UNIT_ROWS * TAP_DILATION // width


def store_packed(out_ref, place, smooth):
    rows, width = smooth.shape
    kept_rows = out_ref.shape[1]
    depth = rows - kept_rows
    out_ref[place, :, : width - LANES] = smooth[:kept_rows, : width - LANES]
    kept = lane_of((depth, LANES)) < LANES - TAP_DILATION
    for piece in range(kept_rows // depth):
        tile = piece * TAP_DILATION // LANES
        shift = (LANES - TAP_DILATION - piece * TAP_DILATION) % LANES
        moved = smooth[kept_rows:, tile * LANES : (tile + 1) * LANES]
        if shift:
            moved = pltpu.roll(moved, shift, 1)
        last = smooth[piece * depth : (piece + 1) * depth, width - LANES :]
        out_ref[place, pl.ds(piece * depth, depth), width - LANES :] = jnp.where(kept, last, moved)


def completed(strip):
    width = strip.shape[1]
    last = strip[:, width - LANES :]
    lane = lane_of(last.shape)
    kept = lane < LANES - TAP_DILATION
    total = jnp.where(kept, last, 0.0)
    for start in range(0, width - LANES, LANES):
        total = total + strip[:, start : start + LANES]
    odd = (lane // TAP_DILATION) % 2 == 1
    total = jnp.where(odd, -total, total)
    total = total + pltpu.roll(total, 2 * TAP_DILATION, 1)
    total = total + pltpu.roll(total, TAP_DILATION, 1)
    return jnp.concatenate([strip[:, : width - LANES], jnp.where(kept, last, total)], axis=1)


def unpacked(weights, refs, use):
    kept_rows, width = refs[0].shape[1:]
    depth = UNIT_ROWS - kept_rows
    tiles = [None] * (width // LANES)
    for piece in range(kept_rows // depth):
        rows = pl.ds(piece * depth, depth)
        strip = weighted(weights, [ref[0, rows, :] for ref in refs])
        tile = piece * TAP_DILATION // LANES
        shift = (piece * TAP_DILATION - (LANES - TAP_DILATION)) % LANES
        moved = strip[:, width - LANES :]
        if shift:
            moved = pltpu.roll(moved, shift, 1)
        if tiles[tile] is None:
            tiles[tile] = moved
        else:
            here = lane_of(moved.shape) // TAP_DILATION == piece % (LANES // TAP_DILATION)
            tiles[tile] = jnp.where(here, moved, tiles[tile])
        use(rows, completed(strip))
    use(pl.ds(kept_rows, depth), completed(jnp.concatenate(tiles, axis=1)))


def weighted(weights, values):
    total = None
    for weight, value in zip(weights, values):
        term = weight * value
        total = term if total is None else total + term
    return total


def pair_kernel(units_ref, out_ref, read_ref, read_sem):
    read = pltpu.make_async_copy(units_ref.at[0], read_ref, read_sem)
    read.start()
    read.wait()
    store_packed(out_ref, 0, pair_sums(read_ref[...]))


def x_kernel(first, units_ref, out_ref, read_ref, matrix_ref, read_sems):
    count = out_ref.shape[0]

    def read(unit):
        return pltpu.make_async_copy(units_ref.at[first + unit], read_ref.at[unit], read_sems.at[unit])

    for unit in range(count):
        read(unit).start()
    fill_matrix(matrix_ref, x_taps())

    @pl.loop(0, count)
    def _(unit):
        read(unit).wait()
        store_packed(out_ref, unit, x_smoothed(read_ref[unit], matrix_ref[...]))


def extended_groups(before_ref, c_ref, after_ref, offset):
    groups = []
    for ref in (before_ref, c_ref, after_ref):
        for start in range(0, ref.shape[1], TAP_DILATION):
            groups.append(ref[0, pl.ds(start + offset, STRIP), :])
    return groups


def yx_kernel(before_ref, c_ref, after_ref, *refs):
    *out_refs, matrix_ref, smooth_ref = refs
    pl.when(pl.program_id(0) == 0)(lambda: fill_matrix(matrix_ref, x_taps()))
    for within in range(TAP_DILATION // STRIP):
        groups = y_sums(extended_groups(before_ref, c_ref, after_ref, within * STRIP))
        for group, strip in enumerate(groups):
            smooth_ref[pl.ds(group * TAP_DILATION + within * STRIP, STRIP), :] = strip * (1.0 / 16.0)
    places = [(ref, place) for ref in out_refs for place in range(ref.shape[0])]
    for unit, (ref, place) in enumerate(places):
        smooth = x_smoothed(smooth_ref[pl.ds(unit * UNIT_ROWS, UNIT_ROWS), :], matrix_ref[...])
        store_packed(ref, place, smooth)


def z_kernel(weights, *refs):
    whole_ref = refs[-1]

    def use(rows, strip):
        whole_ref[0, rows, :] = strip

    unpacked(weights, refs[: len(weights)], use)


def pair_z_kernel(weights, *refs):
    whole_ref, matrix_ref, pair_ref = refs[-3:]
    fill_matrix(matrix_ref, rest_taps())

    def use(rows, strip):
        pair_ref[rows, :] = strip

    unpacked(weights, refs[: len(weights)], use)
    whole_ref[0] = x_smoothed(pair_ref[...], matrix_ref[...])


def y_kernel(before_ref, whole_ref, after_ref, c_ref, detail_ref, coarse_ref):
    scale = 1.0 / 16.0
    for within in range(TAP_DILATION // STRIP):
        groups = y_sums(extended_groups(before_ref, whole_ref, after_ref, within * STRIP))
        for group, strip in enumerate(groups):
            rows = pl.ds(group * TAP_DILATION + within * STRIP, STRIP)
            coarse = strip * scale
            coarse_ref[0, rows, :] = coarse
            detail_ref[0, rows, :] = c_ref[0, rows, :] - coarse


def finish_kernel(weights, *refs):
    c_ref, _, _, detail_ref, coarse_ref = refs[len(weights) :]

    def use(rows, strip):
        coarse_ref[0, rows, :] = strip
        detail_ref[0, rows, :] = c_ref[0, rows, :] - strip

    unpacked(weights, refs[: len(weights)], use)


def last_kernel(weights, place, *refs):
    units_ref, _, _, detail_ref, coarse_ref, results_ref, write_sems = refs[len(weights) :]
    half = UNIT_ROWS // 2

    def write(piece, output, ref):
        rows = pl.ds(piece * half, half)
        source = results_ref.at[output, rows]
        return pltpu.make_async_copy(source, ref.at[place, rows], write_sems.at[piece, output])

    writes = [[write(piece, 0, detail_ref), write(piece, 1, coarse_ref)] for piece in range(2)]

    def use(rows, strip):
        results_ref[1, rows, :] = strip
        results_ref[0, rows, :] = units_ref[place, rows, :] - strip
        piece, left = divmod(rows.start + rows.size, half)
        if left == 0:
            for copy in writes[piece - 1]:
                copy.start()

    unpacked(weights, refs[: len(weights)], use)
    for copies in writes:
        for copy in copies:
            copy.wait()


def block_of(rows, width, first=0, depth=1):
    return pl.BlockSpec((depth, rows, width), lambda step: (first + step, 0, 0))


def anywhere():
    return pl.BlockSpec(memory_space=pl.ANY)


def in_vmem():
    return pl.BlockSpec(memory_space=pltpu.VMEM)


def call(kernel, name, steps, in_specs, out_specs, out_shape, args, aliases=None, scratch=(), grant=24):
    blocks = [spec.block_shape for spec in (*in_specs, *out_specs) if spec.block_shape]
    moved = 4 * max(steps, 1) * sum(math.prod(block) for block in blocks)
    return pl.pallas_call(
        kernel,
        grid=(steps,) if steps else (),
        in_specs=in_specs,
        out_specs=out_specs,
        out_shape=out_shape,
        scratch_shapes=scratch,
        input_output_aliases=aliases or {},
        compiler_params=pltpu.CompilerParams(vmem_limit_bytes=grant * 1024 * 1024),
        cost_estimate=pl.CostEstimate(flops=moved * 2, bytes_accessed=moved, transcendentals=0),
        name=name,
    )(*args)


def in_hbm(x):
    return pltpu.with_memory_space_constraint(x, pltpu.HBM)


def f32(*shape):
    return jax.ShapeDtypeStruct(shape, jnp.float32)


def shards(coarse_six):
    planes, rows, width = coarse_six.shape
    short = packed_rows(width)
    own, shifts = z_taps(planes, lax.axis_size("gz"))
    weights = (own, *shifts.values())
    count = len(weights)
    whole, unit, packed, edge = (functools.partial(block_of, n, width) for n in (rows, UNIT_ROWS, short, REACH))
    parts = rows // UNIT_ROWS
    units = coarse_six.reshape(planes * parts, UNIT_ROWS, width)
    matrix = pltpu.VMEM((width, width), jnp.bfloat16)

    def along_gz(x):
        return [passed_along(x, "gz", moved) for moved in shifts]

    def halo(source, start, stop):
        top, bottom = source[start:stop, :REACH], source[start:stop, rows - REACH :]
        return passed_along(bottom, "gy", 1), passed_along(top, "gy", -1)

    sums_shape = f32(FIRST_PLANES * parts, UNIT_ROWS, width)
    lead = call(
        pair_kernel,
        "pair_x",
        0,
        [anywhere()],
        [in_vmem()],
        [pltpu.VMEM((1, short, width), jnp.float32)],
        [in_hbm(units)],
        scratch=[pltpu.VMEM((UNIT_ROWS, width), jnp.float32), pltpu.SemaphoreType.DMA(())],
    )[0]
    lead, ready = lax.optimization_barrier((lead, units))
    lead_moved = along_gz(lead)
    first = FIRST_PLANES * parts - 1
    first_block = call(
        functools.partial(x_kernel, 1),
        "smooth_x",
        0,
        [anywhere()],
        [in_vmem()],
        [pltpu.VMEM((first, short, width), jnp.float32)],
        [in_hbm(ready)],
        scratch=[
            pltpu.VMEM((first, UNIT_ROWS, width), jnp.float32),
            matrix,
            pltpu.SemaphoreType.DMA((first,)),
        ],
    )[0]
    first_block, ready = lax.optimization_barrier((first_block, ready))
    first_moved = along_gz(first_block)
    sums = call(
        functools.partial(pair_z_kernel, weights),
        "smooth_zx",
        1,
        [packed()] * count,
        [unit()],
        [sums_shape],
        [lead, *lead_moved],
        scratch=[matrix, pltpu.VMEM((UNIT_ROWS, width), jnp.float32)],
    )

    later = []
    start = FIRST_PLANES
    sums, ready = lax.optimization_barrier((sums, coarse_six))
    near = halo(ready, start, start + sum(size for size, _ in LATER_GROUPS[0]))
    for number, sizes in enumerate(LATER_GROUPS):
        offset = 0
        for size, messages in sizes:
            depth = parts // messages
            blocks = call(
                yx_kernel,
                "smooth_yx",
                size,
                [edge(offset), whole(start + offset), edge(offset)],
                [packed(depth=depth)] * messages,
                [f32(size * depth, short, width)] * messages,
                [near[0], in_hbm(coarse_six), near[1]],
                scratch=[matrix, pltpu.VMEM((rows, width), jnp.float32)],
            )
            for message, block in enumerate(blocks):
                place = (start + offset) * parts + message * depth
                later.append((place, size * depth, (block, *along_gz(block))))
            offset += size
        start += offset
        if number == 0:
            block, ready = lax.optimization_barrier((block, ready))
            block, *first_moved = lax.optimization_barrier((block, *first_moved))
            sums = call(
                functools.partial(z_kernel, weights),
                "smooth_z",
                first,
                [packed()] * count + [anywhere()],
                [unit(1)],
                [sums_shape],
                [first_block, *first_moved, *sums],
                {count: 0},
            )[0]
            along_z = sums.reshape(FIRST_PLANES, rows, width)
            sides = halo(along_z, 0, FIRST_PLANES)
        if number + 1 < len(LATER_GROUPS):
            near = halo(ready, start, start + sum(size for size, _ in LATER_GROUPS[number + 1]))
            near, along_z = lax.optimization_barrier((near, along_z))

    block, sides = lax.optimization_barrier((block, sides))
    outs = call(
        y_kernel,
        "smooth_y",
        FIRST_PLANES,
        [edge(), whole(), edge(), whole()],
        [whole(), whole()],
        [f32(planes, rows, width)] * 2,
        [sides[0], along_z, sides[1], coarse_six],
    )
    outs = [out.reshape(units.shape) for out in outs]
    for place, size, blocks in later[:-1]:
        outs, blocks = lax.optimization_barrier((outs, blocks))
        outs = call(
            functools.partial(finish_kernel, weights),
            "finish",
            size,
            [packed()] * count + [unit(place)] + [anywhere()] * 2,
            [unit(place)] * 2,
            [f32(*units.shape)] * 2,
            [*blocks, units, *outs],
            {count + 1: 0, count + 2: 1},
        )
    place, _, blocks = later[-1]
    outs, blocks = lax.optimization_barrier((outs, blocks))
    outs = call(
        functools.partial(last_kernel, weights, place),
        "finish_last",
        0,
        [in_vmem()] * (count + 1) + [anywhere()] * 2,
        [anywhere()] * 2,
        [f32(*units.shape)] * 2,
        [*blocks, units, *outs],
        {count + 1: 0, count + 2: 1},
        scratch=[
            pltpu.VMEM((2, UNIT_ROWS, width), jnp.float32),
            pltpu.SemaphoreType.DMA((2, 2)),
        ],
    )
    return tuple(out.reshape(coarse_six.shape) for out in outs)


def solution(mesh):
    return jax.shard_map(
        shards,
        mesh=mesh,
        in_specs=(P("gz", "gy", None),),
        out_specs=(P("gz", "gy", None), P("gz", "gy", None)),
        check_vma=False,
    )
```

```python
import functools
import math

import jax
import jax.numpy as jnp
from jax import lax
from jax.experimental import pallas as pl
from jax.experimental.pallas import tpu as pltpu
from jax.sharding import PartitionSpec as P

TAP_DILATION = 32
REACH = 2 * TAP_DILATION
LANES = 128
STRIP = 8
UNIT_ROWS = 128
FIRST_PLANES = 3
LATER_GROUPS = (((2, 0),), ((1, 0), (1, 1), (1, 2)))

kernel_weights = (0.0625, 0.25, 0.375, 0.25, 0.0625)


def passed_along(x, axis, by):
    peers = lax.axis_size(axis)
    return lax.ppermute(x, axis, [(i, (i + by) % peers) for i in range(peers)])


def z_taps(plane_stack, count):
    weights = {}
    for cell_position in range(5):
        filter_reach = (cell_position - 2) * TAP_DILATION // plane_stack
        moved = -filter_reach % count
        weights[moved] = weights.get(moved, 0.0) + kernel_weights[cell_position]
    own = weights.pop(0, 0.0)
    return own, weights


def lane_of(shape):
    return lax.broadcasted_iota(jnp.int32, shape, 1)


def x_taps():
    return {(cell_position - 2) * TAP_DILATION: kernel_weights[cell_position] for cell_position in range(5)}


def rest_taps():
    return {(cell_position - 2) * TAP_DILATION: weight for cell_position, weight in enumerate((0.125, 0.375, 0.375, 0.125))}


def pair_sums(rows):
    return (rows + pltpu.roll(rows, rows.shape[1] - TAP_DILATION, 1)) * 0.5


def fill_matrix(matrix_ref, taps):
    depth, width = matrix_ref.shape
    for start in range(0, depth, LANES):
        shape = (LANES, width)
        row = start + lax.broadcasted_iota(jnp.int32, shape, 0)
        offset = row - lax.broadcasted_iota(jnp.int32, shape, 1)
        offset = jnp.where(offset < 0, offset + width, offset)
        values = jnp.zeros(shape, jnp.float32)
        for tap, weight in taps.items():
            values = jnp.where(offset == tap % width, weight, values)
        matrix_ref[pl.ds(start, LANES), :] = values.astype(jnp.bfloat16)


def x_smoothed(rows, matrix):
    parts = []
    for _ in range(3):
        parts.append(rows.astype(jnp.bfloat16))
        rows = rows - parts[-1].astype(jnp.float32)
    terms = jnp.dot(jnp.concatenate(parts), matrix, preferred_element_type=jnp.float32)
    high, middle, low = jnp.split(terms, 3)
    return high + middle + low


def y_sums(groups):
    for _ in range(4):
        groups = [a + b for a, b in zip(groups[:-1], groups[1:])]
    return groups


def packed_rows(width):
    return UNIT_ROWS - UNIT_ROWS * TAP_DILATION // width


def store_packed(out_ref, place, smooth):
    rows, width = smooth.shape
    kept_rows = out_ref.shape[1]
    depth = rows - kept_rows
    out_ref[place, :, : width - LANES] = smooth[:kept_rows, : width - LANES]
    kept = lane_of((depth, LANES)) < LANES - TAP_DILATION
    for piece in range(kept_rows // depth):
        tile = piece * TAP_DILATION // LANES
        shift = (LANES - TAP_DILATION - piece * TAP_DILATION) % LANES
        moved = smooth[kept_rows:, tile * LANES : (tile + 1) * LANES]
        if shift:
            moved = pltpu.roll(moved, shift, 1)
        last = smooth[piece * depth : (piece + 1) * depth, width - LANES :]
        out_ref[place, pl.ds(piece * depth, depth), width - LANES :] = jnp.where(kept, last, moved)


def completed(strip):
    width = strip.shape[1]
    last = strip[:, width - LANES :]
    lane = lane_of(last.shape)
    kept = lane < LANES - TAP_DILATION
    total = jnp.where(kept, last, 0.0)
    for start in range(0, width - LANES, LANES):
        total = total + strip[:, start : start + LANES]
    odd = (lane // TAP_DILATION) % 2 == 1
    total = jnp.where(odd, -total, total)
    total = total + pltpu.roll(total, 2 * TAP_DILATION, 1)
    total = total + pltpu.roll(total, TAP_DILATION, 1)
    return jnp.concatenate([strip[:, : width - LANES], jnp.where(kept, last, total)], axis=1)


def unpacked(weights, refs, use):
    kept_rows, width = refs[0].shape[1:]
    depth = UNIT_ROWS - kept_rows
    tiles = [None] * (width // LANES)
    for piece in range(kept_rows // depth):
        rows = pl.ds(piece * depth, depth)
        strip = weighted(weights, [ref[0, rows, :] for ref in refs])
        tile = piece * TAP_DILATION // LANES
        shift = (piece * TAP_DILATION - (LANES - TAP_DILATION)) % LANES
        moved = strip[:, width - LANES :]
        if shift:
            moved = pltpu.roll(moved, shift, 1)
        if tiles[tile] is None:
            tiles[tile] = moved
        else:
            here = lane_of(moved.shape) // TAP_DILATION == piece % (LANES // TAP_DILATION)
            tiles[tile] = jnp.where(here, moved, tiles[tile])
        use(rows, completed(strip))
    use(pl.ds(kept_rows, depth), completed(jnp.concatenate(tiles, axis=1)))


def weighted(weights, values):
    total = None
    for weight, value in zip(weights, values):
        term = weight * value
        total = term if total is None else total + term
    return total


def pair_kernel(units_ref, out_ref, read_ref, read_sem):
    read = pltpu.make_async_copy(units_ref.at[0], read_ref, read_sem)
    read.start()
    read.wait()
    store_packed(out_ref, 0, pair_sums(read_ref[...]))


def x_kernel(first, units_ref, out_ref, read_ref, matrix_ref, read_sems):
    count = out_ref.shape[0]

    def read(unit):
        return pltpu.make_async_copy(units_ref.at[first + unit], read_ref.at[unit], read_sems.at[unit])

    for unit in range(count):
        read(unit).start()
    fill_matrix(matrix_ref, x_taps())

    @pl.loop(0, count)
    def _(unit):
        read(unit).wait()
        store_packed(out_ref, unit, x_smoothed(read_ref[unit], matrix_ref[...]))


def extended_groups(before_ref, c_ref, after_ref, offset):
    groups = []
    for ref in (before_ref, c_ref, after_ref):
        for start in range(0, ref.shape[1], TAP_DILATION):
            groups.append(ref[0, pl.ds(start + offset, STRIP), :])
    return groups


def y_smoothed(before_ref, c_ref, after_ref, smooth_ref):
    for within in range(TAP_DILATION // STRIP):
        groups = y_sums(extended_groups(before_ref, c_ref, after_ref, within * STRIP))
        for group, strip in enumerate(groups):
            smooth_ref[pl.ds(group * TAP_DILATION + within * STRIP, STRIP), :] = strip * (1.0 / 16.0)


def yx_kernel(before_ref, c_ref, after_ref, *refs):
    *out_refs, matrix_ref, smooth_ref = refs
    pl.when(pl.program_id(0) == 0)(lambda: fill_matrix(matrix_ref, x_taps()))
    y_smoothed(before_ref, c_ref, after_ref, smooth_ref)
    places = [(ref, place) for ref in out_refs for place in range(ref.shape[0])]
    for unit, (ref, place) in enumerate(places):
        smooth = x_smoothed(smooth_ref[pl.ds(unit * UNIT_ROWS, UNIT_ROWS), :], matrix_ref[...])
        store_packed(ref, place, smooth)


def z_kernel(weights, *refs):
    whole_ref = refs[-1]

    def use(rows, strip):
        whole_ref[0, rows, :] = strip

    unpacked(weights, refs[: len(weights)], use)


def group_of(shape):
    return lane_of(shape) // TAP_DILATION


def spread(tile, group):
    tile = jnp.where(group_of(tile.shape) == group, tile, 0.0)
    tile = tile + pltpu.roll(tile, 2 * TAP_DILATION, 1)
    return tile + pltpu.roll(tile, TAP_DILATION, 1)


def strip_rows(rows, ahead):
    per_group = TAP_DILATION // STRIP
    strip = lax.rem(lax.axis_index("gy") + ahead, per_group)
    return pl.ds(pl.multiple_of(rows - TAP_DILATION + strip * STRIP, STRIP), STRIP)


def short_strips(rows):
    half = rows - UNIT_ROWS
    fixed = [pl.ds(row, STRIP) for row in range(0, rows - TAP_DILATION, STRIP)]
    moving = [strip_rows(rows, ahead) for ahead in range(1, TAP_DILATION // STRIP)]
    return fixed[: half // STRIP], fixed[half // STRIP :] + moving


def short_tiles(rows, width):
    return (rows // STRIP - 3) * (width // LANES)


def short_kernel(before_ref, c_ref, after_ref, out_ref, matrix_ref, smooth_ref):
    plane = pl.program_id(0)

    @pl.when(plane == 0)
    def _():
        fill_matrix(matrix_ref, x_taps())
        out_ref[out_ref.shape[0] - 1] = jnp.zeros((STRIP, LANES), jnp.float32)

    y_smoothed(before_ref, c_ref, after_ref, smooth_ref)
    rows, width = smooth_ref.shape
    for start in range(0, rows, UNIT_ROWS):
        unit = pl.ds(start, UNIT_ROWS)
        smooth_ref[unit, :] = x_smoothed(smooth_ref[unit, :], matrix_ref[...])
    index = plane * short_tiles(rows, width)
    groups = LANES // TAP_DILATION
    for places in short_strips(rows):
        *places, last_place = places
        last = smooth_ref[last_place, :]
        for piece, place in enumerate(places):
            strip = smooth_ref[place, :]
            tile = piece // groups * LANES
            moved = last[:, tile : tile + LANES]
            shift = (groups - 1 - piece) % groups * TAP_DILATION
            if shift:
                moved = pltpu.roll(moved, shift, 1)
            for start in range(0, width - LANES, LANES):
                out_ref[index] = strip[:, start : start + LANES]
                index += 1
            here = group_of(moved.shape) == groups - 1
            out_ref[index] = jnp.where(here, moved, strip[:, width - LANES :])
            index += 1
    left = spread(last[:, width - LANES :], groups - 2)
    end = out_ref.shape[0] - 1
    out_ref[end] = jnp.where(group_of(left.shape) == plane, left, out_ref[end])


def short_z_kernel(weights, *refs):
    packed, (whole_ref, *sum_refs) = refs[: len(weights)], refs[-4:]
    rows, width = whole_ref.shape[1:]
    plane = pl.program_id(0)
    index = plane * short_tiles(rows, width)
    groups, tiles = LANES // TAP_DILATION, width // LANES
    for places in short_strips(rows):
        *places, last_place = places
        last = [None] * tiles
        for piece, place in enumerate(places):
            strip = [weighted(weights, [ref[index + tile] for ref in packed]) for tile in range(tiles)]
            index += tiles
            tile, group = divmod(piece, groups)
            shift = (group + 1 - groups) % groups * TAP_DILATION
            moved = pltpu.roll(strip[-1], shift, 1) if shift else strip[-1]
            here = group_of(moved.shape) == group
            last[tile] = moved if last[tile] is None else jnp.where(here, moved, last[tile])
            whole_ref[0, place, :] = completed(jnp.concatenate(strip, axis=1))
        if len(places) < tiles * groups - 1:
            end = packed[0].shape[0] - 1
            left = spread(weighted(weights, [ref[end] for ref in packed]), plane)
            last[-1] = jnp.where(group_of(left.shape) == groups - 2, left, last[-1])
        whole_ref[0, last_place, :] = completed(jnp.concatenate(last, axis=1))

    groups = rows // TAP_DILATION
    for ahead in range(TAP_DILATION // STRIP):
        total = None
        for group in range(groups if ahead else groups - 1):
            strip = whole_ref[0, strip_rows((group + 1) * TAP_DILATION, ahead), :]
            if total is None:
                total = strip
            else:
                total = total + strip if group % 2 == 0 else total - strip
        if ahead:
            sum_refs[ahead - 1][0] = total
        else:
            whole_ref[0, strip_rows(rows, 0), :] = total


def short_finish_kernel(whole_ref, *refs):
    *sum_refs, c_ref, _, _, detail_ref, coarse_ref = refs
    missing = strip_rows(whole_ref.shape[1], 0)
    coarse_ref[...] = whole_ref[...]
    coarse_ref[0, missing, :] = whole_ref[0, missing, :] + sum(ref[0] for ref in sum_refs)
    detail_ref[...] = c_ref[...] - coarse_ref[...]


def pair_z_kernel(weights, *refs):
    whole_ref, matrix_ref, pair_ref = refs[-3:]
    fill_matrix(matrix_ref, rest_taps())

    def use(rows, strip):
        pair_ref[rows, :] = strip

    unpacked(weights, refs[: len(weights)], use)
    whole_ref[0] = x_smoothed(pair_ref[...], matrix_ref[...])


def y_kernel(before_ref, whole_ref, after_ref, c_ref, detail_ref, coarse_ref):
    scale = 1.0 / 16.0
    for within in range(TAP_DILATION // STRIP):
        groups = y_sums(extended_groups(before_ref, whole_ref, after_ref, within * STRIP))
        for group, strip in enumerate(groups):
            rows = pl.ds(group * TAP_DILATION + within * STRIP, STRIP)
            coarse = strip * scale
            coarse_ref[0, rows, :] = coarse
            detail_ref[0, rows, :] = c_ref[0, rows, :] - coarse


def finish_kernel(weights, *refs):
    c_ref, _, _, detail_ref, coarse_ref = refs[len(weights) :]

    def use(rows, strip):
        coarse_ref[0, rows, :] = strip
        detail_ref[0, rows, :] = c_ref[0, rows, :] - strip

    unpacked(weights, refs[: len(weights)], use)


def last_kernel(weights, place, *refs):
    units_ref, _, _, detail_ref, coarse_ref, results_ref, write_sems = refs[len(weights) :]
    half = UNIT_ROWS // 2

    def write(piece, output, ref):
        rows = pl.ds(piece * half, half)
        source = results_ref.at[output, rows]
        return pltpu.make_async_copy(source, ref.at[place, rows], write_sems.at[piece, output])

    writes = [[write(piece, 0, detail_ref), write(piece, 1, coarse_ref)] for piece in range(2)]

    def use(rows, strip):
        results_ref[1, rows, :] = strip
        results_ref[0, rows, :] = units_ref[place, rows, :] - strip
        piece, left = divmod(rows.start + rows.size, half)
        if left == 0:
            for copy in writes[piece - 1]:
                copy.start()

    unpacked(weights, refs[: len(weights)], use)
    for copies in writes:
        for copy in copies:
            copy.wait()


def block_of(rows, width, first=0, depth=1):
    return pl.BlockSpec((depth, rows, width), lambda step: (first + step, 0, 0))


def anywhere():
    return pl.BlockSpec(memory_space=pl.ANY)


def tiles_of(pieces):
    return pl.BlockSpec((pieces, STRIP, LANES), lambda step: (0, 0, 0))


def in_vmem():
    return pl.BlockSpec(memory_space=pltpu.VMEM)


def call(kernel, name, steps, in_specs, out_specs, out_shape, args, aliases=None, scratch=(), grant=24):
    blocks = [spec.block_shape for spec in (*in_specs, *out_specs) if spec.block_shape]
    moved = 4 * max(steps, 1) * sum(math.prod(block) for block in blocks)
    return pl.pallas_call(
        kernel,
        grid=(steps,) if steps else (),
        in_specs=in_specs,
        out_specs=out_specs,
        out_shape=out_shape,
        scratch_shapes=scratch,
        input_output_aliases=aliases or {},
        compiler_params=pltpu.CompilerParams(vmem_limit_bytes=grant * 1024 * 1024),
        cost_estimate=pl.CostEstimate(flops=moved * 2, bytes_accessed=moved, transcendentals=0),
        name=name,
    )(*args)


def in_hbm(x):
    return pltpu.with_memory_space_constraint(x, pltpu.HBM)


def f32(*shape):
    return jax.ShapeDtypeStruct(shape, jnp.float32)


def can_shorten(rows, width):
    strips = TAP_DILATION // STRIP
    return lax.axis_size("gy") == strips and rows // TAP_DILATION % 2 == 0 and UNIT_ROWS // STRIP == width // TAP_DILATION


def shards(coarse_six):
    planes, rows, width = coarse_six.shape
    short = packed_rows(width)
    own, shifts = z_taps(planes, lax.axis_size("gz"))
    weights = (own, *shifts.values())
    count = len(weights)
    whole, unit, packed, edge = (functools.partial(block_of, n, width) for n in (rows, UNIT_ROWS, short, REACH))
    parts = rows // UNIT_ROWS
    units = coarse_six.reshape(planes * parts, UNIT_ROWS, width)
    matrix = pltpu.VMEM((width, width), jnp.bfloat16)

    def along_gz(x):
        return [passed_along(x, "gz", moved) for moved in shifts]

    def halo(source, start, stop):
        top, bottom = source[start:stop, :REACH], source[start:stop, rows - REACH :]
        return passed_along(bottom, "gy", 1), passed_along(top, "gy", -1)

    sums_shape = f32(FIRST_PLANES * parts, UNIT_ROWS, width)
    lead = call(
        pair_kernel,
        "pair_x",
        0,
        [anywhere()],
        [in_vmem()],
        [pltpu.VMEM((1, short, width), jnp.float32)],
        [in_hbm(units)],
        scratch=[pltpu.VMEM((UNIT_ROWS, width), jnp.float32), pltpu.SemaphoreType.DMA(())],
    )[0]
    lead, ready = lax.optimization_barrier((lead, units))
    lead_moved = along_gz(lead)
    first = FIRST_PLANES * parts - 1
    first_block = call(
        functools.partial(x_kernel, 1),
        "smooth_x",
        0,
        [anywhere()],
        [in_vmem()],
        [pltpu.VMEM((first, short, width), jnp.float32)],
        [in_hbm(ready)],
        scratch=[
            pltpu.VMEM((first, UNIT_ROWS, width), jnp.float32),
            matrix,
            pltpu.SemaphoreType.DMA((first,)),
        ],
    )[0]
    first_block, ready = lax.optimization_barrier((first_block, ready))
    first_moved = along_gz(first_block)
    sums = call(
        functools.partial(pair_z_kernel, weights),
        "smooth_zx",
        1,
        [packed()] * count,
        [unit()],
        [sums_shape],
        [lead, *lead_moved],
        scratch=[matrix, pltpu.VMEM((UNIT_ROWS, width), jnp.float32)],
    )

    later, short_sent = [], []
    start = FIRST_PLANES
    sums, ready = lax.optimization_barrier((sums, coarse_six))
    near = halo(ready, start, start + sum(size for size, _ in LATER_GROUPS[0]))
    for number, sizes in enumerate(LATER_GROUPS):
        offset = 0
        for size, messages in sizes:
            place = start + offset
            sources = [near[0], in_hbm(coarse_six), near[1]]
            specs = [edge(offset), whole(place), edge(offset)]
            scratch = [matrix, pltpu.VMEM((rows, width), jnp.float32)]
            if messages or not can_shorten(rows, width):
                messages = max(messages, 1)
                depth = parts // messages
                blocks = call(
                    yx_kernel,
                    "smooth_yx",
                    size,
                    specs,
                    [packed(depth=depth)] * messages,
                    [f32(size * depth, short, width)] * messages,
                    sources,
                    scratch=scratch,
                )
                for message, block in enumerate(blocks):
                    later.append((place * parts + message * depth, size * depth, (block, *along_gz(block))))
            else:
                pieces = size * short_tiles(rows, width) + 1
                block = call(
                    short_kernel,
                    "smooth_yx_short",
                    size,
                    specs,
                    [tiles_of(pieces)],
                    [f32(pieces, STRIP, LANES)],
                    sources,
                    scratch=scratch,
                )[0]
                short_sent.append((place, size, (block, *along_gz(block))))
            offset += size
        start += offset
        if number == 0:
            block, ready = lax.optimization_barrier((block, ready))
            block, *first_moved = lax.optimization_barrier((block, *first_moved))
            sums = call(
                functools.partial(z_kernel, weights),
                "smooth_z",
                first,
                [packed()] * count + [anywhere()],
                [unit(1)],
                [sums_shape],
                [first_block, *first_moved, *sums],
                {count: 0},
            )[0]
            along_z = sums.reshape(FIRST_PLANES, rows, width)
            sides = halo(along_z, 0, FIRST_PLANES)
        if number + 1 < len(LATER_GROUPS):
            near = halo(ready, start, start + sum(size for size, _ in LATER_GROUPS[number + 1]))
            near, along_z = lax.optimization_barrier((near, along_z))

    short_sums, shortened = [], sum(size for _, size, _ in short_sent)
    if short_sent:
        step = 0
        for place, size, blocks in short_sent:
            short_sums = call(
                functools.partial(short_z_kernel, weights),
                "smooth_z_short",
                size,
                [tiles_of(blocks[0].shape[0])] * count + [anywhere()] * len(short_sums),
                [whole(step)] + [block_of(STRIP, width, step)] * 3,
                [f32(shortened, rows, width)] + [f32(shortened, STRIP, width)] * 3,
                [*blocks, *short_sums],
                {count + at: at for at in range(len(short_sums))},
            )
            step += size
        moved_sums = [passed_along(total, "gy", ahead) for ahead, total in enumerate(short_sums[1:], 1)]
        block = short_sums[0]

    block, sides = lax.optimization_barrier((block, sides))
    outs = call(
        y_kernel,
        "smooth_y",
        FIRST_PLANES,
        [edge(), whole(), edge(), whole()],
        [whole(), whole()],
        [f32(planes, rows, width)] * 2,
        [sides[0], along_z, sides[1], coarse_six],
    )
    if short_sent:
        outs, moved_sums = lax.optimization_barrier((outs, moved_sums))
        outs = call(
            short_finish_kernel,
            "finish_short",
            shortened,
            [whole()] + [block_of(STRIP, width)] * 3 + [whole(short_sent[0][0])] + [anywhere()] * 2,
            [whole(short_sent[0][0])] * 2,
            [f32(planes, rows, width)] * 2,
            [short_sums[0], *moved_sums, coarse_six, *outs],
            {5: 0, 6: 1},
        )
    outs = [out.reshape(units.shape) for out in outs]
    for place, size, blocks in later[:-1]:
        outs, blocks = lax.optimization_barrier((outs, blocks))
        outs = call(
            functools.partial(finish_kernel, weights),
            "finish",
            size,
            [packed()] * count + [unit(place)] + [anywhere()] * 2,
            [unit(place)] * 2,
            [f32(*units.shape)] * 2,
            [*blocks, units, *outs],
            {count + 1: 0, count + 2: 1},
        )
    place, _, blocks = later[-1]
    outs, blocks = lax.optimization_barrier((outs, blocks))
    outs = call(
        functools.partial(last_kernel, weights, place),
        "finish_last",
        0,
        [in_vmem()] * (count + 1) + [anywhere()] * 2,
        [anywhere()] * 2,
        [f32(*units.shape)] * 2,
        [*blocks, units, *outs],
        {count + 1: 0, count + 2: 1},
        scratch=[
            pltpu.VMEM((2, UNIT_ROWS, width), jnp.float32),
            pltpu.SemaphoreType.DMA((2, 2)),
        ],
    )
    return tuple(out.reshape(coarse_six.shape) for out in outs)


def solution(mesh):
    return jax.shard_map(
        shards,
        mesh=mesh,
        in_specs=(P("gz", "gy", None),),
        out_specs=(P("gz", "gy", None), P("gz", "gy", None)),
        check_vma=False,
    )
```

```python
import functools
import math

import jax
import jax.numpy as jnp
from jax import lax
from jax.experimental import pallas as pl
from jax.experimental.pallas import tpu as pltpu
from jax.sharding import PartitionSpec as P

TAP_DILATION = 32
REACH = 2 * TAP_DILATION
LANES = 128
STRIP = 8
UNIT_ROWS = 128
FIRST_PLANES = 3
LATER_GROUPS = (((2, 0),), ((1, 0), (1, 0), (1, 2)))
SHORT_FIRST = 2

kernel_weights = (0.0625, 0.25, 0.375, 0.25, 0.0625)


def passed_along(x, axis, by):
    peers = lax.axis_size(axis)
    return lax.ppermute(x, axis, [(i, (i + by) % peers) for i in range(peers)])


def z_taps(plane_stack, count):
    weights = {}
    for cell_position in range(5):
        filter_reach = (cell_position - 2) * TAP_DILATION // plane_stack
        moved = -filter_reach % count
        weights[moved] = weights.get(moved, 0.0) + kernel_weights[cell_position]
    own = weights.pop(0, 0.0)
    return own, weights


def lane_of(shape):
    return lax.broadcasted_iota(jnp.int32, shape, 1)


def x_taps():
    return {(cell_position - 2) * TAP_DILATION: kernel_weights[cell_position] for cell_position in range(5)}


def rest_taps():
    return {(cell_position - 2) * TAP_DILATION: weight for cell_position, weight in enumerate((0.125, 0.375, 0.375, 0.125))}


def pair_sums(rows):
    return (rows + pltpu.roll(rows, rows.shape[1] - TAP_DILATION, 1)) * 0.5


def fill_matrix(matrix_ref, taps):
    depth, width = matrix_ref.shape
    for start in range(0, depth, LANES):
        shape = (LANES, width)
        row = start + lax.broadcasted_iota(jnp.int32, shape, 0)
        offset = row - lax.broadcasted_iota(jnp.int32, shape, 1)
        offset = jnp.where(offset < 0, offset + width, offset)
        values = jnp.zeros(shape, jnp.float32)
        for tap, weight in taps.items():
            values = jnp.where(offset == tap % width, weight, values)
        matrix_ref[pl.ds(start, LANES), :] = values.astype(jnp.bfloat16)


def x_smoothed(rows, matrix):
    parts = []
    for _ in range(3):
        parts.append(rows.astype(jnp.bfloat16))
        rows = rows - parts[-1].astype(jnp.float32)
    terms = jnp.dot(jnp.concatenate(parts), matrix, preferred_element_type=jnp.float32)
    high, middle, low = jnp.split(terms, 3)
    return high + middle + low


def y_sums(groups):
    for _ in range(4):
        groups = [a + b for a, b in zip(groups[:-1], groups[1:])]
    return groups


def packed_rows(width):
    return UNIT_ROWS - UNIT_ROWS * TAP_DILATION // width


def store_packed(out_ref, place, smooth):
    rows, width = smooth.shape
    kept_rows = out_ref.shape[1]
    depth = rows - kept_rows
    out_ref[place, :, : width - LANES] = smooth[:kept_rows, : width - LANES]
    kept = lane_of((depth, LANES)) < LANES - TAP_DILATION
    for piece in range(kept_rows // depth):
        tile = piece * TAP_DILATION // LANES
        shift = (LANES - TAP_DILATION - piece * TAP_DILATION) % LANES
        moved = smooth[kept_rows:, tile * LANES : (tile + 1) * LANES]
        if shift:
            moved = pltpu.roll(moved, shift, 1)
        last = smooth[piece * depth : (piece + 1) * depth, width - LANES :]
        out_ref[place, pl.ds(piece * depth, depth), width - LANES :] = jnp.where(kept, last, moved)


def completed(strip):
    width = strip.shape[1]
    last = strip[:, width - LANES :]
    lane = lane_of(last.shape)
    kept = lane < LANES - TAP_DILATION
    total = jnp.where(kept, last, 0.0)
    for start in range(0, width - LANES, LANES):
        total = total + strip[:, start : start + LANES]
    odd = (lane // TAP_DILATION) % 2 == 1
    total = jnp.where(odd, -total, total)
    total = total + pltpu.roll(total, 2 * TAP_DILATION, 1)
    total = total + pltpu.roll(total, TAP_DILATION, 1)
    return jnp.concatenate([strip[:, : width - LANES], jnp.where(kept, last, total)], axis=1)


def unpacked(weights, refs, use):
    kept_rows, width = refs[0].shape[1:]
    depth = UNIT_ROWS - kept_rows
    tiles = [None] * (width // LANES)
    for piece in range(kept_rows // depth):
        rows = pl.ds(piece * depth, depth)
        strip = weighted(weights, [ref[0, rows, :] for ref in refs])
        tile = piece * TAP_DILATION // LANES
        shift = (piece * TAP_DILATION - (LANES - TAP_DILATION)) % LANES
        moved = strip[:, width - LANES :]
        if shift:
            moved = pltpu.roll(moved, shift, 1)
        if tiles[tile] is None:
            tiles[tile] = moved
        else:
            here = lane_of(moved.shape) // TAP_DILATION == piece % (LANES // TAP_DILATION)
            tiles[tile] = jnp.where(here, moved, tiles[tile])
        use(rows, completed(strip))
    use(pl.ds(kept_rows, depth), completed(jnp.concatenate(tiles, axis=1)))


def weighted(weights, values):
    total = None
    for weight, value in zip(weights, values):
        term = weight * value
        total = term if total is None else total + term
    return total


def pair_kernel(units_ref, out_ref, read_ref, read_sem):
    read = pltpu.make_async_copy(units_ref.at[0], read_ref, read_sem)
    read.start()
    read.wait()
    store_packed(out_ref, 0, pair_sums(read_ref[...]))


def x_kernel(first, units_ref, out_ref, read_ref, matrix_ref, read_sems):
    count = out_ref.shape[0]

    def read(unit):
        return pltpu.make_async_copy(units_ref.at[first + unit], read_ref.at[unit], read_sems.at[unit])

    for unit in range(count):
        read(unit).start()
    fill_matrix(matrix_ref, x_taps())

    @pl.loop(0, count)
    def _(unit):
        read(unit).wait()
        store_packed(out_ref, unit, x_smoothed(read_ref[unit], matrix_ref[...]))


def extended_groups(before_ref, c_ref, after_ref, offset):
    groups = []
    for ref in (before_ref, c_ref, after_ref):
        for start in range(0, ref.shape[1], TAP_DILATION):
            groups.append(ref[0, pl.ds(start + offset, STRIP), :])
    return groups


def y_smoothed(before_ref, c_ref, after_ref, smooth_ref):
    for within in range(TAP_DILATION // STRIP):
        groups = y_sums(extended_groups(before_ref, c_ref, after_ref, within * STRIP))
        for group, strip in enumerate(groups):
            smooth_ref[pl.ds(group * TAP_DILATION + within * STRIP, STRIP), :] = strip * (1.0 / 16.0)


def yx_kernel(before_ref, c_ref, after_ref, *refs):
    *out_refs, matrix_ref, smooth_ref = refs
    pl.when(pl.program_id(0) == 0)(lambda: fill_matrix(matrix_ref, x_taps()))
    y_smoothed(before_ref, c_ref, after_ref, smooth_ref)
    places = [(ref, place) for ref in out_refs for place in range(ref.shape[0])]
    for unit, (ref, place) in enumerate(places):
        smooth = x_smoothed(smooth_ref[pl.ds(unit * UNIT_ROWS, UNIT_ROWS), :], matrix_ref[...])
        store_packed(ref, place, smooth)


def z_kernel(weights, *refs):
    whole_ref = refs[-1]

    def use(rows, strip):
        whole_ref[0, rows, :] = strip

    unpacked(weights, refs[: len(weights)], use)


def group_of(shape):
    return lane_of(shape) // TAP_DILATION


def spread(tile, group):
    tile = jnp.where(group_of(tile.shape) == group, tile, 0.0)
    tile = tile + pltpu.roll(tile, 2 * TAP_DILATION, 1)
    return tile + pltpu.roll(tile, TAP_DILATION, 1)


def strip_rows(rows, ahead):
    per_group = TAP_DILATION // STRIP
    strip = lax.rem(lax.axis_index("gy") + ahead, per_group)
    return pl.ds(pl.multiple_of(rows - TAP_DILATION + strip * STRIP, STRIP), STRIP)


def short_strips(rows):
    half = rows - UNIT_ROWS
    fixed = [pl.ds(row, STRIP) for row in range(0, rows - TAP_DILATION, STRIP)]
    moving = [strip_rows(rows, ahead) for ahead in range(1, TAP_DILATION // STRIP)]
    return fixed[: half // STRIP], fixed[half // STRIP :] + moving


def short_tiles(rows, width):
    return (rows // STRIP - 3) * (width // LANES)


def short_kernel(before_ref, c_ref, after_ref, out_ref, matrix_ref, smooth_ref):
    plane = pl.program_id(0)

    @pl.when(plane == 0)
    def _():
        fill_matrix(matrix_ref, x_taps())
        out_ref[out_ref.shape[0] - 1] = jnp.zeros((STRIP, LANES), jnp.float32)

    y_smoothed(before_ref, c_ref, after_ref, smooth_ref)
    rows, width = smooth_ref.shape
    for start in range(0, rows, UNIT_ROWS):
        unit = pl.ds(start, UNIT_ROWS)
        smooth_ref[unit, :] = x_smoothed(smooth_ref[unit, :], matrix_ref[...])
    index = plane * short_tiles(rows, width)
    groups = LANES // TAP_DILATION
    for places in short_strips(rows):
        *places, last_place = places
        last = smooth_ref[last_place, :]
        for piece, place in enumerate(places):
            strip = smooth_ref[place, :]
            tile = piece // groups * LANES
            moved = last[:, tile : tile + LANES]
            shift = (groups - 1 - piece) % groups * TAP_DILATION
            if shift:
                moved = pltpu.roll(moved, shift, 1)
            for start in range(0, width - LANES, LANES):
                out_ref[index] = strip[:, start : start + LANES]
                index += 1
            here = group_of(moved.shape) == groups - 1
            out_ref[index] = jnp.where(here, moved, strip[:, width - LANES :])
            index += 1
    left = spread(last[:, width - LANES :], groups - 2)
    end = out_ref.shape[0] - 1
    out_ref[end] = jnp.where(group_of(left.shape) == plane, left, out_ref[end])


def short_z_kernel(weights, *refs):
    packed, (whole_ref, *sum_refs) = refs[: len(weights)], refs[-4:]
    rows, width = whole_ref.shape[1:]
    plane = pl.program_id(0)
    index = plane * short_tiles(rows, width)
    groups, tiles = LANES // TAP_DILATION, width // LANES
    for places in short_strips(rows):
        *places, last_place = places
        last = [None] * tiles
        for piece, place in enumerate(places):
            strip = [weighted(weights, [ref[index + tile] for ref in packed]) for tile in range(tiles)]
            index += tiles
            tile, group = divmod(piece, groups)
            shift = (group + 1 - groups) % groups * TAP_DILATION
            moved = pltpu.roll(strip[-1], shift, 1) if shift else strip[-1]
            here = group_of(moved.shape) == group
            last[tile] = moved if last[tile] is None else jnp.where(here, moved, last[tile])
            whole_ref[0, place, :] = completed(jnp.concatenate(strip, axis=1))
        if len(places) < tiles * groups - 1:
            end = packed[0].shape[0] - 1
            left = spread(weighted(weights, [ref[end] for ref in packed]), plane)
            last[-1] = jnp.where(group_of(left.shape) == groups - 2, left, last[-1])
        whole_ref[0, last_place, :] = completed(jnp.concatenate(last, axis=1))

    groups = rows // TAP_DILATION
    for ahead in range(TAP_DILATION // STRIP):
        total = None
        for group in range(groups if ahead else groups - 1):
            strip = whole_ref[0, strip_rows((group + 1) * TAP_DILATION, ahead), :]
            if total is None:
                total = strip
            else:
                total = total + strip if group % 2 == 0 else total - strip
        if ahead:
            sum_refs[ahead - 1][0] = total
        else:
            whole_ref[0, strip_rows(rows, 0), :] = total


def short_finish_kernel(whole_ref, *refs):
    *sum_refs, c_ref, _, _, detail_ref, coarse_ref = refs
    missing = strip_rows(whole_ref.shape[1], 0)
    coarse_ref[...] = whole_ref[...]
    coarse_ref[0, missing, :] = whole_ref[0, missing, :] + sum(ref[0] for ref in sum_refs)
    detail_ref[...] = c_ref[...] - coarse_ref[...]


def pair_z_kernel(weights, *refs):
    whole_ref, matrix_ref, pair_ref = refs[-3:]
    fill_matrix(matrix_ref, rest_taps())

    def use(rows, strip):
        pair_ref[rows, :] = strip

    unpacked(weights, refs[: len(weights)], use)
    whole_ref[0] = x_smoothed(pair_ref[...], matrix_ref[...])


def y_kernel(before_ref, whole_ref, after_ref, c_ref, detail_ref, coarse_ref):
    scale = 1.0 / 16.0
    for within in range(TAP_DILATION // STRIP):
        groups = y_sums(extended_groups(before_ref, whole_ref, after_ref, within * STRIP))
        for group, strip in enumerate(groups):
            rows = pl.ds(group * TAP_DILATION + within * STRIP, STRIP)
            coarse = strip * scale
            coarse_ref[0, rows, :] = coarse
            detail_ref[0, rows, :] = c_ref[0, rows, :] - coarse


def finish_kernel(weights, *refs):
    c_ref, _, _, detail_ref, coarse_ref = refs[len(weights) :]

    def use(rows, strip):
        coarse_ref[0, rows, :] = strip
        detail_ref[0, rows, :] = c_ref[0, rows, :] - strip

    unpacked(weights, refs[: len(weights)], use)


def last_kernel(weights, place, *refs):
    units_ref, _, _, detail_ref, coarse_ref, results_ref, write_sems = refs[len(weights) :]
    half = UNIT_ROWS // 2

    def write(piece, output, ref):
        rows = pl.ds(piece * half, half)
        source = results_ref.at[output, rows]
        return pltpu.make_async_copy(source, ref.at[place, rows], write_sems.at[piece, output])

    writes = [[write(piece, 0, detail_ref), write(piece, 1, coarse_ref)] for piece in range(2)]

    def use(rows, strip):
        results_ref[1, rows, :] = strip
        results_ref[0, rows, :] = units_ref[place, rows, :] - strip
        piece, left = divmod(rows.start + rows.size, half)
        if left == 0:
            for copy in writes[piece - 1]:
                copy.start()

    unpacked(weights, refs[: len(weights)], use)
    for copies in writes:
        for copy in copies:
            copy.wait()


def block_of(rows, width, first=0, depth=1):
    return pl.BlockSpec((depth, rows, width), lambda step: (first + step, 0, 0))


def anywhere():
    return pl.BlockSpec(memory_space=pl.ANY)


def tiles_of(pieces):
    return pl.BlockSpec((pieces, STRIP, LANES), lambda step: (0, 0, 0))


def in_vmem():
    return pl.BlockSpec(memory_space=pltpu.VMEM)


def call(kernel, name, steps, in_specs, out_specs, out_shape, args, aliases=None, scratch=(), grant=24):
    blocks = [spec.block_shape for spec in (*in_specs, *out_specs) if spec.block_shape]
    moved = 4 * max(steps, 1) * sum(math.prod(block) for block in blocks)
    return pl.pallas_call(
        kernel,
        grid=(steps,) if steps else (),
        in_specs=in_specs,
        out_specs=out_specs,
        out_shape=out_shape,
        scratch_shapes=scratch,
        input_output_aliases=aliases or {},
        compiler_params=pltpu.CompilerParams(vmem_limit_bytes=grant * 1024 * 1024),
        cost_estimate=pl.CostEstimate(flops=moved * 2, bytes_accessed=moved, transcendentals=0),
        name=name,
    )(*args)


def in_hbm(x):
    return pltpu.with_memory_space_constraint(x, pltpu.HBM)


def f32(*shape):
    return jax.ShapeDtypeStruct(shape, jnp.float32)


def can_shorten(rows, width):
    strips = TAP_DILATION // STRIP
    return lax.axis_size("gy") == strips and rows // TAP_DILATION % 2 == 0 and UNIT_ROWS // STRIP == width // TAP_DILATION


def shards(coarse_six):
    planes, rows, width = coarse_six.shape
    short = packed_rows(width)
    own, shifts = z_taps(planes, lax.axis_size("gz"))
    weights = (own, *shifts.values())
    count = len(weights)
    whole, unit, packed, edge = (functools.partial(block_of, n, width) for n in (rows, UNIT_ROWS, short, REACH))
    parts = rows // UNIT_ROWS
    units = coarse_six.reshape(planes * parts, UNIT_ROWS, width)
    matrix = pltpu.VMEM((width, width), jnp.bfloat16)

    def along_gz(x):
        return [passed_along(x, "gz", moved) for moved in shifts]

    def halo(source, start, stop):
        top, bottom = source[start:stop, :REACH], source[start:stop, rows - REACH :]
        return passed_along(bottom, "gy", 1), passed_along(top, "gy", -1)

    sums_shape = f32(FIRST_PLANES * parts, UNIT_ROWS, width)
    lead = call(
        pair_kernel,
        "pair_x",
        0,
        [anywhere()],
        [in_vmem()],
        [pltpu.VMEM((1, short, width), jnp.float32)],
        [in_hbm(units)],
        scratch=[pltpu.VMEM((UNIT_ROWS, width), jnp.float32), pltpu.SemaphoreType.DMA(())],
    )[0]
    lead, ready = lax.optimization_barrier((lead, units))
    lead_moved = along_gz(lead)
    first = FIRST_PLANES * parts - 1
    first_block = call(
        functools.partial(x_kernel, 1),
        "smooth_x",
        0,
        [anywhere()],
        [in_vmem()],
        [pltpu.VMEM((first, short, width), jnp.float32)],
        [in_hbm(ready)],
        scratch=[
            pltpu.VMEM((first, UNIT_ROWS, width), jnp.float32),
            matrix,
            pltpu.SemaphoreType.DMA((first,)),
        ],
    )[0]
    first_block, ready = lax.optimization_barrier((first_block, ready))
    first_moved = along_gz(first_block)
    sums = call(
        functools.partial(pair_z_kernel, weights),
        "smooth_zx",
        1,
        [packed()] * count,
        [unit()],
        [sums_shape],
        [lead, *lead_moved],
        scratch=[matrix, pltpu.VMEM((UNIT_ROWS, width), jnp.float32)],
    )

    later, short_sent = [], []
    start = FIRST_PLANES
    sums, ready = lax.optimization_barrier((sums, coarse_six))
    near = halo(ready, start, start + sum(size for size, _ in LATER_GROUPS[0]))
    for number, sizes in enumerate(LATER_GROUPS):
        offset = 0
        for size, messages in sizes:
            place = start + offset
            if number and offset and short_sent:
                near, _ = lax.optimization_barrier((near, short_sent[0][2]))
            sources = [near[0], in_hbm(coarse_six), near[1]]
            specs = [edge(offset), whole(place), edge(offset)]
            scratch = [matrix, pltpu.VMEM((rows, width), jnp.float32)]
            if messages or not can_shorten(rows, width):
                messages = max(messages, 1)
                depth = parts // messages
                blocks = call(
                    yx_kernel,
                    "smooth_yx",
                    size,
                    specs,
                    [packed(depth=depth)] * messages,
                    [f32(size * depth, short, width)] * messages,
                    sources,
                    scratch=scratch,
                )
                for message, block in enumerate(blocks):
                    later.append((place * parts + message * depth, size * depth, (block, *along_gz(block))))
            else:
                pieces = size * short_tiles(rows, width) + 1
                block = call(
                    short_kernel,
                    "smooth_yx_short",
                    size,
                    specs,
                    [tiles_of(pieces)],
                    [f32(pieces, STRIP, LANES)],
                    sources,
                    scratch=scratch,
                )[0]
                short_sent.append((place, size, (block, *along_gz(block))))
            offset += size
        start += offset
        if number == 0:
            block, ready = lax.optimization_barrier((block, ready))
            block, *first_moved = lax.optimization_barrier((block, *first_moved))
            sums = call(
                functools.partial(z_kernel, weights),
                "smooth_z",
                first,
                [packed()] * count + [anywhere()],
                [unit(1)],
                [sums_shape],
                [first_block, *first_moved, *sums],
                {count: 0},
            )[0]
            along_z = sums.reshape(FIRST_PLANES, rows, width)
        if number + 1 < len(LATER_GROUPS):
            near = halo(ready, start, start + sum(size for size, _ in LATER_GROUPS[number + 1]))
            near, along_z = lax.optimization_barrier((near, along_z))
            sides = halo(along_z, 0, FIRST_PLANES)

    def sum_short(batch):
        planes_in = sum(size for _, size, _ in batch)
        step, sums = 0, []
        for _, size, blocks in batch:
            sums = call(
                functools.partial(short_z_kernel, weights),
                "smooth_z_short",
                size,
                [tiles_of(blocks[0].shape[0])] * count + [anywhere()] * len(sums),
                [whole(step)] + [block_of(STRIP, width, step)] * 3,
                [f32(planes_in, rows, width)] + [f32(planes_in, STRIP, width)] * 3,
                [*blocks, *sums],
                {count + at: at for at in range(len(sums))},
            )
            step += size
        return sums[0], [passed_along(total, "gy", ahead) for ahead, total in enumerate(sums[1:], 1)]

    def finish_short(batch, sums, outs):
        start, size = batch[0][0], sum(size for _, size, _ in batch)
        along_z, moved = sums
        outs, moved = lax.optimization_barrier((outs, moved))
        return call(
            short_finish_kernel,
            "finish_short",
            size,
            [whole()] + [block_of(STRIP, width)] * 3 + [whole(start)] + [anywhere()] * 2,
            [whole(start)] * 2,
            [f32(planes, rows, width)] * 2,
            [along_z, *moved, coarse_six, *outs],
            {5: 0, 6: 1},
        )

    batches = [short_sent[:SHORT_FIRST], short_sent[SHORT_FIRST:]] if short_sent else []
    block, sides = lax.optimization_barrier((block, sides))
    outs = call(
        y_kernel,
        "smooth_y",
        FIRST_PLANES,
        [edge(), whole(), edge(), whole()],
        [whole(), whole()],
        [f32(planes, rows, width)] * 2,
        [sides[0], along_z, sides[1], coarse_six],
    )
    for batch in batches:
        outs, blocks = lax.optimization_barrier((outs, [blocks for _, _, blocks in batch]))
        sums = sum_short([(place, size, block) for (place, size, _), block in zip(batch, blocks)])
        outs = finish_short(batch, sums, outs)
    outs = [out.reshape(units.shape) for out in outs]
    for place, size, blocks in later[:-1]:
        outs, blocks = lax.optimization_barrier((outs, blocks))
        outs = call(
            functools.partial(finish_kernel, weights),
            "finish",
            size,
            [packed()] * count + [unit(place)] + [anywhere()] * 2,
            [unit(place)] * 2,
            [f32(*units.shape)] * 2,
            [*blocks, units, *outs],
            {count + 1: 0, count + 2: 1},
        )
    place, _, blocks = later[-1]
    outs, blocks = lax.optimization_barrier((outs, blocks))
    outs = call(
        functools.partial(last_kernel, weights, place),
        "finish_last",
        0,
        [in_vmem()] * (count + 1) + [anywhere()] * 2,
        [anywhere()] * 2,
        [f32(*units.shape)] * 2,
        [*blocks, units, *outs],
        {count + 1: 0, count + 2: 1},
        scratch=[
            pltpu.VMEM((2, UNIT_ROWS, width), jnp.float32),
            pltpu.SemaphoreType.DMA((2, 2)),
        ],
    )
    return tuple(out.reshape(coarse_six.shape) for out in outs)


def solution(mesh):
    return jax.shard_map(
        shards,
        mesh=mesh,
        in_specs=(P("gz", "gy", None),),
        out_specs=(P("gz", "gy", None), P("gz", "gy", None)),
        check_vma=False,
    )
```

```python
import functools
import math

import jax
import jax.numpy as jnp
from jax import lax
from jax.experimental import pallas as pl
from jax.experimental.pallas import tpu as pltpu
from jax.sharding import PartitionSpec as P

TAP_DILATION = 32
REACH = 2 * TAP_DILATION
LANES = 128
STRIP = 8
UNIT_ROWS = 128
FIRST_PLANES = 2
LEAD_UNITS = 2
LATER_GROUPS = (((2, 0),), ((2, 0),), ((1, 1), (1, 2)))
SHORT_FIRST = 2

kernel_weights = (0.0625, 0.25, 0.375, 0.25, 0.0625)


def passed_along(x, axis, by):
    peers = lax.axis_size(axis)
    return lax.ppermute(x, axis, [(i, (i + by) % peers) for i in range(peers)])


def z_taps(plane_stack, count):
    weights = {}
    for cell_position in range(5):
        filter_reach = (cell_position - 2) * TAP_DILATION // plane_stack
        moved = -filter_reach % count
        weights[moved] = weights.get(moved, 0.0) + kernel_weights[cell_position]
    own = weights.pop(0, 0.0)
    return own, weights


def lane_of(shape):
    return lax.broadcasted_iota(jnp.int32, shape, 1)


def x_taps():
    return {(cell_position - 2) * TAP_DILATION: kernel_weights[cell_position] for cell_position in range(5)}


def rest_taps():
    return {(cell_position - 2) * TAP_DILATION: weight for cell_position, weight in enumerate((0.125, 0.375, 0.375, 0.125))}


def pair_sums(rows):
    return (rows + pltpu.roll(rows, rows.shape[1] - TAP_DILATION, 1)) * 0.5


def fill_matrix(matrix_ref, taps):
    depth, width = matrix_ref.shape
    for start in range(0, depth, LANES):
        shape = (LANES, width)
        row = start + lax.broadcasted_iota(jnp.int32, shape, 0)
        offset = row - lax.broadcasted_iota(jnp.int32, shape, 1)
        offset = jnp.where(offset < 0, offset + width, offset)
        values = jnp.zeros(shape, jnp.float32)
        for tap, weight in taps.items():
            values = jnp.where(offset == tap % width, weight, values)
        matrix_ref[pl.ds(start, LANES), :] = values.astype(jnp.bfloat16)


def x_smoothed(rows, matrix):
    parts = []
    for _ in range(3):
        parts.append(rows.astype(jnp.bfloat16))
        rows = rows - parts[-1].astype(jnp.float32)
    terms = jnp.dot(jnp.concatenate(parts), matrix, preferred_element_type=jnp.float32)
    high, middle, low = jnp.split(terms, 3)
    return high + middle + low


def y_sums(groups):
    for _ in range(4):
        groups = [a + b for a, b in zip(groups[:-1], groups[1:])]
    return groups


def packed_rows(width):
    return UNIT_ROWS - UNIT_ROWS * TAP_DILATION // width


def store_packed(out_ref, place, smooth):
    rows, width = smooth.shape
    kept_rows = out_ref.shape[1]
    depth = rows - kept_rows
    out_ref[place, :, : width - LANES] = smooth[:kept_rows, : width - LANES]
    kept = lane_of((depth, LANES)) < LANES - TAP_DILATION
    for piece in range(kept_rows // depth):
        tile = piece * TAP_DILATION // LANES
        shift = (LANES - TAP_DILATION - piece * TAP_DILATION) % LANES
        moved = smooth[kept_rows:, tile * LANES : (tile + 1) * LANES]
        if shift:
            moved = pltpu.roll(moved, shift, 1)
        last = smooth[piece * depth : (piece + 1) * depth, width - LANES :]
        out_ref[place, pl.ds(piece * depth, depth), width - LANES :] = jnp.where(kept, last, moved)


def completed(strip):
    width = strip.shape[1]
    last = strip[:, width - LANES :]
    lane = lane_of(last.shape)
    kept = lane < LANES - TAP_DILATION
    total = jnp.where(kept, last, 0.0)
    for start in range(0, width - LANES, LANES):
        total = total + strip[:, start : start + LANES]
    odd = (lane // TAP_DILATION) % 2 == 1
    total = jnp.where(odd, -total, total)
    total = total + pltpu.roll(total, 2 * TAP_DILATION, 1)
    total = total + pltpu.roll(total, TAP_DILATION, 1)
    return jnp.concatenate([strip[:, : width - LANES], jnp.where(kept, last, total)], axis=1)


def unpacked(weights, refs, use):
    kept_rows, width = refs[0].shape[1:]
    depth = UNIT_ROWS - kept_rows
    tiles = [None] * (width // LANES)
    for piece in range(kept_rows // depth):
        rows = pl.ds(piece * depth, depth)
        strip = weighted(weights, [ref[0, rows, :] for ref in refs])
        tile = piece * TAP_DILATION // LANES
        shift = (piece * TAP_DILATION - (LANES - TAP_DILATION)) % LANES
        moved = strip[:, width - LANES :]
        if shift:
            moved = pltpu.roll(moved, shift, 1)
        if tiles[tile] is None:
            tiles[tile] = moved
        else:
            here = lane_of(moved.shape) // TAP_DILATION == piece % (LANES // TAP_DILATION)
            tiles[tile] = jnp.where(here, moved, tiles[tile])
        use(rows, completed(strip))
    use(pl.ds(kept_rows, depth), completed(jnp.concatenate(tiles, axis=1)))


def weighted(weights, values):
    total = None
    for weight, value in zip(weights, values):
        term = weight * value
        total = term if total is None else total + term
    return total


def pair_kernel(units_ref, out_ref, read_ref, read_sems):
    def read(unit):
        return pltpu.make_async_copy(units_ref.at[unit], read_ref.at[unit], read_sems.at[unit])

    for unit in range(out_ref.shape[0]):
        read(unit).start()
    for unit in range(out_ref.shape[0]):
        read(unit).wait()
        store_packed(out_ref, unit, pair_sums(read_ref[unit]))


def x_kernel(first, units_ref, out_ref, read_ref, matrix_ref, read_sems):
    count = out_ref.shape[0]

    def read(unit):
        return pltpu.make_async_copy(units_ref.at[first + unit], read_ref.at[unit], read_sems.at[unit])

    for unit in range(count):
        read(unit).start()
    fill_matrix(matrix_ref, x_taps())

    @pl.loop(0, count)
    def _(unit):
        read(unit).wait()
        store_packed(out_ref, unit, x_smoothed(read_ref[unit], matrix_ref[...]))


def extended_groups(before_ref, c_ref, after_ref, offset):
    groups = []
    for ref in (before_ref, c_ref, after_ref):
        for start in range(0, ref.shape[1], TAP_DILATION):
            groups.append(ref[0, pl.ds(start + offset, STRIP), :])
    return groups


def y_smoothed(before_ref, c_ref, after_ref, smooth_ref):
    for within in range(TAP_DILATION // STRIP):
        groups = y_sums(extended_groups(before_ref, c_ref, after_ref, within * STRIP))
        for group, strip in enumerate(groups):
            smooth_ref[pl.ds(group * TAP_DILATION + within * STRIP, STRIP), :] = strip * (1.0 / 16.0)


def yx_kernel(before_ref, c_ref, after_ref, *refs):
    *out_refs, matrix_ref, smooth_ref = refs
    pl.when(pl.program_id(0) == 0)(lambda: fill_matrix(matrix_ref, x_taps()))
    y_smoothed(before_ref, c_ref, after_ref, smooth_ref)
    places = [(ref, place) for ref in out_refs for place in range(ref.shape[0])]
    for unit, (ref, place) in enumerate(places):
        smooth = x_smoothed(smooth_ref[pl.ds(unit * UNIT_ROWS, UNIT_ROWS), :], matrix_ref[...])
        store_packed(ref, place, smooth)


def z_kernel(weights, *refs):
    whole_ref = refs[-1]

    def use(rows, strip):
        whole_ref[0, rows, :] = strip

    unpacked(weights, refs[: len(weights)], use)


def group_of(shape):
    return lane_of(shape) // TAP_DILATION


def spread(tile, group):
    tile = jnp.where(group_of(tile.shape) == group, tile, 0.0)
    tile = tile + pltpu.roll(tile, 2 * TAP_DILATION, 1)
    return tile + pltpu.roll(tile, TAP_DILATION, 1)


def strip_rows(rows, ahead):
    per_group = TAP_DILATION // STRIP
    strip = lax.rem(lax.axis_index("gy") + ahead, per_group)
    return pl.ds(pl.multiple_of(rows - TAP_DILATION + strip * STRIP, STRIP), STRIP)


def short_strips(rows):
    half = rows - UNIT_ROWS
    fixed = [pl.ds(row, STRIP) for row in range(0, rows - TAP_DILATION, STRIP)]
    moving = [strip_rows(rows, ahead) for ahead in range(1, TAP_DILATION // STRIP)]
    return fixed[: half // STRIP], fixed[half // STRIP :] + moving


def short_tiles(rows, width):
    return (rows // STRIP - 3) * (width // LANES)


def short_kernel(before_ref, c_ref, after_ref, out_ref, matrix_ref, smooth_ref):
    plane = pl.program_id(0)

    @pl.when(plane == 0)
    def _():
        fill_matrix(matrix_ref, x_taps())
        out_ref[out_ref.shape[0] - 1] = jnp.zeros((STRIP, LANES), jnp.float32)

    y_smoothed(before_ref, c_ref, after_ref, smooth_ref)
    rows, width = smooth_ref.shape
    for start in range(0, rows, UNIT_ROWS):
        unit = pl.ds(start, UNIT_ROWS)
        smooth_ref[unit, :] = x_smoothed(smooth_ref[unit, :], matrix_ref[...])
    index = plane * short_tiles(rows, width)
    groups = LANES // TAP_DILATION
    for places in short_strips(rows):
        *places, last_place = places
        last = smooth_ref[last_place, :]
        for piece, place in enumerate(places):
            strip = smooth_ref[place, :]
            tile = piece // groups * LANES
            moved = last[:, tile : tile + LANES]
            shift = (groups - 1 - piece) % groups * TAP_DILATION
            if shift:
                moved = pltpu.roll(moved, shift, 1)
            for start in range(0, width - LANES, LANES):
                out_ref[index] = strip[:, start : start + LANES]
                index += 1
            here = group_of(moved.shape) == groups - 1
            out_ref[index] = jnp.where(here, moved, strip[:, width - LANES :])
            index += 1
    left = spread(last[:, width - LANES :], groups - 2)
    end = out_ref.shape[0] - 1
    out_ref[end] = jnp.where(group_of(left.shape) == plane, left, out_ref[end])


def short_z_kernel(weights, *refs):
    packed, (whole_ref, *sum_refs) = refs[: len(weights)], refs[-4:]
    rows, width = whole_ref.shape[1:]
    plane = pl.program_id(0)
    index = plane * short_tiles(rows, width)
    groups, tiles = LANES // TAP_DILATION, width // LANES
    for places in short_strips(rows):
        *places, last_place = places
        last = [None] * tiles
        for piece, place in enumerate(places):
            strip = [weighted(weights, [ref[index + tile] for ref in packed]) for tile in range(tiles)]
            index += tiles
            tile, group = divmod(piece, groups)
            shift = (group + 1 - groups) % groups * TAP_DILATION
            moved = pltpu.roll(strip[-1], shift, 1) if shift else strip[-1]
            here = group_of(moved.shape) == group
            last[tile] = moved if last[tile] is None else jnp.where(here, moved, last[tile])
            whole_ref[0, place, :] = completed(jnp.concatenate(strip, axis=1))
        if len(places) < tiles * groups - 1:
            end = packed[0].shape[0] - 1
            left = spread(weighted(weights, [ref[end] for ref in packed]), plane)
            last[-1] = jnp.where(group_of(left.shape) == groups - 2, left, last[-1])
        whole_ref[0, last_place, :] = completed(jnp.concatenate(last, axis=1))

    groups = rows // TAP_DILATION
    for ahead in range(TAP_DILATION // STRIP):
        total = None
        for group in range(groups if ahead else groups - 1):
            strip = whole_ref[0, strip_rows((group + 1) * TAP_DILATION, ahead), :]
            if total is None:
                total = strip
            else:
                total = total + strip if group % 2 == 0 else total - strip
        if ahead:
            sum_refs[ahead - 1][0] = total
        else:
            whole_ref[0, strip_rows(rows, 0), :] = total


def short_finish_kernel(whole_ref, *refs):
    *sum_refs, c_ref, _, _, detail_ref, coarse_ref = refs
    missing = strip_rows(whole_ref.shape[1], 0)
    coarse_ref[...] = whole_ref[...]
    coarse_ref[0, missing, :] = whole_ref[0, missing, :] + sum(ref[0] for ref in sum_refs)
    detail_ref[...] = c_ref[...] - coarse_ref[...]


def pair_z_kernel(weights, *refs):
    whole_ref, matrix_ref, pair_ref = refs[-3:]
    pl.when(pl.program_id(0) == 0)(lambda: fill_matrix(matrix_ref, rest_taps()))

    def use(rows, strip):
        pair_ref[rows, :] = strip

    unpacked(weights, refs[: len(weights)], use)
    whole_ref[0] = x_smoothed(pair_ref[...], matrix_ref[...])


def y_kernel(before_ref, whole_ref, after_ref, c_ref, detail_ref, coarse_ref):
    scale = 1.0 / 16.0
    for within in range(TAP_DILATION // STRIP):
        groups = y_sums(extended_groups(before_ref, whole_ref, after_ref, within * STRIP))
        for group, strip in enumerate(groups):
            rows = pl.ds(group * TAP_DILATION + within * STRIP, STRIP)
            coarse = strip * scale
            coarse_ref[0, rows, :] = coarse
            detail_ref[0, rows, :] = c_ref[0, rows, :] - coarse


def finish_kernel(weights, *refs):
    c_ref, _, _, detail_ref, coarse_ref = refs[len(weights) :]

    def use(rows, strip):
        coarse_ref[0, rows, :] = strip
        detail_ref[0, rows, :] = c_ref[0, rows, :] - strip

    unpacked(weights, refs[: len(weights)], use)


def last_kernel(weights, place, *refs):
    units_ref, _, _, detail_ref, coarse_ref, results_ref, write_sems = refs[len(weights) :]
    half = UNIT_ROWS // 2

    def write(piece, output, ref):
        rows = pl.ds(piece * half, half)
        source = results_ref.at[output, rows]
        return pltpu.make_async_copy(source, ref.at[place, rows], write_sems.at[piece, output])

    writes = [[write(piece, 0, detail_ref), write(piece, 1, coarse_ref)] for piece in range(2)]

    def use(rows, strip):
        results_ref[1, rows, :] = strip
        results_ref[0, rows, :] = units_ref[place, rows, :] - strip
        piece, left = divmod(rows.start + rows.size, half)
        if left == 0:
            for copy in writes[piece - 1]:
                copy.start()

    unpacked(weights, refs[: len(weights)], use)
    for copies in writes:
        for copy in copies:
            copy.wait()


def block_of(rows, width, first=0, depth=1):
    return pl.BlockSpec((depth, rows, width), lambda step: (first + step, 0, 0))


def anywhere():
    return pl.BlockSpec(memory_space=pl.ANY)


def tiles_of(pieces):
    return pl.BlockSpec((pieces, STRIP, LANES), lambda step: (0, 0, 0))


def in_vmem():
    return pl.BlockSpec(memory_space=pltpu.VMEM)


def call(kernel, name, steps, in_specs, out_specs, out_shape, args, aliases=None, scratch=(), grant=24):
    blocks = [spec.block_shape for spec in (*in_specs, *out_specs) if spec.block_shape]
    moved = 4 * max(steps, 1) * sum(math.prod(block) for block in blocks)
    return pl.pallas_call(
        kernel,
        grid=(steps,) if steps else (),
        in_specs=in_specs,
        out_specs=out_specs,
        out_shape=out_shape,
        scratch_shapes=scratch,
        input_output_aliases=aliases or {},
        compiler_params=pltpu.CompilerParams(vmem_limit_bytes=grant * 1024 * 1024),
        cost_estimate=pl.CostEstimate(flops=moved * 2, bytes_accessed=moved, transcendentals=0),
        name=name,
    )(*args)


def in_hbm(x):
    return pltpu.with_memory_space_constraint(x, pltpu.HBM)


def f32(*shape):
    return jax.ShapeDtypeStruct(shape, jnp.float32)


def can_shorten(rows, width):
    strips = TAP_DILATION // STRIP
    return lax.axis_size("gy") == strips and rows // TAP_DILATION % 2 == 0 and UNIT_ROWS // STRIP == width // TAP_DILATION


def shards(coarse_six):
    planes, rows, width = coarse_six.shape
    short = packed_rows(width)
    own, shifts = z_taps(planes, lax.axis_size("gz"))
    weights = (own, *shifts.values())
    count = len(weights)
    whole, unit, packed, edge = (functools.partial(block_of, n, width) for n in (rows, UNIT_ROWS, short, REACH))
    parts = rows // UNIT_ROWS
    units = coarse_six.reshape(planes * parts, UNIT_ROWS, width)
    matrix = pltpu.VMEM((width, width), jnp.bfloat16)

    def along_gz(x):
        return [passed_along(x, "gz", moved) for moved in shifts]

    def halo(source, start, stop):
        top, bottom = source[start:stop, :REACH], source[start:stop, rows - REACH :]
        return passed_along(bottom, "gy", 1), passed_along(top, "gy", -1)

    sums_shape = f32(FIRST_PLANES * parts, UNIT_ROWS, width)
    lead = call(
        pair_kernel,
        "pair_x",
        0,
        [anywhere()],
        [in_vmem()],
        [pltpu.VMEM((LEAD_UNITS, short, width), jnp.float32)],
        [in_hbm(units)],
        scratch=[pltpu.VMEM((LEAD_UNITS, UNIT_ROWS, width), jnp.float32), pltpu.SemaphoreType.DMA((LEAD_UNITS,))],
    )[0]
    lead, ready = lax.optimization_barrier((lead, units))
    lead_moved = along_gz(lead)
    first = FIRST_PLANES * parts - LEAD_UNITS
    first_block = call(
        functools.partial(x_kernel, LEAD_UNITS),
        "smooth_x",
        0,
        [anywhere()],
        [in_vmem()],
        [pltpu.VMEM((first, short, width), jnp.float32)],
        [in_hbm(ready)],
        scratch=[
            pltpu.VMEM((first, UNIT_ROWS, width), jnp.float32),
            matrix,
            pltpu.SemaphoreType.DMA((first,)),
        ],
    )[0]
    first_block, ready = lax.optimization_barrier((first_block, coarse_six))
    first_moved = along_gz(first_block)
    sums = call(
        functools.partial(pair_z_kernel, weights),
        "smooth_zx",
        LEAD_UNITS,
        [packed()] * count,
        [unit()],
        [sums_shape],
        [lead, *lead_moved],
        scratch=[matrix, pltpu.VMEM((UNIT_ROWS, width), jnp.float32)],
    )

    later, short_sent = [], []
    start = FIRST_PLANES
    near = halo(ready, start, start + sum(size for size, _ in LATER_GROUPS[0]))
    near, sums = lax.optimization_barrier((near, sums))
    for number, sizes in enumerate(LATER_GROUPS):
        offset = 0
        for size, messages in sizes:
            place = start + offset
            sources = [near[0], in_hbm(coarse_six), near[1]]
            specs = [edge(offset), whole(place), edge(offset)]
            scratch = [matrix, pltpu.VMEM((rows, width), jnp.float32)]
            if messages or not can_shorten(rows, width):
                messages = max(messages, 1)
                depth = parts // messages
                blocks = call(
                    yx_kernel,
                    "smooth_yx",
                    size,
                    specs,
                    [packed(depth=depth)] * messages,
                    [f32(size * depth, short, width)] * messages,
                    sources,
                    scratch=scratch,
                )
                for message, block in enumerate(blocks):
                    later.append((place * parts + message * depth, size * depth, (block, *along_gz(block))))
            else:
                pieces = size * short_tiles(rows, width) + 1
                block = call(
                    short_kernel,
                    "smooth_yx_short",
                    size,
                    specs,
                    [tiles_of(pieces)],
                    [f32(pieces, STRIP, LANES)],
                    sources,
                    scratch=scratch,
                )[0]
                short_sent.append((place, size, (block, *along_gz(block))))
            offset += size
        start += offset
        if number == 0:
            block, ready = lax.optimization_barrier((block, ready))
            block, *first_moved = lax.optimization_barrier((block, *first_moved))
            sums = call(
                functools.partial(z_kernel, weights),
                "smooth_z",
                first,
                [packed()] * count + [anywhere()],
                [unit(LEAD_UNITS)],
                [sums_shape],
                [first_block, *first_moved, *sums],
                {count: 0},
            )[0]
            along_z = sums.reshape(FIRST_PLANES, rows, width)
        if number + 1 < len(LATER_GROUPS):
            block, ready = lax.optimization_barrier((block, ready))
            near = halo(ready, start, start + sum(size for size, _ in LATER_GROUPS[number + 1]))
        if number and short_sent:
            near, _ = lax.optimization_barrier((near, short_sent[0][2]))
        if number == 0:
            near, along_z = lax.optimization_barrier((near, along_z))
            sides = halo(along_z, 0, FIRST_PLANES)

    def sum_short(batch):
        planes_in = sum(size for _, size, _ in batch)
        step, sums = 0, []
        for _, size, blocks in batch:
            sums = call(
                functools.partial(short_z_kernel, weights),
                "smooth_z_short",
                size,
                [tiles_of(blocks[0].shape[0])] * count + [anywhere()] * len(sums),
                [whole(step)] + [block_of(STRIP, width, step)] * 3,
                [f32(planes_in, rows, width)] + [f32(planes_in, STRIP, width)] * 3,
                [*blocks, *sums],
                {count + at: at for at in range(len(sums))},
            )
            step += size
        return sums[0], [passed_along(total, "gy", ahead) for ahead, total in enumerate(sums[1:], 1)]

    def finish_short(batch, sums, outs):
        start, size = batch[0][0], sum(size for _, size, _ in batch)
        along_z, moved = sums
        outs, moved = lax.optimization_barrier((outs, moved))
        return call(
            short_finish_kernel,
            "finish_short",
            size,
            [whole()] + [block_of(STRIP, width)] * 3 + [whole(start)] + [anywhere()] * 2,
            [whole(start)] * 2,
            [f32(planes, rows, width)] * 2,
            [along_z, *moved, coarse_six, *outs],
            {5: 0, 6: 1},
        )

    batches = [batch for batch in (short_sent[:SHORT_FIRST], short_sent[SHORT_FIRST:]) if batch]
    block, sides = lax.optimization_barrier((block, sides))
    outs = call(
        y_kernel,
        "smooth_y",
        FIRST_PLANES,
        [edge(), whole(), edge(), whole()],
        [whole(), whole()],
        [f32(planes, rows, width)] * 2,
        [sides[0], along_z, sides[1], coarse_six],
    )
    for batch in batches:
        outs, blocks = lax.optimization_barrier((outs, [blocks for _, _, blocks in batch]))
        sums = sum_short([(place, size, block) for (place, size, _), block in zip(batch, blocks)])
        outs = finish_short(batch, sums, outs)
    outs = [out.reshape(units.shape) for out in outs]
    for place, size, blocks in later[:-1]:
        outs, blocks = lax.optimization_barrier((outs, blocks))
        outs = call(
            functools.partial(finish_kernel, weights),
            "finish",
            size,
            [packed()] * count + [unit(place)] + [anywhere()] * 2,
            [unit(place)] * 2,
            [f32(*units.shape)] * 2,
            [*blocks, units, *outs],
            {count + 1: 0, count + 2: 1},
        )
    place, _, blocks = later[-1]
    outs, blocks = lax.optimization_barrier((outs, blocks))
    outs = call(
        functools.partial(last_kernel, weights, place),
        "finish_last",
        0,
        [in_vmem()] * (count + 1) + [anywhere()] * 2,
        [anywhere()] * 2,
        [f32(*units.shape)] * 2,
        [*blocks, units, *outs],
        {count + 1: 0, count + 2: 1},
        scratch=[
            pltpu.VMEM((2, UNIT_ROWS, width), jnp.float32),
            pltpu.SemaphoreType.DMA((2, 2)),
        ],
    )
    return tuple(out.reshape(coarse_six.shape) for out in outs)


def solution(mesh):
    return jax.shard_map(
        shards,
        mesh=mesh,
        in_specs=(P("gz", "gy", None),),
        out_specs=(P("gz", "gy", None), P("gz", "gy", None)),
        check_vma=False,
    )
```

```python
import functools
import math

import jax
import jax.numpy as jnp
from jax import lax
from jax.experimental import pallas as pl
from jax.experimental.pallas import tpu as pltpu
from jax.sharding import PartitionSpec as P

TAP_DILATION = 32
REACH = 2 * TAP_DILATION
LANES = 128
STRIP = 8
UNIT_ROWS = 128
FIRST_PLANES = 3
LATER_GROUPS = ((2, ()), (1, ()), (2, (2, 1, 1)))

kernel_weights = (0.0625, 0.25, 0.375, 0.25, 0.0625)


def passed_along(x, axis, by):
    peers = lax.axis_size(axis)
    return lax.ppermute(x, axis, [(i, (i + by) % peers) for i in range(peers)])


def z_taps(plane_stack, count):
    weights = {}
    for cell_position in range(5):
        filter_reach = (cell_position - 2) * TAP_DILATION // plane_stack
        moved = -filter_reach % count
        weights[moved] = weights.get(moved, 0.0) + kernel_weights[cell_position]
    own = weights.pop(0, 0.0)
    return own, weights


def lane_of(shape):
    return lax.broadcasted_iota(jnp.int32, shape, 1)


def x_taps():
    return {(cell_position - 2) * TAP_DILATION: kernel_weights[cell_position] for cell_position in range(5)}


def rest_taps():
    return {(cell_position - 2) * TAP_DILATION: weight for cell_position, weight in enumerate((0.125, 0.375, 0.375, 0.125))}


def pair_sums(rows):
    return (rows + pltpu.roll(rows, rows.shape[1] - TAP_DILATION, 1)) * 0.5


def fill_matrix(matrix_ref, taps):
    depth, width = matrix_ref.shape
    for start in range(0, depth, LANES):
        shape = (LANES, width)
        row = start + lax.broadcasted_iota(jnp.int32, shape, 0)
        offset = row - lax.broadcasted_iota(jnp.int32, shape, 1)
        offset = jnp.where(offset < 0, offset + width, offset)
        values = jnp.zeros(shape, jnp.float32)
        for tap, weight in taps.items():
            values = jnp.where(offset == tap % width, weight, values)
        matrix_ref[pl.ds(start, LANES), :] = values.astype(jnp.bfloat16)


def x_smoothed(rows, matrix):
    parts = []
    for _ in range(3):
        parts.append(rows.astype(jnp.bfloat16))
        rows = rows - parts[-1].astype(jnp.float32)
    terms = jnp.dot(jnp.concatenate(parts), matrix, preferred_element_type=jnp.float32)
    high, middle, low = jnp.split(terms, 3)
    return high + middle + low


def y_sums(groups, factors=4):
    for _ in range(factors):
        groups = [a + b for a, b in zip(groups[:-1], groups[1:])]
    return groups


def packed_rows(width):
    return UNIT_ROWS - UNIT_ROWS * TAP_DILATION // width


def store_packed(out_ref, place, smooth):
    rows, width = smooth.shape
    kept_rows = out_ref.shape[1]
    depth = rows - kept_rows
    out_ref[place, :, : width - LANES] = smooth[:kept_rows, : width - LANES]
    kept = lane_of((depth, LANES)) < LANES - TAP_DILATION
    for piece in range(kept_rows // depth):
        tile = piece * TAP_DILATION // LANES
        shift = (LANES - TAP_DILATION - piece * TAP_DILATION) % LANES
        moved = smooth[kept_rows:, tile * LANES : (tile + 1) * LANES]
        if shift:
            moved = pltpu.roll(moved, shift, 1)
        last = smooth[piece * depth : (piece + 1) * depth, width - LANES :]
        out_ref[place, pl.ds(piece * depth, depth), width - LANES :] = jnp.where(kept, last, moved)


def completed(strip):
    width = strip.shape[1]
    last = strip[:, width - LANES :]
    lane = lane_of(last.shape)
    kept = lane < LANES - TAP_DILATION
    total = jnp.where(kept, last, 0.0)
    for start in range(0, width - LANES, LANES):
        total = total + strip[:, start : start + LANES]
    odd = (lane // TAP_DILATION) % 2 == 1
    total = jnp.where(odd, -total, total)
    total = total + pltpu.roll(total, 2 * TAP_DILATION, 1)
    total = total + pltpu.roll(total, TAP_DILATION, 1)
    return jnp.concatenate([strip[:, : width - LANES], jnp.where(kept, last, total)], axis=1)


def unpacked(weights, refs, use):
    kept_rows, width = refs[0].shape[1:]
    depth = UNIT_ROWS - kept_rows
    tiles = [None] * (width // LANES)
    for piece in range(kept_rows // depth):
        rows = pl.ds(piece * depth, depth)
        strip = weighted(weights, [ref[0, rows, :] for ref in refs])
        tile = piece * TAP_DILATION // LANES
        shift = (piece * TAP_DILATION - (LANES - TAP_DILATION)) % LANES
        moved = strip[:, width - LANES :]
        if shift:
            moved = pltpu.roll(moved, shift, 1)
        if tiles[tile] is None:
            tiles[tile] = moved
        else:
            here = lane_of(moved.shape) // TAP_DILATION == piece % (LANES // TAP_DILATION)
            tiles[tile] = jnp.where(here, moved, tiles[tile])
        use(rows, completed(strip))
    use(pl.ds(kept_rows, depth), completed(jnp.concatenate(tiles, axis=1)))


def weighted(weights, values):
    total = None
    for weight, value in zip(weights, values):
        term = weight * value
        total = term if total is None else total + term
    return total


def pair_kernel(units_ref, out_ref, read_ref, read_sems):
    def read(unit):
        return pltpu.make_async_copy(units_ref.at[unit], read_ref.at[unit], read_sems.at[unit])

    for unit in range(out_ref.shape[0]):
        read(unit).start()
    for unit in range(out_ref.shape[0]):
        read(unit).wait()
        store_packed(out_ref, unit, pair_sums(read_ref[unit]))


def extended_groups(refs, offset):
    groups = []
    for ref in refs:
        for start in range(0, ref.shape[1], TAP_DILATION):
            groups.append(ref[0, pl.ds(start + offset, STRIP), :])
    return groups


def y_smoothed(before_ref, c_ref, after_ref, smooth_ref):
    for within in range(TAP_DILATION // STRIP):
        groups = y_sums(extended_groups((before_ref, c_ref, after_ref), within * STRIP))
        for group, strip in enumerate(groups):
            smooth_ref[pl.ds(group * TAP_DILATION + within * STRIP, STRIP), :] = strip * (1.0 / 16.0)


def y_pairs(c_ref, after_ref, smooth_ref):
    for within in range(TAP_DILATION // STRIP):
        groups = extended_groups((c_ref, after_ref), within * STRIP)
        for group, (strip, following) in enumerate(zip(groups[:-1], groups[1:])):
            smooth_ref[pl.ds(group * TAP_DILATION + within * STRIP, STRIP), :] = (strip + following) * 0.5


def yx_kernel(before_ref, c_ref, after_ref, *refs):
    *out_refs, matrix_ref, smooth_ref = refs
    plane = pl.program_id(0)
    pl.when(plane == 0)(lambda: fill_matrix(matrix_ref, x_taps()))
    y_smoothed(before_ref, c_ref, after_ref, smooth_ref)
    parts = smooth_ref.shape[0] // UNIT_ROWS
    for part in range(parts):
        smooth = x_smoothed(smooth_ref[pl.ds(part * UNIT_ROWS, UNIT_ROWS), :], matrix_ref[...])
        places = [(ref, place) for ref in out_refs for place in range(ref.shape[0])][part::parts]
        for at, (ref, place) in enumerate(places):
            pl.when(plane == at)(functools.partial(store_packed, ref, place, smooth))


def group_of(shape):
    return lane_of(shape) // TAP_DILATION


def spread(tile, group):
    tile = jnp.where(group_of(tile.shape) == group, tile, 0.0)
    tile = tile + pltpu.roll(tile, 2 * TAP_DILATION, 1)
    return tile + pltpu.roll(tile, TAP_DILATION, 1)


def strip_rows(rows, ahead):
    per_group = TAP_DILATION // STRIP
    strip = lax.rem(lax.axis_index("gy") + ahead, per_group)
    return pl.ds(pl.multiple_of(rows - TAP_DILATION + strip * STRIP, STRIP), STRIP)


def short_strips(rows):
    half = rows - UNIT_ROWS
    fixed = [pl.ds(row, STRIP) for row in range(0, rows - TAP_DILATION, STRIP)]
    moving = [strip_rows(rows, ahead) for ahead in range(1, TAP_DILATION // STRIP)]
    return fixed[: half // STRIP], fixed[half // STRIP :] + moving


def short_tiles(rows, width):
    return (rows // STRIP - 3) * (width // LANES)


def short_kernel(filter_y, *refs):
    *sources, out_ref, matrix_ref, smooth_ref = refs
    plane = pl.program_id(0)

    @pl.when(plane == 0)
    def _():
        fill_matrix(matrix_ref, x_taps())
        out_ref[out_ref.shape[0] - 1] = jnp.zeros((STRIP, LANES), jnp.float32)

    filter_y(*sources, smooth_ref)
    rows, width = smooth_ref.shape
    for start in range(0, rows, UNIT_ROWS):
        unit = pl.ds(start, UNIT_ROWS)
        smooth_ref[unit, :] = x_smoothed(smooth_ref[unit, :], matrix_ref[...])
    index = plane * short_tiles(rows, width)
    groups = LANES // TAP_DILATION
    for places in short_strips(rows):
        *places, last_place = places
        last = smooth_ref[last_place, :]
        for piece, place in enumerate(places):
            strip = smooth_ref[place, :]
            tile = piece // groups * LANES
            moved = last[:, tile : tile + LANES]
            shift = (groups - 1 - piece) % groups * TAP_DILATION
            if shift:
                moved = pltpu.roll(moved, shift, 1)
            for start in range(0, width - LANES, LANES):
                out_ref[index] = strip[:, start : start + LANES]
                index += 1
            here = group_of(moved.shape) == groups - 1
            out_ref[index] = jnp.where(here, moved, strip[:, width - LANES :])
            index += 1
    left = spread(last[:, width - LANES :], groups - 2)
    end = out_ref.shape[0] - 1
    out_ref[end] = jnp.where(group_of(left.shape) == plane, left, out_ref[end])


def short_z_kernel(weights, *refs):
    packed, (whole_ref, *sum_refs) = refs[: len(weights)], refs[-4:]
    rows, width = whole_ref.shape[1:]
    plane = pl.program_id(0)
    index = plane * short_tiles(rows, width)
    groups, tiles = LANES // TAP_DILATION, width // LANES
    for places in short_strips(rows):
        *places, last_place = places
        last = [None] * tiles
        for piece, place in enumerate(places):
            strip = [weighted(weights, [ref[index + tile] for ref in packed]) for tile in range(tiles)]
            index += tiles
            tile, group = divmod(piece, groups)
            shift = (group + 1 - groups) % groups * TAP_DILATION
            moved = pltpu.roll(strip[-1], shift, 1) if shift else strip[-1]
            here = group_of(moved.shape) == group
            last[tile] = moved if last[tile] is None else jnp.where(here, moved, last[tile])
            whole_ref[0, place, :] = completed(jnp.concatenate(strip, axis=1))
        if len(places) < tiles * groups - 1:
            end = packed[0].shape[0] - 1
            left = spread(weighted(weights, [ref[end] for ref in packed]), plane)
            last[-1] = jnp.where(group_of(left.shape) == groups - 2, left, last[-1])
        whole_ref[0, last_place, :] = completed(jnp.concatenate(last, axis=1))

    groups = rows // TAP_DILATION
    for ahead in range(TAP_DILATION // STRIP):
        total = None
        for group in range(groups if ahead else groups - 1):
            strip = whole_ref[0, strip_rows((group + 1) * TAP_DILATION, ahead), :]
            if total is None:
                total = strip
            else:
                total = total + strip if group % 2 == 0 else total - strip
        if ahead:
            sum_refs[ahead - 1][0] = total
        else:
            whole_ref[0, strip_rows(rows, 0), :] = total


def short_finish_kernel(whole_ref, *refs):
    *sum_refs, c_ref, _, _, detail_ref, coarse_ref = refs
    missing = strip_rows(whole_ref.shape[1], 0)
    coarse_ref[...] = whole_ref[...]
    coarse_ref[0, missing, :] = whole_ref[0, missing, :] + sum(ref[0] for ref in sum_refs)
    detail_ref[...] = c_ref[...] - coarse_ref[...]


def pair_z_kernel(weights, *refs):
    whole_ref, matrix_ref, pair_ref = refs[-3:]
    pl.when(pl.program_id(0) == 0)(lambda: fill_matrix(matrix_ref, rest_taps()))

    def use(rows, strip):
        pair_ref[rows, :] = strip

    unpacked(weights, refs[: len(weights)], use)
    whole_ref[0] = x_smoothed(pair_ref[...], matrix_ref[...])


def y_kernel(factors, before_ref, whole_ref, after_ref, c_ref, *refs):
    detail_ref, coarse_ref = refs[-2:]
    scale = 0.5**factors
    for within in range(TAP_DILATION // STRIP):
        groups = y_sums(extended_groups((before_ref, whole_ref, after_ref), within * STRIP), factors)
        for group in range(whole_ref.shape[1] // TAP_DILATION):
            rows = pl.ds(group * TAP_DILATION + within * STRIP, STRIP)
            coarse = groups[group] * scale
            coarse_ref[0, rows, :] = coarse
            detail_ref[0, rows, :] = c_ref[0, rows, :] - coarse


def complete_kernel(group_ref, *refs):
    *sum_refs, out_ref = refs
    missing = strip_rows(group_ref.shape[1], 0)
    out_ref[...] = group_ref[...]
    out_ref[0, missing, :] = group_ref[0, missing, :] + sum(ref[0] for ref in sum_refs)


def finish_kernel(weights, *refs):
    c_ref, _, _, detail_ref, coarse_ref = refs[len(weights) :]

    def use(rows, strip):
        coarse_ref[0, rows, :] = strip
        detail_ref[0, rows, :] = c_ref[0, rows, :] - strip

    unpacked(weights, refs[: len(weights)], use)


def last_kernel(weights, place, *refs):
    units_ref, _, _, detail_ref, coarse_ref, results_ref, write_sems = refs[len(weights) :]
    half = UNIT_ROWS // 2

    def write(piece, output, ref):
        rows = pl.ds(piece * half, half)
        source = results_ref.at[output, rows]
        return pltpu.make_async_copy(source, ref.at[place, rows], write_sems.at[piece, output])

    writes = [[write(piece, 0, detail_ref), write(piece, 1, coarse_ref)] for piece in range(2)]

    def use(rows, strip):
        results_ref[1, rows, :] = strip
        results_ref[0, rows, :] = units_ref[place, rows, :] - strip
        piece, left = divmod(rows.start + rows.size, half)
        if left == 0:
            for copy in writes[piece - 1]:
                copy.start()

    unpacked(weights, refs[: len(weights)], use)
    for copies in writes:
        for copy in copies:
            copy.wait()


def block_of(rows, width, first=0, depth=1):
    return pl.BlockSpec((depth, rows, width), lambda step: (first + step, 0, 0))


def anywhere():
    return pl.BlockSpec(memory_space=pl.ANY)


def all_of(*shape):
    return pl.BlockSpec(shape, lambda step: (0, 0, 0))


def in_vmem():
    return pl.BlockSpec(memory_space=pltpu.VMEM)


def call(kernel, name, steps, in_specs, out_specs, out_shape, args, aliases=None, scratch=(), grant=24):
    blocks = [spec.block_shape for spec in (*in_specs, *out_specs) if spec.block_shape]
    moved = 4 * max(steps, 1) * sum(math.prod(block) for block in blocks)
    return pl.pallas_call(
        kernel,
        grid=(steps,) if steps else (),
        in_specs=in_specs,
        out_specs=out_specs,
        out_shape=out_shape,
        scratch_shapes=scratch,
        input_output_aliases=aliases or {},
        compiler_params=pltpu.CompilerParams(vmem_limit_bytes=grant * 1024 * 1024),
        cost_estimate=pl.CostEstimate(flops=moved * 2, bytes_accessed=moved, transcendentals=0),
        name=name,
    )(*args)


def in_hbm(x):
    return pltpu.with_memory_space_constraint(x, pltpu.HBM)


def f32(*shape):
    return jax.ShapeDtypeStruct(shape, jnp.float32)


def can_shorten(rows, width):
    strips = TAP_DILATION // STRIP
    return lax.axis_size("gy") == strips and rows // TAP_DILATION % 2 == 0 and UNIT_ROWS // STRIP == width // TAP_DILATION


def shards(coarse_six):
    planes, rows, width = coarse_six.shape
    assert can_shorten(rows, width)
    short = packed_rows(width)
    own, shifts = z_taps(planes, lax.axis_size("gz"))
    weights = (own, *shifts.values())
    count = len(weights)
    whole, unit, packed, edge = (functools.partial(block_of, n, width) for n in (rows, UNIT_ROWS, short, REACH))
    strip = functools.partial(block_of, STRIP, width)
    parts = rows // UNIT_ROWS
    units = coarse_six.reshape(planes * parts, UNIT_ROWS, width)
    matrix = pltpu.VMEM((width, width), jnp.bfloat16)
    smooth = pltpu.VMEM((rows, width), jnp.float32)

    def along_gz(x):
        return [passed_along(x, "gz", moved) for moved in shifts]

    def halo(source, start, stop):
        top, bottom = source[start:stop, :REACH], source[start:stop, rows - REACH :]
        return passed_along(bottom, "gy", 1), passed_along(top, "gy", -1)

    def send_short(filter_y, size, specs, sources):
        pieces = size * short_tiles(rows, width) + 1
        block = call(
            functools.partial(short_kernel, filter_y),
            "smooth_yx_short",
            size,
            specs,
            [all_of(pieces, STRIP, LANES)],
            [f32(pieces, STRIP, LANES)],
            sources,
            scratch=[matrix, smooth],
        )[0]
        return block, *along_gz(block)

    def sum_short(batch, into=(), first=0):
        size_of_all = sum(size for _, size, _ in batch)
        whole_shape = into[0].shape if into else (size_of_all, rows, width)
        step, sums = 0, list(into)
        for _, size, blocks in batch:
            sums = call(
                functools.partial(short_z_kernel, weights),
                "smooth_z_short",
                size,
                [all_of(*blocks[0].shape)] * count + [anywhere()] * len(sums),
                [whole(first + step)] + [strip(step)] * 3,
                [f32(*whole_shape)] + [f32(size_of_all, STRIP, width)] * 3,
                [*blocks, *sums],
                {count + at: at for at in range(len(sums))},
            )
            step += size
        return sums[0], [passed_along(total, "gy", ahead) for ahead, total in enumerate(sums[1:], 1)]

    lead = call(
        pair_kernel,
        "pair_x",
        0,
        [anywhere()],
        [in_vmem()],
        [pltpu.VMEM((parts, short, width), jnp.float32)],
        [in_hbm(units)],
        scratch=[pltpu.VMEM((parts, UNIT_ROWS, width), jnp.float32), pltpu.SemaphoreType.DMA((parts,))],
    )[0]
    lead, ready = lax.optimization_barrier((lead, coarse_six))
    lead_moved = along_gz(lead)
    others = FIRST_PLANES - 1
    following = passed_along(ready[1:FIRST_PLANES, :TAP_DILATION], "gy", -1)
    first_sent = send_short(
        y_pairs, others, [whole(1), block_of(TAP_DILATION, width)], [in_hbm(coarse_six), following]
    )
    sums = call(
        functools.partial(pair_z_kernel, weights),
        "smooth_zx",
        parts,
        [packed()] * count,
        [unit()],
        [f32(FIRST_PLANES * parts, UNIT_ROWS, width)],
        [lead, *lead_moved],
        scratch=[matrix, pltpu.VMEM((UNIT_ROWS, width), jnp.float32)],
    )[0]

    later, short_sent = [], []
    start = FIRST_PLANES
    lead_moved, ready = lax.optimization_barrier((lead_moved, ready))
    near = halo(ready, start, start + LATER_GROUPS[0][0])
    near, sums = lax.optimization_barrier((near, sums))
    for number, (size, messages) in enumerate(LATER_GROUPS):
        sources = [near[0], in_hbm(coarse_six), near[1]]
        specs = [edge(), whole(start), edge()]
        if messages:
            blocks = call(
                yx_kernel,
                "smooth_yx",
                size,
                specs,
                [all_of(length, short, width) for length in messages],
                [f32(length, short, width) for length in messages],
                sources,
                scratch=[matrix, smooth],
            )
            place = start * parts
            for block, length in zip(blocks, messages):
                later.append((place, length, (block, *along_gz(block))))
                place += length
        else:
            blocks = send_short(y_smoothed, size, specs, sources)
            short_sent.append((start, size, blocks))
            block = blocks[0]
        start += size
        if number == 1:
            block, ready = lax.optimization_barrier((block, ready))
            near = halo(ready, start, start + LATER_GROUPS[2][0])
        if number == 0:
            block, ready = lax.optimization_barrier((block, ready))
            block, first_sent = lax.optimization_barrier((block, first_sent))
            along_z, moved_sums = sum_short([(1, others, first_sent)], [sums.reshape(FIRST_PLANES, rows, width)], 1)
            near = halo(ready, start, start + LATER_GROUPS[1][0])
            near, along_z = lax.optimization_barrier((near, along_z))
            last_group = pl.BlockSpec((1, TAP_DILATION, width), lambda step: (1 + step, rows // TAP_DILATION - 1, 0))
            along_z = call(
                complete_kernel,
                "complete",
                others,
                [last_group] + [strip()] * 3,
                [last_group],
                [f32(*along_z.shape)],
                [along_z, *moved_sums],
                {0: 0},
            )[0]
            sides = halo(along_z, 0, FIRST_PLANES)

    short_sums = sum_short(short_sent)
    short_whole, sides = lax.optimization_barrier((short_sums[0], sides))
    outs = ()
    for place, size, factors in ((0, 1, 4), (1, others, 3)):
        outs = call(
            functools.partial(y_kernel, factors),
            "smooth_y",
            size,
            [edge(place), whole(place), edge(place), whole(place)] + [anywhere()] * len(outs),
            [whole(place)] * 2,
            [f32(planes, rows, width)] * 2,
            [sides[0], along_z, sides[1], coarse_six, *outs],
            {4 + at: at for at in range(len(outs))},
        )
    outs, moved_sums = lax.optimization_barrier((outs, short_sums[1]))
    place = short_sent[0][0]
    outs = call(
        short_finish_kernel,
        "finish_short",
        sum(size for _, size, _ in short_sent),
        [whole()] + [strip()] * 3 + [whole(place)] + [anywhere()] * 2,
        [whole(place)] * 2,
        [f32(planes, rows, width)] * 2,
        [short_whole, *moved_sums, coarse_six, *outs],
        {5: 0, 6: 1},
    )
    outs = [out.reshape(units.shape) for out in outs]
    for place, size, blocks in later[:-1]:
        outs, blocks = lax.optimization_barrier((outs, blocks))
        outs = call(
            functools.partial(finish_kernel, weights),
            "finish",
            size,
            [packed()] * count + [unit(place)] + [anywhere()] * 2,
            [unit(place)] * 2,
            [f32(*units.shape)] * 2,
            [*blocks, units, *outs],
            {count + 1: 0, count + 2: 1},
        )
    place, _, blocks = later[-1]
    outs, blocks = lax.optimization_barrier((outs, blocks))
    outs = call(
        functools.partial(last_kernel, weights, place),
        "finish_last",
        0,
        [in_vmem()] * (count + 1) + [anywhere()] * 2,
        [anywhere()] * 2,
        [f32(*units.shape)] * 2,
        [*blocks, units, *outs],
        {count + 1: 0, count + 2: 1},
        scratch=[
            pltpu.VMEM((2, UNIT_ROWS, width), jnp.float32),
            pltpu.SemaphoreType.DMA((2, 2)),
        ],
    )
    return tuple(out.reshape(coarse_six.shape) for out in outs)


def solution(mesh):
    return jax.shard_map(
        shards,
        mesh=mesh,
        in_specs=(P("gz", "gy", None),),
        out_specs=(P("gz", "gy", None), P("gz", "gy", None)),
        check_vma=False,
    )
```

```python
import functools
import math

import jax
import jax.numpy as jnp
from jax import lax
from jax.experimental import pallas as pl
from jax.experimental.pallas import tpu as pltpu
from jax.sharding import PartitionSpec as P

TAP_DILATION = 32
REACH = 2 * TAP_DILATION
LANES = 128
STRIP = 8
UNIT_ROWS = 128
FIRST_PLANES = 3
LATER_GROUPS = (((2, 0),), ((1, 0), (1, 0), (1, 2)))
SHORT_FIRST = 2

kernel_weights = (0.0625, 0.25, 0.375, 0.25, 0.0625)


def passed_along(x, axis, by):
    peers = lax.axis_size(axis)
    return lax.ppermute(x, axis, [(i, (i + by) % peers) for i in range(peers)])


def z_taps(plane_stack, count):
    weights = {}
    for cell_position in range(5):
        filter_reach = (cell_position - 2) * TAP_DILATION // plane_stack
        moved = -filter_reach % count
        weights[moved] = weights.get(moved, 0.0) + kernel_weights[cell_position]
    own = weights.pop(0, 0.0)
    return own, weights


def lane_of(shape):
    return lax.broadcasted_iota(jnp.int32, shape, 1)


def x_taps():
    return {(cell_position - 2) * TAP_DILATION: kernel_weights[cell_position] for cell_position in range(5)}


def rest_taps():
    return {(cell_position - 2) * TAP_DILATION: weight for cell_position, weight in enumerate((0.125, 0.375, 0.375, 0.125))}


def pair_sums(rows):
    return (rows + pltpu.roll(rows, rows.shape[1] - TAP_DILATION, 1)) * 0.5


def fill_matrix(matrix_ref, taps):
    depth, width = matrix_ref.shape
    for start in range(0, depth, LANES):
        shape = (LANES, width)
        row = start + lax.broadcasted_iota(jnp.int32, shape, 0)
        offset = row - lax.broadcasted_iota(jnp.int32, shape, 1)
        offset = jnp.where(offset < 0, offset + width, offset)
        values = jnp.zeros(shape, jnp.float32)
        for tap, weight in taps.items():
            values = jnp.where(offset == tap % width, weight, values)
        matrix_ref[pl.ds(start, LANES), :] = values.astype(jnp.bfloat16)


def x_smoothed(rows, matrix):
    parts = []
    for _ in range(3):
        parts.append(rows.astype(jnp.bfloat16))
        rows = rows - parts[-1].astype(jnp.float32)
    terms = jnp.dot(jnp.concatenate(parts), matrix, preferred_element_type=jnp.float32)
    high, middle, low = jnp.split(terms, 3)
    return high + middle + low


def y_sums(groups):
    for _ in range(4):
        groups = [a + b for a, b in zip(groups[:-1], groups[1:])]
    return groups


def packed_rows(width):
    return UNIT_ROWS - UNIT_ROWS * TAP_DILATION // width


def store_packed(out_ref, place, smooth):
    rows, width = smooth.shape
    kept_rows = out_ref.shape[1]
    depth = rows - kept_rows
    out_ref[place, :, : width - LANES] = smooth[:kept_rows, : width - LANES]
    kept = lane_of((depth, LANES)) < LANES - TAP_DILATION
    for piece in range(kept_rows // depth):
        tile = piece * TAP_DILATION // LANES
        shift = (LANES - TAP_DILATION - piece * TAP_DILATION) % LANES
        moved = smooth[kept_rows:, tile * LANES : (tile + 1) * LANES]
        if shift:
            moved = pltpu.roll(moved, shift, 1)
        last = smooth[piece * depth : (piece + 1) * depth, width - LANES :]
        out_ref[place, pl.ds(piece * depth, depth), width - LANES :] = jnp.where(kept, last, moved)


def completed(strip):
    width = strip.shape[1]
    last = strip[:, width - LANES :]
    lane = lane_of(last.shape)
    kept = lane < LANES - TAP_DILATION
    total = jnp.where(kept, last, 0.0)
    for start in range(0, width - LANES, LANES):
        total = total + strip[:, start : start + LANES]
    odd = (lane // TAP_DILATION) % 2 == 1
    total = jnp.where(odd, -total, total)
    total = total + pltpu.roll(total, 2 * TAP_DILATION, 1)
    total = total + pltpu.roll(total, TAP_DILATION, 1)
    return jnp.concatenate([strip[:, : width - LANES], jnp.where(kept, last, total)], axis=1)


def unpacked(weights, refs, use):
    kept_rows, width = refs[0].shape[1:]
    depth = UNIT_ROWS - kept_rows
    tiles = [None] * (width // LANES)
    for piece in range(kept_rows // depth):
        rows = pl.ds(piece * depth, depth)
        strip = weighted(weights, [ref[0, rows, :] for ref in refs])
        tile = piece * TAP_DILATION // LANES
        shift = (piece * TAP_DILATION - (LANES - TAP_DILATION)) % LANES
        moved = strip[:, width - LANES :]
        if shift:
            moved = pltpu.roll(moved, shift, 1)
        if tiles[tile] is None:
            tiles[tile] = moved
        else:
            here = lane_of(moved.shape) // TAP_DILATION == piece % (LANES // TAP_DILATION)
            tiles[tile] = jnp.where(here, moved, tiles[tile])
        use(rows, completed(strip))
    use(pl.ds(kept_rows, depth), completed(jnp.concatenate(tiles, axis=1)))


def weighted(weights, values):
    total = None
    for weight, value in zip(weights, values):
        term = weight * value
        total = term if total is None else total + term
    return total


def pair_kernel(units_ref, out_ref, read_ref, read_sem):
    read = pltpu.make_async_copy(units_ref.at[0], read_ref, read_sem)
    read.start()
    read.wait()
    store_packed(out_ref, 0, pair_sums(read_ref[...]))


def x_kernel(first, units_ref, out_ref, read_ref, matrix_ref, read_sems):
    count = out_ref.shape[0]

    def read(unit):
        return pltpu.make_async_copy(units_ref.at[first + unit], read_ref.at[unit], read_sems.at[unit])

    for unit in range(count):
        read(unit).start()
    fill_matrix(matrix_ref, x_taps())

    @pl.loop(0, count)
    def _(unit):
        read(unit).wait()
        store_packed(out_ref, unit, x_smoothed(read_ref[unit], matrix_ref[...]))


def extended_groups(before_ref, c_ref, after_ref, offset):
    groups = []
    for ref in (before_ref, c_ref, after_ref):
        for start in range(0, ref.shape[1], TAP_DILATION):
            groups.append(ref[0, pl.ds(start + offset, STRIP), :])
    return groups


def y_smoothed(before_ref, c_ref, after_ref, smooth_ref):
    for within in range(TAP_DILATION // STRIP):
        groups = y_sums(extended_groups(before_ref, c_ref, after_ref, within * STRIP))
        for group, strip in enumerate(groups):
            smooth_ref[pl.ds(group * TAP_DILATION + within * STRIP, STRIP), :] = strip * (1.0 / 16.0)


def yx_kernel(before_ref, c_ref, after_ref, *refs):
    *out_refs, matrix_ref, smooth_ref = refs
    pl.when(pl.program_id(0) == 0)(lambda: fill_matrix(matrix_ref, x_taps()))
    y_smoothed(before_ref, c_ref, after_ref, smooth_ref)
    places = [(ref, place) for ref in out_refs for place in range(ref.shape[0])]
    for unit, (ref, place) in enumerate(places):
        smooth = x_smoothed(smooth_ref[pl.ds(unit * UNIT_ROWS, UNIT_ROWS), :], matrix_ref[...])
        store_packed(ref, place, smooth)


def z_kernel(weights, *refs):
    whole_ref = refs[-1]

    def use(rows, strip):
        whole_ref[0, rows, :] = strip

    unpacked(weights, refs[: len(weights)], use)


def group_of(shape):
    return lane_of(shape) // TAP_DILATION


def spread(tile, group):
    tile = jnp.where(group_of(tile.shape) == group, tile, 0.0)
    tile = tile + pltpu.roll(tile, 2 * TAP_DILATION, 1)
    return tile + pltpu.roll(tile, TAP_DILATION, 1)


def strip_rows(rows, ahead):
    per_group = TAP_DILATION // STRIP
    strip = lax.rem(lax.axis_index("gy") + ahead, per_group)
    return pl.ds(pl.multiple_of(rows - TAP_DILATION + strip * STRIP, STRIP), STRIP)


def short_strips(rows):
    half = rows - UNIT_ROWS
    fixed = [pl.ds(row, STRIP) for row in range(0, rows - TAP_DILATION, STRIP)]
    moving = [strip_rows(rows, ahead) for ahead in range(1, TAP_DILATION // STRIP)]
    return fixed[: half // STRIP], fixed[half // STRIP :] + moving


def short_tiles(rows, width):
    return (rows // STRIP - 3) * (width // LANES)


def short_kernel(before_ref, c_ref, after_ref, out_ref, matrix_ref, smooth_ref):
    plane = pl.program_id(0)

    @pl.when(plane == 0)
    def _():
        fill_matrix(matrix_ref, x_taps())
        out_ref[out_ref.shape[0] - 1] = jnp.zeros((STRIP, LANES), jnp.float32)

    y_smoothed(before_ref, c_ref, after_ref, smooth_ref)
    rows, width = smooth_ref.shape
    for start in range(0, rows, UNIT_ROWS):
        unit = pl.ds(start, UNIT_ROWS)
        smooth_ref[unit, :] = x_smoothed(smooth_ref[unit, :], matrix_ref[...])
    index = plane * short_tiles(rows, width)
    groups = LANES // TAP_DILATION
    for places in short_strips(rows):
        *places, last_place = places
        last = smooth_ref[last_place, :]
        for piece, place in enumerate(places):
            strip = smooth_ref[place, :]
            tile = piece // groups * LANES
            moved = last[:, tile : tile + LANES]
            shift = (groups - 1 - piece) % groups * TAP_DILATION
            if shift:
                moved = pltpu.roll(moved, shift, 1)
            for start in range(0, width - LANES, LANES):
                out_ref[index] = strip[:, start : start + LANES]
                index += 1
            here = group_of(moved.shape) == groups - 1
            out_ref[index] = jnp.where(here, moved, strip[:, width - LANES :])
            index += 1
    left = spread(last[:, width - LANES :], groups - 2)
    end = out_ref.shape[0] - 1
    out_ref[end] = jnp.where(group_of(left.shape) == plane, left, out_ref[end])


def short_z_kernel(weights, *refs):
    packed, (whole_ref, sums_ref) = refs[: len(weights)], refs[-2:]
    rows, width = whole_ref.shape[1:]
    plane = pl.program_id(0)
    index = plane * short_tiles(rows, width)
    groups, tiles = LANES // TAP_DILATION, width // LANES
    for places in short_strips(rows):
        *places, last_place = places
        last = [None] * tiles
        for piece, place in enumerate(places):
            strip = [weighted(weights, [ref[index + tile] for ref in packed]) for tile in range(tiles)]
            index += tiles
            tile, group = divmod(piece, groups)
            shift = (group + 1 - groups) % groups * TAP_DILATION
            moved = pltpu.roll(strip[-1], shift, 1) if shift else strip[-1]
            here = group_of(moved.shape) == group
            last[tile] = moved if last[tile] is None else jnp.where(here, moved, last[tile])
            whole_ref[0, place, :] = completed(jnp.concatenate(strip, axis=1))
        if len(places) < tiles * groups - 1:
            end = packed[0].shape[0] - 1
            left = spread(weighted(weights, [ref[end] for ref in packed]), plane)
            last[-1] = jnp.where(group_of(left.shape) == groups - 2, left, last[-1])
        whole_ref[0, last_place, :] = completed(jnp.concatenate(last, axis=1))

    groups = rows // TAP_DILATION
    for ahead in range(TAP_DILATION // STRIP):
        total = None
        for group in range(groups if ahead else groups - 1):
            strip = whole_ref[0, strip_rows((group + 1) * TAP_DILATION, ahead), :]
            if total is None:
                total = strip
            else:
                total = total + strip if group % 2 == 0 else total - strip
        strip = lax.rem(lax.axis_index("gy") + ahead, TAP_DILATION // STRIP)
        sums_ref[strip, 0] = total


def short_finish_kernel(whole_ref, *refs):
    sum_ref, c_ref, _, _, detail_ref, coarse_ref = refs
    coarse_ref[...] = whole_ref[...]
    coarse_ref[0, strip_rows(whole_ref.shape[1], 0), :] = sum_ref[0]
    detail_ref[...] = c_ref[...] - coarse_ref[...]


def pair_z_kernel(weights, *refs):
    whole_ref, matrix_ref, pair_ref = refs[-3:]
    fill_matrix(matrix_ref, rest_taps())

    def use(rows, strip):
        pair_ref[rows, :] = strip

    unpacked(weights, refs[: len(weights)], use)
    whole_ref[0] = x_smoothed(pair_ref[...], matrix_ref[...])


def y_kernel(before_ref, whole_ref, after_ref, c_ref, detail_ref, coarse_ref):
    scale = 1.0 / 16.0
    for within in range(TAP_DILATION // STRIP):
        groups = y_sums(extended_groups(before_ref, whole_ref, after_ref, within * STRIP))
        for group, strip in enumerate(groups):
            rows = pl.ds(group * TAP_DILATION + within * STRIP, STRIP)
            coarse = strip * scale
            coarse_ref[0, rows, :] = coarse
            detail_ref[0, rows, :] = c_ref[0, rows, :] - coarse


def finish_kernel(weights, *refs):
    c_ref, _, _, detail_ref, coarse_ref = refs[len(weights) :]

    def use(rows, strip):
        coarse_ref[0, rows, :] = strip
        detail_ref[0, rows, :] = c_ref[0, rows, :] - strip

    unpacked(weights, refs[: len(weights)], use)


def last_kernel(weights, place, *refs):
    units_ref, _, _, detail_ref, coarse_ref, results_ref, write_sems = refs[len(weights) :]
    half = UNIT_ROWS // 2

    def write(piece, output, ref):
        rows = pl.ds(piece * half, half)
        source = results_ref.at[output, rows]
        return pltpu.make_async_copy(source, ref.at[place, rows], write_sems.at[piece, output])

    writes = [[write(piece, 0, detail_ref), write(piece, 1, coarse_ref)] for piece in range(2)]

    def use(rows, strip):
        results_ref[1, rows, :] = strip
        results_ref[0, rows, :] = units_ref[place, rows, :] - strip
        piece, left = divmod(rows.start + rows.size, half)
        if left == 0:
            for copy in writes[piece - 1]:
                copy.start()

    unpacked(weights, refs[: len(weights)], use)
    for copies in writes:
        for copy in copies:
            copy.wait()


def block_of(rows, width, first=0, depth=1):
    return pl.BlockSpec((depth, rows, width), lambda step: (first + step, 0, 0))


def anywhere():
    return pl.BlockSpec(memory_space=pl.ANY)


def tiles_of(pieces):
    return pl.BlockSpec((pieces, STRIP, LANES), lambda step: (0, 0, 0))


def in_vmem():
    return pl.BlockSpec(memory_space=pltpu.VMEM)


def call(kernel, name, steps, in_specs, out_specs, out_shape, args, aliases=None, scratch=(), grant=24):
    blocks = [spec.block_shape for spec in (*in_specs, *out_specs) if spec.block_shape]
    moved = 4 * max(steps, 1) * sum(math.prod(block) for block in blocks)
    return pl.pallas_call(
        kernel,
        grid=(steps,) if steps else (),
        in_specs=in_specs,
        out_specs=out_specs,
        out_shape=out_shape,
        scratch_shapes=scratch,
        input_output_aliases=aliases or {},
        compiler_params=pltpu.CompilerParams(vmem_limit_bytes=grant * 1024 * 1024),
        cost_estimate=pl.CostEstimate(flops=moved * 2, bytes_accessed=moved, transcendentals=0),
        name=name,
    )(*args)


def in_hbm(x):
    return pltpu.with_memory_space_constraint(x, pltpu.HBM)


def f32(*shape):
    return jax.ShapeDtypeStruct(shape, jnp.float32)


def can_shorten(rows, width):
    strips = TAP_DILATION // STRIP
    return lax.axis_size("gy") == strips and rows // TAP_DILATION % 2 == 0 and UNIT_ROWS // STRIP == width // TAP_DILATION


def shards(coarse_six):
    planes, rows, width = coarse_six.shape
    short = packed_rows(width)
    own, shifts = z_taps(planes, lax.axis_size("gz"))
    weights = (own, *shifts.values())
    count = len(weights)
    whole, unit, packed, edge = (functools.partial(block_of, n, width) for n in (rows, UNIT_ROWS, short, REACH))
    parts = rows // UNIT_ROWS
    units = coarse_six.reshape(planes * parts, UNIT_ROWS, width)
    matrix = pltpu.VMEM((width, width), jnp.bfloat16)

    def along_gz(x):
        return [passed_along(x, "gz", moved) for moved in shifts]

    def halo(source, start, stop):
        top, bottom = source[start:stop, :REACH], source[start:stop, rows - REACH :]
        return passed_along(bottom, "gy", 1), passed_along(top, "gy", -1)

    sums_shape = f32(FIRST_PLANES * parts, UNIT_ROWS, width)
    lead = call(
        pair_kernel,
        "pair_x",
        0,
        [anywhere()],
        [in_vmem()],
        [pltpu.VMEM((1, short, width), jnp.float32)],
        [in_hbm(units)],
        scratch=[pltpu.VMEM((UNIT_ROWS, width), jnp.float32), pltpu.SemaphoreType.DMA(())],
    )[0]
    lead, ready = lax.optimization_barrier((lead, units))
    lead_moved = along_gz(lead)
    first = FIRST_PLANES * parts - 1
    first_block = call(
        functools.partial(x_kernel, 1),
        "smooth_x",
        0,
        [anywhere()],
        [in_vmem()],
        [pltpu.VMEM((first, short, width), jnp.float32)],
        [in_hbm(ready)],
        scratch=[
            pltpu.VMEM((first, UNIT_ROWS, width), jnp.float32),
            matrix,
            pltpu.SemaphoreType.DMA((first,)),
        ],
    )[0]
    first_block, ready = lax.optimization_barrier((first_block, ready))
    first_moved = along_gz(first_block)
    sums = call(
        functools.partial(pair_z_kernel, weights),
        "smooth_zx",
        1,
        [packed()] * count,
        [unit()],
        [sums_shape],
        [lead, *lead_moved],
        scratch=[matrix, pltpu.VMEM((UNIT_ROWS, width), jnp.float32)],
    )

    later, short_sent = [], []
    start = FIRST_PLANES
    sums, ready = lax.optimization_barrier((sums, coarse_six))
    near = halo(ready, start, start + sum(size for size, _ in LATER_GROUPS[0]))
    for number, sizes in enumerate(LATER_GROUPS):
        offset = 0
        for size, messages in sizes:
            place = start + offset
            if number and offset and short_sent:
                near, _ = lax.optimization_barrier((near, short_sent[0][2]))
            sources = [near[0], in_hbm(coarse_six), near[1]]
            specs = [edge(offset), whole(place), edge(offset)]
            scratch = [matrix, pltpu.VMEM((rows, width), jnp.float32)]
            if messages or not can_shorten(rows, width):
                messages = max(messages, 1)
                depth = parts // messages
                blocks = call(
                    yx_kernel,
                    "smooth_yx",
                    size,
                    specs,
                    [packed(depth=depth)] * messages,
                    [f32(size * depth, short, width)] * messages,
                    sources,
                    scratch=scratch,
                )
                for message, block in enumerate(blocks):
                    later.append((place * parts + message * depth, size * depth, (block, *along_gz(block))))
            else:
                pieces = size * short_tiles(rows, width) + 1
                block = call(
                    short_kernel,
                    "smooth_yx_short",
                    size,
                    specs,
                    [tiles_of(pieces)],
                    [f32(pieces, STRIP, LANES)],
                    sources,
                    scratch=scratch,
                )[0]
                short_sent.append((place, size, (block, *along_gz(block))))
            offset += size
        start += offset
        if number == 0:
            block, ready = lax.optimization_barrier((block, ready))
            block, *first_moved = lax.optimization_barrier((block, *first_moved))
            sums = call(
                functools.partial(z_kernel, weights),
                "smooth_z",
                first,
                [packed()] * count + [anywhere()],
                [unit(1)],
                [sums_shape],
                [first_block, *first_moved, *sums],
                {count: 0},
            )[0]
            along_z = sums.reshape(FIRST_PLANES, rows, width)
        if number + 1 < len(LATER_GROUPS):
            near = halo(ready, start, start + sum(size for size, _ in LATER_GROUPS[number + 1]))
            near, along_z = lax.optimization_barrier((near, along_z))
            sides = halo(along_z, 0, FIRST_PLANES)

    strips = TAP_DILATION // STRIP

    def strips_of(first):
        return pl.BlockSpec((strips, 1, STRIP, width), lambda step: (0, first + step, 0, 0))

    def sum_short(batch):
        planes_in = sum(size for _, size, _ in batch)
        step, sums = 0, []
        for _, size, blocks in batch:
            sums = call(
                functools.partial(short_z_kernel, weights),
                "smooth_z_short",
                size,
                [tiles_of(blocks[0].shape[0])] * count + [anywhere()] * len(sums),
                [whole(step), strips_of(step)],
                [f32(planes_in, rows, width), f32(strips, planes_in, STRIP, width)],
                [*blocks, *sums],
                {count + at: at for at in range(len(sums))},
            )
            step += size
        return sums[0], lax.psum_scatter(sums[1], "gy")

    def finish_short(batch, sums, outs):
        start, size = batch[0][0], sum(size for _, size, _ in batch)
        along_z, moved = sums
        outs, moved = lax.optimization_barrier((outs, moved))
        return call(
            short_finish_kernel,
            "finish_short",
            size,
            [whole(), block_of(STRIP, width), whole(start)] + [anywhere()] * 2,
            [whole(start)] * 2,
            [f32(planes, rows, width)] * 2,
            [along_z, moved, coarse_six, *outs],
            {3: 0, 4: 1},
        )

    batches = [short_sent[:SHORT_FIRST], short_sent[SHORT_FIRST:]] if short_sent else []
    block, sides = lax.optimization_barrier((block, sides))
    outs = call(
        y_kernel,
        "smooth_y",
        FIRST_PLANES,
        [edge(), whole(), edge(), whole()],
        [whole(), whole()],
        [f32(planes, rows, width)] * 2,
        [sides[0], along_z, sides[1], coarse_six],
    )
    def reshaped(outs, shape):
        return [out.reshape(shape) for out in outs]

    pending = []
    for batch in batches:
        outs, blocks = lax.optimization_barrier((outs, [blocks for _, _, blocks in batch]))
        pending.append(sum_short([(place, size, block) for (place, size, _), block in zip(batch, blocks)]))
        outs, first_whole = lax.optimization_barrier((outs, pending[-1][0]))
        pending[-1] = (first_whole, pending[-1][1])
    if pending:
        outs = finish_short(batches[0], pending[0], outs)
    outs = reshaped(outs, units.shape)
    for place, size, blocks in later[:-1]:
        outs, blocks = lax.optimization_barrier((outs, blocks))
        outs = call(
            functools.partial(finish_kernel, weights),
            "finish",
            size,
            [packed()] * count + [unit(place)] + [anywhere()] * 2,
            [unit(place)] * 2,
            [f32(*units.shape)] * 2,
            [*blocks, units, *outs],
            {count + 1: 0, count + 2: 1},
        )
    for batch, sums in zip(batches[1:], pending[1:]):
        outs = reshaped(finish_short(batch, sums, reshaped(outs, coarse_six.shape)), units.shape)
    place, _, blocks = later[-1]
    outs, blocks = lax.optimization_barrier((outs, blocks))
    outs = call(
        functools.partial(last_kernel, weights, place),
        "finish_last",
        0,
        [in_vmem()] * (count + 1) + [anywhere()] * 2,
        [anywhere()] * 2,
        [f32(*units.shape)] * 2,
        [*blocks, units, *outs],
        {count + 1: 0, count + 2: 1},
        scratch=[
            pltpu.VMEM((2, UNIT_ROWS, width), jnp.float32),
            pltpu.SemaphoreType.DMA((2, 2)),
        ],
    )
    return tuple(out.reshape(coarse_six.shape) for out in outs)


def solution(mesh):
    return jax.shard_map(
        shards,
        mesh=mesh,
        in_specs=(P("gz", "gy", None),),
        out_specs=(P("gz", "gy", None), P("gz", "gy", None)),
        check_vma=False,
    )
```

```python
import functools
import math

import jax
import jax.numpy as jnp
from jax import lax
from jax.experimental import pallas as pl
from jax.experimental.pallas import tpu as pltpu
from jax.sharding import PartitionSpec as P

TAP_DILATION = 32
REACH = 2 * TAP_DILATION
LANES = 128
STRIP = 8
UNIT_ROWS = 128
FIRST_PLANES = 2
LEAD_UNITS = 2
LATER_GROUPS = ((2, ()), (2, ()), (2, (3, 1)))
SHORT_FIRST = 2

kernel_weights = (0.0625, 0.25, 0.375, 0.25, 0.0625)


def passed_along(x, axis, by):
    peers = lax.axis_size(axis)
    return lax.ppermute(x, axis, [(i, (i + by) % peers) for i in range(peers)])


def z_taps(plane_stack, count):
    weights = {}
    for cell_position in range(5):
        filter_reach = (cell_position - 2) * TAP_DILATION // plane_stack
        moved = -filter_reach % count
        weights[moved] = weights.get(moved, 0.0) + kernel_weights[cell_position]
    own = weights.pop(0, 0.0)
    return own, weights


def lane_of(shape):
    return lax.broadcasted_iota(jnp.int32, shape, 1)


def x_taps():
    return {(cell_position - 2) * TAP_DILATION: kernel_weights[cell_position] for cell_position in range(5)}


def rest_taps():
    return {(cell_position - 2) * TAP_DILATION: weight for cell_position, weight in enumerate((0.125, 0.375, 0.375, 0.125))}


def pair_sums(rows):
    return (rows + pltpu.roll(rows, rows.shape[1] - TAP_DILATION, 1)) * 0.5


def fill_matrix(matrix_ref, taps):
    depth, width = matrix_ref.shape
    for start in range(0, depth, LANES):
        shape = (LANES, width)
        row = start + lax.broadcasted_iota(jnp.int32, shape, 0)
        offset = row - lax.broadcasted_iota(jnp.int32, shape, 1)
        offset = jnp.where(offset < 0, offset + width, offset)
        values = jnp.zeros(shape, jnp.float32)
        for tap, weight in taps.items():
            values = jnp.where(offset == tap % width, weight, values)
        matrix_ref[pl.ds(start, LANES), :] = values.astype(jnp.bfloat16)


def x_smoothed(rows, matrix):
    parts = []
    for _ in range(3):
        parts.append(rows.astype(jnp.bfloat16))
        rows = rows - parts[-1].astype(jnp.float32)
    terms = jnp.dot(jnp.concatenate(parts), matrix, preferred_element_type=jnp.float32)
    high, middle, low = jnp.split(terms, 3)
    return high + middle + low


def y_sums(groups):
    for _ in range(4):
        groups = [a + b for a, b in zip(groups[:-1], groups[1:])]
    return groups


def packed_rows(width):
    return UNIT_ROWS - UNIT_ROWS * TAP_DILATION // width


def store_packed(out_ref, place, smooth):
    rows, width = smooth.shape
    kept_rows = out_ref.shape[1]
    depth = rows - kept_rows
    out_ref[place, :, : width - LANES] = smooth[:kept_rows, : width - LANES]
    kept = lane_of((depth, LANES)) < LANES - TAP_DILATION
    for piece in range(kept_rows // depth):
        tile = piece * TAP_DILATION // LANES
        shift = (LANES - TAP_DILATION - piece * TAP_DILATION) % LANES
        moved = smooth[kept_rows:, tile * LANES : (tile + 1) * LANES]
        if shift:
            moved = pltpu.roll(moved, shift, 1)
        last = smooth[piece * depth : (piece + 1) * depth, width - LANES :]
        out_ref[place, pl.ds(piece * depth, depth), width - LANES :] = jnp.where(kept, last, moved)


def completed(strip):
    width = strip.shape[1]
    last = strip[:, width - LANES :]
    lane = lane_of(last.shape)
    kept = lane < LANES - TAP_DILATION
    total = jnp.where(kept, last, 0.0)
    for start in range(0, width - LANES, LANES):
        total = total + strip[:, start : start + LANES]
    odd = (lane // TAP_DILATION) % 2 == 1
    total = jnp.where(odd, -total, total)
    total = total + pltpu.roll(total, 2 * TAP_DILATION, 1)
    total = total + pltpu.roll(total, TAP_DILATION, 1)
    return jnp.concatenate([strip[:, : width - LANES], jnp.where(kept, last, total)], axis=1)


def unpacked(weights, refs, use):
    kept_rows, width = refs[0].shape[1:]
    depth = UNIT_ROWS - kept_rows
    tiles = [None] * (width // LANES)
    for piece in range(kept_rows // depth):
        rows = pl.ds(piece * depth, depth)
        strip = weighted(weights, [ref[0, rows, :] for ref in refs])
        tile = piece * TAP_DILATION // LANES
        shift = (piece * TAP_DILATION - (LANES - TAP_DILATION)) % LANES
        moved = strip[:, width - LANES :]
        if shift:
            moved = pltpu.roll(moved, shift, 1)
        if tiles[tile] is None:
            tiles[tile] = moved
        else:
            here = lane_of(moved.shape) // TAP_DILATION == piece % (LANES // TAP_DILATION)
            tiles[tile] = jnp.where(here, moved, tiles[tile])
        use(rows, completed(strip))
    use(pl.ds(kept_rows, depth), completed(jnp.concatenate(tiles, axis=1)))


def weighted(weights, values):
    total = None
    for weight, value in zip(weights, values):
        term = weight * value
        total = term if total is None else total + term
    return total


def pair_kernel(units_ref, out_ref, read_ref, read_sems):
    def read(unit):
        return pltpu.make_async_copy(units_ref.at[unit], read_ref.at[unit], read_sems.at[unit])

    for unit in range(out_ref.shape[0]):
        read(unit).start()
    for unit in range(out_ref.shape[0]):
        read(unit).wait()
        store_packed(out_ref, unit, pair_sums(read_ref[unit]))


def x_kernel(first, units_ref, out_ref, read_ref, matrix_ref, read_sems):
    count = out_ref.shape[0]

    def read(unit):
        return pltpu.make_async_copy(units_ref.at[first + unit], read_ref.at[unit], read_sems.at[unit])

    for unit in range(count):
        read(unit).start()
    fill_matrix(matrix_ref, x_taps())

    @pl.loop(0, count)
    def _(unit):
        read(unit).wait()
        store_packed(out_ref, unit, x_smoothed(read_ref[unit], matrix_ref[...]))


def extended_groups(before_ref, c_ref, after_ref, offset):
    groups = []
    for ref in (before_ref, c_ref, after_ref):
        for start in range(0, ref.shape[1], TAP_DILATION):
            groups.append(ref[0, pl.ds(start + offset, STRIP), :])
    return groups


def y_smoothed(before_ref, c_ref, after_ref, smooth_ref):
    for within in range(TAP_DILATION // STRIP):
        groups = y_sums(extended_groups(before_ref, c_ref, after_ref, within * STRIP))
        for group, strip in enumerate(groups):
            smooth_ref[pl.ds(group * TAP_DILATION + within * STRIP, STRIP), :] = strip * (1.0 / 16.0)


def yx_kernel(before_ref, c_ref, after_ref, *refs):
    *out_refs, matrix_ref, smooth_ref = refs
    plane = pl.program_id(0)
    pl.when(plane == 0)(lambda: fill_matrix(matrix_ref, x_taps()))
    y_smoothed(before_ref, c_ref, after_ref, smooth_ref)
    parts = smooth_ref.shape[0] // UNIT_ROWS
    for part in range(parts):
        smooth = x_smoothed(smooth_ref[pl.ds(part * UNIT_ROWS, UNIT_ROWS), :], matrix_ref[...])
        places = [(ref, place) for ref in out_refs for place in range(ref.shape[0])][part::parts]
        for at, (ref, place) in enumerate(places):
            pl.when(plane == at)(functools.partial(store_packed, ref, place, smooth))


def z_kernel(weights, *refs):
    whole_ref = refs[-1]

    def use(rows, strip):
        whole_ref[0, rows, :] = strip

    unpacked(weights, refs[: len(weights)], use)


def group_of(shape):
    return lane_of(shape) // TAP_DILATION


def spread(tile, group):
    tile = jnp.where(group_of(tile.shape) == group, tile, 0.0)
    tile = tile + pltpu.roll(tile, 2 * TAP_DILATION, 1)
    return tile + pltpu.roll(tile, TAP_DILATION, 1)


def strip_rows(rows, ahead):
    per_group = TAP_DILATION // STRIP
    strip = lax.rem(lax.axis_index("gy") + ahead, per_group)
    return pl.ds(pl.multiple_of(rows - TAP_DILATION + strip * STRIP, STRIP), STRIP)


def short_strips(rows):
    half = rows - UNIT_ROWS
    fixed = [pl.ds(row, STRIP) for row in range(0, rows - TAP_DILATION, STRIP)]
    moving = [strip_rows(rows, ahead) for ahead in range(1, TAP_DILATION // STRIP)]
    return fixed[: half // STRIP], fixed[half // STRIP :] + moving


def short_tiles(rows, width):
    return (rows // STRIP - 3) * (width // LANES)


def short_kernel(before_ref, c_ref, after_ref, out_ref, matrix_ref, smooth_ref):
    plane = pl.program_id(0)

    @pl.when(plane == 0)
    def _():
        fill_matrix(matrix_ref, x_taps())
        out_ref[out_ref.shape[0] - 1] = jnp.zeros((STRIP, LANES), jnp.float32)

    y_smoothed(before_ref, c_ref, after_ref, smooth_ref)
    rows, width = smooth_ref.shape
    for start in range(0, rows, UNIT_ROWS):
        unit = pl.ds(start, UNIT_ROWS)
        smooth_ref[unit, :] = x_smoothed(smooth_ref[unit, :], matrix_ref[...])
    index = plane * short_tiles(rows, width)
    groups = LANES // TAP_DILATION
    for places in short_strips(rows):
        *places, last_place = places
        last = smooth_ref[last_place, :]
        for piece, place in enumerate(places):
            strip = smooth_ref[place, :]
            tile = piece // groups * LANES
            moved = last[:, tile : tile + LANES]
            shift = (groups - 1 - piece) % groups * TAP_DILATION
            if shift:
                moved = pltpu.roll(moved, shift, 1)
            for start in range(0, width - LANES, LANES):
                out_ref[index] = strip[:, start : start + LANES]
                index += 1
            here = group_of(moved.shape) == groups - 1
            out_ref[index] = jnp.where(here, moved, strip[:, width - LANES :])
            index += 1
    left = spread(last[:, width - LANES :], groups - 2)
    end = out_ref.shape[0] - 1
    out_ref[end] = jnp.where(group_of(left.shape) == plane, left, out_ref[end])


def short_z_kernel(weights, *refs):
    packed, (whole_ref, sums_ref) = refs[: len(weights)], refs[-2:]
    rows, width = whole_ref.shape[1:]
    plane = pl.program_id(0)
    index = plane * short_tiles(rows, width)
    groups, tiles = LANES // TAP_DILATION, width // LANES
    for places in short_strips(rows):
        *places, last_place = places
        last = [None] * tiles
        for piece, place in enumerate(places):
            strip = [weighted(weights, [ref[index + tile] for ref in packed]) for tile in range(tiles)]
            index += tiles
            tile, group = divmod(piece, groups)
            shift = (group + 1 - groups) % groups * TAP_DILATION
            moved = pltpu.roll(strip[-1], shift, 1) if shift else strip[-1]
            here = group_of(moved.shape) == group
            last[tile] = moved if last[tile] is None else jnp.where(here, moved, last[tile])
            whole_ref[0, place, :] = completed(jnp.concatenate(strip, axis=1))
        if len(places) < tiles * groups - 1:
            end = packed[0].shape[0] - 1
            left = spread(weighted(weights, [ref[end] for ref in packed]), plane)
            last[-1] = jnp.where(group_of(left.shape) == groups - 2, left, last[-1])
        whole_ref[0, last_place, :] = completed(jnp.concatenate(last, axis=1))

    groups = rows // TAP_DILATION
    for ahead in range(TAP_DILATION // STRIP):
        total = None
        for group in range(groups if ahead else groups - 1):
            strip = whole_ref[0, strip_rows((group + 1) * TAP_DILATION, ahead), :]
            if total is None:
                total = strip
            else:
                total = total + strip if group % 2 == 0 else total - strip
        strip = lax.rem(lax.axis_index("gy") + ahead, TAP_DILATION // STRIP)
        sums_ref[strip, 0] = total


def short_finish_kernel(whole_ref, *refs):
    sums_ref, c_ref, _, _, detail_ref, coarse_ref = refs
    coarse_ref[...] = whole_ref[...]
    coarse_ref[0, strip_rows(whole_ref.shape[1], 0), :] = sum(sums_ref[at, 0] for at in range(sums_ref.shape[0]))
    detail_ref[...] = c_ref[...] - coarse_ref[...]


def pair_z_kernel(weights, *refs):
    whole_ref, matrix_ref, pair_ref = refs[-3:]
    pl.when(pl.program_id(0) == 0)(lambda: fill_matrix(matrix_ref, rest_taps()))

    def use(rows, strip):
        pair_ref[rows, :] = strip

    unpacked(weights, refs[: len(weights)], use)
    whole_ref[0] = x_smoothed(pair_ref[...], matrix_ref[...])


def y_kernel(before_ref, whole_ref, after_ref, c_ref, detail_ref, coarse_ref):
    scale = 1.0 / 16.0
    for within in range(TAP_DILATION // STRIP):
        groups = y_sums(extended_groups(before_ref, whole_ref, after_ref, within * STRIP))
        for group, strip in enumerate(groups):
            rows = pl.ds(group * TAP_DILATION + within * STRIP, STRIP)
            coarse = strip * scale
            coarse_ref[0, rows, :] = coarse
            detail_ref[0, rows, :] = c_ref[0, rows, :] - coarse


def finish_kernel(weights, *refs):
    c_ref, _, _, detail_ref, coarse_ref = refs[len(weights) :]

    def use(rows, strip):
        coarse_ref[0, rows, :] = strip
        detail_ref[0, rows, :] = c_ref[0, rows, :] - strip

    unpacked(weights, refs[: len(weights)], use)


def last_kernel(weights, place, *refs):
    units_ref, _, _, detail_ref, coarse_ref, results_ref, write_sems = refs[len(weights) :]
    half = UNIT_ROWS // 2

    def write(piece, output, ref):
        rows = pl.ds(piece * half, half)
        source = results_ref.at[output, rows]
        return pltpu.make_async_copy(source, ref.at[place, rows], write_sems.at[piece, output])

    writes = [[write(piece, 0, detail_ref), write(piece, 1, coarse_ref)] for piece in range(2)]

    def use(rows, strip):
        results_ref[1, rows, :] = strip
        results_ref[0, rows, :] = units_ref[place, rows, :] - strip
        piece, left = divmod(rows.start + rows.size, half)
        if left == 0:
            for copy in writes[piece - 1]:
                copy.start()

    unpacked(weights, refs[: len(weights)], use)
    for copies in writes:
        for copy in copies:
            copy.wait()


def block_of(rows, width, first=0, depth=1):
    return pl.BlockSpec((depth, rows, width), lambda step: (first + step, 0, 0))


def anywhere():
    return pl.BlockSpec(memory_space=pl.ANY)


def all_of(*shape):
    return pl.BlockSpec(shape, lambda step: (0, 0, 0))


def in_vmem():
    return pl.BlockSpec(memory_space=pltpu.VMEM)


def call(kernel, name, steps, in_specs, out_specs, out_shape, args, aliases=None, scratch=(), grant=24):
    blocks = [spec.block_shape for spec in (*in_specs, *out_specs) if spec.block_shape]
    moved = 4 * max(steps, 1) * sum(math.prod(block) for block in blocks)
    return pl.pallas_call(
        kernel,
        grid=(steps,) if steps else (),
        in_specs=in_specs,
        out_specs=out_specs,
        out_shape=out_shape,
        scratch_shapes=scratch,
        input_output_aliases=aliases or {},
        compiler_params=pltpu.CompilerParams(vmem_limit_bytes=grant * 1024 * 1024),
        cost_estimate=pl.CostEstimate(flops=moved * 2, bytes_accessed=moved, transcendentals=0),
        name=name,
    )(*args)


def in_hbm(x):
    return pltpu.with_memory_space_constraint(x, pltpu.HBM)


def f32(*shape):
    return jax.ShapeDtypeStruct(shape, jnp.float32)


def can_shorten(rows, width):
    strips = TAP_DILATION // STRIP
    return lax.axis_size("gy") == strips and rows // TAP_DILATION % 2 == 0 and UNIT_ROWS // STRIP == width // TAP_DILATION


def shards(coarse_six):
    planes, rows, width = coarse_six.shape
    short = packed_rows(width)
    own, shifts = z_taps(planes, lax.axis_size("gz"))
    weights = (own, *shifts.values())
    count = len(weights)
    whole, unit, packed, edge = (functools.partial(block_of, n, width) for n in (rows, UNIT_ROWS, short, REACH))
    parts = rows // UNIT_ROWS
    units = coarse_six.reshape(planes * parts, UNIT_ROWS, width)
    matrix = pltpu.VMEM((width, width), jnp.bfloat16)

    def along_gz(x):
        return [passed_along(x, "gz", moved) for moved in shifts]

    def edges(source, start, stop):
        return source[start:stop, :REACH], source[start:stop, rows - REACH :]

    def swapped(top, bottom):
        return passed_along(bottom, "gy", 1), passed_along(top, "gy", -1)

    def halo(source, start, stop):
        return swapped(*edges(source, start, stop))

    sums_shape = f32(FIRST_PLANES * parts, UNIT_ROWS, width)
    lead = call(
        pair_kernel,
        "pair_x",
        0,
        [anywhere()],
        [in_vmem()],
        [pltpu.VMEM((LEAD_UNITS, short, width), jnp.float32)],
        [in_hbm(units)],
        scratch=[pltpu.VMEM((LEAD_UNITS, UNIT_ROWS, width), jnp.float32), pltpu.SemaphoreType.DMA((LEAD_UNITS,))],
    )[0]
    lead, ready = lax.optimization_barrier((lead, units))
    lead_moved = along_gz(lead)
    first = FIRST_PLANES * parts - LEAD_UNITS
    first_block = call(
        functools.partial(x_kernel, LEAD_UNITS),
        "smooth_x",
        0,
        [anywhere()],
        [in_vmem()],
        [pltpu.VMEM((first, short, width), jnp.float32)],
        [in_hbm(ready)],
        scratch=[
            pltpu.VMEM((first, UNIT_ROWS, width), jnp.float32),
            matrix,
            pltpu.SemaphoreType.DMA((first,)),
        ],
    )[0]
    first_block, ready = lax.optimization_barrier((first_block, coarse_six))
    first_moved = along_gz(first_block)
    sums = call(
        functools.partial(pair_z_kernel, weights),
        "smooth_zx",
        LEAD_UNITS,
        [packed()] * count,
        [unit()],
        [sums_shape],
        [lead, *lead_moved],
        scratch=[matrix, pltpu.VMEM((UNIT_ROWS, width), jnp.float32)],
    )

    later, short_sent = [], []
    start = FIRST_PLANES
    near = halo(ready, start, start + LATER_GROUPS[0][0])
    near, sums = lax.optimization_barrier((near, sums))
    for number, (size, messages) in enumerate(LATER_GROUPS):
        sources = [near[0], in_hbm(coarse_six), near[1]]
        specs = [edge(), whole(start), edge()]
        scratch = [matrix, pltpu.VMEM((rows, width), jnp.float32)]
        if messages or not can_shorten(rows, width):
            messages = messages or (size * parts,)
            blocks = call(
                yx_kernel,
                "smooth_yx",
                size,
                specs,
                [all_of(length, short, width) for length in messages],
                [f32(length, short, width) for length in messages],
                sources,
                scratch=scratch,
            )
            place = start * parts
            for block, length in zip(blocks, messages):
                later.append((place, length, (block, *along_gz(block))))
                place += length
        else:
            pieces = size * short_tiles(rows, width) + 1
            block = call(
                short_kernel,
                "smooth_yx_short",
                size,
                specs,
                [all_of(pieces, STRIP, LANES)],
                [f32(pieces, STRIP, LANES)],
                sources,
                scratch=scratch,
            )[0]
            short_sent.append((start, size, (block, *along_gz(block))))
        start += size
        if number == 0:
            block, ready = lax.optimization_barrier((block, ready))
            block, *first_moved = lax.optimization_barrier((block, *first_moved))
            sums = call(
                functools.partial(z_kernel, weights),
                "smooth_z",
                first,
                [packed()] * count + [anywhere()],
                [unit(LEAD_UNITS)],
                [sums_shape],
                [first_block, *first_moved, *sums],
                {count: 0},
            )[0]
            along_z = sums.reshape(FIRST_PLANES, rows, width)
            along_z, ready = lax.optimization_barrier((along_z, ready))
        if number + 1 < len(LATER_GROUPS):
            block, ready = lax.optimization_barrier((block, ready))
            if number:
                ready, _ = lax.optimization_barrier((ready, short_sent[0][2]))
            near = edges(ready, start, start + LATER_GROUPS[number + 1][0])
            if number:
                near, sides = lax.optimization_barrier((near, sides))
                sides = swapped(*sides)
            near = swapped(*near)
        if number and short_sent:
            near, _ = lax.optimization_barrier((near, short_sent[0][2]))
        if number == 0:
            near, along_z = lax.optimization_barrier((near, along_z))
            sides = edges(along_z, 0, FIRST_PLANES)

    strips = TAP_DILATION // STRIP

    def strips_of(first):
        return pl.BlockSpec((strips, 1, STRIP, width), lambda step: (0, first + step, 0, 0))

    def sum_short(batch):
        planes_in = sum(size for _, size, _ in batch)
        step, sums = 0, []
        for _, size, blocks in batch:
            sums = call(
                functools.partial(short_z_kernel, weights),
                "smooth_z_short",
                size,
                [all_of(*blocks[0].shape)] * count + [anywhere()] * len(sums),
                [whole(step), strips_of(step)],
                [f32(planes_in, rows, width), f32(strips, planes_in, STRIP, width)],
                [*blocks, *sums],
                {count + at: at for at in range(len(sums))},
            )
            step += size
        return sums[0], lax.all_to_all(sums[1], "gy", 0, 0)

    def finish_short(batch, sums, outs):
        start, size = batch[0][0], sum(size for _, size, _ in batch)
        along_z, moved = sums
        outs, moved = lax.optimization_barrier((outs, moved))
        return call(
            short_finish_kernel,
            "finish_short",
            size,
            [whole(), strips_of(0), whole(start)] + [anywhere()] * 2,
            [whole(start)] * 2,
            [f32(planes, rows, width)] * 2,
            [along_z, moved, coarse_six, *outs],
            {3: 0, 4: 1},
        )

    batches = [batch for batch in (short_sent[:SHORT_FIRST], short_sent[SHORT_FIRST:]) if batch]
    first_sums = sum_short(batches[0])
    first_sums, sides = lax.optimization_barrier((first_sums, sides))
    outs = call(
        y_kernel,
        "smooth_y",
        FIRST_PLANES,
        [edge(), whole(), edge(), whole()],
        [whole(), whole()],
        [f32(planes, rows, width)] * 2,
        [sides[0], along_z, sides[1], coarse_six],
    )
    outs = finish_short(batches[0], first_sums, outs)
    outs = [out.reshape(units.shape) for out in outs]
    for place, size, blocks in later[:-1]:
        outs, blocks = lax.optimization_barrier((outs, blocks))
        outs = call(
            functools.partial(finish_kernel, weights),
            "finish",
            size,
            [packed()] * count + [unit(place)] + [anywhere()] * 2,
            [unit(place)] * 2,
            [f32(*units.shape)] * 2,
            [*blocks, units, *outs],
            {count + 1: 0, count + 2: 1},
        )
    place, _, blocks = later[-1]
    outs, blocks = lax.optimization_barrier((outs, blocks))
    outs = call(
        functools.partial(last_kernel, weights, place),
        "finish_last",
        0,
        [in_vmem()] * (count + 1) + [anywhere()] * 2,
        [anywhere()] * 2,
        [f32(*units.shape)] * 2,
        [*blocks, units, *outs],
        {count + 1: 0, count + 2: 1},
        scratch=[
            pltpu.VMEM((2, UNIT_ROWS, width), jnp.float32),
            pltpu.SemaphoreType.DMA((2, 2)),
        ],
    )
    return tuple(out.reshape(coarse_six.shape) for out in outs)


def solution(mesh):
    return jax.shard_map(
        shards,
        mesh=mesh,
        in_specs=(P("gz", "gy", None),),
        out_specs=(P("gz", "gy", None), P("gz", "gy", None)),
        check_vma=False,
    )
```

```python
import functools
import math

import jax
import jax.numpy as jnp
from jax import lax
from jax.experimental import pallas as pl
from jax.experimental.pallas import tpu as pltpu
from jax.sharding import PartitionSpec as P

TAP_DILATION = 32
REACH = 2 * TAP_DILATION
LANES = 128
STRIP = 8
UNIT_ROWS = 128
PIECES = 4
FIRST_PLANES = 3
LATER_GROUPS = (((2, 0),), ((1, 0), (1, 1), (1, 2)))

kernel_weights = (0.0625, 0.25, 0.375, 0.25, 0.0625)


def passed_along(x, axis, by):
    peers = lax.axis_size(axis)
    return lax.ppermute(x, axis, [(i, (i + by) % peers) for i in range(peers)])


def z_taps(plane_stack, count):
    weights = {}
    for cell_position in range(5):
        filter_reach = (cell_position - 2) * TAP_DILATION // plane_stack
        moved = -filter_reach % count
        weights[moved] = weights.get(moved, 0.0) + kernel_weights[cell_position]
    own = weights.pop(0, 0.0)
    return own, weights


def lane_of(shape):
    return lax.broadcasted_iota(jnp.int32, shape, 1)


def x_taps():
    return {(cell_position - 2) * TAP_DILATION: kernel_weights[cell_position] for cell_position in range(5)}


def rest_taps():
    return {(cell_position - 2) * TAP_DILATION: weight for cell_position, weight in enumerate((0.125, 0.375, 0.375, 0.125))}


def pair_sums(rows):
    return (rows + pltpu.roll(rows, rows.shape[1] - TAP_DILATION, 1)) * 0.5


def fill_matrix(matrix_ref, taps):
    depth, width = matrix_ref.shape
    for start in range(0, depth, LANES):
        shape = (LANES, width)
        row = start + lax.broadcasted_iota(jnp.int32, shape, 0)
        offset = row - lax.broadcasted_iota(jnp.int32, shape, 1)
        offset = jnp.where(offset < 0, offset + width, offset)
        values = jnp.zeros(shape, jnp.float32)
        for tap, weight in taps.items():
            values = jnp.where(offset == tap % width, weight, values)
        matrix_ref[pl.ds(start, LANES), :] = values.astype(jnp.bfloat16)


def x_smoothed(rows, matrix):
    parts = []
    for _ in range(3):
        parts.append(rows.astype(jnp.bfloat16))
        rows = rows - parts[-1].astype(jnp.float32)
    terms = jnp.dot(jnp.concatenate(parts), matrix, preferred_element_type=jnp.float32)
    high, middle, low = jnp.split(terms, 3)
    return high + middle + low


def y_sums(groups):
    for _ in range(4):
        groups = [a + b for a, b in zip(groups[:-1], groups[1:])]
    return groups


def packed_rows(width):
    return UNIT_ROWS - UNIT_ROWS * TAP_DILATION // width


def store_packed(out_ref, place, smooth):
    rows, width = smooth.shape
    kept_rows = out_ref.shape[1]
    depth = rows - kept_rows
    out_ref[place, :, : width - LANES] = smooth[:kept_rows, : width - LANES]
    kept = lane_of((depth, LANES)) < LANES - TAP_DILATION
    for piece in range(kept_rows // depth):
        tile = piece * TAP_DILATION // LANES
        shift = (LANES - TAP_DILATION - piece * TAP_DILATION) % LANES
        moved = smooth[kept_rows:, tile * LANES : (tile + 1) * LANES]
        if shift:
            moved = pltpu.roll(moved, shift, 1)
        last = smooth[piece * depth : (piece + 1) * depth, width - LANES :]
        out_ref[place, pl.ds(piece * depth, depth), width - LANES :] = jnp.where(kept, last, moved)


def completed(strip):
    width = strip.shape[1]
    last = strip[:, width - LANES :]
    lane = lane_of(last.shape)
    kept = lane < LANES - TAP_DILATION
    total = jnp.where(kept, last, 0.0)
    for start in range(0, width - LANES, LANES):
        total = total + strip[:, start : start + LANES]
    odd = (lane // TAP_DILATION) % 2 == 1
    total = jnp.where(odd, -total, total)
    total = total + pltpu.roll(total, 2 * TAP_DILATION, 1)
    total = total + pltpu.roll(total, TAP_DILATION, 1)
    return jnp.concatenate([strip[:, : width - LANES], jnp.where(kept, last, total)], axis=1)


def unpacked(weights, refs, use):
    kept_rows, width = refs[0].shape[1:]
    depth = UNIT_ROWS - kept_rows
    tiles = [None] * (width // LANES)
    for piece in range(kept_rows // depth):
        rows = pl.ds(piece * depth, depth)
        strip = weighted(weights, [ref[0, rows, :] for ref in refs])
        tile = piece * TAP_DILATION // LANES
        shift = (piece * TAP_DILATION - (LANES - TAP_DILATION)) % LANES
        moved = strip[:, width - LANES :]
        if shift:
            moved = pltpu.roll(moved, shift, 1)
        if tiles[tile] is None:
            tiles[tile] = moved
        else:
            here = lane_of(moved.shape) // TAP_DILATION == piece % (LANES // TAP_DILATION)
            tiles[tile] = jnp.where(here, moved, tiles[tile])
        use(rows, completed(strip))
    use(pl.ds(kept_rows, depth), completed(jnp.concatenate(tiles, axis=1)))


def weighted(weights, values):
    total = None
    for weight, value in zip(weights, values):
        term = weight * value
        total = term if total is None else total + term
    return total


def pair_kernel(units_ref, out_ref, read_ref, read_sems):
    pieces = read_sems.shape[0]
    depth = UNIT_ROWS // pieces
    kept_strips = out_ref.shape[1] // STRIP
    width = read_ref.shape[1]
    kept = lane_of((STRIP, LANES)) < LANES - TAP_DILATION

    def read(piece):
        rows = pl.ds(piece * depth, depth)
        return pltpu.make_async_copy(units_ref.at[0, rows], read_ref.at[rows], read_sems.at[piece])

    order = [pieces - 1, *range(pieces - 1)]
    for piece in order:
        read(piece).start()
    source = None
    for piece in order:
        read(piece).wait()
        smooth = pair_sums(read_ref[pl.ds(piece * depth, depth), :])
        if source is None:
            source = smooth[depth - STRIP :]
        for at in range(depth // STRIP):
            number = piece * depth // STRIP + at
            if number == kept_strips:
                continue
            strip = smooth[at * STRIP : (at + 1) * STRIP]
            tile = number * TAP_DILATION // LANES
            shift = (LANES - TAP_DILATION - number * TAP_DILATION) % LANES
            moved = source[:, tile * LANES : (tile + 1) * LANES]
            if shift:
                moved = pltpu.roll(moved, shift, 1)
            rows = pl.ds(number * STRIP, STRIP)
            out_ref[0, rows, : width - LANES] = strip[:, : width - LANES]
            out_ref[0, rows, width - LANES :] = jnp.where(kept, strip[:, width - LANES :], moved)


def x_kernel(first, units_ref, out_ref, read_ref, matrix_ref, read_sems):
    count = out_ref.shape[0]

    def read(unit):
        return pltpu.make_async_copy(units_ref.at[first + unit], read_ref.at[unit], read_sems.at[unit])

    for unit in range(count):
        read(unit).start()
    fill_matrix(matrix_ref, x_taps())

    @pl.loop(0, count)
    def _(unit):
        read(unit).wait()
        store_packed(out_ref, unit, x_smoothed(read_ref[unit], matrix_ref[...]))


def extended_groups(before_ref, c_ref, after_ref, offset):
    groups = []
    for ref in (before_ref, c_ref, after_ref):
        for start in range(0, ref.shape[1], TAP_DILATION):
            groups.append(ref[0, pl.ds(start + offset, STRIP), :])
    return groups


def y_smoothed(before_ref, c_ref, after_ref, smooth_ref):
    for within in range(TAP_DILATION // STRIP):
        groups = y_sums(extended_groups(before_ref, c_ref, after_ref, within * STRIP))
        for group, strip in enumerate(groups):
            smooth_ref[pl.ds(group * TAP_DILATION + within * STRIP, STRIP), :] = strip * (1.0 / 16.0)


def yx_kernel(before_ref, c_ref, after_ref, *refs):
    *out_refs, matrix_ref, smooth_ref = refs
    pl.when(pl.program_id(0) == 0)(lambda: fill_matrix(matrix_ref, x_taps()))
    y_smoothed(before_ref, c_ref, after_ref, smooth_ref)
    places = [(ref, place) for ref in out_refs for place in range(ref.shape[0])]
    for unit, (ref, place) in enumerate(places):
        smooth = x_smoothed(smooth_ref[pl.ds(unit * UNIT_ROWS, UNIT_ROWS), :], matrix_ref[...])
        store_packed(ref, place, smooth)


def z_kernel(weights, *refs):
    whole_ref = refs[-1]

    def use(rows, strip):
        whole_ref[0, rows, :] = strip

    unpacked(weights, refs[: len(weights)], use)


def group_of(shape):
    return lane_of(shape) // TAP_DILATION


def spread(tile, group):
    tile = jnp.where(group_of(tile.shape) == group, tile, 0.0)
    tile = tile + pltpu.roll(tile, 2 * TAP_DILATION, 1)
    return tile + pltpu.roll(tile, TAP_DILATION, 1)


def strip_rows(rows, ahead):
    per_group = TAP_DILATION // STRIP
    strip = lax.rem(lax.axis_index("gy") + ahead, per_group)
    return pl.ds(pl.multiple_of(rows - TAP_DILATION + strip * STRIP, STRIP), STRIP)


def short_strips(rows):
    half = rows - UNIT_ROWS
    fixed = [pl.ds(row, STRIP) for row in range(0, rows - TAP_DILATION, STRIP)]
    moving = [strip_rows(rows, ahead) for ahead in range(1, TAP_DILATION // STRIP)]
    return fixed[: half // STRIP], fixed[half // STRIP :] + moving


def short_tiles(rows, width):
    return (rows // STRIP - 3) * (width // LANES)


def short_kernel(before_ref, c_ref, after_ref, out_ref, matrix_ref, smooth_ref):
    plane = pl.program_id(0)

    @pl.when(plane == 0)
    def _():
        fill_matrix(matrix_ref, x_taps())
        out_ref[out_ref.shape[0] - 1] = jnp.zeros((STRIP, LANES), jnp.float32)

    y_smoothed(before_ref, c_ref, after_ref, smooth_ref)
    rows, width = smooth_ref.shape
    for start in range(0, rows, UNIT_ROWS):
        unit = pl.ds(start, UNIT_ROWS)
        smooth_ref[unit, :] = x_smoothed(smooth_ref[unit, :], matrix_ref[...])
    index = plane * short_tiles(rows, width)
    groups = LANES // TAP_DILATION
    for places in short_strips(rows):
        *places, last_place = places
        last = smooth_ref[last_place, :]
        for piece, place in enumerate(places):
            strip = smooth_ref[place, :]
            tile = piece // groups * LANES
            moved = last[:, tile : tile + LANES]
            shift = (groups - 1 - piece) % groups * TAP_DILATION
            if shift:
                moved = pltpu.roll(moved, shift, 1)
            for start in range(0, width - LANES, LANES):
                out_ref[index] = strip[:, start : start + LANES]
                index += 1
            here = group_of(moved.shape) == groups - 1
            out_ref[index] = jnp.where(here, moved, strip[:, width - LANES :])
            index += 1
    left = spread(last[:, width - LANES :], groups - 2)
    end = out_ref.shape[0] - 1
    out_ref[end] = jnp.where(group_of(left.shape) == plane, left, out_ref[end])


def short_z_kernel(weights, *refs):
    packed, (whole_ref, *sum_refs) = refs[: len(weights)], refs[-4:]
    rows, width = whole_ref.shape[1:]
    plane = pl.program_id(0)
    index = plane * short_tiles(rows, width)
    groups, tiles = LANES // TAP_DILATION, width // LANES
    for places in short_strips(rows):
        *places, last_place = places
        last = [None] * tiles
        for piece, place in enumerate(places):
            strip = [weighted(weights, [ref[index + tile] for ref in packed]) for tile in range(tiles)]
            index += tiles
            tile, group = divmod(piece, groups)
            shift = (group + 1 - groups) % groups * TAP_DILATION
            moved = pltpu.roll(strip[-1], shift, 1) if shift else strip[-1]
            here = group_of(moved.shape) == group
            last[tile] = moved if last[tile] is None else jnp.where(here, moved, last[tile])
            whole_ref[0, place, :] = completed(jnp.concatenate(strip, axis=1))
        if len(places) < tiles * groups - 1:
            end = packed[0].shape[0] - 1
            left = spread(weighted(weights, [ref[end] for ref in packed]), plane)
            last[-1] = jnp.where(group_of(left.shape) == groups - 2, left, last[-1])
        whole_ref[0, last_place, :] = completed(jnp.concatenate(last, axis=1))

    groups = rows // TAP_DILATION
    for ahead in range(TAP_DILATION // STRIP):
        total = None
        for group in range(groups if ahead else groups - 1):
            strip = whole_ref[0, strip_rows((group + 1) * TAP_DILATION, ahead), :]
            if total is None:
                total = strip
            else:
                total = total + strip if group % 2 == 0 else total - strip
        if ahead:
            sum_refs[ahead - 1][0] = total
        else:
            whole_ref[0, strip_rows(rows, 0), :] = total


def short_finish_kernel(whole_ref, *refs):
    *sum_refs, c_ref, _, _, detail_ref, coarse_ref = refs
    missing = strip_rows(whole_ref.shape[1], 0)
    coarse_ref[...] = whole_ref[...]
    coarse_ref[0, missing, :] = whole_ref[0, missing, :] + sum(ref[0] for ref in sum_refs)
    detail_ref[...] = c_ref[...] - coarse_ref[...]


def pair_z_kernel(weights, *refs):
    whole_ref, matrix_ref, pair_ref = refs[-3:]
    fill_matrix(matrix_ref, rest_taps())

    def use(rows, strip):
        pair_ref[rows, :] = strip

    unpacked(weights, refs[: len(weights)], use)
    whole_ref[0] = x_smoothed(pair_ref[...], matrix_ref[...])


def y_kernel(before_ref, whole_ref, after_ref, c_ref, detail_ref, coarse_ref):
    scale = 1.0 / 16.0
    for within in range(TAP_DILATION // STRIP):
        groups = y_sums(extended_groups(before_ref, whole_ref, after_ref, within * STRIP))
        for group, strip in enumerate(groups):
            rows = pl.ds(group * TAP_DILATION + within * STRIP, STRIP)
            coarse = strip * scale
            coarse_ref[0, rows, :] = coarse
            detail_ref[0, rows, :] = c_ref[0, rows, :] - coarse


def finish_kernel(weights, *refs):
    c_ref, _, _, detail_ref, coarse_ref = refs[len(weights) :]

    def use(rows, strip):
        coarse_ref[0, rows, :] = strip
        detail_ref[0, rows, :] = c_ref[0, rows, :] - strip

    unpacked(weights, refs[: len(weights)], use)


def last_kernel(weights, place, *refs):
    units_ref, _, _, detail_ref, coarse_ref, results_ref, write_sems = refs[len(weights) :]
    depth = UNIT_ROWS // PIECES

    def write(piece, output, ref):
        rows = pl.ds(piece * depth, depth)
        source = results_ref.at[output, rows]
        return pltpu.make_async_copy(source, ref.at[place, rows], write_sems.at[piece, output])

    writes = [[write(piece, 0, detail_ref), write(piece, 1, coarse_ref)] for piece in range(PIECES)]

    def use(rows, strip):
        results_ref[1, rows, :] = strip
        results_ref[0, rows, :] = units_ref[place, rows, :] - strip
        piece, left = divmod(rows.start + rows.size, depth)
        if left == 0:
            for copy in writes[piece - 1]:
                copy.start()

    unpacked(weights, refs[: len(weights)], use)
    for copies in writes:
        for copy in copies:
            copy.wait()


def block_of(rows, width, first=0, depth=1):
    return pl.BlockSpec((depth, rows, width), lambda step: (first + step, 0, 0))


def anywhere():
    return pl.BlockSpec(memory_space=pl.ANY)


def tiles_of(pieces):
    return pl.BlockSpec((pieces, STRIP, LANES), lambda step: (0, 0, 0))


def in_vmem():
    return pl.BlockSpec(memory_space=pltpu.VMEM)


def call(kernel, name, steps, in_specs, out_specs, out_shape, args, aliases=None, scratch=(), grant=24):
    blocks = [spec.block_shape for spec in (*in_specs, *out_specs) if spec.block_shape]
    moved = 4 * max(steps, 1) * sum(math.prod(block) for block in blocks)
    return pl.pallas_call(
        kernel,
        grid=(steps,) if steps else (),
        in_specs=in_specs,
        out_specs=out_specs,
        out_shape=out_shape,
        scratch_shapes=scratch,
        input_output_aliases=aliases or {},
        compiler_params=pltpu.CompilerParams(vmem_limit_bytes=grant * 1024 * 1024),
        cost_estimate=pl.CostEstimate(flops=moved * 2, bytes_accessed=moved, transcendentals=0),
        name=name,
    )(*args)


def in_hbm(x):
    return pltpu.with_memory_space_constraint(x, pltpu.HBM)


def f32(*shape):
    return jax.ShapeDtypeStruct(shape, jnp.float32)


def can_shorten(rows, width):
    strips = TAP_DILATION // STRIP
    return lax.axis_size("gy") == strips and rows // TAP_DILATION % 2 == 0 and UNIT_ROWS // STRIP == width // TAP_DILATION


def shards(coarse_six):
    planes, rows, width = coarse_six.shape
    short = packed_rows(width)
    own, shifts = z_taps(planes, lax.axis_size("gz"))
    weights = (own, *shifts.values())
    count = len(weights)
    whole, unit, packed, edge = (functools.partial(block_of, n, width) for n in (rows, UNIT_ROWS, short, REACH))
    parts = rows // UNIT_ROWS
    units = coarse_six.reshape(planes * parts, UNIT_ROWS, width)
    matrix = pltpu.VMEM((width, width), jnp.bfloat16)

    def along_gz(x):
        return [passed_along(x, "gz", moved) for moved in shifts]

    def halo(source, start, stop):
        top, bottom = source[start:stop, :REACH], source[start:stop, rows - REACH :]
        return passed_along(bottom, "gy", 1), passed_along(top, "gy", -1)

    sums_shape = f32(FIRST_PLANES * parts, UNIT_ROWS, width)
    lead = call(
        pair_kernel,
        "pair_x",
        0,
        [anywhere()],
        [in_vmem()],
        [pltpu.VMEM((1, short, width), jnp.float32)],
        [in_hbm(units)],
        scratch=[pltpu.VMEM((UNIT_ROWS, width), jnp.float32), pltpu.SemaphoreType.DMA((PIECES,))],
    )[0]
    lead, ready = lax.optimization_barrier((lead, units))
    lead_moved = along_gz(lead)
    first = FIRST_PLANES * parts - 1
    first_block = call(
        functools.partial(x_kernel, 1),
        "smooth_x",
        0,
        [anywhere()],
        [in_vmem()],
        [pltpu.VMEM((first, short, width), jnp.float32)],
        [in_hbm(ready)],
        scratch=[
            pltpu.VMEM((first, UNIT_ROWS, width), jnp.float32),
            matrix,
            pltpu.SemaphoreType.DMA((first,)),
        ],
    )[0]
    first_block, ready = lax.optimization_barrier((first_block, ready))
    first_moved = along_gz(first_block)
    sums = call(
        functools.partial(pair_z_kernel, weights),
        "smooth_zx",
        1,
        [packed()] * count,
        [unit()],
        [sums_shape],
        [lead, *lead_moved],
        scratch=[matrix, pltpu.VMEM((UNIT_ROWS, width), jnp.float32)],
    )

    later, short_sent = [], []
    start = FIRST_PLANES
    sums, ready = lax.optimization_barrier((sums, coarse_six))
    near = halo(ready, start, start + sum(size for size, _ in LATER_GROUPS[0]))
    for number, sizes in enumerate(LATER_GROUPS):
        offset = 0
        for size, messages in sizes:
            place = start + offset
            sources = [near[0], in_hbm(coarse_six), near[1]]
            specs = [edge(offset), whole(place), edge(offset)]
            scratch = [matrix, pltpu.VMEM((rows, width), jnp.float32)]
            if messages or not can_shorten(rows, width):
                messages = max(messages, 1)
                depth = parts // messages
                blocks = call(
                    yx_kernel,
                    "smooth_yx",
                    size,
                    specs,
                    [packed(depth=depth)] * messages,
                    [f32(size * depth, short, width)] * messages,
                    sources,
                    scratch=scratch,
                )
                for message, block in enumerate(blocks):
                    later.append((place * parts + message * depth, size * depth, (block, *along_gz(block))))
            else:
                pieces = size * short_tiles(rows, width) + 1
                block = call(
                    short_kernel,
                    "smooth_yx_short",
                    size,
                    specs,
                    [tiles_of(pieces)],
                    [f32(pieces, STRIP, LANES)],
                    sources,
                    scratch=scratch,
                )[0]
                short_sent.append((place, size, (block, *along_gz(block))))
            offset += size
        start += offset
        if number == 0:
            block, ready = lax.optimization_barrier((block, ready))
            block, *first_moved = lax.optimization_barrier((block, *first_moved))
            sums = call(
                functools.partial(z_kernel, weights),
                "smooth_z",
                first,
                [packed()] * count + [anywhere()],
                [unit(1)],
                [sums_shape],
                [first_block, *first_moved, *sums],
                {count: 0},
            )[0]
            along_z = sums.reshape(FIRST_PLANES, rows, width)
            sides = halo(along_z, 0, FIRST_PLANES)
        if number + 1 < len(LATER_GROUPS):
            near = halo(ready, start, start + sum(size for size, _ in LATER_GROUPS[number + 1]))
            near, along_z = lax.optimization_barrier((near, along_z))

    short_sums, shortened = [], sum(size for _, size, _ in short_sent)
    if short_sent:
        step = 0
        for place, size, blocks in short_sent:
            short_sums = call(
                functools.partial(short_z_kernel, weights),
                "smooth_z_short",
                size,
                [tiles_of(blocks[0].shape[0])] * count + [anywhere()] * len(short_sums),
                [whole(step)] + [block_of(STRIP, width, step)] * 3,
                [f32(shortened, rows, width)] + [f32(shortened, STRIP, width)] * 3,
                [*blocks, *short_sums],
                {count + at: at for at in range(len(short_sums))},
            )
            step += size
        moved_sums = [passed_along(total, "gy", ahead) for ahead, total in enumerate(short_sums[1:], 1)]
        block = short_sums[0]

    block, sides = lax.optimization_barrier((block, sides))
    outs = call(
        y_kernel,
        "smooth_y",
        FIRST_PLANES,
        [edge(), whole(), edge(), whole()],
        [whole(), whole()],
        [f32(planes, rows, width)] * 2,
        [sides[0], along_z, sides[1], coarse_six],
    )
    if short_sent:
        outs, moved_sums = lax.optimization_barrier((outs, moved_sums))
        outs = call(
            short_finish_kernel,
            "finish_short",
            shortened,
            [whole()] + [block_of(STRIP, width)] * 3 + [whole(short_sent[0][0])] + [anywhere()] * 2,
            [whole(short_sent[0][0])] * 2,
            [f32(planes, rows, width)] * 2,
            [short_sums[0], *moved_sums, coarse_six, *outs],
            {5: 0, 6: 1},
        )
    outs = [out.reshape(units.shape) for out in outs]
    for place, size, blocks in later[:-1]:
        outs, blocks = lax.optimization_barrier((outs, blocks))
        outs = call(
            functools.partial(finish_kernel, weights),
            "finish",
            size,
            [packed()] * count + [unit(place)] + [anywhere()] * 2,
            [unit(place)] * 2,
            [f32(*units.shape)] * 2,
            [*blocks, units, *outs],
            {count + 1: 0, count + 2: 1},
        )
    place, _, blocks = later[-1]
    outs, blocks = lax.optimization_barrier((outs, blocks))
    outs = call(
        functools.partial(last_kernel, weights, place),
        "finish_last",
        0,
        [in_vmem()] * (count + 1) + [anywhere()] * 2,
        [anywhere()] * 2,
        [f32(*units.shape)] * 2,
        [*blocks, units, *outs],
        {count + 1: 0, count + 2: 1},
        scratch=[
            pltpu.VMEM((2, UNIT_ROWS, width), jnp.float32),
            pltpu.SemaphoreType.DMA((PIECES, 2)),
        ],
    )
    return tuple(out.reshape(coarse_six.shape) for out in outs)


def solution(mesh):
    return jax.shard_map(
        shards,
        mesh=mesh,
        in_specs=(P("gz", "gy", None),),
        out_specs=(P("gz", "gy", None), P("gz", "gy", None)),
        check_vma=False,
    )
```

```python
import functools
import math

import jax
import jax.numpy as jnp
from jax import lax
from jax.experimental import pallas as pl
from jax.experimental.pallas import tpu as pltpu
from jax.sharding import PartitionSpec as P

TAP_DILATION = 32
REACH = 2 * TAP_DILATION
LANES = 128
STRIP = 8
UNIT_ROWS = 128
FIRST_PLANES = 2
LEAD_UNITS = 2
LATER_GROUPS = (((2, 0),), ((2, 0),), ((1, 1), (1, 2)))
SHORT_FIRST = 2

kernel_weights = (0.0625, 0.25, 0.375, 0.25, 0.0625)


def passed_along(x, axis, by):
    peers = lax.axis_size(axis)
    return lax.ppermute(x, axis, [(i, (i + by) % peers) for i in range(peers)])


def z_taps(plane_stack, count):
    weights = {}
    for cell_position in range(5):
        filter_reach = (cell_position - 2) * TAP_DILATION // plane_stack
        moved = -filter_reach % count
        weights[moved] = weights.get(moved, 0.0) + kernel_weights[cell_position]
    own = weights.pop(0, 0.0)
    return own, weights


def lane_of(shape):
    return lax.broadcasted_iota(jnp.int32, shape, 1)


def x_taps():
    return {(cell_position - 2) * TAP_DILATION: kernel_weights[cell_position] for cell_position in range(5)}


def rest_taps():
    return {(cell_position - 2) * TAP_DILATION: weight for cell_position, weight in enumerate((0.125, 0.375, 0.375, 0.125))}


def pair_sums(rows):
    return (rows + pltpu.roll(rows, rows.shape[1] - TAP_DILATION, 1)) * 0.5


def fill_matrix(matrix_ref, taps):
    depth, width = matrix_ref.shape
    for start in range(0, depth, LANES):
        shape = (LANES, width)
        row = start + lax.broadcasted_iota(jnp.int32, shape, 0)
        offset = row - lax.broadcasted_iota(jnp.int32, shape, 1)
        offset = jnp.where(offset < 0, offset + width, offset)
        values = jnp.zeros(shape, jnp.float32)
        for tap, weight in taps.items():
            values = jnp.where(offset == tap % width, weight, values)
        matrix_ref[pl.ds(start, LANES), :] = values.astype(jnp.bfloat16)


def x_smoothed(rows, matrix):
    parts = []
    for _ in range(3):
        parts.append(rows.astype(jnp.bfloat16))
        rows = rows - parts[-1].astype(jnp.float32)
    terms = jnp.dot(jnp.concatenate(parts), matrix, preferred_element_type=jnp.float32)
    high, middle, low = jnp.split(terms, 3)
    return high + middle + low


def y_sums(groups):
    for _ in range(4):
        groups = [a + b for a, b in zip(groups[:-1], groups[1:])]
    return groups


def packed_rows(width):
    return UNIT_ROWS - UNIT_ROWS * TAP_DILATION // width


def store_packed(out_ref, place, smooth):
    rows, width = smooth.shape
    kept_rows = out_ref.shape[1]
    depth = rows - kept_rows
    out_ref[place, :, : width - LANES] = smooth[:kept_rows, : width - LANES]
    kept = lane_of((depth, LANES)) < LANES - TAP_DILATION
    for piece in range(kept_rows // depth):
        tile = piece * TAP_DILATION // LANES
        shift = (LANES - TAP_DILATION - piece * TAP_DILATION) % LANES
        moved = smooth[kept_rows:, tile * LANES : (tile + 1) * LANES]
        if shift:
            moved = pltpu.roll(moved, shift, 1)
        last = smooth[piece * depth : (piece + 1) * depth, width - LANES :]
        out_ref[place, pl.ds(piece * depth, depth), width - LANES :] = jnp.where(kept, last, moved)


def completed(strip):
    width = strip.shape[1]
    last = strip[:, width - LANES :]
    lane = lane_of(last.shape)
    kept = lane < LANES - TAP_DILATION
    total = jnp.where(kept, last, 0.0)
    for start in range(0, width - LANES, LANES):
        total = total + strip[:, start : start + LANES]
    odd = (lane // TAP_DILATION) % 2 == 1
    total = jnp.where(odd, -total, total)
    total = total + pltpu.roll(total, 2 * TAP_DILATION, 1)
    total = total + pltpu.roll(total, TAP_DILATION, 1)
    return jnp.concatenate([strip[:, : width - LANES], jnp.where(kept, last, total)], axis=1)


def unpacked(weights, refs, use):
    kept_rows, width = refs[0].shape[1:]
    depth = UNIT_ROWS - kept_rows
    tiles = [None] * (width // LANES)
    for piece in range(kept_rows // depth):
        rows = pl.ds(piece * depth, depth)
        strip = weighted(weights, [ref[0, rows, :] for ref in refs])
        tile = piece * TAP_DILATION // LANES
        shift = (piece * TAP_DILATION - (LANES - TAP_DILATION)) % LANES
        moved = strip[:, width - LANES :]
        if shift:
            moved = pltpu.roll(moved, shift, 1)
        if tiles[tile] is None:
            tiles[tile] = moved
        else:
            here = lane_of(moved.shape) // TAP_DILATION == piece % (LANES // TAP_DILATION)
            tiles[tile] = jnp.where(here, moved, tiles[tile])
        use(rows, completed(strip))
    use(pl.ds(kept_rows, depth), completed(jnp.concatenate(tiles, axis=1)))


def weighted(weights, values):
    total = None
    for weight, value in zip(weights, values):
        term = weight * value
        total = term if total is None else total + term
    return total


def pair_kernel(units_ref, out_ref, read_ref, read_sems):
    def read(unit):
        return pltpu.make_async_copy(units_ref.at[unit], read_ref.at[unit], read_sems.at[unit])

    for unit in range(out_ref.shape[0]):
        read(unit).start()
    for unit in range(out_ref.shape[0]):
        read(unit).wait()
        store_packed(out_ref, unit, pair_sums(read_ref[unit]))


def x_kernel(first, units_ref, out_ref, read_ref, matrix_ref, read_sems):
    count = out_ref.shape[0]

    def read(unit):
        return pltpu.make_async_copy(units_ref.at[first + unit], read_ref.at[unit], read_sems.at[unit])

    for unit in range(count):
        read(unit).start()
    fill_matrix(matrix_ref, x_taps())

    @pl.loop(0, count)
    def _(unit):
        read(unit).wait()
        store_packed(out_ref, unit, x_smoothed(read_ref[unit], matrix_ref[...]))


def extended_groups(before_ref, c_ref, after_ref, offset):
    groups = []
    for ref in (before_ref, c_ref, after_ref):
        for start in range(0, ref.shape[1], TAP_DILATION):
            groups.append(ref[0, pl.ds(start + offset, STRIP), :])
    return groups


def y_smoothed(before_ref, c_ref, after_ref, smooth_ref):
    for within in range(TAP_DILATION // STRIP):
        groups = y_sums(extended_groups(before_ref, c_ref, after_ref, within * STRIP))
        for group, strip in enumerate(groups):
            smooth_ref[pl.ds(group * TAP_DILATION + within * STRIP, STRIP), :] = strip * (1.0 / 16.0)


def yx_kernel(before_ref, c_ref, after_ref, *refs):
    *out_refs, matrix_ref, smooth_ref = refs
    pl.when(pl.program_id(0) == 0)(lambda: fill_matrix(matrix_ref, x_taps()))
    y_smoothed(before_ref, c_ref, after_ref, smooth_ref)
    places = [(ref, place) for ref in out_refs for place in range(ref.shape[0])]
    for unit, (ref, place) in enumerate(places):
        smooth = x_smoothed(smooth_ref[pl.ds(unit * UNIT_ROWS, UNIT_ROWS), :], matrix_ref[...])
        store_packed(ref, place, smooth)


def z_kernel(weights, *refs):
    whole_ref = refs[-1]

    def use(rows, strip):
        whole_ref[0, rows, :] = strip

    unpacked(weights, refs[: len(weights)], use)


def group_of(shape):
    return lane_of(shape) // TAP_DILATION


def spread(tile, group):
    tile = jnp.where(group_of(tile.shape) == group, tile, 0.0)
    tile = tile + pltpu.roll(tile, 2 * TAP_DILATION, 1)
    return tile + pltpu.roll(tile, TAP_DILATION, 1)


def strip_rows(rows, ahead):
    per_group = TAP_DILATION // STRIP
    strip = lax.rem(lax.axis_index("gy") + ahead, per_group)
    return pl.ds(pl.multiple_of(rows - TAP_DILATION + strip * STRIP, STRIP), STRIP)


def short_strips(rows):
    half = rows - UNIT_ROWS
    fixed = [pl.ds(row, STRIP) for row in range(0, rows - TAP_DILATION, STRIP)]
    moving = [strip_rows(rows, ahead) for ahead in range(1, TAP_DILATION // STRIP)]
    return fixed[: half // STRIP], fixed[half // STRIP :] + moving


def short_tiles(rows, width):
    return (rows // STRIP - 3) * (width // LANES)


def short_kernel(before_ref, c_ref, after_ref, out_ref, matrix_ref, smooth_ref):
    plane = pl.program_id(0)

    @pl.when(plane == 0)
    def _():
        fill_matrix(matrix_ref, x_taps())
        out_ref[out_ref.shape[0] - 1] = jnp.zeros((STRIP, LANES), jnp.float32)

    y_smoothed(before_ref, c_ref, after_ref, smooth_ref)
    rows, width = smooth_ref.shape
    for start in range(0, rows, UNIT_ROWS):
        unit = pl.ds(start, UNIT_ROWS)
        smooth_ref[unit, :] = x_smoothed(smooth_ref[unit, :], matrix_ref[...])
    index = plane * short_tiles(rows, width)
    groups = LANES // TAP_DILATION
    for places in short_strips(rows):
        *places, last_place = places
        last = smooth_ref[last_place, :]
        for piece, place in enumerate(places):
            strip = smooth_ref[place, :]
            tile = piece // groups * LANES
            moved = last[:, tile : tile + LANES]
            shift = (groups - 1 - piece) % groups * TAP_DILATION
            if shift:
                moved = pltpu.roll(moved, shift, 1)
            for start in range(0, width - LANES, LANES):
                out_ref[index] = strip[:, start : start + LANES]
                index += 1
            here = group_of(moved.shape) == groups - 1
            out_ref[index] = jnp.where(here, moved, strip[:, width - LANES :])
            index += 1
    left = spread(last[:, width - LANES :], groups - 2)
    end = out_ref.shape[0] - 1
    out_ref[end] = jnp.where(group_of(left.shape) == plane, left, out_ref[end])


def short_z_kernel(weights, *refs):
    packed, (whole_ref, *sum_refs) = refs[: len(weights)], refs[-4:]
    rows, width = whole_ref.shape[1:]
    plane = pl.program_id(0)
    index = plane * short_tiles(rows, width)
    groups, tiles = LANES // TAP_DILATION, width // LANES
    for places in short_strips(rows):
        *places, last_place = places
        last = [None] * tiles
        for piece, place in enumerate(places):
            strip = [weighted(weights, [ref[index + tile] for ref in packed]) for tile in range(tiles)]
            index += tiles
            tile, group = divmod(piece, groups)
            shift = (group + 1 - groups) % groups * TAP_DILATION
            moved = pltpu.roll(strip[-1], shift, 1) if shift else strip[-1]
            here = group_of(moved.shape) == group
            last[tile] = moved if last[tile] is None else jnp.where(here, moved, last[tile])
            whole_ref[0, place, :] = completed(jnp.concatenate(strip, axis=1))
        if len(places) < tiles * groups - 1:
            end = packed[0].shape[0] - 1
            left = spread(weighted(weights, [ref[end] for ref in packed]), plane)
            last[-1] = jnp.where(group_of(left.shape) == groups - 2, left, last[-1])
        whole_ref[0, last_place, :] = completed(jnp.concatenate(last, axis=1))

    groups = rows // TAP_DILATION
    for ahead in range(TAP_DILATION // STRIP):
        total = None
        for group in range(groups if ahead else groups - 1):
            strip = whole_ref[0, strip_rows((group + 1) * TAP_DILATION, ahead), :]
            if total is None:
                total = strip
            else:
                total = total + strip if group % 2 == 0 else total - strip
        if ahead:
            sum_refs[ahead - 1][0] = total
        else:
            whole_ref[0, strip_rows(rows, 0), :] = total


def short_finish_kernel(whole_ref, *refs):
    *sum_refs, c_ref, _, _, detail_ref, coarse_ref = refs
    missing = strip_rows(whole_ref.shape[1], 0)
    coarse_ref[...] = whole_ref[...]
    coarse_ref[0, missing, :] = whole_ref[0, missing, :] + sum(ref[0] for ref in sum_refs)
    detail_ref[...] = c_ref[...] - coarse_ref[...]


def pair_z_kernel(weights, *refs):
    whole_ref, matrix_ref, pair_ref = refs[-3:]
    pl.when(pl.program_id(0) == 0)(lambda: fill_matrix(matrix_ref, rest_taps()))

    def use(rows, strip):
        pair_ref[rows, :] = strip

    unpacked(weights, refs[: len(weights)], use)
    whole_ref[0] = x_smoothed(pair_ref[...], matrix_ref[...])


def y_kernel(before_ref, whole_ref, after_ref, c_ref, detail_ref, coarse_ref):
    scale = 1.0 / 16.0
    for within in range(TAP_DILATION // STRIP):
        groups = y_sums(extended_groups(before_ref, whole_ref, after_ref, within * STRIP))
        for group, strip in enumerate(groups):
            rows = pl.ds(group * TAP_DILATION + within * STRIP, STRIP)
            coarse = strip * scale
            coarse_ref[0, rows, :] = coarse
            detail_ref[0, rows, :] = c_ref[0, rows, :] - coarse


def finish_kernel(weights, *refs):
    c_ref, _, _, detail_ref, coarse_ref = refs[len(weights) :]

    def use(rows, strip):
        coarse_ref[0, rows, :] = strip
        detail_ref[0, rows, :] = c_ref[0, rows, :] - strip

    unpacked(weights, refs[: len(weights)], use)


def last_kernel(weights, place, *refs):
    units_ref, _, _, detail_ref, coarse_ref, results_ref, write_sems = refs[len(weights) :]
    half = UNIT_ROWS // 2

    def write(piece, output, ref):
        rows = pl.ds(piece * half, half)
        source = results_ref.at[output, rows]
        return pltpu.make_async_copy(source, ref.at[place, rows], write_sems.at[piece, output])

    writes = [[write(piece, 0, detail_ref), write(piece, 1, coarse_ref)] for piece in range(2)]

    def use(rows, strip):
        results_ref[1, rows, :] = strip
        results_ref[0, rows, :] = units_ref[place, rows, :] - strip
        piece, left = divmod(rows.start + rows.size, half)
        if left == 0:
            for copy in writes[piece - 1]:
                copy.start()

    unpacked(weights, refs[: len(weights)], use)
    for copies in writes:
        for copy in copies:
            copy.wait()


def block_of(rows, width, first=0, depth=1):
    return pl.BlockSpec((depth, rows, width), lambda step: (first + step, 0, 0))


def anywhere():
    return pl.BlockSpec(memory_space=pl.ANY)


def tiles_of(pieces):
    return pl.BlockSpec((pieces, STRIP, LANES), lambda step: (0, 0, 0))


def in_vmem():
    return pl.BlockSpec(memory_space=pltpu.VMEM)


def call(kernel, name, steps, in_specs, out_specs, out_shape, args, aliases=None, scratch=(), grant=24):
    blocks = [spec.block_shape for spec in (*in_specs, *out_specs) if spec.block_shape]
    moved = 4 * max(steps, 1) * sum(math.prod(block) for block in blocks)
    return pl.pallas_call(
        kernel,
        grid=(steps,) if steps else (),
        in_specs=in_specs,
        out_specs=out_specs,
        out_shape=out_shape,
        scratch_shapes=scratch,
        input_output_aliases=aliases or {},
        compiler_params=pltpu.CompilerParams(vmem_limit_bytes=grant * 1024 * 1024),
        cost_estimate=pl.CostEstimate(flops=moved * 2, bytes_accessed=moved, transcendentals=0),
        name=name,
    )(*args)


def in_hbm(x):
    return pltpu.with_memory_space_constraint(x, pltpu.HBM)


def f32(*shape):
    return jax.ShapeDtypeStruct(shape, jnp.float32)


def can_shorten(rows, width):
    strips = TAP_DILATION // STRIP
    return lax.axis_size("gy") == strips and rows // TAP_DILATION % 2 == 0 and UNIT_ROWS // STRIP == width // TAP_DILATION


def shards(coarse_six):
    planes, rows, width = coarse_six.shape
    short = packed_rows(width)
    own, shifts = z_taps(planes, lax.axis_size("gz"))
    weights = (own, *shifts.values())
    count = len(weights)
    whole, unit, packed, edge = (functools.partial(block_of, n, width) for n in (rows, UNIT_ROWS, short, REACH))
    parts = rows // UNIT_ROWS
    units = coarse_six.reshape(planes * parts, UNIT_ROWS, width)
    matrix = pltpu.VMEM((width, width), jnp.bfloat16)

    def along_gz(x):
        return [passed_along(x, "gz", moved) for moved in shifts]

    def halo(source, start, stop):
        top, bottom = source[start:stop, :REACH], source[start:stop, rows - REACH :]
        return passed_along(bottom, "gy", 1), passed_along(top, "gy", -1)

    sums_shape = f32(FIRST_PLANES * parts, UNIT_ROWS, width)
    lead = call(
        pair_kernel,
        "pair_x",
        0,
        [anywhere()],
        [in_vmem()],
        [pltpu.VMEM((LEAD_UNITS, short, width), jnp.float32)],
        [in_hbm(units)],
        scratch=[pltpu.VMEM((LEAD_UNITS, UNIT_ROWS, width), jnp.float32), pltpu.SemaphoreType.DMA((LEAD_UNITS,))],
    )[0]
    lead, ready = lax.optimization_barrier((lead, units))
    lead_moved = along_gz(lead)
    first = FIRST_PLANES * parts - LEAD_UNITS
    first_block = call(
        functools.partial(x_kernel, LEAD_UNITS),
        "smooth_x",
        0,
        [anywhere()],
        [in_vmem()],
        [pltpu.VMEM((first, short, width), jnp.float32)],
        [in_hbm(ready)],
        scratch=[
            pltpu.VMEM((first, UNIT_ROWS, width), jnp.float32),
            matrix,
            pltpu.SemaphoreType.DMA((first,)),
        ],
    )[0]
    first_block, ready = lax.optimization_barrier((first_block, coarse_six))
    first_moved = along_gz(first_block)
    sums = call(
        functools.partial(pair_z_kernel, weights),
        "smooth_zx",
        LEAD_UNITS,
        [packed()] * count,
        [unit()],
        [sums_shape],
        [lead, *lead_moved],
        scratch=[matrix, pltpu.VMEM((UNIT_ROWS, width), jnp.float32)],
    )

    later, short_sent = [], []
    start = FIRST_PLANES
    near = halo(ready, start, start + sum(size for size, _ in LATER_GROUPS[0]))
    near, sums = lax.optimization_barrier((near, sums))
    for number, sizes in enumerate(LATER_GROUPS):
        offset = 0
        for size, messages in sizes:
            place = start + offset
            sources = [near[0], in_hbm(coarse_six), near[1]]
            specs = [edge(offset), whole(place), edge(offset)]
            scratch = [matrix, pltpu.VMEM((rows, width), jnp.float32)]
            if messages or not can_shorten(rows, width):
                messages = max(messages, 1)
                depth = parts // messages
                blocks = call(
                    yx_kernel,
                    "smooth_yx",
                    size,
                    specs,
                    [packed(depth=depth)] * messages,
                    [f32(size * depth, short, width)] * messages,
                    sources,
                    scratch=scratch,
                )
                for message, block in enumerate(blocks):
                    last_block = block
                    later.append((place * parts + message * depth, size * depth, (block, *along_gz(block))))
            else:
                pieces = size * short_tiles(rows, width) + 1
                block = call(
                    short_kernel,
                    "smooth_yx_short",
                    size,
                    specs,
                    [tiles_of(pieces)],
                    [f32(pieces, STRIP, LANES)],
                    sources,
                    scratch=scratch,
                )[0]
                short_sent.append((place, size, (block, *along_gz(block))))
            offset += size
        start += offset
        if number == 0:
            block, ready = lax.optimization_barrier((block, ready))
            block, *first_moved = lax.optimization_barrier((block, *first_moved))
            sums = call(
                functools.partial(z_kernel, weights),
                "smooth_z",
                first,
                [packed()] * count + [anywhere()],
                [unit(LEAD_UNITS)],
                [sums_shape],
                [first_block, *first_moved, *sums],
                {count: 0},
            )[0]
            along_z = sums.reshape(FIRST_PLANES, rows, width)
            along_z, ready = lax.optimization_barrier((along_z, ready))
        if number + 1 < len(LATER_GROUPS):
            block, ready = lax.optimization_barrier((block, ready))
            if number:
                ready, _ = lax.optimization_barrier((ready, short_sent[0][2]))
            near = halo(ready, start, start + sum(size for size, _ in LATER_GROUPS[number + 1]))
        if number and short_sent:
            near, _ = lax.optimization_barrier((near, short_sent[0][2]))
        if number == 0:
            near, along_z = lax.optimization_barrier((near, along_z))
            sides = halo(along_z, 0, FIRST_PLANES)

    def sum_short(batch):
        planes_in = sum(size for _, size, _ in batch)
        step, sums = 0, []
        for _, size, blocks in batch:
            sums = call(
                functools.partial(short_z_kernel, weights),
                "smooth_z_short",
                size,
                [tiles_of(blocks[0].shape[0])] * count + [anywhere()] * len(sums),
                [whole(step)] + [block_of(STRIP, width, step)] * 3,
                [f32(planes_in, rows, width)] + [f32(planes_in, STRIP, width)] * 3,
                [*blocks, *sums],
                {count + at: at for at in range(len(sums))},
            )
            step += size
        return sums[0], [passed_along(total, "gy", ahead) for ahead, total in enumerate(sums[1:], 1)]

    def finish_short(batch, sums, outs):
        start, size = batch[0][0], sum(size for _, size, _ in batch)
        along_z, moved = sums
        outs, moved = lax.optimization_barrier((outs, moved))
        return call(
            short_finish_kernel,
            "finish_short",
            size,
            [whole()] + [block_of(STRIP, width)] * 3 + [whole(start)] + [anywhere()] * 2,
            [whole(start)] * 2,
            [f32(planes, rows, width)] * 2,
            [along_z, *moved, coarse_six, *outs],
            {5: 0, 6: 1},
        )

    batches = [batch for batch in (short_sent[:SHORT_FIRST], short_sent[SHORT_FIRST:]) if batch]
    batch = batches[0]
    short_sums = sum_short(batch)
    short_whole, sides = lax.optimization_barrier((short_sums[0], sides))
    outs = call(
        y_kernel,
        "smooth_y",
        FIRST_PLANES,
        [edge(), whole(), edge(), whole()],
        [whole(), whole()],
        [f32(planes, rows, width)] * 2,
        [sides[0], along_z, sides[1], coarse_six],
    )
    short_sums, last_block = lax.optimization_barrier(((short_whole, short_sums[1]), last_block))
    last_moved = along_gz(last_block)
    outs = finish_short(batch, short_sums, outs)
    outs = [out.reshape(units.shape) for out in outs]
    for place, size, blocks in later[:-1]:
        outs, blocks = lax.optimization_barrier((outs, blocks))
        outs = call(
            functools.partial(finish_kernel, weights),
            "finish",
            size,
            [packed()] * count + [unit(place)] + [anywhere()] * 2,
            [unit(place)] * 2,
            [f32(*units.shape)] * 2,
            [*blocks, units, *outs],
            {count + 1: 0, count + 2: 1},
        )
    place = later[-1][0]
    blocks = (last_block, *last_moved)
    outs, blocks = lax.optimization_barrier((outs, blocks))
    outs = call(
        functools.partial(last_kernel, weights, place),
        "finish_last",
        0,
        [in_vmem()] * (count + 1) + [anywhere()] * 2,
        [anywhere()] * 2,
        [f32(*units.shape)] * 2,
        [*blocks, units, *outs],
        {count + 1: 0, count + 2: 1},
        scratch=[
            pltpu.VMEM((2, UNIT_ROWS, width), jnp.float32),
            pltpu.SemaphoreType.DMA((2, 2)),
        ],
    )
    return tuple(out.reshape(coarse_six.shape) for out in outs)


def solution(mesh):
    return jax.shard_map(
        shards,
        mesh=mesh,
        in_specs=(P("gz", "gy", None),),
        out_specs=(P("gz", "gy", None), P("gz", "gy", None)),
        check_vma=False,
    )
```

```python
import functools
import math

import jax
import jax.numpy as jnp
from jax import lax
from jax.experimental import pallas as pl
from jax.experimental.pallas import tpu as pltpu
from jax.sharding import PartitionSpec as P

TAP_DILATION = 32
REACH = 2 * TAP_DILATION
LANES = 128
STRIP = 8
UNIT_ROWS = 128
FIRST_PLANES = 2
LEAD_UNITS = 2
LATER_GROUPS = (((2, 0),), ((2, 0),), ((1, 1), (1, 2)))
SHORT_FIRST = 2

kernel_weights = (0.0625, 0.25, 0.375, 0.25, 0.0625)


def passed_along(x, axis, by):
    peers = lax.axis_size(axis)
    return lax.ppermute(x, axis, [(i, (i + by) % peers) for i in range(peers)])


def z_taps(plane_stack, count):
    weights = {}
    for cell_position in range(5):
        filter_reach = (cell_position - 2) * TAP_DILATION // plane_stack
        moved = -filter_reach % count
        weights[moved] = weights.get(moved, 0.0) + kernel_weights[cell_position]
    own = weights.pop(0, 0.0)
    return own, weights


def lane_of(shape):
    return lax.broadcasted_iota(jnp.int32, shape, 1)


def x_taps():
    return {(cell_position - 2) * TAP_DILATION: kernel_weights[cell_position] for cell_position in range(5)}


def rest_taps():
    return {(cell_position - 2) * TAP_DILATION: weight for cell_position, weight in enumerate((0.125, 0.375, 0.375, 0.125))}


def pair_sums(rows):
    return (rows + pltpu.roll(rows, rows.shape[1] - TAP_DILATION, 1)) * 0.5


def fill_matrix(matrix_ref, taps):
    depth, width = matrix_ref.shape
    for start in range(0, depth, LANES):
        shape = (LANES, width)
        row = start + lax.broadcasted_iota(jnp.int32, shape, 0)
        offset = row - lax.broadcasted_iota(jnp.int32, shape, 1)
        offset = jnp.where(offset < 0, offset + width, offset)
        values = jnp.zeros(shape, jnp.float32)
        for tap, weight in taps.items():
            values = jnp.where(offset == tap % width, weight, values)
        matrix_ref[pl.ds(start, LANES), :] = values.astype(jnp.bfloat16)


def x_smoothed(rows, matrix):
    parts = []
    for _ in range(3):
        parts.append(rows.astype(jnp.bfloat16))
        rows = rows - parts[-1].astype(jnp.float32)
    terms = jnp.dot(jnp.concatenate(parts), matrix, preferred_element_type=jnp.float32)
    high, middle, low = jnp.split(terms, 3)
    return high + middle + low


def y_sums(groups):
    for _ in range(4):
        groups = [a + b for a, b in zip(groups[:-1], groups[1:])]
    return groups


def packed_rows(width):
    return UNIT_ROWS - UNIT_ROWS * TAP_DILATION // width


def store_packed(out_ref, place, smooth):
    rows, width = smooth.shape
    kept_rows = out_ref.shape[1]
    depth = rows - kept_rows
    out_ref[place, :, : width - LANES] = smooth[:kept_rows, : width - LANES]
    kept = lane_of((depth, LANES)) < LANES - TAP_DILATION
    for piece in range(kept_rows // depth):
        tile = piece * TAP_DILATION // LANES
        shift = (LANES - TAP_DILATION - piece * TAP_DILATION) % LANES
        moved = smooth[kept_rows:, tile * LANES : (tile + 1) * LANES]
        if shift:
            moved = pltpu.roll(moved, shift, 1)
        last = smooth[piece * depth : (piece + 1) * depth, width - LANES :]
        out_ref[place, pl.ds(piece * depth, depth), width - LANES :] = jnp.where(kept, last, moved)


def completed(strip):
    width = strip.shape[1]
    last = strip[:, width - LANES :]
    lane = lane_of(last.shape)
    kept = lane < LANES - TAP_DILATION
    total = jnp.where(kept, last, 0.0)
    for start in range(0, width - LANES, LANES):
        total = total + strip[:, start : start + LANES]
    odd = (lane // TAP_DILATION) % 2 == 1
    total = jnp.where(odd, -total, total)
    total = total + pltpu.roll(total, 2 * TAP_DILATION, 1)
    total = total + pltpu.roll(total, TAP_DILATION, 1)
    return jnp.concatenate([strip[:, : width - LANES], jnp.where(kept, last, total)], axis=1)


def unpacked(weights, refs, use):
    kept_rows, width = refs[0].shape[1:]
    depth = UNIT_ROWS - kept_rows
    tiles = [None] * (width // LANES)
    for piece in range(kept_rows // depth):
        rows = pl.ds(piece * depth, depth)
        strip = weighted(weights, [ref[0, rows, :] for ref in refs])
        tile = piece * TAP_DILATION // LANES
        shift = (piece * TAP_DILATION - (LANES - TAP_DILATION)) % LANES
        moved = strip[:, width - LANES :]
        if shift:
            moved = pltpu.roll(moved, shift, 1)
        if tiles[tile] is None:
            tiles[tile] = moved
        else:
            here = lane_of(moved.shape) // TAP_DILATION == piece % (LANES // TAP_DILATION)
            tiles[tile] = jnp.where(here, moved, tiles[tile])
        use(rows, completed(strip))
    use(pl.ds(kept_rows, depth), completed(jnp.concatenate(tiles, axis=1)))


def weighted(weights, values):
    total = None
    for weight, value in zip(weights, values):
        term = weight * value
        total = term if total is None else total + term
    return total


def pair_kernel(units_ref, out_ref, read_ref, read_sems):
    def read(unit):
        return pltpu.make_async_copy(units_ref.at[unit], read_ref.at[unit], read_sems.at[unit])

    for unit in range(out_ref.shape[0]):
        read(unit).start()
    for unit in range(out_ref.shape[0]):
        read(unit).wait()
        store_packed(out_ref, unit, pair_sums(read_ref[unit]))


def x_kernel(first, units_ref, out_ref, read_ref, matrix_ref, read_sems):
    count = out_ref.shape[0]

    def read(unit):
        return pltpu.make_async_copy(units_ref.at[first + unit], read_ref.at[unit], read_sems.at[unit])

    for unit in range(count):
        read(unit).start()
    fill_matrix(matrix_ref, x_taps())

    @pl.loop(0, count)
    def _(unit):
        read(unit).wait()
        store_packed(out_ref, unit, x_smoothed(read_ref[unit], matrix_ref[...]))


def extended_groups(before_ref, c_ref, after_ref, offset):
    groups = []
    for ref in (before_ref, c_ref, after_ref):
        for start in range(0, ref.shape[1], TAP_DILATION):
            groups.append(ref[0, pl.ds(start + offset, STRIP), :])
    return groups


def y_smoothed(before_ref, c_ref, after_ref, smooth_ref):
    for within in range(TAP_DILATION // STRIP):
        groups = y_sums(extended_groups(before_ref, c_ref, after_ref, within * STRIP))
        for group, strip in enumerate(groups):
            smooth_ref[pl.ds(group * TAP_DILATION + within * STRIP, STRIP), :] = strip * (1.0 / 16.0)


def yx_kernel(before_ref, c_ref, after_ref, *refs):
    *out_refs, matrix_ref, smooth_ref = refs
    pl.when(pl.program_id(0) == 0)(lambda: fill_matrix(matrix_ref, x_taps()))
    y_smoothed(before_ref, c_ref, after_ref, smooth_ref)
    places = [(ref, place) for ref in out_refs for place in range(ref.shape[0])]
    for unit, (ref, place) in enumerate(places):
        smooth = x_smoothed(smooth_ref[pl.ds(unit * UNIT_ROWS, UNIT_ROWS), :], matrix_ref[...])
        store_packed(ref, place, smooth)


def z_kernel(weights, *refs):
    whole_ref = refs[-1]

    def use(rows, strip):
        whole_ref[0, rows, :] = strip

    unpacked(weights, refs[: len(weights)], use)


def group_of(shape):
    return lane_of(shape) // TAP_DILATION


def spread(tile, group):
    tile = jnp.where(group_of(tile.shape) == group, tile, 0.0)
    tile = tile + pltpu.roll(tile, 2 * TAP_DILATION, 1)
    return tile + pltpu.roll(tile, TAP_DILATION, 1)


def strip_rows(rows, ahead):
    per_group = TAP_DILATION // STRIP
    strip = lax.rem(lax.axis_index("gy") + ahead, per_group)
    return pl.ds(pl.multiple_of(rows - TAP_DILATION + strip * STRIP, STRIP), STRIP)


def short_strips(rows):
    half = rows - UNIT_ROWS
    fixed = [pl.ds(row, STRIP) for row in range(0, rows - TAP_DILATION, STRIP)]
    moving = [strip_rows(rows, ahead) for ahead in range(1, TAP_DILATION // STRIP)]
    return fixed[: half // STRIP], fixed[half // STRIP :] + moving


def short_tiles(rows, width):
    return (rows // STRIP - 3) * (width // LANES)


def short_kernel(before_ref, c_ref, after_ref, out_ref, matrix_ref, smooth_ref):
    plane = pl.program_id(0)

    @pl.when(plane == 0)
    def _():
        fill_matrix(matrix_ref, x_taps())
        out_ref[out_ref.shape[0] - 1] = jnp.zeros((STRIP, LANES), jnp.float32)

    y_smoothed(before_ref, c_ref, after_ref, smooth_ref)
    rows, width = smooth_ref.shape
    for start in range(0, rows, UNIT_ROWS):
        unit = pl.ds(start, UNIT_ROWS)
        smooth_ref[unit, :] = x_smoothed(smooth_ref[unit, :], matrix_ref[...])
    index = plane * short_tiles(rows, width)
    groups = LANES // TAP_DILATION
    for places in short_strips(rows):
        *places, last_place = places
        last = smooth_ref[last_place, :]
        for piece, place in enumerate(places):
            strip = smooth_ref[place, :]
            tile = piece // groups * LANES
            moved = last[:, tile : tile + LANES]
            shift = (groups - 1 - piece) % groups * TAP_DILATION
            if shift:
                moved = pltpu.roll(moved, shift, 1)
            for start in range(0, width - LANES, LANES):
                out_ref[index] = strip[:, start : start + LANES]
                index += 1
            here = group_of(moved.shape) == groups - 1
            out_ref[index] = jnp.where(here, moved, strip[:, width - LANES :])
            index += 1
    left = spread(last[:, width - LANES :], groups - 2)
    end = out_ref.shape[0] - 1
    out_ref[end] = jnp.where(group_of(left.shape) == plane, left, out_ref[end])


def short_z_kernel(weights, *refs):
    packed, (whole_ref, *sum_refs) = refs[: len(weights)], refs[-4:]
    rows, width = whole_ref.shape[1:]
    plane = pl.program_id(0)
    index = plane * short_tiles(rows, width)
    groups, tiles = LANES // TAP_DILATION, width // LANES
    for places in short_strips(rows):
        *places, last_place = places
        last = [None] * tiles
        for piece, place in enumerate(places):
            strip = [weighted(weights, [ref[index + tile] for ref in packed]) for tile in range(tiles)]
            index += tiles
            tile, group = divmod(piece, groups)
            shift = (group + 1 - groups) % groups * TAP_DILATION
            moved = pltpu.roll(strip[-1], shift, 1) if shift else strip[-1]
            here = group_of(moved.shape) == group
            last[tile] = moved if last[tile] is None else jnp.where(here, moved, last[tile])
            whole_ref[0, place, :] = completed(jnp.concatenate(strip, axis=1))
        if len(places) < tiles * groups - 1:
            end = packed[0].shape[0] - 1
            left = spread(weighted(weights, [ref[end] for ref in packed]), plane)
            last[-1] = jnp.where(group_of(left.shape) == groups - 2, left, last[-1])
        whole_ref[0, last_place, :] = completed(jnp.concatenate(last, axis=1))

    groups = rows // TAP_DILATION
    for ahead in range(TAP_DILATION // STRIP):
        total = None
        for group in range(groups if ahead else groups - 1):
            strip = whole_ref[0, strip_rows((group + 1) * TAP_DILATION, ahead), :]
            if total is None:
                total = strip
            else:
                total = total + strip if group % 2 == 0 else total - strip
        if ahead:
            sum_refs[ahead - 1][0] = total
        else:
            whole_ref[0, strip_rows(rows, 0), :] = total


def short_finish_kernel(whole_ref, *refs):
    *sum_refs, c_ref, _, _, detail_ref, coarse_ref = refs
    missing = strip_rows(whole_ref.shape[1], 0)
    coarse_ref[...] = whole_ref[...]
    coarse_ref[0, missing, :] = whole_ref[0, missing, :] + sum(ref[0] for ref in sum_refs)
    detail_ref[...] = c_ref[...] - coarse_ref[...]


def pair_z_kernel(weights, *refs):
    whole_ref, matrix_ref, pair_ref = refs[-3:]
    pl.when(pl.program_id(0) == 0)(lambda: fill_matrix(matrix_ref, rest_taps()))

    def use(rows, strip):
        pair_ref[rows, :] = strip

    unpacked(weights, refs[: len(weights)], use)
    whole_ref[0] = x_smoothed(pair_ref[...], matrix_ref[...])


def y_kernel(before_ref, whole_ref, after_ref, c_ref, detail_ref, coarse_ref):
    scale = 1.0 / 16.0
    for within in range(TAP_DILATION // STRIP):
        groups = y_sums(extended_groups(before_ref, whole_ref, after_ref, within * STRIP))
        for group, strip in enumerate(groups):
            rows = pl.ds(group * TAP_DILATION + within * STRIP, STRIP)
            coarse = strip * scale
            coarse_ref[0, rows, :] = coarse
            detail_ref[0, rows, :] = c_ref[0, rows, :] - coarse


def finish_kernel(weights, *refs):
    c_ref, _, _, detail_ref, coarse_ref = refs[len(weights) :]

    def use(rows, strip):
        coarse_ref[0, rows, :] = strip
        detail_ref[0, rows, :] = c_ref[0, rows, :] - strip

    unpacked(weights, refs[: len(weights)], use)


def last_kernel(weights, place, *refs):
    units_ref, _, _, detail_ref, coarse_ref, results_ref, write_sems = refs[len(weights) :]
    half = UNIT_ROWS // 2

    def write(piece, output, ref):
        rows = pl.ds(piece * half, half)
        source = results_ref.at[output, rows]
        return pltpu.make_async_copy(source, ref.at[place, rows], write_sems.at[piece, output])

    writes = [[write(piece, 0, detail_ref), write(piece, 1, coarse_ref)] for piece in range(2)]

    def use(rows, strip):
        results_ref[1, rows, :] = strip
        results_ref[0, rows, :] = units_ref[place, rows, :] - strip
        piece, left = divmod(rows.start + rows.size, half)
        if left == 0:
            for copy in writes[piece - 1]:
                copy.start()

    unpacked(weights, refs[: len(weights)], use)
    for copies in writes:
        for copy in copies:
            copy.wait()


def block_of(rows, width, first=0, depth=1):
    return pl.BlockSpec((depth, rows, width), lambda step: (first + step, 0, 0))


def anywhere():
    return pl.BlockSpec(memory_space=pl.ANY)


def tiles_of(pieces):
    return pl.BlockSpec((pieces, STRIP, LANES), lambda step: (0, 0, 0))


def in_vmem():
    return pl.BlockSpec(memory_space=pltpu.VMEM)


def call(kernel, name, steps, in_specs, out_specs, out_shape, args, aliases=None, scratch=(), grant=24):
    blocks = [spec.block_shape for spec in (*in_specs, *out_specs) if spec.block_shape]
    moved = 4 * max(steps, 1) * sum(math.prod(block) for block in blocks)
    return pl.pallas_call(
        kernel,
        grid=(steps,) if steps else (),
        in_specs=in_specs,
        out_specs=out_specs,
        out_shape=out_shape,
        scratch_shapes=scratch,
        input_output_aliases=aliases or {},
        compiler_params=pltpu.CompilerParams(vmem_limit_bytes=grant * 1024 * 1024),
        cost_estimate=pl.CostEstimate(flops=moved * 2, bytes_accessed=moved, transcendentals=0),
        name=name,
    )(*args)


def in_hbm(x):
    return pltpu.with_memory_space_constraint(x, pltpu.HBM)


def f32(*shape):
    return jax.ShapeDtypeStruct(shape, jnp.float32)


def can_shorten(rows, width):
    strips = TAP_DILATION // STRIP
    return lax.axis_size("gy") == strips and rows // TAP_DILATION % 2 == 0 and UNIT_ROWS // STRIP == width // TAP_DILATION


def shards(coarse_six):
    planes, rows, width = coarse_six.shape
    short = packed_rows(width)
    own, shifts = z_taps(planes, lax.axis_size("gz"))
    weights = (own, *shifts.values())
    count = len(weights)
    whole, unit, packed, edge = (functools.partial(block_of, n, width) for n in (rows, UNIT_ROWS, short, REACH))
    parts = rows // UNIT_ROWS
    units = coarse_six.reshape(planes * parts, UNIT_ROWS, width)
    matrix = pltpu.VMEM((width, width), jnp.bfloat16)

    def along_gz(x):
        return [passed_along(x, "gz", moved) for moved in shifts]

    def halo(source, start, stop):
        top, bottom = source[start:stop, :REACH], source[start:stop, rows - REACH :]
        return passed_along(bottom, "gy", 1), passed_along(top, "gy", -1)

    sums_shape = f32(FIRST_PLANES * parts, UNIT_ROWS, width)
    lead = call(
        pair_kernel,
        "pair_x",
        0,
        [anywhere()],
        [in_vmem()],
        [pltpu.VMEM((LEAD_UNITS, short, width), jnp.float32)],
        [in_hbm(units)],
        scratch=[pltpu.VMEM((LEAD_UNITS, UNIT_ROWS, width), jnp.float32), pltpu.SemaphoreType.DMA((LEAD_UNITS,))],
    )[0]
    lead, ready = lax.optimization_barrier((lead, units))
    lead_moved = along_gz(lead)
    first = FIRST_PLANES * parts - LEAD_UNITS
    first_block = call(
        functools.partial(x_kernel, LEAD_UNITS),
        "smooth_x",
        0,
        [anywhere()],
        [in_vmem()],
        [pltpu.VMEM((first, short, width), jnp.float32)],
        [in_hbm(ready)],
        scratch=[
            pltpu.VMEM((first, UNIT_ROWS, width), jnp.float32),
            matrix,
            pltpu.SemaphoreType.DMA((first,)),
        ],
    )[0]
    first_block, ready = lax.optimization_barrier((first_block, coarse_six))
    first_moved = along_gz(first_block)
    sums = call(
        functools.partial(pair_z_kernel, weights),
        "smooth_zx",
        LEAD_UNITS,
        [packed()] * count,
        [unit()],
        [sums_shape],
        [lead, *lead_moved],
        scratch=[matrix, pltpu.VMEM((UNIT_ROWS, width), jnp.float32)],
    )

    later, short_sent = [], []
    start = FIRST_PLANES
    near = halo(ready, start, start + sum(size for size, _ in LATER_GROUPS[0]))
    near, sums = lax.optimization_barrier((near, sums))
    for number, sizes in enumerate(LATER_GROUPS):
        offset = 0
        for size, messages in sizes:
            place = start + offset
            sources = [near[0], in_hbm(coarse_six), near[1]]
            specs = [edge(offset), whole(place), edge(offset)]
            scratch = [matrix, pltpu.VMEM((rows, width), jnp.float32)]
            if messages or not can_shorten(rows, width):
                messages = max(messages, 1)
                depth = parts // messages
                blocks = call(
                    yx_kernel,
                    "smooth_yx",
                    size,
                    specs,
                    [packed(depth=depth)] * messages,
                    [f32(size * depth, short, width)] * messages,
                    sources,
                    scratch=scratch,
                )
                for message, block in enumerate(blocks):
                    last_block = block
                    later.append((place * parts + message * depth, size * depth, (block, *along_gz(block))))
            else:
                pieces = size * short_tiles(rows, width) + 1
                block = call(
                    short_kernel,
                    "smooth_yx_short",
                    size,
                    specs,
                    [tiles_of(pieces)],
                    [f32(pieces, STRIP, LANES)],
                    sources,
                    scratch=scratch,
                )[0]
                short_sent.append((place, size, (block, *along_gz(block))))
            offset += size
        start += offset
        if number == 0:
            block, ready = lax.optimization_barrier((block, ready))
            block, *first_moved = lax.optimization_barrier((block, *first_moved))
            sums = call(
                functools.partial(z_kernel, weights),
                "smooth_z",
                first,
                [packed()] * count + [anywhere()],
                [unit(LEAD_UNITS)],
                [sums_shape],
                [first_block, *first_moved, *sums],
                {count: 0},
            )[0]
            along_z = sums.reshape(FIRST_PLANES, rows, width)
            along_z, ready = lax.optimization_barrier((along_z, ready))
        if number + 1 < len(LATER_GROUPS):
            block, ready = lax.optimization_barrier((block, ready))
            if number:
                ready, _ = lax.optimization_barrier((ready, short_sent[0][2]))
            near = halo(ready, start, start + sum(size for size, _ in LATER_GROUPS[number + 1]))
        if number == 1:
            first_near, along_z = lax.optimization_barrier((near[0], along_z))
            near = (first_near, near[1])
            sides = halo(along_z, 0, FIRST_PLANES)
        if number and short_sent:
            near, _ = lax.optimization_barrier((near, short_sent[0][2]))
        if number == 0:
            near, along_z = lax.optimization_barrier((near, along_z))

    def sum_short(batch):
        planes_in = sum(size for _, size, _ in batch)
        step, sums = 0, []
        for _, size, blocks in batch:
            sums = call(
                functools.partial(short_z_kernel, weights),
                "smooth_z_short",
                size,
                [tiles_of(blocks[0].shape[0])] * count + [anywhere()] * len(sums),
                [whole(step)] + [block_of(STRIP, width, step)] * 3,
                [f32(planes_in, rows, width)] + [f32(planes_in, STRIP, width)] * 3,
                [*blocks, *sums],
                {count + at: at for at in range(len(sums))},
            )
            step += size
        return sums[0], [passed_along(total, "gy", ahead) for ahead, total in enumerate(sums[1:], 1)]

    def finish_short(batch, sums, outs):
        start, size = batch[0][0], sum(size for _, size, _ in batch)
        along_z, moved = sums
        outs, moved = lax.optimization_barrier((outs, moved))
        return call(
            short_finish_kernel,
            "finish_short",
            size,
            [whole()] + [block_of(STRIP, width)] * 3 + [whole(start)] + [anywhere()] * 2,
            [whole(start)] * 2,
            [f32(planes, rows, width)] * 2,
            [along_z, *moved, coarse_six, *outs],
            {5: 0, 6: 1},
        )

    batches = [batch for batch in (short_sent[:SHORT_FIRST], short_sent[SHORT_FIRST:]) if batch]
    batch = batches[0]
    short_sums = sum_short(batch)
    short_whole, sides = lax.optimization_barrier((short_sums[0], sides))
    outs = call(
        y_kernel,
        "smooth_y",
        FIRST_PLANES,
        [edge(), whole(), edge(), whole()],
        [whole(), whole()],
        [f32(planes, rows, width)] * 2,
        [sides[0], along_z, sides[1], coarse_six],
    )
    short_sums, last_block = lax.optimization_barrier(((short_whole, short_sums[1]), last_block))
    last_moved = along_gz(last_block)
    outs = finish_short(batch, short_sums, outs)
    outs = [out.reshape(units.shape) for out in outs]
    for place, size, blocks in later[:-1]:
        outs, blocks = lax.optimization_barrier((outs, blocks))
        outs = call(
            functools.partial(finish_kernel, weights),
            "finish",
            size,
            [packed()] * count + [unit(place)] + [anywhere()] * 2,
            [unit(place)] * 2,
            [f32(*units.shape)] * 2,
            [*blocks, units, *outs],
            {count + 1: 0, count + 2: 1},
        )
    place = later[-1][0]
    blocks = (last_block, *last_moved)
    outs, blocks = lax.optimization_barrier((outs, blocks))
    outs = call(
        functools.partial(last_kernel, weights, place),
        "finish_last",
        0,
        [in_vmem()] * (count + 1) + [anywhere()] * 2,
        [anywhere()] * 2,
        [f32(*units.shape)] * 2,
        [*blocks, units, *outs],
        {count + 1: 0, count + 2: 1},
        scratch=[
            pltpu.VMEM((2, UNIT_ROWS, width), jnp.float32),
            pltpu.SemaphoreType.DMA((2, 2)),
        ],
    )
    return tuple(out.reshape(coarse_six.shape) for out in outs)


def solution(mesh):
    return jax.shard_map(
        shards,
        mesh=mesh,
        in_specs=(P("gz", "gy", None),),
        out_specs=(P("gz", "gy", None), P("gz", "gy", None)),
        check_vma=False,
    )
```

```python
import functools
import math

import jax
import jax.numpy as jnp
from jax import lax
from jax.experimental import pallas as pl
from jax.experimental.pallas import tpu as pltpu
from jax.sharding import PartitionSpec as P

TAP_DILATION = 32
REACH = 2 * TAP_DILATION
LANES = 128
STRIP = 8
UNIT_ROWS = 128
FIRST_PLANES = 2
LEAD_UNITS = 2
LATER_GROUPS = (((2, 0),), ((2, 0),), ((1, 1), (1, 2)))
SHORT_FIRST = 2

kernel_weights = (0.0625, 0.25, 0.375, 0.25, 0.0625)


def passed_along(x, axis, by):
    peers = lax.axis_size(axis)
    return lax.ppermute(x, axis, [(i, (i + by) % peers) for i in range(peers)])


def z_taps(plane_stack, count):
    weights = {}
    for cell_position in range(5):
        filter_reach = (cell_position - 2) * TAP_DILATION // plane_stack
        moved = -filter_reach % count
        weights[moved] = weights.get(moved, 0.0) + kernel_weights[cell_position]
    own = weights.pop(0, 0.0)
    return own, weights


def lane_of(shape):
    return lax.broadcasted_iota(jnp.int32, shape, 1)


def x_taps():
    return {(cell_position - 2) * TAP_DILATION: kernel_weights[cell_position] for cell_position in range(5)}


def rest_taps():
    return {(cell_position - 2) * TAP_DILATION: weight for cell_position, weight in enumerate((0.125, 0.375, 0.375, 0.125))}


def pair_sums(rows):
    return (rows + pltpu.roll(rows, rows.shape[1] - TAP_DILATION, 1)) * 0.5


def fill_matrix(matrix_ref, taps):
    depth, width = matrix_ref.shape
    for start in range(0, depth, LANES):
        shape = (LANES, width)
        row = start + lax.broadcasted_iota(jnp.int32, shape, 0)
        offset = row - lax.broadcasted_iota(jnp.int32, shape, 1)
        offset = jnp.where(offset < 0, offset + width, offset)
        values = jnp.zeros(shape, jnp.float32)
        for tap, weight in taps.items():
            values = jnp.where(offset == tap % width, weight, values)
        matrix_ref[pl.ds(start, LANES), :] = values.astype(jnp.bfloat16)


def x_smoothed(rows, matrix):
    parts = []
    for _ in range(3):
        parts.append(rows.astype(jnp.bfloat16))
        rows = rows - parts[-1].astype(jnp.float32)
    terms = jnp.dot(jnp.concatenate(parts), matrix, preferred_element_type=jnp.float32)
    high, middle, low = jnp.split(terms, 3)
    return high + middle + low


def y_sums(groups):
    for _ in range(4):
        groups = [a + b for a, b in zip(groups[:-1], groups[1:])]
    return groups


def packed_rows(width):
    return UNIT_ROWS - UNIT_ROWS * TAP_DILATION // width


def store_packed(out_ref, place, smooth):
    rows, width = smooth.shape
    kept_rows = out_ref.shape[1]
    depth = rows - kept_rows
    out_ref[place, :, : width - LANES] = smooth[:kept_rows, : width - LANES]
    kept = lane_of((depth, LANES)) < LANES - TAP_DILATION
    for piece in range(kept_rows // depth):
        tile = piece * TAP_DILATION // LANES
        shift = (LANES - TAP_DILATION - piece * TAP_DILATION) % LANES
        moved = smooth[kept_rows:, tile * LANES : (tile + 1) * LANES]
        if shift:
            moved = pltpu.roll(moved, shift, 1)
        last = smooth[piece * depth : (piece + 1) * depth, width - LANES :]
        out_ref[place, pl.ds(piece * depth, depth), width - LANES :] = jnp.where(kept, last, moved)


def completed(strip):
    width = strip.shape[1]
    last = strip[:, width - LANES :]
    lane = lane_of(last.shape)
    kept = lane < LANES - TAP_DILATION
    total = jnp.where(kept, last, 0.0)
    for start in range(0, width - LANES, LANES):
        total = total + strip[:, start : start + LANES]
    odd = (lane // TAP_DILATION) % 2 == 1
    total = jnp.where(odd, -total, total)
    total = total + pltpu.roll(total, 2 * TAP_DILATION, 1)
    total = total + pltpu.roll(total, TAP_DILATION, 1)
    return jnp.concatenate([strip[:, : width - LANES], jnp.where(kept, last, total)], axis=1)


def unpacked(weights, refs, use):
    kept_rows, width = refs[0].shape[1:]
    depth = UNIT_ROWS - kept_rows
    tiles = [None] * (width // LANES)
    for piece in range(kept_rows // depth):
        rows = pl.ds(piece * depth, depth)
        strip = weighted(weights, [ref[0, rows, :] for ref in refs])
        tile = piece * TAP_DILATION // LANES
        shift = (piece * TAP_DILATION - (LANES - TAP_DILATION)) % LANES
        moved = strip[:, width - LANES :]
        if shift:
            moved = pltpu.roll(moved, shift, 1)
        if tiles[tile] is None:
            tiles[tile] = moved
        else:
            here = lane_of(moved.shape) // TAP_DILATION == piece % (LANES // TAP_DILATION)
            tiles[tile] = jnp.where(here, moved, tiles[tile])
        use(rows, completed(strip))
    use(pl.ds(kept_rows, depth), completed(jnp.concatenate(tiles, axis=1)))


def weighted(weights, values):
    total = None
    for weight, value in zip(weights, values):
        term = weight * value
        total = term if total is None else total + term
    return total


def pair_kernel(units_ref, out_ref, read_ref, read_sems):
    def read(unit):
        return pltpu.make_async_copy(units_ref.at[unit], read_ref.at[unit], read_sems.at[unit])

    for unit in range(out_ref.shape[0]):
        read(unit).start()
    for unit in range(out_ref.shape[0]):
        read(unit).wait()
        store_packed(out_ref, unit, pair_sums(read_ref[unit]))


def x_kernel(first, units_ref, out_ref, read_ref, matrix_ref, read_sems):
    count = out_ref.shape[0]

    def read(unit):
        return pltpu.make_async_copy(units_ref.at[first + unit], read_ref.at[unit], read_sems.at[unit])

    for unit in range(count):
        read(unit).start()
    fill_matrix(matrix_ref, x_taps())

    @pl.loop(0, count)
    def _(unit):
        read(unit).wait()
        store_packed(out_ref, unit, x_smoothed(read_ref[unit], matrix_ref[...]))


def extended_groups(before_ref, c_ref, after_ref, offset):
    groups = []
    for ref in (before_ref, c_ref, after_ref):
        for start in range(0, ref.shape[1], TAP_DILATION):
            groups.append(ref[0, pl.ds(start + offset, STRIP), :])
    return groups


def y_smoothed(before_ref, c_ref, after_ref, smooth_ref):
    for within in range(TAP_DILATION // STRIP):
        groups = y_sums(extended_groups(before_ref, c_ref, after_ref, within * STRIP))
        for group, strip in enumerate(groups):
            smooth_ref[pl.ds(group * TAP_DILATION + within * STRIP, STRIP), :] = strip * (1.0 / 16.0)


def yx_kernel(before_ref, c_ref, after_ref, *refs):
    *out_refs, matrix_ref, smooth_ref = refs
    pl.when(pl.program_id(0) == 0)(lambda: fill_matrix(matrix_ref, x_taps()))
    y_smoothed(before_ref, c_ref, after_ref, smooth_ref)
    places = [(ref, place) for ref in out_refs for place in range(ref.shape[0])]
    for unit, (ref, place) in enumerate(places):
        smooth = x_smoothed(smooth_ref[pl.ds(unit * UNIT_ROWS, UNIT_ROWS), :], matrix_ref[...])
        store_packed(ref, place, smooth)


def z_kernel(weights, *refs):
    whole_ref = refs[-1]

    def use(rows, strip):
        whole_ref[0, rows, :] = strip

    unpacked(weights, refs[: len(weights)], use)


def group_of(shape):
    return lane_of(shape) // TAP_DILATION


def spread(tile, group):
    tile = jnp.where(group_of(tile.shape) == group, tile, 0.0)
    tile = tile + pltpu.roll(tile, 2 * TAP_DILATION, 1)
    return tile + pltpu.roll(tile, TAP_DILATION, 1)


def strip_rows(rows, ahead):
    per_group = TAP_DILATION // STRIP
    strip = lax.rem(lax.axis_index("gy") + ahead, per_group)
    return pl.ds(pl.multiple_of(rows - TAP_DILATION + strip * STRIP, STRIP), STRIP)


def short_strips(rows):
    half = rows - UNIT_ROWS
    fixed = [pl.ds(row, STRIP) for row in range(0, rows - TAP_DILATION, STRIP)]
    moving = [strip_rows(rows, ahead) for ahead in range(1, TAP_DILATION // STRIP)]
    return fixed[: half // STRIP], fixed[half // STRIP :] + moving


def short_tiles(rows, width):
    return (rows // STRIP - 3) * (width // LANES)


def short_kernel(before_ref, c_ref, after_ref, out_ref, matrix_ref, smooth_ref):
    plane = pl.program_id(0)

    @pl.when(plane == 0)
    def _():
        fill_matrix(matrix_ref, x_taps())
        out_ref[out_ref.shape[0] - 1] = jnp.zeros((STRIP, LANES), jnp.float32)

    y_smoothed(before_ref, c_ref, after_ref, smooth_ref)
    rows, width = smooth_ref.shape
    for start in range(0, rows, UNIT_ROWS):
        unit = pl.ds(start, UNIT_ROWS)
        smooth_ref[unit, :] = x_smoothed(smooth_ref[unit, :], matrix_ref[...])
    index = plane * short_tiles(rows, width)
    groups = LANES // TAP_DILATION
    for places in short_strips(rows):
        *places, last_place = places
        last = smooth_ref[last_place, :]
        for piece, place in enumerate(places):
            strip = smooth_ref[place, :]
            tile = piece // groups * LANES
            moved = last[:, tile : tile + LANES]
            shift = (groups - 1 - piece) % groups * TAP_DILATION
            if shift:
                moved = pltpu.roll(moved, shift, 1)
            for start in range(0, width - LANES, LANES):
                out_ref[index] = strip[:, start : start + LANES]
                index += 1
            here = group_of(moved.shape) == groups - 1
            out_ref[index] = jnp.where(here, moved, strip[:, width - LANES :])
            index += 1
    left = spread(last[:, width - LANES :], groups - 2)
    end = out_ref.shape[0] - 1
    out_ref[end] = jnp.where(group_of(left.shape) == plane, left, out_ref[end])


def short_z_kernel(weights, *refs):
    packed, (whole_ref, *sum_refs) = refs[: len(weights)], refs[-4:]
    rows, width = whole_ref.shape[1:]
    plane = pl.program_id(0)
    index = plane * short_tiles(rows, width)
    groups, tiles = LANES // TAP_DILATION, width // LANES
    for places in short_strips(rows):
        *places, last_place = places
        last = [None] * tiles
        for piece, place in enumerate(places):
            strip = [weighted(weights, [ref[index + tile] for ref in packed]) for tile in range(tiles)]
            index += tiles
            tile, group = divmod(piece, groups)
            shift = (group + 1 - groups) % groups * TAP_DILATION
            moved = pltpu.roll(strip[-1], shift, 1) if shift else strip[-1]
            here = group_of(moved.shape) == group
            last[tile] = moved if last[tile] is None else jnp.where(here, moved, last[tile])
            whole_ref[0, place, :] = completed(jnp.concatenate(strip, axis=1))
        if len(places) < tiles * groups - 1:
            end = packed[0].shape[0] - 1
            left = spread(weighted(weights, [ref[end] for ref in packed]), plane)
            last[-1] = jnp.where(group_of(left.shape) == groups - 2, left, last[-1])
        whole_ref[0, last_place, :] = completed(jnp.concatenate(last, axis=1))

    groups = rows // TAP_DILATION
    for ahead in range(TAP_DILATION // STRIP):
        total = None
        for group in range(groups if ahead else groups - 1):
            strip = whole_ref[0, strip_rows((group + 1) * TAP_DILATION, ahead), :]
            if total is None:
                total = strip
            else:
                total = total + strip if group % 2 == 0 else total - strip
        if ahead:
            sum_refs[ahead - 1][0] = total
        else:
            whole_ref[0, strip_rows(rows, 0), :] = total


def short_finish_kernel(whole_ref, *refs):
    *sum_refs, c_ref, _, _, detail_ref, coarse_ref = refs
    missing = strip_rows(whole_ref.shape[1], 0)
    coarse_ref[...] = whole_ref[...]
    coarse_ref[0, missing, :] = whole_ref[0, missing, :] + sum(ref[0] for ref in sum_refs)
    detail_ref[...] = c_ref[...] - coarse_ref[...]


def pair_z_kernel(weights, *refs):
    whole_ref, matrix_ref, pair_ref = refs[-3:]
    pl.when(pl.program_id(0) == 0)(lambda: fill_matrix(matrix_ref, rest_taps()))

    def use(rows, strip):
        pair_ref[rows, :] = strip

    unpacked(weights, refs[: len(weights)], use)
    whole_ref[0] = x_smoothed(pair_ref[...], matrix_ref[...])


def y_kernel(before_ref, whole_ref, after_ref, c_ref, detail_ref, coarse_ref):
    scale = 1.0 / 16.0
    for within in range(TAP_DILATION // STRIP):
        groups = y_sums(extended_groups(before_ref, whole_ref, after_ref, within * STRIP))
        for group, strip in enumerate(groups):
            rows = pl.ds(group * TAP_DILATION + within * STRIP, STRIP)
            coarse = strip * scale
            coarse_ref[0, rows, :] = coarse
            detail_ref[0, rows, :] = c_ref[0, rows, :] - coarse


def finish_kernel(weights, *refs):
    c_ref, _, _, detail_ref, coarse_ref = refs[len(weights) :]

    def use(rows, strip):
        coarse_ref[0, rows, :] = strip
        detail_ref[0, rows, :] = c_ref[0, rows, :] - strip

    unpacked(weights, refs[: len(weights)], use)


def last_kernel(weights, place, *refs):
    units_ref, _, _, detail_ref, coarse_ref, results_ref, write_sems = refs[len(weights) :]
    half = UNIT_ROWS // 2

    def write(piece, output, ref):
        rows = pl.ds(piece * half, half)
        source = results_ref.at[output, rows]
        return pltpu.make_async_copy(source, ref.at[place, rows], write_sems.at[piece, output])

    writes = [[write(piece, 0, detail_ref), write(piece, 1, coarse_ref)] for piece in range(2)]

    def use(rows, strip):
        results_ref[1, rows, :] = strip
        results_ref[0, rows, :] = units_ref[place, rows, :] - strip
        piece, left = divmod(rows.start + rows.size, half)
        if left == 0:
            for copy in writes[piece - 1]:
                copy.start()

    unpacked(weights, refs[: len(weights)], use)
    for copies in writes:
        for copy in copies:
            copy.wait()


def block_of(rows, width, first=0, depth=1):
    return pl.BlockSpec((depth, rows, width), lambda step: (first + step, 0, 0))


def anywhere():
    return pl.BlockSpec(memory_space=pl.ANY)


def tiles_of(pieces):
    return pl.BlockSpec((pieces, STRIP, LANES), lambda step: (0, 0, 0))


def in_vmem():
    return pl.BlockSpec(memory_space=pltpu.VMEM)


def call(kernel, name, steps, in_specs, out_specs, out_shape, args, aliases=None, scratch=(), grant=24):
    blocks = [spec.block_shape for spec in (*in_specs, *out_specs) if spec.block_shape]
    moved = 4 * max(steps, 1) * sum(math.prod(block) for block in blocks)
    return pl.pallas_call(
        kernel,
        grid=(steps,) if steps else (),
        in_specs=in_specs,
        out_specs=out_specs,
        out_shape=out_shape,
        scratch_shapes=scratch,
        input_output_aliases=aliases or {},
        compiler_params=pltpu.CompilerParams(vmem_limit_bytes=grant * 1024 * 1024),
        cost_estimate=pl.CostEstimate(flops=moved * 2, bytes_accessed=moved, transcendentals=0),
        name=name,
    )(*args)


def in_hbm(x):
    return pltpu.with_memory_space_constraint(x, pltpu.HBM)


def f32(*shape):
    return jax.ShapeDtypeStruct(shape, jnp.float32)


def can_shorten(rows, width):
    strips = TAP_DILATION // STRIP
    return lax.axis_size("gy") == strips and rows // TAP_DILATION % 2 == 0 and UNIT_ROWS // STRIP == width // TAP_DILATION


def shards(coarse_six):
    planes, rows, width = coarse_six.shape
    short = packed_rows(width)
    own, shifts = z_taps(planes, lax.axis_size("gz"))
    weights = (own, *shifts.values())
    count = len(weights)
    whole, unit, packed, edge = (functools.partial(block_of, n, width) for n in (rows, UNIT_ROWS, short, REACH))
    parts = rows // UNIT_ROWS
    units = coarse_six.reshape(planes * parts, UNIT_ROWS, width)
    matrix = pltpu.VMEM((width, width), jnp.bfloat16)

    def along_gz(x):
        return [passed_along(x, "gz", moved) for moved in shifts]

    def halo(source, start, stop):
        top, bottom = source[start:stop, :REACH], source[start:stop, rows - REACH :]
        return passed_along(bottom, "gy", 1), passed_along(top, "gy", -1)

    sums_shape = f32(FIRST_PLANES * parts, UNIT_ROWS, width)
    lead = call(
        pair_kernel,
        "pair_x",
        0,
        [anywhere()],
        [in_vmem()],
        [pltpu.VMEM((LEAD_UNITS, short, width), jnp.float32)],
        [in_hbm(units)],
        scratch=[pltpu.VMEM((LEAD_UNITS, UNIT_ROWS, width), jnp.float32), pltpu.SemaphoreType.DMA((LEAD_UNITS,))],
    )[0]
    lead, ready = lax.optimization_barrier((lead, units))
    lead_moved = along_gz(lead)
    first = FIRST_PLANES * parts - LEAD_UNITS
    first_block = call(
        functools.partial(x_kernel, LEAD_UNITS),
        "smooth_x",
        0,
        [anywhere()],
        [in_vmem()],
        [pltpu.VMEM((first, short, width), jnp.float32)],
        [in_hbm(ready)],
        scratch=[
            pltpu.VMEM((first, UNIT_ROWS, width), jnp.float32),
            matrix,
            pltpu.SemaphoreType.DMA((first,)),
        ],
    )[0]
    first_block, ready = lax.optimization_barrier((first_block, coarse_six))
    first_moved = along_gz(first_block)
    sums = call(
        functools.partial(pair_z_kernel, weights),
        "smooth_zx",
        LEAD_UNITS,
        [packed()] * count,
        [unit()],
        [sums_shape],
        [lead, *lead_moved],
        scratch=[matrix, pltpu.VMEM((UNIT_ROWS, width), jnp.float32)],
    )

    later, short_sent = [], []
    start = FIRST_PLANES
    near = halo(ready, start, start + sum(size for size, _ in LATER_GROUPS[0]))
    near, sums = lax.optimization_barrier((near, sums))
    for number, sizes in enumerate(LATER_GROUPS):
        offset = 0
        for size, messages in sizes:
            place = start + offset
            sources = [near[0], in_hbm(coarse_six), near[1]]
            specs = [edge(offset), whole(place), edge(offset)]
            scratch = [matrix, pltpu.VMEM((rows, width), jnp.float32)]
            if messages or not can_shorten(rows, width):
                messages = max(messages, 1)
                depth = parts // messages
                blocks = call(
                    yx_kernel,
                    "smooth_yx",
                    size,
                    specs,
                    [packed(depth=depth)] * messages,
                    [f32(size * depth, short, width)] * messages,
                    sources,
                    scratch=scratch,
                )
                for message, block in enumerate(blocks):
                    last_block = block
                    later.append((place * parts + message * depth, size * depth, (block, *along_gz(block))))
            else:
                pieces = size * short_tiles(rows, width) + 1
                block = call(
                    short_kernel,
                    "smooth_yx_short",
                    size,
                    specs,
                    [tiles_of(pieces)],
                    [f32(pieces, STRIP, LANES)],
                    sources,
                    scratch=scratch,
                )[0]
                short_sent.append((place, size, (block, *along_gz(block))))
            offset += size
        start += offset
        if number == 0:
            block, ready = lax.optimization_barrier((block, ready))
            block, *first_moved = lax.optimization_barrier((block, *first_moved))
            sums = call(
                functools.partial(z_kernel, weights),
                "smooth_z",
                first,
                [packed()] * count + [anywhere()],
                [unit(LEAD_UNITS)],
                [sums_shape],
                [first_block, *first_moved, *sums],
                {count: 0},
            )[0]
            along_z = sums.reshape(FIRST_PLANES, rows, width)
            along_z, ready = lax.optimization_barrier((along_z, ready))
        if number + 1 < len(LATER_GROUPS):
            if not number:
                block, ready = lax.optimization_barrier((block, ready))
            near = halo(ready, start, start + sum(size for size, _ in LATER_GROUPS[number + 1]))
        if number == 1:
            first_near, along_z, _ = lax.optimization_barrier((near[0], along_z, short_sent[0][2]))
            near = (first_near, near[1])
            sides = halo(along_z, 0, FIRST_PLANES)
        if number and short_sent:
            near, _ = lax.optimization_barrier((near, short_sent[0][2]))
        if number == 0:
            near, along_z = lax.optimization_barrier((near, along_z))

    def sum_short(batch):
        planes_in = sum(size for _, size, _ in batch)
        step, sums = 0, []
        for _, size, blocks in batch:
            sums = call(
                functools.partial(short_z_kernel, weights),
                "smooth_z_short",
                size,
                [tiles_of(blocks[0].shape[0])] * count + [anywhere()] * len(sums),
                [whole(step)] + [block_of(STRIP, width, step)] * 3,
                [f32(planes_in, rows, width)] + [f32(planes_in, STRIP, width)] * 3,
                [*blocks, *sums],
                {count + at: at for at in range(len(sums))},
            )
            step += size
        return sums[0], [passed_along(total, "gy", ahead) for ahead, total in enumerate(sums[1:], 1)]

    def finish_short(batch, sums, outs):
        start, size = batch[0][0], sum(size for _, size, _ in batch)
        along_z, moved = sums
        outs, moved = lax.optimization_barrier((outs, moved))
        return call(
            short_finish_kernel,
            "finish_short",
            size,
            [whole()] + [block_of(STRIP, width)] * 3 + [whole(start)] + [anywhere()] * 2,
            [whole(start)] * 2,
            [f32(planes, rows, width)] * 2,
            [along_z, *moved, coarse_six, *outs],
            {5: 0, 6: 1},
        )

    batches = [batch for batch in (short_sent[:SHORT_FIRST], short_sent[SHORT_FIRST:]) if batch]
    batch = batches[0]
    short_sums = sum_short(batch)
    short_whole, sides = lax.optimization_barrier((short_sums[0], sides))
    outs = call(
        y_kernel,
        "smooth_y",
        FIRST_PLANES,
        [edge(), whole(), edge(), whole()],
        [whole(), whole()],
        [f32(planes, rows, width)] * 2,
        [sides[0], along_z, sides[1], coarse_six],
    )
    short_sums, last_block = lax.optimization_barrier(((short_whole, short_sums[1]), last_block))
    last_moved = along_gz(last_block)
    outs = finish_short(batch, short_sums, outs)
    outs = [out.reshape(units.shape) for out in outs]
    for place, size, blocks in later[:-1]:
        outs, blocks = lax.optimization_barrier((outs, blocks))
        outs = call(
            functools.partial(finish_kernel, weights),
            "finish",
            size,
            [packed()] * count + [unit(place)] + [anywhere()] * 2,
            [unit(place)] * 2,
            [f32(*units.shape)] * 2,
            [*blocks, units, *outs],
            {count + 1: 0, count + 2: 1},
        )
    place = later[-1][0]
    blocks = (last_block, *last_moved)
    outs, blocks = lax.optimization_barrier((outs, blocks))
    outs = call(
        functools.partial(last_kernel, weights, place),
        "finish_last",
        0,
        [in_vmem()] * (count + 1) + [anywhere()] * 2,
        [anywhere()] * 2,
        [f32(*units.shape)] * 2,
        [*blocks, units, *outs],
        {count + 1: 0, count + 2: 1},
        scratch=[
            pltpu.VMEM((2, UNIT_ROWS, width), jnp.float32),
            pltpu.SemaphoreType.DMA((2, 2)),
        ],
    )
    return tuple(out.reshape(coarse_six.shape) for out in outs)


def solution(mesh):
    return jax.shard_map(
        shards,
        mesh=mesh,
        in_specs=(P("gz", "gy", None),),
        out_specs=(P("gz", "gy", None), P("gz", "gy", None)),
        check_vma=False,
    )
```

```python
import functools
import math

import jax
import jax.numpy as jnp
from jax import lax
from jax.experimental import pallas as pl
from jax.experimental.pallas import tpu as pltpu
from jax.sharding import PartitionSpec as P

TAP_DILATION = 32
REACH = 2 * TAP_DILATION
LANES = 128
STRIP = 8
UNIT_ROWS = 128
FIRST_PLANES = 2
LEAD_UNITS = 2
LATER_GROUPS = (((2, 0),), ((2, 0),), ((1, 1), (1, 2)))
SHORT_FIRST = 2

kernel_weights = (0.0625, 0.25, 0.375, 0.25, 0.0625)


def passed_along(x, axis, by):
    peers = lax.axis_size(axis)
    return lax.ppermute(x, axis, [(i, (i + by) % peers) for i in range(peers)])


def z_taps(plane_stack, count):
    weights = {}
    for cell_position in range(5):
        filter_reach = (cell_position - 2) * TAP_DILATION // plane_stack
        moved = -filter_reach % count
        weights[moved] = weights.get(moved, 0.0) + kernel_weights[cell_position]
    own = weights.pop(0, 0.0)
    return own, weights


def lane_of(shape):
    return lax.broadcasted_iota(jnp.int32, shape, 1)


def x_taps():
    return {(cell_position - 2) * TAP_DILATION: kernel_weights[cell_position] for cell_position in range(5)}


def rest_taps():
    return {(cell_position - 2) * TAP_DILATION: weight for cell_position, weight in enumerate((0.125, 0.375, 0.375, 0.125))}


def pair_sums(rows):
    return (rows + pltpu.roll(rows, rows.shape[1] - TAP_DILATION, 1)) * 0.5


def fill_matrix(matrix_ref, taps):
    depth, width = matrix_ref.shape
    for start in range(0, depth, LANES):
        shape = (LANES, width)
        row = start + lax.broadcasted_iota(jnp.int32, shape, 0)
        offset = row - lax.broadcasted_iota(jnp.int32, shape, 1)
        offset = jnp.where(offset < 0, offset + width, offset)
        values = jnp.zeros(shape, jnp.float32)
        for tap, weight in taps.items():
            values = jnp.where(offset == tap % width, weight, values)
        matrix_ref[pl.ds(start, LANES), :] = values.astype(jnp.bfloat16)


def x_smoothed(rows, matrix):
    parts = []
    for _ in range(3):
        parts.append(rows.astype(jnp.bfloat16))
        rows = rows - parts[-1].astype(jnp.float32)
    terms = jnp.dot(jnp.concatenate(parts), matrix, preferred_element_type=jnp.float32)
    high, middle, low = jnp.split(terms, 3)
    return high + middle + low


def y_sums(groups):
    for _ in range(4):
        groups = [a + b for a, b in zip(groups[:-1], groups[1:])]
    return groups


def packed_rows(width):
    return UNIT_ROWS - UNIT_ROWS * TAP_DILATION // width


def store_packed(out_ref, place, smooth):
    rows, width = smooth.shape
    kept_rows = out_ref.shape[1]
    depth = rows - kept_rows
    out_ref[place, :, : width - LANES] = smooth[:kept_rows, : width - LANES]
    kept = lane_of((depth, LANES)) < LANES - TAP_DILATION
    for piece in range(kept_rows // depth):
        tile = piece * TAP_DILATION // LANES
        shift = (LANES - TAP_DILATION - piece * TAP_DILATION) % LANES
        moved = smooth[kept_rows:, tile * LANES : (tile + 1) * LANES]
        if shift:
            moved = pltpu.roll(moved, shift, 1)
        last = smooth[piece * depth : (piece + 1) * depth, width - LANES :]
        out_ref[place, pl.ds(piece * depth, depth), width - LANES :] = jnp.where(kept, last, moved)


def completed(strip):
    width = strip.shape[1]
    last = strip[:, width - LANES :]
    lane = lane_of(last.shape)
    kept = lane < LANES - TAP_DILATION
    total = jnp.where(kept, last, 0.0)
    for start in range(0, width - LANES, LANES):
        total = total + strip[:, start : start + LANES]
    odd = (lane // TAP_DILATION) % 2 == 1
    total = jnp.where(odd, -total, total)
    total = total + pltpu.roll(total, 2 * TAP_DILATION, 1)
    total = total + pltpu.roll(total, TAP_DILATION, 1)
    return jnp.concatenate([strip[:, : width - LANES], jnp.where(kept, last, total)], axis=1)


def unpacked(weights, refs, use):
    kept_rows, width = refs[0].shape[1:]
    depth = UNIT_ROWS - kept_rows
    tiles = [None] * (width // LANES)
    for piece in range(kept_rows // depth):
        rows = pl.ds(piece * depth, depth)
        strip = weighted(weights, [ref[0, rows, :] for ref in refs])
        tile = piece * TAP_DILATION // LANES
        shift = (piece * TAP_DILATION - (LANES - TAP_DILATION)) % LANES
        moved = strip[:, width - LANES :]
        if shift:
            moved = pltpu.roll(moved, shift, 1)
        if tiles[tile] is None:
            tiles[tile] = moved
        else:
            here = lane_of(moved.shape) // TAP_DILATION == piece % (LANES // TAP_DILATION)
            tiles[tile] = jnp.where(here, moved, tiles[tile])
        use(rows, completed(strip))
    use(pl.ds(kept_rows, depth), completed(jnp.concatenate(tiles, axis=1)))


def weighted(weights, values):
    total = None
    for weight, value in zip(weights, values):
        term = weight * value
        total = term if total is None else total + term
    return total


def pair_kernel(units_ref, out_ref, read_ref, read_sems):
    def read(unit):
        return pltpu.make_async_copy(units_ref.at[unit], read_ref.at[unit], read_sems.at[unit])

    for unit in range(out_ref.shape[0]):
        read(unit).start()
    for unit in range(out_ref.shape[0]):
        read(unit).wait()
        store_packed(out_ref, unit, pair_sums(read_ref[unit]))


def x_kernel(first, units_ref, out_ref, read_ref, matrix_ref, read_sems):
    count = out_ref.shape[0]

    def read(unit):
        return pltpu.make_async_copy(units_ref.at[first + unit], read_ref.at[unit], read_sems.at[unit])

    for unit in range(count):
        read(unit).start()
    fill_matrix(matrix_ref, x_taps())

    @pl.loop(0, count)
    def _(unit):
        read(unit).wait()
        store_packed(out_ref, unit, x_smoothed(read_ref[unit], matrix_ref[...]))


def extended_groups(before_ref, c_ref, after_ref, offset):
    groups = []
    for ref in (before_ref, c_ref, after_ref):
        for start in range(0, ref.shape[1], TAP_DILATION):
            groups.append(ref[0, pl.ds(start + offset, STRIP), :])
    return groups


def y_smoothed(before_ref, c_ref, after_ref, smooth_ref):
    for within in range(TAP_DILATION // STRIP):
        groups = y_sums(extended_groups(before_ref, c_ref, after_ref, within * STRIP))
        for group, strip in enumerate(groups):
            smooth_ref[pl.ds(group * TAP_DILATION + within * STRIP, STRIP), :] = strip * (1.0 / 16.0)


def yx_kernel(before_ref, c_ref, after_ref, *refs):
    *out_refs, matrix_ref, smooth_ref = refs
    pl.when(pl.program_id(0) == 0)(lambda: fill_matrix(matrix_ref, x_taps()))
    y_smoothed(before_ref, c_ref, after_ref, smooth_ref)
    places = [(ref, place) for ref in out_refs for place in range(ref.shape[0])]
    for unit, (ref, place) in enumerate(places):
        smooth = x_smoothed(smooth_ref[pl.ds(unit * UNIT_ROWS, UNIT_ROWS), :], matrix_ref[...])
        store_packed(ref, place, smooth)


def z_kernel(weights, *refs):
    whole_ref = refs[-1]

    def use(rows, strip):
        whole_ref[0, rows, :] = strip

    unpacked(weights, refs[: len(weights)], use)


def group_of(shape):
    return lane_of(shape) // TAP_DILATION


def spread(tile, group):
    tile = jnp.where(group_of(tile.shape) == group, tile, 0.0)
    tile = tile + pltpu.roll(tile, 2 * TAP_DILATION, 1)
    return tile + pltpu.roll(tile, TAP_DILATION, 1)


def strip_rows(rows, ahead):
    per_group = TAP_DILATION // STRIP
    strip = lax.rem(lax.axis_index("gy") + ahead, per_group)
    return pl.ds(pl.multiple_of(rows - TAP_DILATION + strip * STRIP, STRIP), STRIP)


def short_strips(rows):
    half = rows - UNIT_ROWS
    fixed = [pl.ds(row, STRIP) for row in range(0, rows - TAP_DILATION, STRIP)]
    moving = [strip_rows(rows, ahead) for ahead in range(1, TAP_DILATION // STRIP)]
    return fixed[: half // STRIP], fixed[half // STRIP :] + moving


def short_tiles(rows, width):
    return (rows // STRIP - 3) * (width // LANES)


def short_kernel(before_ref, c_ref, after_ref, out_ref, matrix_ref, smooth_ref):
    plane = pl.program_id(0)

    @pl.when(plane == 0)
    def _():
        fill_matrix(matrix_ref, x_taps())
        out_ref[out_ref.shape[0] - 1] = jnp.zeros((STRIP, LANES), jnp.float32)

    y_smoothed(before_ref, c_ref, after_ref, smooth_ref)
    rows, width = smooth_ref.shape
    for start in range(0, rows, UNIT_ROWS):
        unit = pl.ds(start, UNIT_ROWS)
        smooth_ref[unit, :] = x_smoothed(smooth_ref[unit, :], matrix_ref[...])
    index = plane * short_tiles(rows, width)
    groups = LANES // TAP_DILATION
    for places in short_strips(rows):
        *places, last_place = places
        last = smooth_ref[last_place, :]
        for piece, place in enumerate(places):
            strip = smooth_ref[place, :]
            tile = piece // groups * LANES
            moved = last[:, tile : tile + LANES]
            shift = (groups - 1 - piece) % groups * TAP_DILATION
            if shift:
                moved = pltpu.roll(moved, shift, 1)
            for start in range(0, width - LANES, LANES):
                out_ref[index] = strip[:, start : start + LANES]
                index += 1
            here = group_of(moved.shape) == groups - 1
            out_ref[index] = jnp.where(here, moved, strip[:, width - LANES :])
            index += 1
    left = spread(last[:, width - LANES :], groups - 2)
    end = out_ref.shape[0] - 1
    out_ref[end] = jnp.where(group_of(left.shape) == plane, left, out_ref[end])


def short_z_kernel(weights, *refs):
    packed, (whole_ref, *sum_refs) = refs[: len(weights)], refs[-4:]
    rows, width = whole_ref.shape[1:]
    plane = pl.program_id(0)
    index = plane * short_tiles(rows, width)
    groups, tiles = LANES // TAP_DILATION, width // LANES
    for places in short_strips(rows):
        *places, last_place = places
        last = [None] * tiles
        for piece, place in enumerate(places):
            strip = [weighted(weights, [ref[index + tile] for ref in packed]) for tile in range(tiles)]
            index += tiles
            tile, group = divmod(piece, groups)
            shift = (group + 1 - groups) % groups * TAP_DILATION
            moved = pltpu.roll(strip[-1], shift, 1) if shift else strip[-1]
            here = group_of(moved.shape) == group
            last[tile] = moved if last[tile] is None else jnp.where(here, moved, last[tile])
            whole_ref[0, place, :] = completed(jnp.concatenate(strip, axis=1))
        if len(places) < tiles * groups - 1:
            end = packed[0].shape[0] - 1
            left = spread(weighted(weights, [ref[end] for ref in packed]), plane)
            last[-1] = jnp.where(group_of(left.shape) == groups - 2, left, last[-1])
        whole_ref[0, last_place, :] = completed(jnp.concatenate(last, axis=1))

    groups = rows // TAP_DILATION
    for ahead in range(TAP_DILATION // STRIP):
        total = None
        for group in range(groups if ahead else groups - 1):
            strip = whole_ref[0, strip_rows((group + 1) * TAP_DILATION, ahead), :]
            if total is None:
                total = strip
            else:
                total = total + strip if group % 2 == 0 else total - strip
        if ahead:
            sum_refs[ahead - 1][0] = total
        else:
            whole_ref[0, strip_rows(rows, 0), :] = total


def short_finish_kernel(whole_ref, *refs):
    *sum_refs, c_ref, _, _, detail_ref, coarse_ref = refs
    missing = strip_rows(whole_ref.shape[1], 0)
    coarse_ref[...] = whole_ref[...]
    coarse_ref[0, missing, :] = whole_ref[0, missing, :] + sum(ref[0] for ref in sum_refs)
    detail_ref[...] = c_ref[...] - coarse_ref[...]


def pair_z_kernel(weights, *refs):
    whole_ref, matrix_ref, pair_ref = refs[-3:]
    pl.when(pl.program_id(0) == 0)(lambda: fill_matrix(matrix_ref, rest_taps()))

    def use(rows, strip):
        pair_ref[rows, :] = strip

    unpacked(weights, refs[: len(weights)], use)
    whole_ref[0] = x_smoothed(pair_ref[...], matrix_ref[...])


def y_kernel(before_ref, whole_ref, after_ref, c_ref, detail_ref, coarse_ref):
    scale = 1.0 / 16.0
    for within in range(TAP_DILATION // STRIP):
        groups = y_sums(extended_groups(before_ref, whole_ref, after_ref, within * STRIP))
        for group, strip in enumerate(groups):
            rows = pl.ds(group * TAP_DILATION + within * STRIP, STRIP)
            coarse = strip * scale
            coarse_ref[0, rows, :] = coarse
            detail_ref[0, rows, :] = c_ref[0, rows, :] - coarse


def finish_kernel(weights, *refs):
    c_ref, _, _, detail_ref, coarse_ref = refs[len(weights) :]

    def use(rows, strip):
        coarse_ref[0, rows, :] = strip
        detail_ref[0, rows, :] = c_ref[0, rows, :] - strip

    unpacked(weights, refs[: len(weights)], use)


def last_kernel(weights, place, *refs):
    units_ref, _, _, detail_ref, coarse_ref, results_ref, write_sems = refs[len(weights) :]
    half = UNIT_ROWS // 2

    def write(piece, output, ref):
        rows = pl.ds(piece * half, half)
        source = results_ref.at[output, rows]
        return pltpu.make_async_copy(source, ref.at[place, rows], write_sems.at[piece, output])

    writes = [[write(piece, 0, detail_ref), write(piece, 1, coarse_ref)] for piece in range(2)]

    def use(rows, strip):
        results_ref[1, rows, :] = strip
        results_ref[0, rows, :] = units_ref[place, rows, :] - strip
        piece, left = divmod(rows.start + rows.size, half)
        if left == 0:
            for copy in writes[piece - 1]:
                copy.start()

    unpacked(weights, refs[: len(weights)], use)
    for copies in writes:
        for copy in copies:
            copy.wait()


def block_of(rows, width, first=0, depth=1):
    return pl.BlockSpec((depth, rows, width), lambda step: (first + step, 0, 0))


def anywhere():
    return pl.BlockSpec(memory_space=pl.ANY)


def tiles_of(pieces):
    return pl.BlockSpec((pieces, STRIP, LANES), lambda step: (0, 0, 0))


def in_vmem():
    return pl.BlockSpec(memory_space=pltpu.VMEM)


def call(kernel, name, steps, in_specs, out_specs, out_shape, args, aliases=None, scratch=(), grant=24):
    blocks = [spec.block_shape for spec in (*in_specs, *out_specs) if spec.block_shape]
    moved = 4 * max(steps, 1) * sum(math.prod(block) for block in blocks)
    return pl.pallas_call(
        kernel,
        grid=(steps,) if steps else (),
        in_specs=in_specs,
        out_specs=out_specs,
        out_shape=out_shape,
        scratch_shapes=scratch,
        input_output_aliases=aliases or {},
        compiler_params=pltpu.CompilerParams(vmem_limit_bytes=grant * 1024 * 1024),
        cost_estimate=pl.CostEstimate(flops=moved * 2, bytes_accessed=moved, transcendentals=0),
        name=name,
    )(*args)


def in_hbm(x):
    return pltpu.with_memory_space_constraint(x, pltpu.HBM)


def f32(*shape):
    return jax.ShapeDtypeStruct(shape, jnp.float32)


def can_shorten(rows, width):
    strips = TAP_DILATION // STRIP
    return lax.axis_size("gy") == strips and rows // TAP_DILATION % 2 == 0 and UNIT_ROWS // STRIP == width // TAP_DILATION


def shards(coarse_six):
    planes, rows, width = coarse_six.shape
    short = packed_rows(width)
    own, shifts = z_taps(planes, lax.axis_size("gz"))
    weights = (own, *shifts.values())
    count = len(weights)
    whole, unit, packed, edge = (functools.partial(block_of, n, width) for n in (rows, UNIT_ROWS, short, REACH))
    parts = rows // UNIT_ROWS
    units = coarse_six.reshape(planes * parts, UNIT_ROWS, width)
    matrix = pltpu.VMEM((width, width), jnp.bfloat16)

    def along_gz(x):
        return [passed_along(x, "gz", moved) for moved in shifts]

    def halo(source, start, stop):
        top, bottom = source[start:stop, :REACH], source[start:stop, rows - REACH :]
        return passed_along(bottom, "gy", 1), passed_along(top, "gy", -1)

    sums_shape = f32(FIRST_PLANES * parts, UNIT_ROWS, width)
    lead = call(
        pair_kernel,
        "pair_x",
        0,
        [anywhere()],
        [in_vmem()],
        [pltpu.VMEM((LEAD_UNITS, short, width), jnp.float32)],
        [in_hbm(units)],
        scratch=[pltpu.VMEM((LEAD_UNITS, UNIT_ROWS, width), jnp.float32), pltpu.SemaphoreType.DMA((LEAD_UNITS,))],
    )[0]
    lead, ready = lax.optimization_barrier((lead, units))
    lead_moved = along_gz(lead)
    first = FIRST_PLANES * parts - LEAD_UNITS
    first_block = call(
        functools.partial(x_kernel, LEAD_UNITS),
        "smooth_x",
        0,
        [anywhere()],
        [in_vmem()],
        [pltpu.VMEM((first, short, width), jnp.float32)],
        [in_hbm(ready)],
        scratch=[
            pltpu.VMEM((first, UNIT_ROWS, width), jnp.float32),
            matrix,
            pltpu.SemaphoreType.DMA((first,)),
        ],
    )[0]
    first_block, ready = lax.optimization_barrier((first_block, coarse_six))
    first_moved = along_gz(first_block)
    sums = call(
        functools.partial(pair_z_kernel, weights),
        "smooth_zx",
        LEAD_UNITS,
        [packed()] * count,
        [unit()],
        [sums_shape],
        [lead, *lead_moved],
        scratch=[matrix, pltpu.VMEM((UNIT_ROWS, width), jnp.float32)],
    )

    later, short_sent = [], []
    start = FIRST_PLANES
    near = halo(ready, start, start + sum(size for size, _ in LATER_GROUPS[0]))
    near, sums = lax.optimization_barrier((near, sums))
    for number, sizes in enumerate(LATER_GROUPS):
        offset = 0
        for size, messages in sizes:
            place = start + offset
            sources = [near[0], in_hbm(coarse_six), near[1]]
            specs = [edge(offset), whole(place), edge(offset)]
            scratch = [matrix, pltpu.VMEM((rows, width), jnp.float32)]
            if messages or not can_shorten(rows, width):
                messages = max(messages, 1)
                depth = parts // messages
                blocks = call(
                    yx_kernel,
                    "smooth_yx",
                    size,
                    specs,
                    [packed(depth=depth)] * messages,
                    [f32(size * depth, short, width)] * messages,
                    sources,
                    scratch=scratch,
                )
                for message, block in enumerate(blocks):
                    last_block = block
                    later.append((place * parts + message * depth, size * depth, (block, *along_gz(block))))
            else:
                pieces = size * short_tiles(rows, width) + 1
                block = call(
                    short_kernel,
                    "smooth_yx_short",
                    size,
                    specs,
                    [tiles_of(pieces)],
                    [f32(pieces, STRIP, LANES)],
                    sources,
                    scratch=scratch,
                )[0]
                short_sent.append((place, size, (block, *along_gz(block))))
            offset += size
        start += offset
        if number == 0:
            block, ready = lax.optimization_barrier((block, ready))
            block, *first_moved = lax.optimization_barrier((block, *first_moved))
            sums = call(
                functools.partial(z_kernel, weights),
                "smooth_z",
                first,
                [packed()] * count + [anywhere()],
                [unit(LEAD_UNITS)],
                [sums_shape],
                [first_block, *first_moved, *sums],
                {count: 0},
            )[0]
            along_z = sums.reshape(FIRST_PLANES, rows, width)
            along_z, ready = lax.optimization_barrier((along_z, ready))
        if number + 1 < len(LATER_GROUPS):
            if not number:
                block, ready = lax.optimization_barrier((block, ready))
            near = halo(ready, start, start + sum(size for size, _ in LATER_GROUPS[number + 1]))
        if number == 1:
            first_near, along_z, _ = lax.optimization_barrier((near[0], along_z, short_sent[0][2]))
            near = (first_near, near[1])
            sides = halo(along_z, 0, FIRST_PLANES)
        if number == 0:
            near, along_z = lax.optimization_barrier((near, along_z))

    def sum_short(batch):
        planes_in = sum(size for _, size, _ in batch)
        step, sums = 0, []
        for _, size, blocks in batch:
            sums = call(
                functools.partial(short_z_kernel, weights),
                "smooth_z_short",
                size,
                [tiles_of(blocks[0].shape[0])] * count + [anywhere()] * len(sums),
                [whole(step)] + [block_of(STRIP, width, step)] * 3,
                [f32(planes_in, rows, width)] + [f32(planes_in, STRIP, width)] * 3,
                [*blocks, *sums],
                {count + at: at for at in range(len(sums))},
            )
            step += size
        return sums[0], [passed_along(total, "gy", ahead) for ahead, total in enumerate(sums[1:], 1)]

    def finish_short(batch, sums, outs):
        start, size = batch[0][0], sum(size for _, size, _ in batch)
        along_z, moved = sums
        outs, moved = lax.optimization_barrier((outs, moved))
        return call(
            short_finish_kernel,
            "finish_short",
            size,
            [whole()] + [block_of(STRIP, width)] * 3 + [whole(start)] + [anywhere()] * 2,
            [whole(start)] * 2,
            [f32(planes, rows, width)] * 2,
            [along_z, *moved, coarse_six, *outs],
            {5: 0, 6: 1},
        )

    batches = [batch for batch in (short_sent[:SHORT_FIRST], short_sent[SHORT_FIRST:]) if batch]
    batch = batches[0]
    short_sums = sum_short(batch)
    short_whole, sides = lax.optimization_barrier((short_sums[0], sides))
    outs = call(
        y_kernel,
        "smooth_y",
        FIRST_PLANES,
        [edge(), whole(), edge(), whole()],
        [whole(), whole()],
        [f32(planes, rows, width)] * 2,
        [sides[0], along_z, sides[1], coarse_six],
    )
    short_sums, last_block = lax.optimization_barrier(((short_whole, short_sums[1]), last_block))
    last_moved = along_gz(last_block)
    outs = finish_short(batch, short_sums, outs)
    outs = [out.reshape(units.shape) for out in outs]
    for place, size, blocks in later[:-1]:
        outs, blocks = lax.optimization_barrier((outs, blocks))
        outs = call(
            functools.partial(finish_kernel, weights),
            "finish",
            size,
            [packed()] * count + [unit(place)] + [anywhere()] * 2,
            [unit(place)] * 2,
            [f32(*units.shape)] * 2,
            [*blocks, units, *outs],
            {count + 1: 0, count + 2: 1},
        )
    place = later[-1][0]
    blocks = (last_block, *last_moved)
    outs, blocks = lax.optimization_barrier((outs, blocks))
    outs = call(
        functools.partial(last_kernel, weights, place),
        "finish_last",
        0,
        [in_vmem()] * (count + 1) + [anywhere()] * 2,
        [anywhere()] * 2,
        [f32(*units.shape)] * 2,
        [*blocks, units, *outs],
        {count + 1: 0, count + 2: 1},
        scratch=[
            pltpu.VMEM((2, UNIT_ROWS, width), jnp.float32),
            pltpu.SemaphoreType.DMA((2, 2)),
        ],
    )
    return tuple(out.reshape(coarse_six.shape) for out in outs)


def solution(mesh):
    return jax.shard_map(
        shards,
        mesh=mesh,
        in_specs=(P("gz", "gy", None),),
        out_specs=(P("gz", "gy", None), P("gz", "gy", None)),
        check_vma=False,
    )
```

```python
import functools
import math

import jax
import jax.numpy as jnp
from jax import lax
from jax.experimental import pallas as pl
from jax.experimental.pallas import tpu as pltpu
from jax.sharding import PartitionSpec as P

TAP_DILATION = 32
REACH = 2 * TAP_DILATION
LANES = 128
STRIP = 8
UNIT_ROWS = 128
FIRST_PLANES = 2
LEAD_UNITS = 2
LATER_GROUPS = (((2, 0),), ((2, 0),), ((1, 1), (1, 2)))
SHORT_FIRST = 2

kernel_weights = (0.0625, 0.25, 0.375, 0.25, 0.0625)


def passed_along(x, axis, by):
    peers = lax.axis_size(axis)
    return lax.ppermute(x, axis, [(i, (i + by) % peers) for i in range(peers)])


def z_taps(plane_stack, count):
    weights = {}
    for cell_position in range(5):
        filter_reach = (cell_position - 2) * TAP_DILATION // plane_stack
        moved = -filter_reach % count
        weights[moved] = weights.get(moved, 0.0) + kernel_weights[cell_position]
    own = weights.pop(0, 0.0)
    return own, weights


def lane_of(shape):
    return lax.broadcasted_iota(jnp.int32, shape, 1)


def x_taps():
    return {(cell_position - 2) * TAP_DILATION: kernel_weights[cell_position] for cell_position in range(5)}


def rest_taps():
    return {(cell_position - 2) * TAP_DILATION: weight for cell_position, weight in enumerate((0.125, 0.375, 0.375, 0.125))}


def pair_sums(rows):
    return (rows + pltpu.roll(rows, rows.shape[1] - TAP_DILATION, 1)) * 0.5


def fill_matrix(matrix_ref, taps):
    depth, width = matrix_ref.shape
    for start in range(0, depth, LANES):
        shape = (LANES, width)
        row = start + lax.broadcasted_iota(jnp.int32, shape, 0)
        offset = row - lax.broadcasted_iota(jnp.int32, shape, 1)
        offset = jnp.where(offset < 0, offset + width, offset)
        values = jnp.zeros(shape, jnp.float32)
        for tap, weight in taps.items():
            values = jnp.where(offset == tap % width, weight, values)
        matrix_ref[pl.ds(start, LANES), :] = values.astype(jnp.bfloat16)


def x_smoothed(rows, matrix):
    parts = []
    for _ in range(3):
        parts.append(rows.astype(jnp.bfloat16))
        rows = rows - parts[-1].astype(jnp.float32)
    terms = jnp.dot(jnp.concatenate(parts), matrix, preferred_element_type=jnp.float32)
    high, middle, low = jnp.split(terms, 3)
    return high + middle + low


def y_sums(groups):
    for _ in range(4):
        groups = [a + b for a, b in zip(groups[:-1], groups[1:])]
    return groups


def packed_rows(width):
    return UNIT_ROWS - UNIT_ROWS * TAP_DILATION // width


def store_packed(out_ref, place, smooth):
    rows, width = smooth.shape
    kept_rows = out_ref.shape[1]
    depth = rows - kept_rows
    out_ref[place, :, : width - LANES] = smooth[:kept_rows, : width - LANES]
    kept = lane_of((depth, LANES)) < LANES - TAP_DILATION
    for piece in range(kept_rows // depth):
        tile = piece * TAP_DILATION // LANES
        shift = (LANES - TAP_DILATION - piece * TAP_DILATION) % LANES
        moved = smooth[kept_rows:, tile * LANES : (tile + 1) * LANES]
        if shift:
            moved = pltpu.roll(moved, shift, 1)
        last = smooth[piece * depth : (piece + 1) * depth, width - LANES :]
        out_ref[place, pl.ds(piece * depth, depth), width - LANES :] = jnp.where(kept, last, moved)


def completed(strip):
    width = strip.shape[1]
    last = strip[:, width - LANES :]
    lane = lane_of(last.shape)
    kept = lane < LANES - TAP_DILATION
    total = jnp.where(kept, last, 0.0)
    for start in range(0, width - LANES, LANES):
        total = total + strip[:, start : start + LANES]
    odd = (lane // TAP_DILATION) % 2 == 1
    total = jnp.where(odd, -total, total)
    total = total + pltpu.roll(total, 2 * TAP_DILATION, 1)
    total = total + pltpu.roll(total, TAP_DILATION, 1)
    return jnp.concatenate([strip[:, : width - LANES], jnp.where(kept, last, total)], axis=1)


def unpacked(weights, refs, use):
    kept_rows, width = refs[0].shape[1:]
    depth = UNIT_ROWS - kept_rows
    tiles = [None] * (width // LANES)
    for piece in range(kept_rows // depth):
        rows = pl.ds(piece * depth, depth)
        strip = weighted(weights, [ref[0, rows, :] for ref in refs])
        tile = piece * TAP_DILATION // LANES
        shift = (piece * TAP_DILATION - (LANES - TAP_DILATION)) % LANES
        moved = strip[:, width - LANES :]
        if shift:
            moved = pltpu.roll(moved, shift, 1)
        if tiles[tile] is None:
            tiles[tile] = moved
        else:
            here = lane_of(moved.shape) // TAP_DILATION == piece % (LANES // TAP_DILATION)
            tiles[tile] = jnp.where(here, moved, tiles[tile])
        use(rows, completed(strip))
    use(pl.ds(kept_rows, depth), completed(jnp.concatenate(tiles, axis=1)))


def weighted(weights, values):
    total = None
    for weight, value in zip(weights, values):
        term = weight * value
        total = term if total is None else total + term
    return total


def pair_kernel(units_ref, out_ref, read_ref, read_sems):
    def read(unit):
        return pltpu.make_async_copy(units_ref.at[unit], read_ref.at[unit], read_sems.at[unit])

    for unit in range(out_ref.shape[0]):
        read(unit).start()
    for unit in range(out_ref.shape[0]):
        read(unit).wait()
        store_packed(out_ref, unit, pair_sums(read_ref[unit]))


def x_kernel(first, parts, edge_planes, units_ref, out_ref, top_ref, bottom_ref, read_ref, matrix_ref, read_sems, edge_sems):
    count = out_ref.shape[0]

    def read(unit):
        return pltpu.make_async_copy(units_ref.at[first + unit], read_ref.at[unit], read_sems.at[unit])

    edges = []
    for at, plane in enumerate(edge_planes):
        top = units_ref.at[plane * parts, pl.ds(0, REACH)]
        bottom = units_ref.at[(plane + 1) * parts - 1, pl.ds(UNIT_ROWS - REACH, REACH)]
        edges.append(pltpu.make_async_copy(top, top_ref.at[at], edge_sems.at[at, 0]))
        edges.append(pltpu.make_async_copy(bottom, bottom_ref.at[at], edge_sems.at[at, 1]))

    for unit in range(count):
        read(unit).start()
    for edge in edges:
        edge.start()
    fill_matrix(matrix_ref, x_taps())

    @pl.loop(0, count)
    def _(unit):
        read(unit).wait()
        store_packed(out_ref, unit, x_smoothed(read_ref[unit], matrix_ref[...]))

    for edge in edges:
        edge.wait()


def extended_groups(before_ref, c_ref, after_ref, offset):
    groups = []
    for ref in (before_ref, c_ref, after_ref):
        for start in range(0, ref.shape[1], TAP_DILATION):
            groups.append(ref[0, pl.ds(start + offset, STRIP), :])
    return groups


def y_smoothed(before_ref, c_ref, after_ref, smooth_ref):
    for within in range(TAP_DILATION // STRIP):
        groups = y_sums(extended_groups(before_ref, c_ref, after_ref, within * STRIP))
        for group, strip in enumerate(groups):
            smooth_ref[pl.ds(group * TAP_DILATION + within * STRIP, STRIP), :] = strip * (1.0 / 16.0)


def yx_kernel(before_ref, c_ref, after_ref, *refs):
    *out_refs, matrix_ref, smooth_ref = refs
    pl.when(pl.program_id(0) == 0)(lambda: fill_matrix(matrix_ref, x_taps()))
    y_smoothed(before_ref, c_ref, after_ref, smooth_ref)
    places = [(ref, place) for ref in out_refs for place in range(ref.shape[0])]
    for unit, (ref, place) in enumerate(places):
        smooth = x_smoothed(smooth_ref[pl.ds(unit * UNIT_ROWS, UNIT_ROWS), :], matrix_ref[...])
        store_packed(ref, place, smooth)


def z_kernel(weights, *refs):
    whole_ref = refs[-1]

    def use(rows, strip):
        whole_ref[0, rows, :] = strip

    unpacked(weights, refs[: len(weights)], use)


def group_of(shape):
    return lane_of(shape) // TAP_DILATION


def spread(tile, group):
    tile = jnp.where(group_of(tile.shape) == group, tile, 0.0)
    tile = tile + pltpu.roll(tile, 2 * TAP_DILATION, 1)
    return tile + pltpu.roll(tile, TAP_DILATION, 1)


def strip_rows(rows, ahead):
    per_group = TAP_DILATION // STRIP
    strip = lax.rem(lax.axis_index("gy") + ahead, per_group)
    return pl.ds(pl.multiple_of(rows - TAP_DILATION + strip * STRIP, STRIP), STRIP)


def short_strips(rows):
    half = rows - UNIT_ROWS
    fixed = [pl.ds(row, STRIP) for row in range(0, rows - TAP_DILATION, STRIP)]
    moving = [strip_rows(rows, ahead) for ahead in range(1, TAP_DILATION // STRIP)]
    return fixed[: half // STRIP], fixed[half // STRIP :] + moving


def short_tiles(rows, width):
    return (rows // STRIP - 3) * (width // LANES)


def short_kernel(before_ref, c_ref, after_ref, out_ref, matrix_ref, smooth_ref):
    plane = pl.program_id(0)

    @pl.when(plane == 0)
    def _():
        fill_matrix(matrix_ref, x_taps())
        out_ref[out_ref.shape[0] - 1] = jnp.zeros((STRIP, LANES), jnp.float32)

    y_smoothed(before_ref, c_ref, after_ref, smooth_ref)
    rows, width = smooth_ref.shape
    for start in range(0, rows, UNIT_ROWS):
        unit = pl.ds(start, UNIT_ROWS)
        smooth_ref[unit, :] = x_smoothed(smooth_ref[unit, :], matrix_ref[...])
    index = plane * short_tiles(rows, width)
    groups = LANES // TAP_DILATION
    for places in short_strips(rows):
        *places, last_place = places
        last = smooth_ref[last_place, :]
        for piece, place in enumerate(places):
            strip = smooth_ref[place, :]
            tile = piece // groups * LANES
            moved = last[:, tile : tile + LANES]
            shift = (groups - 1 - piece) % groups * TAP_DILATION
            if shift:
                moved = pltpu.roll(moved, shift, 1)
            for start in range(0, width - LANES, LANES):
                out_ref[index] = strip[:, start : start + LANES]
                index += 1
            here = group_of(moved.shape) == groups - 1
            out_ref[index] = jnp.where(here, moved, strip[:, width - LANES :])
            index += 1
    left = spread(last[:, width - LANES :], groups - 2)
    end = out_ref.shape[0] - 1
    out_ref[end] = jnp.where(group_of(left.shape) == plane, left, out_ref[end])


def short_z_kernel(weights, *refs):
    packed, (whole_ref, *sum_refs) = refs[: len(weights)], refs[-4:]
    rows, width = whole_ref.shape[1:]
    plane = pl.program_id(0)
    index = plane * short_tiles(rows, width)
    groups, tiles = LANES // TAP_DILATION, width // LANES
    for places in short_strips(rows):
        *places, last_place = places
        last = [None] * tiles
        for piece, place in enumerate(places):
            strip = [weighted(weights, [ref[index + tile] for ref in packed]) for tile in range(tiles)]
            index += tiles
            tile, group = divmod(piece, groups)
            shift = (group + 1 - groups) % groups * TAP_DILATION
            moved = pltpu.roll(strip[-1], shift, 1) if shift else strip[-1]
            here = group_of(moved.shape) == group
            last[tile] = moved if last[tile] is None else jnp.where(here, moved, last[tile])
            whole_ref[0, place, :] = completed(jnp.concatenate(strip, axis=1))
        if len(places) < tiles * groups - 1:
            end = packed[0].shape[0] - 1
            left = spread(weighted(weights, [ref[end] for ref in packed]), plane)
            last[-1] = jnp.where(group_of(left.shape) == groups - 2, left, last[-1])
        whole_ref[0, last_place, :] = completed(jnp.concatenate(last, axis=1))

    groups = rows // TAP_DILATION
    for ahead in range(TAP_DILATION // STRIP):
        total = None
        for group in range(groups if ahead else groups - 1):
            strip = whole_ref[0, strip_rows((group + 1) * TAP_DILATION, ahead), :]
            if total is None:
                total = strip
            else:
                total = total + strip if group % 2 == 0 else total - strip
        if ahead:
            sum_refs[ahead - 1][0] = total
        else:
            whole_ref[0, strip_rows(rows, 0), :] = total


def short_finish_kernel(whole_ref, *refs):
    *sum_refs, c_ref, _, _, detail_ref, coarse_ref = refs
    missing = strip_rows(whole_ref.shape[1], 0)
    coarse_ref[...] = whole_ref[...]
    coarse_ref[0, missing, :] = whole_ref[0, missing, :] + sum(ref[0] for ref in sum_refs)
    detail_ref[...] = c_ref[...] - coarse_ref[...]


def pair_z_kernel(weights, *refs):
    whole_ref, matrix_ref, pair_ref = refs[-3:]
    pl.when(pl.program_id(0) == 0)(lambda: fill_matrix(matrix_ref, rest_taps()))

    def use(rows, strip):
        pair_ref[rows, :] = strip

    unpacked(weights, refs[: len(weights)], use)
    whole_ref[0] = x_smoothed(pair_ref[...], matrix_ref[...])


def y_kernel(before_ref, whole_ref, after_ref, c_ref, detail_ref, coarse_ref):
    scale = 1.0 / 16.0
    for within in range(TAP_DILATION // STRIP):
        groups = y_sums(extended_groups(before_ref, whole_ref, after_ref, within * STRIP))
        for group, strip in enumerate(groups):
            rows = pl.ds(group * TAP_DILATION + within * STRIP, STRIP)
            coarse = strip * scale
            coarse_ref[0, rows, :] = coarse
            detail_ref[0, rows, :] = c_ref[0, rows, :] - coarse


def finish_kernel(weights, *refs):
    c_ref, _, _, detail_ref, coarse_ref = refs[len(weights) :]

    def use(rows, strip):
        coarse_ref[0, rows, :] = strip
        detail_ref[0, rows, :] = c_ref[0, rows, :] - strip

    unpacked(weights, refs[: len(weights)], use)


def last_kernel(weights, place, *refs):
    units_ref, _, _, detail_ref, coarse_ref, results_ref, write_sems = refs[len(weights) :]
    half = UNIT_ROWS // 2

    def write(piece, output, ref):
        rows = pl.ds(piece * half, half)
        source = results_ref.at[output, rows]
        return pltpu.make_async_copy(source, ref.at[place, rows], write_sems.at[piece, output])

    writes = [[write(piece, 0, detail_ref), write(piece, 1, coarse_ref)] for piece in range(2)]

    def use(rows, strip):
        results_ref[1, rows, :] = strip
        results_ref[0, rows, :] = units_ref[place, rows, :] - strip
        piece, left = divmod(rows.start + rows.size, half)
        if left == 0:
            for copy in writes[piece - 1]:
                copy.start()

    unpacked(weights, refs[: len(weights)], use)
    for copies in writes:
        for copy in copies:
            copy.wait()


def block_of(rows, width, first=0, depth=1):
    return pl.BlockSpec((depth, rows, width), lambda step: (first + step, 0, 0))


def anywhere():
    return pl.BlockSpec(memory_space=pl.ANY)


def tiles_of(pieces):
    return pl.BlockSpec((pieces, STRIP, LANES), lambda step: (0, 0, 0))


def in_vmem():
    return pl.BlockSpec(memory_space=pltpu.VMEM)


def call(kernel, name, steps, in_specs, out_specs, out_shape, args, aliases=None, scratch=(), grant=24):
    blocks = [spec.block_shape for spec in (*in_specs, *out_specs) if spec.block_shape]
    moved = 4 * max(steps, 1) * sum(math.prod(block) for block in blocks)
    return pl.pallas_call(
        kernel,
        grid=(steps,) if steps else (),
        in_specs=in_specs,
        out_specs=out_specs,
        out_shape=out_shape,
        scratch_shapes=scratch,
        input_output_aliases=aliases or {},
        compiler_params=pltpu.CompilerParams(vmem_limit_bytes=grant * 1024 * 1024),
        cost_estimate=pl.CostEstimate(flops=moved * 2, bytes_accessed=moved, transcendentals=0),
        name=name,
    )(*args)


def in_hbm(x):
    return pltpu.with_memory_space_constraint(x, pltpu.HBM)


def f32(*shape):
    return jax.ShapeDtypeStruct(shape, jnp.float32)


def can_shorten(rows, width):
    strips = TAP_DILATION // STRIP
    return lax.axis_size("gy") == strips and rows // TAP_DILATION % 2 == 0 and UNIT_ROWS // STRIP == width // TAP_DILATION


def shards(coarse_six):
    planes, rows, width = coarse_six.shape
    short = packed_rows(width)
    own, shifts = z_taps(planes, lax.axis_size("gz"))
    weights = (own, *shifts.values())
    count = len(weights)
    whole, unit, packed, edge = (functools.partial(block_of, n, width) for n in (rows, UNIT_ROWS, short, REACH))
    parts = rows // UNIT_ROWS
    units = coarse_six.reshape(planes * parts, UNIT_ROWS, width)
    matrix = pltpu.VMEM((width, width), jnp.bfloat16)

    def along_gz(x):
        return [passed_along(x, "gz", moved) for moved in shifts]

    def halo(source, start, stop):
        top, bottom = source[start:stop, :REACH], source[start:stop, rows - REACH :]
        return passed_along(bottom, "gy", 1), passed_along(top, "gy", -1)

    sums_shape = f32(FIRST_PLANES * parts, UNIT_ROWS, width)
    lead = call(
        pair_kernel,
        "pair_x",
        0,
        [anywhere()],
        [in_vmem()],
        [pltpu.VMEM((LEAD_UNITS, short, width), jnp.float32)],
        [in_hbm(units)],
        scratch=[pltpu.VMEM((LEAD_UNITS, UNIT_ROWS, width), jnp.float32), pltpu.SemaphoreType.DMA((LEAD_UNITS,))],
    )[0]
    lead, ready = lax.optimization_barrier((lead, units))
    lead_moved = along_gz(lead)
    first = FIRST_PLANES * parts - LEAD_UNITS
    edge_planes = range(FIRST_PLANES, FIRST_PLANES + sum(size for size, _ in LATER_GROUPS[0]))
    edges_shape = pltpu.VMEM((len(edge_planes), REACH, width), jnp.float32)
    first_block, top, bottom = call(
        functools.partial(x_kernel, LEAD_UNITS, parts, edge_planes),
        "smooth_x",
        0,
        [anywhere()],
        [in_vmem()] * 3,
        [pltpu.VMEM((first, short, width), jnp.float32), edges_shape, edges_shape],
        [in_hbm(ready)],
        scratch=[
            pltpu.VMEM((first, UNIT_ROWS, width), jnp.float32),
            matrix,
            pltpu.SemaphoreType.DMA((first,)),
            pltpu.SemaphoreType.DMA((len(edge_planes), 2)),
        ],
    )
    first_block, ready = lax.optimization_barrier((first_block, coarse_six))
    first_moved = along_gz(first_block)
    sums = call(
        functools.partial(pair_z_kernel, weights),
        "smooth_zx",
        LEAD_UNITS,
        [packed()] * count,
        [unit()],
        [sums_shape],
        [lead, *lead_moved],
        scratch=[matrix, pltpu.VMEM((UNIT_ROWS, width), jnp.float32)],
    )

    later, short_sent = [], []
    start = FIRST_PLANES
    near = (passed_along(bottom, "gy", 1), passed_along(top, "gy", -1))
    near, sums = lax.optimization_barrier((near, sums))
    for number, sizes in enumerate(LATER_GROUPS):
        offset = 0
        for size, messages in sizes:
            place = start + offset
            sources = [near[0], in_hbm(coarse_six), near[1]]
            specs = [edge(offset), whole(place), edge(offset)]
            scratch = [matrix, pltpu.VMEM((rows, width), jnp.float32)]
            if messages or not can_shorten(rows, width):
                messages = max(messages, 1)
                depth = parts // messages
                blocks = call(
                    yx_kernel,
                    "smooth_yx",
                    size,
                    specs,
                    [packed(depth=depth)] * messages,
                    [f32(size * depth, short, width)] * messages,
                    sources,
                    scratch=scratch,
                )
                for message, block in enumerate(blocks):
                    last_block = block
                    later.append((place * parts + message * depth, size * depth, (block, *along_gz(block))))
            else:
                pieces = size * short_tiles(rows, width) + 1
                block = call(
                    short_kernel,
                    "smooth_yx_short",
                    size,
                    specs,
                    [tiles_of(pieces)],
                    [f32(pieces, STRIP, LANES)],
                    sources,
                    scratch=scratch,
                )[0]
                short_sent.append((place, size, (block, *along_gz(block))))
            offset += size
        start += offset
        if number == 0:
            block, ready = lax.optimization_barrier((block, ready))
            block, *first_moved = lax.optimization_barrier((block, *first_moved))
            sums = call(
                functools.partial(z_kernel, weights),
                "smooth_z",
                first,
                [packed()] * count + [anywhere()],
                [unit(LEAD_UNITS)],
                [sums_shape],
                [first_block, *first_moved, *sums],
                {count: 0},
            )[0]
            along_z = sums.reshape(FIRST_PLANES, rows, width)
            along_z, ready = lax.optimization_barrier((along_z, ready))
        if number + 1 < len(LATER_GROUPS):
            if not number:
                block, ready = lax.optimization_barrier((block, ready))
            near = halo(ready, start, start + sum(size for size, _ in LATER_GROUPS[number + 1]))
        if number == 1:
            first_near, along_z, _ = lax.optimization_barrier((near[0], along_z, short_sent[0][2]))
            near = (first_near, near[1])
            sides = halo(along_z, 0, FIRST_PLANES)
        if number == 0:
            near, along_z = lax.optimization_barrier((near, along_z))

    def sum_short(batch):
        planes_in = sum(size for _, size, _ in batch)
        step, sums = 0, []
        for _, size, blocks in batch:
            sums = call(
                functools.partial(short_z_kernel, weights),
                "smooth_z_short",
                size,
                [tiles_of(blocks[0].shape[0])] * count + [anywhere()] * len(sums),
                [whole(step)] + [block_of(STRIP, width, step)] * 3,
                [f32(planes_in, rows, width)] + [f32(planes_in, STRIP, width)] * 3,
                [*blocks, *sums],
                {count + at: at for at in range(len(sums))},
            )
            step += size
        return sums[0], [passed_along(total, "gy", ahead) for ahead, total in enumerate(sums[1:], 1)]

    def finish_short(batch, sums, outs):
        start, size = batch[0][0], sum(size for _, size, _ in batch)
        along_z, moved = sums
        outs, moved = lax.optimization_barrier((outs, moved))
        return call(
            short_finish_kernel,
            "finish_short",
            size,
            [whole()] + [block_of(STRIP, width)] * 3 + [whole(start)] + [anywhere()] * 2,
            [whole(start)] * 2,
            [f32(planes, rows, width)] * 2,
            [along_z, *moved, coarse_six, *outs],
            {5: 0, 6: 1},
        )

    batches = [batch for batch in (short_sent[:SHORT_FIRST], short_sent[SHORT_FIRST:]) if batch]
    batch = batches[0]
    short_sums = sum_short(batch)
    short_whole, sides = lax.optimization_barrier((short_sums[0], sides))
    outs = call(
        y_kernel,
        "smooth_y",
        FIRST_PLANES,
        [edge(), whole(), edge(), whole()],
        [whole(), whole()],
        [f32(planes, rows, width)] * 2,
        [sides[0], along_z, sides[1], coarse_six],
    )
    short_sums, last_block = lax.optimization_barrier(((short_whole, short_sums[1]), last_block))
    last_moved = along_gz(last_block)
    outs = finish_short(batch, short_sums, outs)
    outs = [out.reshape(units.shape) for out in outs]
    for place, size, blocks in later[:-1]:
        outs, blocks = lax.optimization_barrier((outs, blocks))
        outs = call(
            functools.partial(finish_kernel, weights),
            "finish",
            size,
            [packed()] * count + [unit(place)] + [anywhere()] * 2,
            [unit(place)] * 2,
            [f32(*units.shape)] * 2,
            [*blocks, units, *outs],
            {count + 1: 0, count + 2: 1},
        )
    place = later[-1][0]
    blocks = (last_block, *last_moved)
    outs, blocks = lax.optimization_barrier((outs, blocks))
    outs = call(
        functools.partial(last_kernel, weights, place),
        "finish_last",
        0,
        [in_vmem()] * (count + 1) + [anywhere()] * 2,
        [anywhere()] * 2,
        [f32(*units.shape)] * 2,
        [*blocks, units, *outs],
        {count + 1: 0, count + 2: 1},
        scratch=[
            pltpu.VMEM((2, UNIT_ROWS, width), jnp.float32),
            pltpu.SemaphoreType.DMA((2, 2)),
        ],
    )
    return tuple(out.reshape(coarse_six.shape) for out in outs)


def solution(mesh):
    return jax.shard_map(
        shards,
        mesh=mesh,
        in_specs=(P("gz", "gy", None),),
        out_specs=(P("gz", "gy", None), P("gz", "gy", None)),
        check_vma=False,
    )
```

```python
import functools
import math

import jax
import jax.numpy as jnp
from jax import lax
from jax.experimental import pallas as pl
from jax.experimental.pallas import tpu as pltpu
from jax.sharding import PartitionSpec as P

TAP_DILATION = 32
REACH = 2 * TAP_DILATION
LANES = 128
STRIP = 8
UNIT_ROWS = 128
FIRST_PLANES = 2
LEAD_UNITS = 2
LATER_GROUPS = (((2, 0),), ((2, 0),), ((1, 1), (1, 2)))
SHORT_FIRST = 2

kernel_weights = (0.0625, 0.25, 0.375, 0.25, 0.0625)


def passed_along(x, axis, by):
    peers = lax.axis_size(axis)
    return lax.ppermute(x, axis, [(i, (i + by) % peers) for i in range(peers)])


def z_taps(plane_stack, count):
    weights = {}
    for cell_position in range(5):
        filter_reach = (cell_position - 2) * TAP_DILATION // plane_stack
        moved = -filter_reach % count
        weights[moved] = weights.get(moved, 0.0) + kernel_weights[cell_position]
    own = weights.pop(0, 0.0)
    return own, weights


def lane_of(shape):
    return lax.broadcasted_iota(jnp.int32, shape, 1)


def x_taps():
    return {(cell_position - 2) * TAP_DILATION: kernel_weights[cell_position] for cell_position in range(5)}


def rest_taps():
    return {(cell_position - 2) * TAP_DILATION: weight for cell_position, weight in enumerate((0.125, 0.375, 0.375, 0.125))}


def pair_sums(rows):
    return (rows + pltpu.roll(rows, rows.shape[1] - TAP_DILATION, 1)) * 0.5


def fill_matrix(matrix_ref, taps):
    depth, width = matrix_ref.shape
    for start in range(0, depth, LANES):
        shape = (LANES, width)
        row = start + lax.broadcasted_iota(jnp.int32, shape, 0)
        offset = row - lax.broadcasted_iota(jnp.int32, shape, 1)
        offset = jnp.where(offset < 0, offset + width, offset)
        values = jnp.zeros(shape, jnp.float32)
        for tap, weight in taps.items():
            values = jnp.where(offset == tap % width, weight, values)
        matrix_ref[pl.ds(start, LANES), :] = values.astype(jnp.bfloat16)


def x_smoothed(rows, matrix):
    parts = []
    for _ in range(3):
        parts.append(rows.astype(jnp.bfloat16))
        rows = rows - parts[-1].astype(jnp.float32)
    terms = jnp.dot(jnp.concatenate(parts), matrix, preferred_element_type=jnp.float32)
    high, middle, low = jnp.split(terms, 3)
    return high + middle + low


def y_sums(groups):
    for _ in range(4):
        groups = [a + b for a, b in zip(groups[:-1], groups[1:])]
    return groups


def packed_rows(width):
    return UNIT_ROWS - UNIT_ROWS * TAP_DILATION // width


def store_packed(out_ref, place, smooth):
    rows, width = smooth.shape
    kept_rows = out_ref.shape[1]
    depth = rows - kept_rows
    out_ref[place, :, : width - LANES] = smooth[:kept_rows, : width - LANES]
    kept = lane_of((depth, LANES)) < LANES - TAP_DILATION
    for piece in range(kept_rows // depth):
        tile = piece * TAP_DILATION // LANES
        shift = (LANES - TAP_DILATION - piece * TAP_DILATION) % LANES
        moved = smooth[kept_rows:, tile * LANES : (tile + 1) * LANES]
        if shift:
            moved = pltpu.roll(moved, shift, 1)
        last = smooth[piece * depth : (piece + 1) * depth, width - LANES :]
        out_ref[place, pl.ds(piece * depth, depth), width - LANES :] = jnp.where(kept, last, moved)


def completed(strip):
    width = strip.shape[1]
    last = strip[:, width - LANES :]
    lane = lane_of(last.shape)
    kept = lane < LANES - TAP_DILATION
    total = jnp.where(kept, last, 0.0)
    for start in range(0, width - LANES, LANES):
        total = total + strip[:, start : start + LANES]
    odd = (lane // TAP_DILATION) % 2 == 1
    total = jnp.where(odd, -total, total)
    total = total + pltpu.roll(total, 2 * TAP_DILATION, 1)
    total = total + pltpu.roll(total, TAP_DILATION, 1)
    return jnp.concatenate([strip[:, : width - LANES], jnp.where(kept, last, total)], axis=1)


def unpacked(weights, refs, use):
    kept_rows, width = refs[0].shape[1:]
    depth = UNIT_ROWS - kept_rows
    tiles = [None] * (width // LANES)
    for piece in range(kept_rows // depth):
        rows = pl.ds(piece * depth, depth)
        strip = weighted(weights, [ref[0, rows, :] for ref in refs])
        tile = piece * TAP_DILATION // LANES
        shift = (piece * TAP_DILATION - (LANES - TAP_DILATION)) % LANES
        moved = strip[:, width - LANES :]
        if shift:
            moved = pltpu.roll(moved, shift, 1)
        if tiles[tile] is None:
            tiles[tile] = moved
        else:
            here = lane_of(moved.shape) // TAP_DILATION == piece % (LANES // TAP_DILATION)
            tiles[tile] = jnp.where(here, moved, tiles[tile])
        use(rows, completed(strip))
    use(pl.ds(kept_rows, depth), completed(jnp.concatenate(tiles, axis=1)))


def weighted(weights, values):
    total = None
    for weight, value in zip(weights, values):
        term = weight * value
        total = term if total is None else total + term
    return total


def pair_kernel(units_ref, out_ref, read_ref, read_sems):
    def read(unit):
        return pltpu.make_async_copy(units_ref.at[unit], read_ref.at[unit], read_sems.at[unit])

    for unit in range(out_ref.shape[0]):
        read(unit).start()
    for unit in range(out_ref.shape[0]):
        read(unit).wait()
        store_packed(out_ref, unit, pair_sums(read_ref[unit]))


def x_kernel(first, parts, edge_planes, units_ref, out_ref, *refs):
    *edge_refs, read_ref, matrix_ref, read_sems, edge_sems = refs
    tops = [ref.at[at] for ref in edge_refs[::2] for at in range(ref.shape[0])]
    bottoms = [ref.at[at] for ref in edge_refs[1::2] for at in range(ref.shape[0])]
    count = out_ref.shape[0]

    def read(unit):
        return pltpu.make_async_copy(units_ref.at[first + unit], read_ref.at[unit], read_sems.at[unit])

    edges = []
    for at, plane in enumerate(edge_planes):
        top = units_ref.at[plane * parts, pl.ds(0, REACH)]
        bottom = units_ref.at[(plane + 1) * parts - 1, pl.ds(UNIT_ROWS - REACH, REACH)]
        edges.append(pltpu.make_async_copy(top, tops[at], edge_sems.at[at, 0]))
        edges.append(pltpu.make_async_copy(bottom, bottoms[at], edge_sems.at[at, 1]))

    for unit in range(count):
        read(unit).start()
    for edge in edges:
        edge.start()
    fill_matrix(matrix_ref, x_taps())

    @pl.loop(0, count)
    def _(unit):
        read(unit).wait()
        store_packed(out_ref, unit, x_smoothed(read_ref[unit], matrix_ref[...]))

    for edge in edges:
        edge.wait()


def extended_groups(before_ref, c_ref, after_ref, offset):
    groups = []
    for ref in (before_ref, c_ref, after_ref):
        for start in range(0, ref.shape[1], TAP_DILATION):
            groups.append(ref[0, pl.ds(start + offset, STRIP), :])
    return groups


def y_smoothed(before_ref, c_ref, after_ref, smooth_ref):
    for within in range(TAP_DILATION // STRIP):
        groups = y_sums(extended_groups(before_ref, c_ref, after_ref, within * STRIP))
        for group, strip in enumerate(groups):
            smooth_ref[pl.ds(group * TAP_DILATION + within * STRIP, STRIP), :] = strip * (1.0 / 16.0)


def yx_kernel(before_ref, c_ref, after_ref, *refs):
    *out_refs, matrix_ref, smooth_ref = refs
    pl.when(pl.program_id(0) == 0)(lambda: fill_matrix(matrix_ref, x_taps()))
    y_smoothed(before_ref, c_ref, after_ref, smooth_ref)
    places = [(ref, place) for ref in out_refs for place in range(ref.shape[0])]
    for unit, (ref, place) in enumerate(places):
        smooth = x_smoothed(smooth_ref[pl.ds(unit * UNIT_ROWS, UNIT_ROWS), :], matrix_ref[...])
        store_packed(ref, place, smooth)


def z_kernel(weights, *refs):
    whole_ref = refs[-1]

    def use(rows, strip):
        whole_ref[0, rows, :] = strip

    unpacked(weights, refs[: len(weights)], use)


def group_of(shape):
    return lane_of(shape) // TAP_DILATION


def spread(tile, group):
    tile = jnp.where(group_of(tile.shape) == group, tile, 0.0)
    tile = tile + pltpu.roll(tile, 2 * TAP_DILATION, 1)
    return tile + pltpu.roll(tile, TAP_DILATION, 1)


def strip_rows(rows, ahead):
    per_group = TAP_DILATION // STRIP
    strip = lax.rem(lax.axis_index("gy") + ahead, per_group)
    return pl.ds(pl.multiple_of(rows - TAP_DILATION + strip * STRIP, STRIP), STRIP)


def short_strips(rows):
    half = rows - UNIT_ROWS
    fixed = [pl.ds(row, STRIP) for row in range(0, rows - TAP_DILATION, STRIP)]
    moving = [strip_rows(rows, ahead) for ahead in range(1, TAP_DILATION // STRIP)]
    return fixed[: half // STRIP], fixed[half // STRIP :] + moving


def short_tiles(rows, width):
    return (rows // STRIP - 3) * (width // LANES)


def short_kernel(before_ref, c_ref, after_ref, out_ref, matrix_ref, smooth_ref):
    plane = pl.program_id(0)

    @pl.when(plane == 0)
    def _():
        fill_matrix(matrix_ref, x_taps())
        out_ref[out_ref.shape[0] - 1] = jnp.zeros((STRIP, LANES), jnp.float32)

    y_smoothed(before_ref, c_ref, after_ref, smooth_ref)
    rows, width = smooth_ref.shape
    for start in range(0, rows, UNIT_ROWS):
        unit = pl.ds(start, UNIT_ROWS)
        smooth_ref[unit, :] = x_smoothed(smooth_ref[unit, :], matrix_ref[...])
    index = plane * short_tiles(rows, width)
    groups = LANES // TAP_DILATION
    for places in short_strips(rows):
        *places, last_place = places
        last = smooth_ref[last_place, :]
        for piece, place in enumerate(places):
            strip = smooth_ref[place, :]
            tile = piece // groups * LANES
            moved = last[:, tile : tile + LANES]
            shift = (groups - 1 - piece) % groups * TAP_DILATION
            if shift:
                moved = pltpu.roll(moved, shift, 1)
            for start in range(0, width - LANES, LANES):
                out_ref[index] = strip[:, start : start + LANES]
                index += 1
            here = group_of(moved.shape) == groups - 1
            out_ref[index] = jnp.where(here, moved, strip[:, width - LANES :])
            index += 1
    left = spread(last[:, width - LANES :], groups - 2)
    end = out_ref.shape[0] - 1
    out_ref[end] = jnp.where(group_of(left.shape) == plane, left, out_ref[end])


def short_z_kernel(weights, *refs):
    packed, (whole_ref, *sum_refs) = refs[: len(weights)], refs[-4:]
    rows, width = whole_ref.shape[1:]
    plane = pl.program_id(0)
    index = plane * short_tiles(rows, width)
    groups, tiles = LANES // TAP_DILATION, width // LANES
    for places in short_strips(rows):
        *places, last_place = places
        last = [None] * tiles
        for piece, place in enumerate(places):
            strip = [weighted(weights, [ref[index + tile] for ref in packed]) for tile in range(tiles)]
            index += tiles
            tile, group = divmod(piece, groups)
            shift = (group + 1 - groups) % groups * TAP_DILATION
            moved = pltpu.roll(strip[-1], shift, 1) if shift else strip[-1]
            here = group_of(moved.shape) == group
            last[tile] = moved if last[tile] is None else jnp.where(here, moved, last[tile])
            whole_ref[0, place, :] = completed(jnp.concatenate(strip, axis=1))
        if len(places) < tiles * groups - 1:
            end = packed[0].shape[0] - 1
            left = spread(weighted(weights, [ref[end] for ref in packed]), plane)
            last[-1] = jnp.where(group_of(left.shape) == groups - 2, left, last[-1])
        whole_ref[0, last_place, :] = completed(jnp.concatenate(last, axis=1))

    groups = rows // TAP_DILATION
    for ahead in range(TAP_DILATION // STRIP):
        total = None
        for group in range(groups if ahead else groups - 1):
            strip = whole_ref[0, strip_rows((group + 1) * TAP_DILATION, ahead), :]
            if total is None:
                total = strip
            else:
                total = total + strip if group % 2 == 0 else total - strip
        if ahead:
            sum_refs[ahead - 1][0] = total
        else:
            whole_ref[0, strip_rows(rows, 0), :] = total


def short_finish_kernel(whole_ref, *refs):
    *sum_refs, c_ref, _, _, detail_ref, coarse_ref = refs
    missing = strip_rows(whole_ref.shape[1], 0)
    coarse_ref[...] = whole_ref[...]
    coarse_ref[0, missing, :] = whole_ref[0, missing, :] + sum(ref[0] for ref in sum_refs)
    detail_ref[...] = c_ref[...] - coarse_ref[...]


def pair_z_kernel(weights, *refs):
    whole_ref, matrix_ref, pair_ref = refs[-3:]
    pl.when(pl.program_id(0) == 0)(lambda: fill_matrix(matrix_ref, rest_taps()))

    def use(rows, strip):
        pair_ref[rows, :] = strip

    unpacked(weights, refs[: len(weights)], use)
    whole_ref[0] = x_smoothed(pair_ref[...], matrix_ref[...])


def y_kernel(before_ref, whole_ref, after_ref, c_ref, detail_ref, coarse_ref):
    scale = 1.0 / 16.0
    for within in range(TAP_DILATION // STRIP):
        groups = y_sums(extended_groups(before_ref, whole_ref, after_ref, within * STRIP))
        for group, strip in enumerate(groups):
            rows = pl.ds(group * TAP_DILATION + within * STRIP, STRIP)
            coarse = strip * scale
            coarse_ref[0, rows, :] = coarse
            detail_ref[0, rows, :] = c_ref[0, rows, :] - coarse


def finish_kernel(weights, *refs):
    c_ref, _, _, detail_ref, coarse_ref = refs[len(weights) :]

    def use(rows, strip):
        coarse_ref[0, rows, :] = strip
        detail_ref[0, rows, :] = c_ref[0, rows, :] - strip

    unpacked(weights, refs[: len(weights)], use)


def last_kernel(weights, place, *refs):
    units_ref, _, _, detail_ref, coarse_ref, results_ref, write_sems = refs[len(weights) :]
    half = UNIT_ROWS // 2

    def write(piece, output, ref):
        rows = pl.ds(piece * half, half)
        source = results_ref.at[output, rows]
        return pltpu.make_async_copy(source, ref.at[place, rows], write_sems.at[piece, output])

    writes = [[write(piece, 0, detail_ref), write(piece, 1, coarse_ref)] for piece in range(2)]

    def use(rows, strip):
        results_ref[1, rows, :] = strip
        results_ref[0, rows, :] = units_ref[place, rows, :] - strip
        piece, left = divmod(rows.start + rows.size, half)
        if left == 0:
            for copy in writes[piece - 1]:
                copy.start()

    unpacked(weights, refs[: len(weights)], use)
    for copies in writes:
        for copy in copies:
            copy.wait()


def block_of(rows, width, first=0, depth=1):
    return pl.BlockSpec((depth, rows, width), lambda step: (first + step, 0, 0))


def anywhere():
    return pl.BlockSpec(memory_space=pl.ANY)


def tiles_of(pieces):
    return pl.BlockSpec((pieces, STRIP, LANES), lambda step: (0, 0, 0))


def in_vmem():
    return pl.BlockSpec(memory_space=pltpu.VMEM)


def call(kernel, name, steps, in_specs, out_specs, out_shape, args, aliases=None, scratch=(), grant=24):
    blocks = [spec.block_shape for spec in (*in_specs, *out_specs) if spec.block_shape]
    moved = 4 * max(steps, 1) * sum(math.prod(block) for block in blocks)
    return pl.pallas_call(
        kernel,
        grid=(steps,) if steps else (),
        in_specs=in_specs,
        out_specs=out_specs,
        out_shape=out_shape,
        scratch_shapes=scratch,
        input_output_aliases=aliases or {},
        compiler_params=pltpu.CompilerParams(vmem_limit_bytes=grant * 1024 * 1024),
        cost_estimate=pl.CostEstimate(flops=moved * 2, bytes_accessed=moved, transcendentals=0),
        name=name,
    )(*args)


def in_hbm(x):
    return pltpu.with_memory_space_constraint(x, pltpu.HBM)


def f32(*shape):
    return jax.ShapeDtypeStruct(shape, jnp.float32)


def can_shorten(rows, width):
    strips = TAP_DILATION // STRIP
    return lax.axis_size("gy") == strips and rows // TAP_DILATION % 2 == 0 and UNIT_ROWS // STRIP == width // TAP_DILATION


def shards(coarse_six):
    planes, rows, width = coarse_six.shape
    short = packed_rows(width)
    own, shifts = z_taps(planes, lax.axis_size("gz"))
    weights = (own, *shifts.values())
    count = len(weights)
    whole, unit, packed, edge = (functools.partial(block_of, n, width) for n in (rows, UNIT_ROWS, short, REACH))
    parts = rows // UNIT_ROWS
    units = coarse_six.reshape(planes * parts, UNIT_ROWS, width)
    matrix = pltpu.VMEM((width, width), jnp.bfloat16)

    def along_gz(x):
        return [passed_along(x, "gz", moved) for moved in shifts]

    def swapped(top, bottom):
        return passed_along(bottom, "gy", 1), passed_along(top, "gy", -1)

    def halo(source, start, stop):
        return swapped(source[start:stop, :REACH], source[start:stop, rows - REACH :])

    sums_shape = f32(FIRST_PLANES * parts, UNIT_ROWS, width)
    lead = call(
        pair_kernel,
        "pair_x",
        0,
        [anywhere()],
        [in_vmem()],
        [pltpu.VMEM((LEAD_UNITS, short, width), jnp.float32)],
        [in_hbm(units)],
        scratch=[pltpu.VMEM((LEAD_UNITS, UNIT_ROWS, width), jnp.float32), pltpu.SemaphoreType.DMA((LEAD_UNITS,))],
    )[0]
    lead, ready = lax.optimization_barrier((lead, units))
    lead_moved = along_gz(lead)
    first = FIRST_PLANES * parts - LEAD_UNITS
    edge_planes = range(FIRST_PLANES, planes)
    sizes_of = [sum(size for size, _ in sizes) for sizes in LATER_GROUPS]
    edge_shapes = [pltpu.VMEM((size, REACH, width), jnp.float32) for size in sizes_of for _ in range(2)]
    first_block, *edges = call(
        functools.partial(x_kernel, LEAD_UNITS, parts, edge_planes),
        "smooth_x",
        0,
        [anywhere()],
        [in_vmem()] * (1 + len(edge_shapes)),
        [pltpu.VMEM((first, short, width), jnp.float32), *edge_shapes],
        [in_hbm(ready)],
        scratch=[
            pltpu.VMEM((first, UNIT_ROWS, width), jnp.float32),
            matrix,
            pltpu.SemaphoreType.DMA((first,)),
            pltpu.SemaphoreType.DMA((len(edge_planes), 2)),
        ],
    )
    first_block, ready = lax.optimization_barrier((first_block, coarse_six))
    first_moved = along_gz(first_block)
    sums = call(
        functools.partial(pair_z_kernel, weights),
        "smooth_zx",
        LEAD_UNITS,
        [packed()] * count,
        [unit()],
        [sums_shape],
        [lead, *lead_moved],
        scratch=[matrix, pltpu.VMEM((UNIT_ROWS, width), jnp.float32)],
    )

    later, short_sent = [], []
    start = FIRST_PLANES
    edges = list(zip(edges[::2], edges[1::2]))
    near = swapped(*edges[0])
    near, sums = lax.optimization_barrier((near, sums))
    for number, sizes in enumerate(LATER_GROUPS):
        offset = 0
        for size, messages in sizes:
            place = start + offset
            sources = [near[0], in_hbm(coarse_six), near[1]]
            specs = [edge(offset), whole(place), edge(offset)]
            scratch = [matrix, pltpu.VMEM((rows, width), jnp.float32)]
            if messages or not can_shorten(rows, width):
                messages = max(messages, 1)
                depth = parts // messages
                blocks = call(
                    yx_kernel,
                    "smooth_yx",
                    size,
                    specs,
                    [packed(depth=depth)] * messages,
                    [f32(size * depth, short, width)] * messages,
                    sources,
                    scratch=scratch,
                )
                for message, block in enumerate(blocks):
                    last_block = block
                    later.append((place * parts + message * depth, size * depth, (block, *along_gz(block))))
            else:
                pieces = size * short_tiles(rows, width) + 1
                block = call(
                    short_kernel,
                    "smooth_yx_short",
                    size,
                    specs,
                    [tiles_of(pieces)],
                    [f32(pieces, STRIP, LANES)],
                    sources,
                    scratch=scratch,
                )[0]
                short_sent.append((place, size, (block, *along_gz(block))))
            offset += size
        start += offset
        if number == 0:
            block, ready = lax.optimization_barrier((block, ready))
            block, *first_moved = lax.optimization_barrier((block, *first_moved))
            sums = call(
                functools.partial(z_kernel, weights),
                "smooth_z",
                first,
                [packed()] * count + [anywhere()],
                [unit(LEAD_UNITS)],
                [sums_shape],
                [first_block, *first_moved, *sums],
                {count: 0},
            )[0]
            along_z = sums.reshape(FIRST_PLANES, rows, width)
            along_z, edges[1] = lax.optimization_barrier((along_z, edges[1]))
        if number + 1 < len(LATER_GROUPS):
            block, edges[number + 1] = lax.optimization_barrier((block, edges[number + 1]))
            near = swapped(*edges[number + 1])
        if number == 1:
            first_near, along_z, _ = lax.optimization_barrier((near[0], along_z, short_sent[0][2]))
            near = (first_near, near[1])
            sides = halo(along_z, 0, FIRST_PLANES)
        if number == 0:
            near, along_z = lax.optimization_barrier((near, along_z))

    def sum_short(batch):
        planes_in = sum(size for _, size, _ in batch)
        step, sums = 0, []
        for _, size, blocks in batch:
            sums = call(
                functools.partial(short_z_kernel, weights),
                "smooth_z_short",
                size,
                [tiles_of(blocks[0].shape[0])] * count + [anywhere()] * len(sums),
                [whole(step)] + [block_of(STRIP, width, step)] * 3,
                [f32(planes_in, rows, width)] + [f32(planes_in, STRIP, width)] * 3,
                [*blocks, *sums],
                {count + at: at for at in range(len(sums))},
            )
            step += size
        return sums[0], [passed_along(total, "gy", ahead) for ahead, total in enumerate(sums[1:], 1)]

    def finish_short(batch, sums, outs):
        start, size = batch[0][0], sum(size for _, size, _ in batch)
        along_z, moved = sums
        outs, moved = lax.optimization_barrier((outs, moved))
        return call(
            short_finish_kernel,
            "finish_short",
            size,
            [whole()] + [block_of(STRIP, width)] * 3 + [whole(start)] + [anywhere()] * 2,
            [whole(start)] * 2,
            [f32(planes, rows, width)] * 2,
            [along_z, *moved, coarse_six, *outs],
            {5: 0, 6: 1},
        )

    batches = [batch for batch in (short_sent[:SHORT_FIRST], short_sent[SHORT_FIRST:]) if batch]
    batch = batches[0]
    short_sums = sum_short(batch)
    short_whole, sides = lax.optimization_barrier((short_sums[0], sides))
    outs = call(
        y_kernel,
        "smooth_y",
        FIRST_PLANES,
        [edge(), whole(), edge(), whole()],
        [whole(), whole()],
        [f32(planes, rows, width)] * 2,
        [sides[0], along_z, sides[1], coarse_six],
    )
    short_sums, last_block = lax.optimization_barrier(((short_whole, short_sums[1]), last_block))
    last_moved = along_gz(last_block)
    outs = finish_short(batch, short_sums, outs)
    outs = [out.reshape(units.shape) for out in outs]
    for place, size, blocks in later[:-1]:
        outs, blocks = lax.optimization_barrier((outs, blocks))
        outs = call(
            functools.partial(finish_kernel, weights),
            "finish",
            size,
            [packed()] * count + [unit(place)] + [anywhere()] * 2,
            [unit(place)] * 2,
            [f32(*units.shape)] * 2,
            [*blocks, units, *outs],
            {count + 1: 0, count + 2: 1},
        )
    place = later[-1][0]
    blocks = (last_block, *last_moved)
    outs, blocks = lax.optimization_barrier((outs, blocks))
    outs = call(
        functools.partial(last_kernel, weights, place),
        "finish_last",
        0,
        [in_vmem()] * (count + 1) + [anywhere()] * 2,
        [anywhere()] * 2,
        [f32(*units.shape)] * 2,
        [*blocks, units, *outs],
        {count + 1: 0, count + 2: 1},
        scratch=[
            pltpu.VMEM((2, UNIT_ROWS, width), jnp.float32),
            pltpu.SemaphoreType.DMA((2, 2)),
        ],
    )
    return tuple(out.reshape(coarse_six.shape) for out in outs)


def solution(mesh):
    return jax.shard_map(
        shards,
        mesh=mesh,
        in_specs=(P("gz", "gy", None),),
        out_specs=(P("gz", "gy", None), P("gz", "gy", None)),
        check_vma=False,
    )
```

```python
import functools
import math

import jax
import jax.numpy as jnp
from jax import lax
from jax.experimental import pallas as pl
from jax.experimental.pallas import tpu as pltpu
from jax.sharding import PartitionSpec as P

TAP_DILATION = 32
REACH = 2 * TAP_DILATION
LANES = 128
STRIP = 8
UNIT_ROWS = 128
FIRST_PLANES = 2
LEAD_UNITS = 2
LATER_GROUPS = (((2, 0),), ((2, 0),), ((1, 1), (1, 2)))
SHORT_FIRST = 2

kernel_weights = (0.0625, 0.25, 0.375, 0.25, 0.0625)


def passed_along(x, axis, by):
    peers = lax.axis_size(axis)
    return lax.ppermute(x, axis, [(i, (i + by) % peers) for i in range(peers)])


def z_taps(plane_stack, count):
    weights = {}
    for cell_position in range(5):
        filter_reach = (cell_position - 2) * TAP_DILATION // plane_stack
        moved = -filter_reach % count
        weights[moved] = weights.get(moved, 0.0) + kernel_weights[cell_position]
    own = weights.pop(0, 0.0)
    return own, weights


def lane_of(shape):
    return lax.broadcasted_iota(jnp.int32, shape, 1)


def x_taps():
    return {(cell_position - 2) * TAP_DILATION: kernel_weights[cell_position] for cell_position in range(5)}


def rest_taps():
    return {(cell_position - 2) * TAP_DILATION: weight for cell_position, weight in enumerate((0.125, 0.375, 0.375, 0.125))}


def pair_sums(rows):
    return (rows + pltpu.roll(rows, rows.shape[1] - TAP_DILATION, 1)) * 0.5


def fill_matrix(matrix_ref, taps):
    depth, width = matrix_ref.shape
    for start in range(0, depth, LANES):
        shape = (LANES, width)
        row = start + lax.broadcasted_iota(jnp.int32, shape, 0)
        offset = row - lax.broadcasted_iota(jnp.int32, shape, 1)
        offset = jnp.where(offset < 0, offset + width, offset)
        values = jnp.zeros(shape, jnp.float32)
        for tap, weight in taps.items():
            values = jnp.where(offset == tap % width, weight, values)
        matrix_ref[pl.ds(start, LANES), :] = values.astype(jnp.bfloat16)


def x_smoothed(rows, matrix):
    parts = []
    for _ in range(3):
        parts.append(rows.astype(jnp.bfloat16))
        rows = rows - parts[-1].astype(jnp.float32)
    terms = jnp.dot(jnp.concatenate(parts), matrix, preferred_element_type=jnp.float32)
    high, middle, low = jnp.split(terms, 3)
    return high + middle + low


def y_sums(groups):
    for _ in range(4):
        groups = [a + b for a, b in zip(groups[:-1], groups[1:])]
    return groups


def packed_rows(width):
    return UNIT_ROWS - UNIT_ROWS * TAP_DILATION // width


def store_packed(out_ref, place, smooth):
    rows, width = smooth.shape
    kept_rows = out_ref.shape[1]
    depth = rows - kept_rows
    out_ref[place, :, : width - LANES] = smooth[:kept_rows, : width - LANES]
    kept = lane_of((depth, LANES)) < LANES - TAP_DILATION
    for piece in range(kept_rows // depth):
        tile = piece * TAP_DILATION // LANES
        shift = (LANES - TAP_DILATION - piece * TAP_DILATION) % LANES
        moved = smooth[kept_rows:, tile * LANES : (tile + 1) * LANES]
        if shift:
            moved = pltpu.roll(moved, shift, 1)
        last = smooth[piece * depth : (piece + 1) * depth, width - LANES :]
        out_ref[place, pl.ds(piece * depth, depth), width - LANES :] = jnp.where(kept, last, moved)


def completed(strip):
    width = strip.shape[1]
    last = strip[:, width - LANES :]
    lane = lane_of(last.shape)
    kept = lane < LANES - TAP_DILATION
    total = jnp.where(kept, last, 0.0)
    for start in range(0, width - LANES, LANES):
        total = total + strip[:, start : start + LANES]
    odd = (lane // TAP_DILATION) % 2 == 1
    total = jnp.where(odd, -total, total)
    total = total + pltpu.roll(total, 2 * TAP_DILATION, 1)
    total = total + pltpu.roll(total, TAP_DILATION, 1)
    return jnp.concatenate([strip[:, : width - LANES], jnp.where(kept, last, total)], axis=1)


def unpacked(weights, refs, use):
    kept_rows, width = refs[0].shape[1:]
    depth = UNIT_ROWS - kept_rows
    tiles = [None] * (width // LANES)
    for piece in range(kept_rows // depth):
        rows = pl.ds(piece * depth, depth)
        strip = weighted(weights, [ref[0, rows, :] for ref in refs])
        tile = piece * TAP_DILATION // LANES
        shift = (piece * TAP_DILATION - (LANES - TAP_DILATION)) % LANES
        moved = strip[:, width - LANES :]
        if shift:
            moved = pltpu.roll(moved, shift, 1)
        if tiles[tile] is None:
            tiles[tile] = moved
        else:
            here = lane_of(moved.shape) // TAP_DILATION == piece % (LANES // TAP_DILATION)
            tiles[tile] = jnp.where(here, moved, tiles[tile])
        use(rows, completed(strip))
    use(pl.ds(kept_rows, depth), completed(jnp.concatenate(tiles, axis=1)))


def weighted(weights, values):
    total = None
    for weight, value in zip(weights, values):
        term = weight * value
        total = term if total is None else total + term
    return total


def pair_kernel(units_ref, out_ref, read_ref, read_sem):
    count = out_ref.shape[0]
    read = pltpu.make_async_copy(units_ref.at[pl.ds(0, count)], read_ref, read_sem)
    read.start()
    read.wait()
    for unit in range(count):
        store_packed(out_ref, unit, pair_sums(read_ref[unit]))


def x_kernel(first, parts, edge_planes, units_ref, out_ref, *refs):
    *edge_refs, read_ref, matrix_ref, read_sems, edge_sems = refs
    tops = [ref.at[at] for ref in edge_refs[::2] for at in range(ref.shape[0])]
    bottoms = [ref.at[at] for ref in edge_refs[1::2] for at in range(ref.shape[0])]
    count = out_ref.shape[0]

    def read(unit):
        return pltpu.make_async_copy(units_ref.at[first + unit], read_ref.at[unit], read_sems.at[unit])

    edges = []
    for at, plane in enumerate(edge_planes):
        top = units_ref.at[plane * parts, pl.ds(0, REACH)]
        bottom = units_ref.at[(plane + 1) * parts - 1, pl.ds(UNIT_ROWS - REACH, REACH)]
        edges.append(pltpu.make_async_copy(top, tops[at], edge_sems.at[at, 0]))
        edges.append(pltpu.make_async_copy(bottom, bottoms[at], edge_sems.at[at, 1]))

    for unit in range(count):
        read(unit).start()
    for edge in edges:
        edge.start()
    fill_matrix(matrix_ref, x_taps())

    @pl.loop(0, count)
    def _(unit):
        read(unit).wait()
        store_packed(out_ref, unit, x_smoothed(read_ref[unit], matrix_ref[...]))

    for edge in edges:
        edge.wait()


def extended_groups(before_ref, c_ref, after_ref, offset):
    groups = []
    for ref in (before_ref, c_ref, after_ref):
        for start in range(0, ref.shape[1], TAP_DILATION):
            groups.append(ref[0, pl.ds(start + offset, STRIP), :])
    return groups


def y_smoothed(before_ref, c_ref, after_ref, smooth_ref):
    for within in range(TAP_DILATION // STRIP):
        groups = y_sums(extended_groups(before_ref, c_ref, after_ref, within * STRIP))
        for group, strip in enumerate(groups):
            smooth_ref[pl.ds(group * TAP_DILATION + within * STRIP, STRIP), :] = strip * (1.0 / 16.0)


def yx_kernel(before_ref, c_ref, after_ref, *refs):
    *out_refs, matrix_ref, smooth_ref = refs
    pl.when(pl.program_id(0) == 0)(lambda: fill_matrix(matrix_ref, x_taps()))
    y_smoothed(before_ref, c_ref, after_ref, smooth_ref)
    places = [(ref, place) for ref in out_refs for place in range(ref.shape[0])]
    for unit, (ref, place) in enumerate(places):
        smooth = x_smoothed(smooth_ref[pl.ds(unit * UNIT_ROWS, UNIT_ROWS), :], matrix_ref[...])
        store_packed(ref, place, smooth)


def z_kernel(weights, *refs):
    whole_ref = refs[-1]

    def use(rows, strip):
        whole_ref[0, rows, :] = strip

    unpacked(weights, refs[: len(weights)], use)


def group_of(shape):
    return lane_of(shape) // TAP_DILATION


def spread(tile, group):
    tile = jnp.where(group_of(tile.shape) == group, tile, 0.0)
    tile = tile + pltpu.roll(tile, 2 * TAP_DILATION, 1)
    return tile + pltpu.roll(tile, TAP_DILATION, 1)


def strip_rows(rows, ahead):
    per_group = TAP_DILATION // STRIP
    strip = lax.rem(lax.axis_index("gy") + ahead, per_group)
    return pl.ds(pl.multiple_of(rows - TAP_DILATION + strip * STRIP, STRIP), STRIP)


def short_strips(rows):
    half = rows - UNIT_ROWS
    fixed = [pl.ds(row, STRIP) for row in range(0, rows - TAP_DILATION, STRIP)]
    moving = [strip_rows(rows, ahead) for ahead in range(1, TAP_DILATION // STRIP)]
    return fixed[: half // STRIP], fixed[half // STRIP :] + moving


def short_tiles(rows, width):
    return (rows // STRIP - 3) * (width // LANES)


def short_kernel(before_ref, c_ref, after_ref, out_ref, matrix_ref, smooth_ref):
    plane = pl.program_id(0)

    @pl.when(plane == 0)
    def _():
        fill_matrix(matrix_ref, x_taps())
        out_ref[out_ref.shape[0] - 1] = jnp.zeros((STRIP, LANES), jnp.float32)

    y_smoothed(before_ref, c_ref, after_ref, smooth_ref)
    rows, width = smooth_ref.shape
    for start in range(0, rows, UNIT_ROWS):
        unit = pl.ds(start, UNIT_ROWS)
        smooth_ref[unit, :] = x_smoothed(smooth_ref[unit, :], matrix_ref[...])
    index = plane * short_tiles(rows, width)
    groups = LANES // TAP_DILATION
    for places in short_strips(rows):
        *places, last_place = places
        last = smooth_ref[last_place, :]
        for piece, place in enumerate(places):
            strip = smooth_ref[place, :]
            tile = piece // groups * LANES
            moved = last[:, tile : tile + LANES]
            shift = (groups - 1 - piece) % groups * TAP_DILATION
            if shift:
                moved = pltpu.roll(moved, shift, 1)
            for start in range(0, width - LANES, LANES):
                out_ref[index] = strip[:, start : start + LANES]
                index += 1
            here = group_of(moved.shape) == groups - 1
            out_ref[index] = jnp.where(here, moved, strip[:, width - LANES :])
            index += 1
    left = spread(last[:, width - LANES :], groups - 2)
    end = out_ref.shape[0] - 1
    out_ref[end] = jnp.where(group_of(left.shape) == plane, left, out_ref[end])


def short_z_kernel(weights, *refs):
    packed, (whole_ref, *sum_refs) = refs[: len(weights)], refs[-4:]
    rows, width = whole_ref.shape[1:]
    plane = pl.program_id(0)
    index = plane * short_tiles(rows, width)
    groups, tiles = LANES // TAP_DILATION, width // LANES
    for places in short_strips(rows):
        *places, last_place = places
        last = [None] * tiles
        for piece, place in enumerate(places):
            strip = [weighted(weights, [ref[index + tile] for ref in packed]) for tile in range(tiles)]
            index += tiles
            tile, group = divmod(piece, groups)
            shift = (group + 1 - groups) % groups * TAP_DILATION
            moved = pltpu.roll(strip[-1], shift, 1) if shift else strip[-1]
            here = group_of(moved.shape) == group
            last[tile] = moved if last[tile] is None else jnp.where(here, moved, last[tile])
            whole_ref[0, place, :] = completed(jnp.concatenate(strip, axis=1))
        if len(places) < tiles * groups - 1:
            end = packed[0].shape[0] - 1
            left = spread(weighted(weights, [ref[end] for ref in packed]), plane)
            last[-1] = jnp.where(group_of(left.shape) == groups - 2, left, last[-1])
        whole_ref[0, last_place, :] = completed(jnp.concatenate(last, axis=1))

    groups = rows // TAP_DILATION
    for ahead in range(TAP_DILATION // STRIP):
        total = None
        for group in range(groups if ahead else groups - 1):
            strip = whole_ref[0, strip_rows((group + 1) * TAP_DILATION, ahead), :]
            if total is None:
                total = strip
            else:
                total = total + strip if group % 2 == 0 else total - strip
        if ahead:
            sum_refs[ahead - 1][0] = total
        else:
            whole_ref[0, strip_rows(rows, 0), :] = total


def short_finish_kernel(whole_ref, *refs):
    *sum_refs, c_ref, _, _, detail_ref, coarse_ref = refs
    missing = strip_rows(whole_ref.shape[1], 0)
    coarse_ref[...] = whole_ref[...]
    coarse_ref[0, missing, :] = whole_ref[0, missing, :] + sum(ref[0] for ref in sum_refs)
    detail_ref[...] = c_ref[...] - coarse_ref[...]


def pair_z_kernel(weights, *refs):
    whole_ref, matrix_ref, pair_ref = refs[-3:]
    pl.when(pl.program_id(0) == 0)(lambda: fill_matrix(matrix_ref, rest_taps()))

    def use(rows, strip):
        pair_ref[rows, :] = strip

    unpacked(weights, refs[: len(weights)], use)
    whole_ref[0] = x_smoothed(pair_ref[...], matrix_ref[...])


def y_kernel(before_ref, whole_ref, after_ref, c_ref, detail_ref, coarse_ref):
    scale = 1.0 / 16.0
    for within in range(TAP_DILATION // STRIP):
        groups = y_sums(extended_groups(before_ref, whole_ref, after_ref, within * STRIP))
        for group, strip in enumerate(groups):
            rows = pl.ds(group * TAP_DILATION + within * STRIP, STRIP)
            coarse = strip * scale
            coarse_ref[0, rows, :] = coarse
            detail_ref[0, rows, :] = c_ref[0, rows, :] - coarse


def finish_kernel(weights, *refs):
    c_ref, _, _, detail_ref, coarse_ref = refs[len(weights) :]

    def use(rows, strip):
        coarse_ref[0, rows, :] = strip
        detail_ref[0, rows, :] = c_ref[0, rows, :] - strip

    unpacked(weights, refs[: len(weights)], use)


def last_kernel(weights, place, *refs):
    units_ref, _, _, detail_ref, coarse_ref, results_ref, write_sems = refs[len(weights) :]
    half = UNIT_ROWS // 2

    def write(piece, output, ref):
        rows = pl.ds(piece * half, half)
        source = results_ref.at[output, rows]
        return pltpu.make_async_copy(source, ref.at[place, rows], write_sems.at[piece, output])

    writes = [[write(piece, 0, detail_ref), write(piece, 1, coarse_ref)] for piece in range(2)]

    def use(rows, strip):
        results_ref[1, rows, :] = strip
        results_ref[0, rows, :] = units_ref[place, rows, :] - strip
        piece, left = divmod(rows.start + rows.size, half)
        if left == 0:
            for copy in writes[piece - 1]:
                copy.start()

    unpacked(weights, refs[: len(weights)], use)
    for copies in writes:
        for copy in copies:
            copy.wait()


def block_of(rows, width, first=0, depth=1):
    return pl.BlockSpec((depth, rows, width), lambda step: (first + step, 0, 0))


def anywhere():
    return pl.BlockSpec(memory_space=pl.ANY)


def tiles_of(pieces):
    return pl.BlockSpec((pieces, STRIP, LANES), lambda step: (0, 0, 0))


def in_vmem():
    return pl.BlockSpec(memory_space=pltpu.VMEM)


def call(kernel, name, steps, in_specs, out_specs, out_shape, args, aliases=None, scratch=(), grant=24):
    blocks = [spec.block_shape for spec in (*in_specs, *out_specs) if spec.block_shape]
    moved = 4 * max(steps, 1) * sum(math.prod(block) for block in blocks)
    return pl.pallas_call(
        kernel,
        grid=(steps,) if steps else (),
        in_specs=in_specs,
        out_specs=out_specs,
        out_shape=out_shape,
        scratch_shapes=scratch,
        input_output_aliases=aliases or {},
        compiler_params=pltpu.CompilerParams(vmem_limit_bytes=grant * 1024 * 1024),
        cost_estimate=pl.CostEstimate(flops=moved * 2, bytes_accessed=moved, transcendentals=0),
        name=name,
    )(*args)


def in_hbm(x):
    return pltpu.with_memory_space_constraint(x, pltpu.HBM)


def f32(*shape):
    return jax.ShapeDtypeStruct(shape, jnp.float32)


def can_shorten(rows, width):
    strips = TAP_DILATION // STRIP
    return lax.axis_size("gy") == strips and rows // TAP_DILATION % 2 == 0 and UNIT_ROWS // STRIP == width // TAP_DILATION


def shards(coarse_six):
    planes, rows, width = coarse_six.shape
    short = packed_rows(width)
    own, shifts = z_taps(planes, lax.axis_size("gz"))
    weights = (own, *shifts.values())
    count = len(weights)
    whole, unit, packed, edge = (functools.partial(block_of, n, width) for n in (rows, UNIT_ROWS, short, REACH))
    parts = rows // UNIT_ROWS
    units = coarse_six.reshape(planes * parts, UNIT_ROWS, width)
    matrix = pltpu.VMEM((width, width), jnp.bfloat16)

    def along_gz(x):
        return [passed_along(x, "gz", moved) for moved in shifts]

    def swapped(top, bottom):
        return passed_along(bottom, "gy", 1), passed_along(top, "gy", -1)

    def halo(source, start, stop):
        return swapped(source[start:stop, :REACH], source[start:stop, rows - REACH :])

    sums_shape = f32(FIRST_PLANES * parts, UNIT_ROWS, width)
    lead = call(
        pair_kernel,
        "pair_x",
        0,
        [anywhere()],
        [in_vmem()],
        [pltpu.VMEM((LEAD_UNITS, short, width), jnp.float32)],
        [in_hbm(units)],
        scratch=[pltpu.VMEM((LEAD_UNITS, UNIT_ROWS, width), jnp.float32), pltpu.SemaphoreType.DMA(())],
    )[0]
    lead, ready = lax.optimization_barrier((lead, units))
    lead_moved = along_gz(lead)
    first = FIRST_PLANES * parts - LEAD_UNITS
    edge_planes = range(FIRST_PLANES, planes)
    sizes_of = [sum(size for size, _ in sizes) for sizes in LATER_GROUPS]
    edge_shapes = [pltpu.VMEM((size, REACH, width), jnp.float32) for size in sizes_of for _ in range(2)]
    first_block, *edges = call(
        functools.partial(x_kernel, LEAD_UNITS, parts, edge_planes),
        "smooth_x",
        0,
        [anywhere()],
        [in_vmem()] * (1 + len(edge_shapes)),
        [pltpu.VMEM((first, short, width), jnp.float32), *edge_shapes],
        [in_hbm(ready)],
        scratch=[
            pltpu.VMEM((first, UNIT_ROWS, width), jnp.float32),
            matrix,
            pltpu.SemaphoreType.DMA((first,)),
            pltpu.SemaphoreType.DMA((len(edge_planes), 2)),
        ],
    )
    first_block, ready = lax.optimization_barrier((first_block, coarse_six))
    first_moved = along_gz(first_block)
    sums = call(
        functools.partial(pair_z_kernel, weights),
        "smooth_zx",
        LEAD_UNITS,
        [packed()] * count,
        [unit()],
        [sums_shape],
        [lead, *lead_moved],
        scratch=[matrix, pltpu.VMEM((UNIT_ROWS, width), jnp.float32)],
    )

    later, short_sent = [], []
    start = FIRST_PLANES
    edges = list(zip(edges[::2], edges[1::2]))
    near = swapped(*edges[0])
    near, sums = lax.optimization_barrier((near, sums))
    for number, sizes in enumerate(LATER_GROUPS):
        offset = 0
        for size, messages in sizes:
            place = start + offset
            sources = [near[0], in_hbm(coarse_six), near[1]]
            specs = [edge(offset), whole(place), edge(offset)]
            scratch = [matrix, pltpu.VMEM((rows, width), jnp.float32)]
            if messages or not can_shorten(rows, width):
                messages = max(messages, 1)
                depth = parts // messages
                blocks = call(
                    yx_kernel,
                    "smooth_yx",
                    size,
                    specs,
                    [packed(depth=depth)] * messages,
                    [f32(size * depth, short, width)] * messages,
                    sources,
                    scratch=scratch,
                )
                for message, block in enumerate(blocks):
                    last_block = block
                    later.append((place * parts + message * depth, size * depth, (block, *along_gz(block))))
            else:
                pieces = size * short_tiles(rows, width) + 1
                block = call(
                    short_kernel,
                    "smooth_yx_short",
                    size,
                    specs,
                    [tiles_of(pieces)],
                    [f32(pieces, STRIP, LANES)],
                    sources,
                    scratch=scratch,
                )[0]
                short_sent.append((place, size, (block, *along_gz(block))))
            offset += size
        start += offset
        if number == 0:
            block, ready = lax.optimization_barrier((block, ready))
            block, *first_moved = lax.optimization_barrier((block, *first_moved))
            sums = call(
                functools.partial(z_kernel, weights),
                "smooth_z",
                first,
                [packed()] * count + [anywhere()],
                [unit(LEAD_UNITS)],
                [sums_shape],
                [first_block, *first_moved, *sums],
                {count: 0},
            )[0]
            along_z = sums.reshape(FIRST_PLANES, rows, width)
            along_z, edges[1] = lax.optimization_barrier((along_z, edges[1]))
        if number + 1 < len(LATER_GROUPS):
            block, edges[number + 1] = lax.optimization_barrier((block, edges[number + 1]))
            near = swapped(*edges[number + 1])
        if number == 1:
            first_near, along_z, _ = lax.optimization_barrier((near[0], along_z, short_sent[0][2]))
            near = (first_near, near[1])
            sides = halo(along_z, 0, FIRST_PLANES)
        if number == 0:
            near, along_z = lax.optimization_barrier((near, along_z))

    def sum_short(batch):
        planes_in = sum(size for _, size, _ in batch)
        step, sums = 0, []
        for _, size, blocks in batch:
            sums = call(
                functools.partial(short_z_kernel, weights),
                "smooth_z_short",
                size,
                [tiles_of(blocks[0].shape[0])] * count + [anywhere()] * len(sums),
                [whole(step)] + [block_of(STRIP, width, step)] * 3,
                [f32(planes_in, rows, width)] + [f32(planes_in, STRIP, width)] * 3,
                [*blocks, *sums],
                {count + at: at for at in range(len(sums))},
            )
            step += size
        return sums[0], [passed_along(total, "gy", ahead) for ahead, total in enumerate(sums[1:], 1)]

    def finish_short(batch, sums, outs):
        start, size = batch[0][0], sum(size for _, size, _ in batch)
        along_z, moved = sums
        outs, moved = lax.optimization_barrier((outs, moved))
        return call(
            short_finish_kernel,
            "finish_short",
            size,
            [whole()] + [block_of(STRIP, width)] * 3 + [whole(start)] + [anywhere()] * 2,
            [whole(start)] * 2,
            [f32(planes, rows, width)] * 2,
            [along_z, *moved, coarse_six, *outs],
            {5: 0, 6: 1},
        )

    batches = [batch for batch in (short_sent[:SHORT_FIRST], short_sent[SHORT_FIRST:]) if batch]
    batch = batches[0]
    short_sums = sum_short(batch)
    short_whole, sides = lax.optimization_barrier((short_sums[0], sides))
    outs = call(
        y_kernel,
        "smooth_y",
        FIRST_PLANES,
        [edge(), whole(), edge(), whole()],
        [whole(), whole()],
        [f32(planes, rows, width)] * 2,
        [sides[0], along_z, sides[1], coarse_six],
    )
    short_sums, last_block = lax.optimization_barrier(((short_whole, short_sums[1]), last_block))
    last_moved = along_gz(last_block)
    outs = finish_short(batch, short_sums, outs)
    outs = [out.reshape(units.shape) for out in outs]
    for place, size, blocks in later[:-1]:
        outs, blocks = lax.optimization_barrier((outs, blocks))
        outs = call(
            functools.partial(finish_kernel, weights),
            "finish",
            size,
            [packed()] * count + [unit(place)] + [anywhere()] * 2,
            [unit(place)] * 2,
            [f32(*units.shape)] * 2,
            [*blocks, units, *outs],
            {count + 1: 0, count + 2: 1},
        )
    place = later[-1][0]
    blocks = (last_block, *last_moved)
    outs, blocks = lax.optimization_barrier((outs, blocks))
    outs = call(
        functools.partial(last_kernel, weights, place),
        "finish_last",
        0,
        [in_vmem()] * (count + 1) + [anywhere()] * 2,
        [anywhere()] * 2,
        [f32(*units.shape)] * 2,
        [*blocks, units, *outs],
        {count + 1: 0, count + 2: 1},
        scratch=[
            pltpu.VMEM((2, UNIT_ROWS, width), jnp.float32),
            pltpu.SemaphoreType.DMA((2, 2)),
        ],
    )
    return tuple(out.reshape(coarse_six.shape) for out in outs)


def solution(mesh):
    return jax.shard_map(
        shards,
        mesh=mesh,
        in_specs=(P("gz", "gy", None),),
        out_specs=(P("gz", "gy", None), P("gz", "gy", None)),
        check_vma=False,
    )
```
